32 devices in a mesh: dp: 4 (over y, x), mp: 8 (over z, core).
Axes of the slice: x: 2, y: 2, z: 4, core: 2. Of those that a mesh axis runs over, the one named last changes fastest.
Arguments:
- features: bfloat16 [2, 5120, 9216], P(None, 'dp', 'mp'), may hold values from -6 to 6
- counts: int32 [512], P('dp'), may hold values from 1 to 10, as said below
- weights: float32 [2, 9216, 4096], P(None, 'dp', 'mp'), may hold values from -0.09375 to 0.09375
- small_params: float32 [6, 4096], P(None, 'mp'), may hold values from 0.2 to 1
- out_grad: bfloat16 [2, 5120, 4096], P(None, 'dp', 'mp'), may hold values from -6 to 6
- moment_one: float32 [2, 9216, 4096], P(None, 'dp', 'mp'), may hold values from -128 to 128
- moment_two: float32 [2, 9216, 4096], P(None, 'dp', 'mp'), may hold values from 512 to 2048
- average: float32 [2, 9216, 4096], P(None, 'dp', 'mp'), may hold values from -0.0625 to 0.0625
- basis_left: float32 [2, 144, 64, 64, 64], P(None, 'dp', 'mp'), may hold values from -0.75 to 0.75
- basis_right: float32 [2, 144, 64, 64, 64], P(None, 'dp', 'mp'), may hold values from -0.75 to 0.75
- small_moment_one: float32 [6, 4096], P(None, 'mp'), may hold values from -128 to 128
- small_moment_two: float32 [6, 4096], P(None, 'mp'), may hold values from 512 to 2048
- small_average: float32 [6, 4096], P(None, 'mp'), may hold values from 0.2 to 1
Outputs:
- stitched: bfloat16 [2, 5120, 4096], P(None, 'dp')
- d_features: bfloat16 [2, 5120, 9216], P(None, 'dp', 'mp')
- new_moment_one: float32 [2, 9216, 4096], P(None, 'dp', 'mp')
- new_moment_two: float32 [2, 9216, 4096], P(None, 'dp', 'mp')
- new_weights: float32 [2, 9216, 4096], P(None, 'dp', 'mp')
- new_average: float32 [2, 9216, 4096], P(None, 'dp', 'mp')
- weights_copy: bfloat16 [2, 9216, 4096], P(None, 'dp', 'mp')
- small_new_one: float32 [6, 4096], P(None, 'mp')
- small_new_two: float32 [6, 4096], P(None, 'mp')
- small_new: float32 [6, 4096], P(None, 'mp')
- small_new_average: float32 [6, 4096], P(None, 'mp')
The draws below stay inside these ranges and needn't reach their ends.
Inputs may be any that keep to these rules, and one draw needn't show every extreme that they name: `counts`: the images of one index of dp hold at most 1280 crops together, and some index holds exactly 1280; some image has 10 crops and some has 1.
All inputs are finite; a program needn't handle non-finite values.
Results may differ from the reference program's by a relative error of at most 0.0061.
Values may be sent and summed in bfloat16 or wider, within the bound.
A program may use at most 512 MiB of HBM per device.

```python
import math
import jax
import jax.numpy as jnp
from jax import lax

IN = 9216
OUT = 4096
IMG_DEV = 128
MAXC = 10
BLOCK = 64
STEP = 5
ROWS_DEV = 1280
ROWS = 5120
IMAGES = 512
N_DP = 4


def draw_counts(key, part):
    key = jax.random.fold_in(key, 11)
    where = jnp.arange(IMAGES, dtype=jnp.int32)
    owner = where // IMG_DEV
    ceiling = 3 + 7 * owner // (N_DP - 1)
    raw = jax.random.randint(key, (IMAGES,), 0, 1 << 20, dtype=jnp.int32)
    values = raw % ceiling + 1
    values = jnp.where(owner == N_DP - 1, MAXC, values)
    values = jnp.where(where == 0, 1, values)
    return values.astype(jnp.int32)


def spiked(array, rng, source, target, shards_of, factor):
    owner, partner = [(jnp.arange(array.shape[dim]) // (array.shape[dim] // shards_of)).reshape([-1 if axis == dim else 1 for axis in range(array.ndim)]) for dim in (source, target)]
    chosen = jax.random.permutation(rng, shards_of)[partner]
    strong = (owner == chosen) | (owner == (partner + shards_of // 2) % shards_of)
    return jnp.where(strong, factor * array, array)


def level_of(rng, shape, split, smallest, high):
    gain, own = 1.0, jax.random.fold_in(rng, 6)
    for position, blocks in split:
        heights = jnp.exp(jax.random.uniform(jax.random.fold_in(own, position), (blocks,), jnp.float32, smallest / len(split), high / len(split)))
        gain = gain * jnp.repeat(heights, shape[position] // blocks).reshape([-1 if axis == position else 1 for axis in range(len(shape))])
    return gain


def centred(own_key, dims, width, limit, shards=(), kind=jnp.bfloat16):
    values = jax.random.normal(own_key, dims, jnp.float32) * width
    if len(shards) > 0:
        values = level_of(own_key, dims, shards, -0.22, 0.18) * values
    return jnp.clip(values, min=-limit, max=limit).astype(kind)


def bell_draw_with(stream_key, dims, deviation, bound, cuts, heavy, held_as=jnp.bfloat16):
    array = deviation * jax.random.normal(stream_key, dims, jnp.float32)
    if cuts:
        array = array * level_of(stream_key, dims, cuts, -0.22, 0.18)
    return jnp.clip(spiked(array, jax.random.fold_in(stream_key, 3), *heavy), -bound, bound).astype(held_as)


def setup_inputs(seed: int = 0) -> dict:
    seeds = jax.random.split(jax.random.key(seed), 14)
    return {
        "features": centred(seeds[0], (2, ROWS, IN), 1.0, 6.0, ((1, 4), (2, 8))),
        "counts": draw_counts(jax.random.fold_in(seeds[13], 71), 0),
        "weights": bell_draw_with(seeds[2], (2, IN, OUT), IN ** -0.5, 0.09375, ((1, 4), (2, 8)), (2, 1, 8, 2.0), jnp.float32),
        "small_params": jnp.clip(0.2 + 0.8 * jax.random.uniform(seeds[3], (6, OUT), jnp.float32) ** level_of(seeds[3], (6, OUT), ((1, 8),), -0.2, 0.2), 0.2, 1.0),
        "out_grad": centred(seeds[4], (2, ROWS, OUT), 1.0, 6.0, ((1, 4), (2, 8))),
        "moment_one": centred(seeds[5], (2, IN, OUT), ((0.1 * ROWS_DEV * N_DP) ** 0.5), 128.0, ((1, 4), (2, 8)), jnp.float32),
        "moment_two": jnp.clip(jnp.exp(math.log(2048.0) - 1.3862944 * jax.random.uniform(seeds[6], (2, IN, OUT), jnp.float32) ** level_of(seeds[6], (2, IN, OUT), ((1, 4), (2, 8)), -0.2, 0.2)), 512.0, 2048.0),
        "average": centred(seeds[7], (2, IN, OUT), IN ** -0.5, 0.0625, ((1, 4), (2, 8)), jnp.float32),
        "basis_left": centred(seeds[8], (2, IN // BLOCK, OUT // BLOCK, BLOCK, BLOCK), BLOCK ** -0.5, 0.75, ((1, 4), (2, 8)), jnp.float32),
        "basis_right": centred(seeds[9], (2, IN // BLOCK, OUT // BLOCK, BLOCK, BLOCK), BLOCK ** -0.5, 0.75, ((1, 4), (2, 8)), jnp.float32),
        "small_moment_one": centred(seeds[10], (6, OUT), ((0.1 * ROWS_DEV * N_DP) ** 0.5), 128.0, ((1, 8),), jnp.float32),
        "small_moment_two": jnp.clip(jnp.exp(math.log(2048.0) - 1.3862944 * jax.random.uniform(seeds[11], (6, OUT), jnp.float32) ** level_of(seeds[11], (6, OUT), ((1, 8),), -0.2, 0.2)), 512.0, 2048.0),
        "small_average": jnp.clip(0.2 + 0.8 * jax.random.uniform(seeds[12], (6, OUT), jnp.float32) ** level_of(seeds[12], (6, OUT), ((1, 8),), -0.2, 0.2), 0.2, 1.0),
    }


beta_one = 0.5
beta_two = 0.5
ema_decay = 0.5
rate_main = 0.01
rate_small = 0.05
decay_weight = 0.01
eps = 1e-08

@jax.custom_vjp
def low(v):
    return lax.optimization_barrier(v.astype(jnp.bfloat16)).astype(jnp.float32)

@jax.custom_vjp
def low_back(v):
    return v

def low_keep(v):
    return (low(v), None)

def low_pass(kept, grad):
    return (grad,)

def back_keep(v):
    return (v, None)

def back_low(kept, grad):
    return (low(grad),)
low.defvjp(low_keep, low_pass)
low_back.defvjp(back_keep, back_low)

def forward(feats, weight_full, small, live_rows):
    product = jnp.einsum('tri,tio->tro', feats, low(weight_full), precision=lax.Precision.HIGHEST)
    pre_act = low_back(product) + small[0:2][:, None, :]
    activated = jax.nn.gelu(pre_act, approximate=True)
    first = small[2] * activated[0] + small[3] * activated[1]
    second = small[4] * activated[0] + small[5] * activated[1]
    return jnp.stack([first, second]) * live_rows[None, :, None]

def adam_part(moment_a, moment_b, grad):
    first = beta_one * moment_a + (1.0 - beta_one) * grad
    second = beta_two * moment_b + (1.0 - beta_two) * grad * grad
    direction = first / (1.0 - beta_one ** STEP) / (jnp.sqrt(second / (1.0 - beta_two ** STEP)) + eps)
    return (first, second, direction)

def reference(features, counts, weights, small_params, out_grad, moment_one, moment_two, average, basis_left, basis_right, small_moment_one, small_moment_two, small_average):
    totals = lax.optimization_barrier(jnp.sum(counts.reshape(N_DP, IMG_DEV), axis=1))
    live_rows = (jnp.arange(ROWS_DEV, dtype=jnp.int32)[None, :] < totals[:, None]).reshape(-1).astype(jnp.float32)
    feats = features.astype(jnp.float32)
    result, back = jax.vjp(lambda a, b, c: forward(a, b, c, live_rows), feats, weights, small_params)
    d_feat, grad, small_grad = back(out_grad.astype(jnp.float32))
    towers, n_in, n_out = grad.shape
    blocks = grad.reshape(towers, n_in // BLOCK, BLOCK, n_out // BLOCK, BLOCK)
    rotated = jnp.einsum('trcai,tracb,trcbj->tricj', basis_left, blocks, basis_right, precision=lax.Precision.HIGHEST).reshape(towers, n_in, n_out)
    first, second, direction = adam_part(moment_one, moment_two, rotated)
    turned = direction.reshape(towers, n_in // BLOCK, BLOCK, n_out // BLOCK, BLOCK)
    step_back = jnp.einsum('trcai,tricj,trcbj->tracb', basis_left, turned, basis_right, precision=lax.Precision.HIGHEST).reshape(towers, n_in, n_out)
    new_weights = weights - rate_main * (step_back + decay_weight * weights)
    new_average = ema_decay * average + (1.0 - ema_decay) * new_weights
    small_first, small_second, small_dir = adam_part(small_moment_one, small_moment_two, small_grad)
    small_new = small_params - rate_small * small_dir
    small_avg_new = ema_decay * small_average + (1.0 - ema_decay) * small_new
    return (result.astype(jnp.bfloat16), d_feat.astype(jnp.bfloat16), first, second, new_weights, new_average, new_weights.astype(jnp.bfloat16), small_first, small_second, small_new, small_avg_new)
```

```python
import jax
import jax.numpy as jnp
from jax import lax
from jax.sharding import PartitionSpec as P

BLOCK = 64
STEP = 5


beta_one = 0.5
beta_two = 0.5
ema_decay = 0.5
rate_main = 0.01
rate_small = 0.05
decay_weight = 0.01
eps = 1e-08


def stitch_local(product, small, live_rows):
    pre_act = product + small[0:2][:, None, :]
    activated = jax.nn.gelu(pre_act, approximate=True)
    first = small[2] * activated[0] + small[3] * activated[1]
    second = small[4] * activated[0] + small[5] * activated[1]
    return jnp.stack([first, second]) * live_rows[None, :, None]


def adam_part(moment_a, moment_b, grad):
    first = beta_one * moment_a + (1.0 - beta_one) * grad
    second = beta_two * moment_b + (1.0 - beta_two) * grad * grad
    direction = first / (1.0 - beta_one**STEP) / (jnp.sqrt(second / (1.0 - beta_two**STEP)) + eps)
    return (first, second, direction)


def body(
    features,
    counts,
    weights,
    small_params,
    out_grad,
    moment_one,
    moment_two,
    average,
    basis_left,
    basis_right,
    small_moment_one,
    small_moment_two,
    small_average,
):
    slot_count = features.shape[1]
    total = jnp.sum(counts)
    live_rows = (jnp.arange(slot_count, dtype=jnp.int32) < total).astype(jnp.float32)
    weights_low = lax.all_gather(weights.astype(jnp.bfloat16), "dp", axis=1, tiled=True)
    feats_full = lax.all_gather(features, "mp", axis=2, tiled=True)
    product = jnp.einsum(
        "tri,tio->tro", feats_full, weights_low, preferred_element_type=jnp.float32
    )
    result, back = jax.vjp(lambda a, b: stitch_local(a, b, live_rows), product, small_params)
    stitched = lax.all_gather(result.astype(jnp.bfloat16), "mp", axis=2, tiled=True)
    dz, small_part = back(out_grad.astype(jnp.float32))
    dz_low = dz.astype(jnp.bfloat16)
    grad_part = jnp.einsum("tri,tro->tio", feats_full, dz_low, preferred_element_type=jnp.float32)
    partial_sums = jnp.einsum(
        "tro,tio->tri", dz_low, weights_low, preferred_element_type=jnp.float32
    )
    d_feat = lax.psum_scatter(
        partial_sums.astype(jnp.bfloat16), "mp", scatter_dimension=2, tiled=True
    )
    grad = lax.psum_scatter(
        grad_part.astype(jnp.bfloat16), "dp", scatter_dimension=1, tiled=True
    ).astype(jnp.float32)
    small_grad = lax.psum(small_part, "dp")
    towers, n_in, n_out = grad.shape
    blocks = grad.reshape(towers, n_in // BLOCK, BLOCK, n_out // BLOCK, BLOCK)
    rotated = jnp.einsum(
        "trcai,tracb,trcbj->tricj", basis_left, blocks, basis_right, precision=lax.Precision.HIGHEST
    ).reshape(towers, n_in, n_out)
    first, second, direction = adam_part(moment_one, moment_two, rotated)
    turned = direction.reshape(towers, n_in // BLOCK, BLOCK, n_out // BLOCK, BLOCK)
    step_back = jnp.einsum(
        "trcai,tricj,trcbj->tracb", basis_left, turned, basis_right, precision=lax.Precision.HIGHEST
    ).reshape(towers, n_in, n_out)
    new_weights = weights - rate_main * (step_back + decay_weight * weights)
    new_average = ema_decay * average + (1.0 - ema_decay) * new_weights
    small_first, small_second, small_dir = adam_part(small_moment_one, small_moment_two, small_grad)
    small_new = small_params - rate_small * small_dir
    small_avg_new = ema_decay * small_average + (1.0 - ema_decay) * small_new
    return (
        stitched,
        d_feat.astype(jnp.bfloat16),
        first,
        second,
        new_weights,
        new_average,
        new_weights.astype(jnp.bfloat16),
        small_first,
        small_second,
        small_new,
        small_avg_new,
    )


def solution(mesh):
    return jax.shard_map(
        body,
        mesh=mesh,
        in_specs=(
            P(None, "dp", "mp"),
            P("dp"),
            P(None, "dp", "mp"),
            P(None, "mp"),
            P(None, "dp", "mp"),
            P(None, "dp", "mp"),
            P(None, "dp", "mp"),
            P(None, "dp", "mp"),
            P(None, "dp", "mp", None, None),
            P(None, "dp", "mp", None, None),
            P(None, "mp"),
            P(None, "mp"),
            P(None, "mp"),
        ),
        out_specs=(
            P(None, "dp", None),
            P(None, "dp", "mp"),
            P(None, "dp", "mp"),
            P(None, "dp", "mp"),
            P(None, "dp", "mp"),
            P(None, "dp", "mp"),
            P(None, "dp", "mp"),
            P(None, "mp"),
            P(None, "mp"),
            P(None, "mp"),
            P(None, "mp"),
        ),
        check_vma=False,
    )
```

```python
import functools

import jax
import jax.numpy as jnp
from jax import lax
from jax.experimental import pallas as pl
from jax.experimental.pallas import tpu as pltpu
from jax.sharding import PartitionSpec as P

BLOCK = 64
STEP = 5


beta_one = 0.5
beta_two = 0.5
ema_decay = 0.5
rate_main = 0.01
rate_small = 0.05
decay_weight = 0.01
eps = 1e-08


def stitch_local(product, small, live_rows):
    pre_act = product + small[0:2][:, None, :]
    activated = jax.nn.gelu(pre_act, approximate=True)
    first = small[2] * activated[0] + small[3] * activated[1]
    second = small[4] * activated[0] + small[5] * activated[1]
    return jnp.stack([first, second]) * live_rows[None, :, None]


def adam_part(moment_a, moment_b, grad):
    first = beta_one * moment_a + (1.0 - beta_one) * grad
    second = beta_two * moment_b + (1.0 - beta_two) * grad * grad
    direction = first / (1.0 - beta_one**STEP) / (jnp.sqrt(second / (1.0 - beta_two**STEP)) + eps)
    return (first, second, direction)

def split(v):
    high = v.astype(jnp.bfloat16)
    return high, (v - high.astype(jnp.float32)).astype(jnp.bfloat16)

def soap_pair(grad, left, right, moment_a, moment_b):
    row = lax.broadcasted_iota(jnp.int32, (2 * BLOCK, 2 * BLOCK), 0) // BLOCK
    lane = lax.broadcasted_iota(jnp.int32, (2 * BLOCK, 2 * BLOCK), 1) // BLOCK
    own = row == lane
    def diagonal(v):
        return jnp.where(own, jnp.concatenate([v, v], axis=0), 0.0)
    def beside(v):
        return jnp.concatenate([v[0], v[1]], axis=1)
    def dot(a, b, ca, cb):
        return lax.dot_general(a, b, (((ca,), (cb,)), ((), ())), preferred_element_type=jnp.float32)
    right_high, right_low = split(diagonal(beside(right)))
    left_high, left_low = split(beside(left))
    up_high, up_low = split(left.reshape(2 * BLOCK, BLOCK))
    def turn(v, cb):
        high, low = split(v)
        return (dot(jnp.concatenate([high, low], axis=1), jnp.concatenate([right_high, right_high], axis=cb), 1, cb)
                + dot(high, right_low, 1, cb))
    high, low = split(diagonal(turn(grad, 0)))
    rotated = dot(jnp.concatenate([up_high, up_high, up_low], axis=0), jnp.concatenate([high, low, high], axis=0), 0, 0)
    first, second, direction = adam_part(moment_a, moment_b, rotated)
    high, low = split(diagonal(turn(direction, 1)))
    step = dot(jnp.concatenate([left_high, left_high, left_low], axis=1), jnp.concatenate([high, low, high], axis=0), 1, 0)
    return first, second, step

def soap_body(parts, weights, moment_a, moment_b, average, left, right, first, second, new_weights, new_average, copy):
    groups, pairs = left.shape[1], left.shape[2] // 2
    def strip(g, _):
        rows = pl.ds(pl.multiple_of(g * BLOCK, BLOCK), BLOCK)
        for q in range(pairs):
            cols = pl.ds(2 * BLOCK * q, 2 * BLOCK)
            at = (0, rows, cols)
            grad = parts[(0, 0) + at].astype(jnp.float32)
            for k in range(1, parts.shape[0]):
                grad = grad + parts[(k, 0) + at].astype(jnp.float32)
            one, two, step = soap_pair(grad, left[0, g, 2 * q:2 * q + 2], right[0, g, 2 * q:2 * q + 2], moment_a[at], moment_b[at])
            first[at] = one
            second[at] = two
            held = weights[at]
            fresh = held - rate_main * (step + decay_weight * held)
            new_weights[at] = fresh
            new_average[at] = ema_decay * average[at] + (1.0 - ema_decay) * fresh
            copy[at] = fresh.astype(jnp.bfloat16)
        return 0
    lax.fori_loop(0, groups, strip, 0)

def soap(parts, weights, moment_a, moment_b, average, left, right, group=3):
    towers, rows, cols = weights.shape
    half = parts.shape[3]
    steps = half // (BLOCK * group)
    flat = lambda t, p, g: (t, p * steps + g, 0)
    basis = lambda t, p, g: (t, p * steps + g, 0, 0, 0)
    state = pl.BlockSpec((1, BLOCK * group, cols), flat)
    base = pl.BlockSpec((1, group, cols // BLOCK, BLOCK, BLOCK), basis)
    full = jax.ShapeDtypeStruct(weights.shape, jnp.float32)
    return pl.pallas_call(
        soap_body,
        grid=(towers, 2, steps),
        in_specs=[pl.BlockSpec((parts.shape[0], 1, 1, BLOCK * group, cols), lambda t, p, g: (0, p, t, g, 0)),
                  state, state, state, state, base, base],
        out_specs=[state] * 5,
        out_shape=[full] * 4 + [jax.ShapeDtypeStruct(weights.shape, jnp.bfloat16)],
        compiler_params=pltpu.CompilerParams(vmem_limit_bytes=48 * 2**20),
        cost_estimate=pl.CostEstimate(flops=8 * 2 * towers * rows * cols * 64, bytes_accessed=130 * 2**20, transcendentals=0),
        name="soap",
    )(parts, weights, moment_a, moment_b, average, left, right)


MESH = pl.DeviceIdType.MESH


def place():
    mp = lax.axis_index("mp")
    return lax.axis_index("dp"), mp // 2, lax.rem(mp, 2)


def meet(devices):
    barrier = pltpu.get_barrier_semaphore()
    expected = 0
    for here, device in devices:
        @pl.when(here)
        def _():
            pl.semaphore_signal(barrier, inc=1, device_id=device, device_id_type=MESH)
        expected = expected + jnp.where(here, 1, 0)
    pl.semaphore_wait(barrier, expected)


def gather_kernel(chips, chunks, f_ref, w_ref, fg_ref, wg_ref, f_send, f_recv, w_send, w_recv, own_sem):
    dp, chip, core = place()
    towers, rows, depth = f_ref.shape
    cols = w_ref.shape[2]
    part = rows // chunks
    across, along = dp ^ 1, dp ^ 2
    at = lambda c, k: (c, 2 * chip + k)

    meet([(chip > 0, (dp, 2 * (chip - 1) + core)), (chip < chips - 1, (dp, 2 * (chip + 1) + core)),
          (chip >= 0, at(dp, 1 - core))] + [(chip >= 0, at(c, k)) for c in (across, along) for k in (0, 1)])

    def feature(step, way, t, k):
        shard = chip - step if way == 0 else chip + step
        there = chip + 1 if way == 0 else chip - 1
        lanes = pl.ds(pl.multiple_of(shard * depth, 128), depth)
        rws = pl.ds(k * part, part)
        src = f_ref.at[t, rws] if step == 0 else fg_ref.at[t, rws, lanes]
        n = ((way * (chips - 1) + step) * towers + t) * chunks + k
        return pltpu.make_async_remote_copy(
            src_ref=src, dst_ref=fg_ref.at[t, rws, lanes], send_sem=f_send.at[n], recv_sem=f_recv.at[n],
            device_id=(dp, 2 * there + core), device_id_type=MESH)

    def sends(step, way):
        return (chip < chips - 1) & (chip >= step) if way == 0 else (chip > 0) & (chip + step < chips)

    def receives(step, way):
        return chip > step if way == 0 else chip + step < chips - 1

    def incoming(step, way, t, k):
        shard = chip - 1 - step if way == 0 else chip + 1 + step
        lanes = pl.ds(pl.multiple_of(shard * depth, 128), depth)
        rws = pl.ds(k * part, part)
        n = ((way * (chips - 1) + step) * towers + t) * chunks + k
        return pltpu.make_async_remote_copy(
            src_ref=f_ref.at[t, rws], dst_ref=fg_ref.at[t, rws, lanes], send_sem=f_send.at[n], recv_sem=f_recv.at[n],
            device_id=(dp, 2 * chip + core), device_id_type=MESH)

    def block(owner, slot, t):
        return wg_ref.at[t, pl.ds(pl.multiple_of(owner * depth, 128), depth), pl.ds(pl.multiple_of(slot * cols, 128), cols)]

    def weight(kind, k, t):
        to = at((across, along, dp)[kind], k)
        n = (kind * 2 + core) * 2 + t
        return pltpu.make_async_remote_copy(
            src_ref=w_ref.at[t, pl.ds(pl.multiple_of(k * depth, 128), depth)], dst_ref=block(dp, k ^ core, t),
            send_sem=w_send.at[(kind * 2 + k) * 2 + t], recv_sem=w_recv.at[n], device_id=to, device_id_type=MESH)

    def forward(kind, slot):
        owner, to, t = ((across, along, 0), (along, across, 1))[kind]
        n = 12 + kind * 2 + slot
        return pltpu.make_async_remote_copy(
            src_ref=block(owner, slot, t), dst_ref=block(owner, slot, t),
            send_sem=w_send.at[n], recv_sem=w_recv.at[n], device_id=at(to, core), device_id_type=MESH)

    def arrived(kind, slot, t):
        owner = (across, along, dp)[kind]
        n = (kind * 2 + (slot ^ core)) * 2 + t
        pltpu.make_async_remote_copy(
            src_ref=block(owner, slot, t), dst_ref=block(owner, slot, t), send_sem=w_send.at[n], recv_sem=w_recv.at[n],
            device_id=at(dp, core), device_id_type=MESH).wait_recv()

    own = [pltpu.make_async_copy(f_ref.at[t], fg_ref.at[t, :, pl.ds(pl.multiple_of(chip * depth, 128), depth)], own_sem.at[t])
           for t in range(towers)]
    own += [pltpu.make_async_copy(w_ref.at[t, pl.ds(pl.multiple_of(core * depth, 128), depth)], block(dp, 0, t), own_sem.at[2 + t])
            for t in range(towers)]

    pieces = [(t, k) for t in range(towers) for k in range(chunks)]
    for t, k in pieces:
        for way in (0, 1):
            @pl.when(sends(0, way))
            def _():
                feature(0, way, t, k).start()
    for t in (0, 1):
        for k in (0, 1):
            weight(0, k, t).start()
            weight(1, k, 1 - t).start()
    for t in (0, 1):
        weight(2, 1 - core, t).start()
    for copy in own:
        copy.start()

    for step in range(chips - 1):
        for t, k in pieces:
            for way in (0, 1):
                @pl.when(receives(step, way))
                def _():
                    incoming(step, way, t, k).wait_recv()
                if step + 1 < chips - 1:
                    @pl.when(sends(step + 1, way))
                    def _():
                        feature(step + 1, way, t, k).start()
            if step == 0 and (t, k) == pieces[len(pieces) // 2 - 1]:
                for slot in (0, 1):
                    arrived(0, slot, 0)
                    forward(0, slot).start()
                    arrived(1, slot, 1)
                    forward(1, slot).start()

    for slot in (0, 1):
        arrived(0, slot, 1)
        arrived(1, slot, 0)
        forward(0, slot).wait_recv()
        forward(1, slot).wait_recv()
    for t in (0, 1):
        arrived(2, 1, t)
    for t in (0, 1):
        for k in (0, 1):
            weight(0, k, t).wait_send()
            weight(1, k, t).wait_send()
        weight(2, 1 - core, t).wait_send()
    for slot in (0, 1):
        forward(0, slot).wait_send()
        forward(1, slot).wait_send()
    for step in range(chips - 1):
        for t, k in pieces:
            for way in (0, 1):
                @pl.when(sends(step, way))
                def _():
                    feature(step, way, t, k).wait_send()
    for copy in own:
        copy.wait()


def gather(features, weights_low, chips, chunks, ident):
    towers, rows, depth = features.shape
    cols = weights_low.shape[2]
    count = 2 * (chips - 1) * towers * chunks
    dma = pltpu.SemaphoreType.DMA
    return pl.pallas_call(
        functools.partial(gather_kernel, chips, chunks),
        out_shape=[jax.ShapeDtypeStruct((towers, rows, chips * depth), jnp.bfloat16),
                   jax.ShapeDtypeStruct((towers, chips * depth, 2 * cols), jnp.bfloat16)],
        in_specs=[pl.BlockSpec(memory_space=pl.ANY)] * 2,
        out_specs=[pl.BlockSpec(memory_space=pl.ANY)] * 2,
        scratch_shapes=[dma((count,)), dma((count,)), dma((16,)), dma((16,)), dma((4,))],
        compiler_params=pltpu.CompilerParams(collective_id=ident, has_side_effects=True),
        cost_estimate=pl.CostEstimate(flops=0, bytes_accessed=800 * 2**20, transcendentals=0),
        name="gather",
    )(features, weights_low)


def reduce_kernel(chips, chunks, pd_ref, pg_ref, ps_ref, d_ref, gr_ref, sr_ref, held, term, total,
                  d_send, d_recv, t_sem, o_sem, g_send, g_recv, s_send, s_recv, own_sem):
    dp, chip, core = place()
    towers, rows, depth = d_ref.shape
    cols = pg_ref.shape[2] // 2
    part = rows // chunks
    across, along = dp ^ 1, dp ^ 2
    others = (across, along, 3 - dp)
    at = lambda c, k: (c, 2 * chip + k)

    meet([(chip > 0, (dp, 2 * (chip - 1) + core)), (chip < chips - 1, (dp, 2 * (chip + 1) + core)),
          (chip >= 0, at(dp, 1 - core))] + [(chip >= 0, at(c, k)) for c in others for k in (0, 1)])

    def grad(kind, k, t):
        owner = (others + (dp,))[kind]
        return pltpu.make_async_remote_copy(
            src_ref=pg_ref.at[t, pl.ds(pl.multiple_of(owner * depth, 128), depth), pl.ds(pl.multiple_of((k ^ core) * cols, 128), cols)],
            dst_ref=gr_ref.at[dp, core, t], send_sem=g_send.at[(kind * 2 + k) * 2 + t],
            recv_sem=g_recv.at[(kind * 2 + core) * 2 + t], device_id=at(owner, k), device_id_type=MESH)

    def grad_arrived(kind, k, t):
        owner = (others + (dp,))[kind]
        pltpu.make_async_remote_copy(
            src_ref=gr_ref.at[owner, k, t], dst_ref=gr_ref.at[owner, k, t], send_sem=g_send.at[0],
            recv_sem=g_recv.at[(kind * 2 + k) * 2 + t], device_id=at(dp, core), device_id_type=MESH).wait_recv()

    def small(kind):
        return pltpu.make_async_remote_copy(
            src_ref=ps_ref, dst_ref=sr_ref.at[dp], send_sem=s_send.at[kind], recv_sem=s_recv.at[kind],
            device_id=at(others[kind], core), device_id_type=MESH)

    def target(step, way):
        return chip + chips - 1 - step if way == 0 else chip - (chips - 1 - step)

    def sends(step, way):
        return (chip < chips - 1) & (chip <= step) if way == 0 else (chip > 0) & (chips - 1 - chip <= step)

    def receives(step, way):
        return (chip > 0) & (chip <= step + 1) if way == 0 else (chip < chips - 1) & (chips - 1 - chip <= step + 1)

    def own_term(goal, t, k):
        return pd_ref.at[t, pl.ds(k * part, part), pl.ds(pl.multiple_of(goal * depth, 128), depth)]

    def partial(step, way, t, k, first):
        n = ((way * (chips - 1) + step) * towers + t) * chunks + k
        src = own_term(target(step, way), t, k) if first else held.at[way, step - 1, t, pl.ds(k * part, part)]
        there = chip + 1 if way == 0 else chip - 1
        return pltpu.make_async_remote_copy(
            src_ref=src, dst_ref=held.at[way, step, t, pl.ds(k * part, part)], send_sem=d_send.at[n], recv_sem=d_recv.at[n],
            device_id=(dp, 2 * there + core), device_id_type=MESH)

    def landed(step, way, t, k):
        n = ((way * (chips - 1) + step) * towers + t) * chunks + k
        ref = held.at[way, step, t, pl.ds(k * part, part)]
        pltpu.make_async_remote_copy(src_ref=ref, dst_ref=ref, send_sem=d_send.at[n], recv_sem=d_recv.at[n],
                                     device_id=(dp, 2 * chip + core), device_id_type=MESH).wait_recv()

    pieces = [(t, k) for t in range(towers) for k in range(chunks)]
    ends = (chip == 0, chip == chips - 1)
    for t, k in pieces:
        for way in (0, 1):
            @pl.when(ends[way])
            def _():
                partial(0, way, t, k, True).start()
    own = [pltpu.make_async_copy(
        pg_ref.at[t, pl.ds(pl.multiple_of(dp * depth, 128), depth), pl.ds(0, cols)], gr_ref.at[dp, core, t], own_sem.at[t])
        for t in range(towers)]
    own.append(pltpu.make_async_copy(ps_ref, sr_ref.at[dp], own_sem.at[towers]))
    for copy in own:
        copy.start()
    for kind in range(3):
        small(kind).start()
    for t in range(towers):
        for kind in (2, 0, 1):
            for k in (0, 1):
                grad(kind, k, t).start()
        grad(3, 1 - core, t).start()

    strip = 32

    for step in range(1, chips - 1):
        for t, k in pieces:
            for way in (0, 1):
                @pl.when(sends(step, way) & ends[way])
                def _():
                    partial(step, way, t, k, True).start()

                @pl.when(sends(step, way) & jnp.logical_not(ends[way]))
                def _():
                    load = pltpu.make_async_copy(own_term(target(step, way), t, k), term.at[way], t_sem.at[way])
                    load.start()
                    landed(step - 1, way, t, k)
                    load.wait()

                    def add(i, _):
                        rws = pl.ds(pl.multiple_of(i * strip, strip), strip)
                        all_rows = pl.ds(pl.multiple_of(k * part + i * strip, strip), strip)
                        held[way, step - 1, t, all_rows] = (
                            held[way, step - 1, t, all_rows].astype(jnp.float32) + term[way, rws].astype(jnp.float32)
                        ).astype(jnp.bfloat16)
                        return 0
                    lax.fori_loop(0, part // strip, add, 0)
                    partial(step, way, t, k, False).start()

    for n, (t, k) in enumerate(pieces):
        s = n % 2
        load = pltpu.make_async_copy(own_term(chip, t, k), term.at[s], t_sem.at[s])
        load.start()
        for way in (0, 1):
            @pl.when(receives(chips - 2, way))
            def _():
                landed(chips - 2, way, t, k)
        load.wait()
        store = pltpu.make_async_copy(total.at[s], d_ref.at[t, pl.ds(k * part, part)], o_sem.at[s])
        if n >= 2:
            store.wait()

        def finish(i, _):
            rws = pl.ds(pl.multiple_of(i * strip, strip), strip)
            all_rows = pl.ds(pl.multiple_of(k * part + i * strip, strip), strip)
            value = term[s, rws].astype(jnp.float32)
            for way in (0, 1):
                here = receives(chips - 2, way)
                value = value + jnp.where(here, held[way, chips - 2, t, all_rows].astype(jnp.float32), 0.0)
            total[s, rws] = value.astype(jnp.bfloat16)
            return 0
        lax.fori_loop(0, part // strip, finish, 0)
        store.start()
    for n in range(min(2, len(pieces))):
        pltpu.make_async_copy(total.at[n], d_ref.at[0, pl.ds(0, part)], o_sem.at[n]).wait()

    for t in range(towers):
        for kind in range(3):
            for k in (0, 1):
                grad_arrived(kind, k, t)
        grad_arrived(3, 1 - core, t)
    for kind in range(3):
        small(kind).wait()
    for t in range(towers):
        for kind in range(3):
            for k in (0, 1):
                grad(kind, k, t).wait_send()
        grad(3, 1 - core, t).wait_send()
    for step in range(chips - 1):
        for t, k in pieces:
            for way in (0, 1):
                @pl.when(sends(step, way))
                def _():
                    partial(step, way, t, k, True).wait_send()
    for copy in own:
        copy.wait()


def reduce(partial_d, partial_g, partial_s, chips, chunks, ident):
    towers, rows, wide = partial_d.shape
    depth, cols = wide // chips, partial_g.shape[2] // 2
    count = 2 * (chips - 1) * towers * chunks
    dma = pltpu.SemaphoreType.DMA
    bf16 = jnp.bfloat16
    return pl.pallas_call(
        functools.partial(reduce_kernel, chips, chunks),
        out_shape=[jax.ShapeDtypeStruct((towers, rows, depth), bf16),
                   jax.ShapeDtypeStruct((4, 2, towers, depth, cols), bf16),
                   jax.ShapeDtypeStruct((4,) + partial_s.shape, jnp.float32)],
        in_specs=[pl.BlockSpec(memory_space=pl.ANY)] * 3,
        out_specs=[pl.BlockSpec(memory_space=pl.ANY)] * 3,
        scratch_shapes=[pltpu.VMEM((2, chips - 1, towers, rows, depth), bf16),
                        pltpu.VMEM((2, rows // chunks, depth), bf16), pltpu.VMEM((2, rows // chunks, depth), bf16),
                        dma((count,)), dma((count,)), dma((2,)), dma((2,)), dma((16,)), dma((16,)), dma((3,)), dma((3,)), dma((towers + 1,))],
        compiler_params=pltpu.CompilerParams(collective_id=ident, has_side_effects=True, vmem_limit_bytes=56 * 2**20),
        cost_estimate=pl.CostEstimate(flops=0, bytes_accessed=800 * 2**20, transcendentals=0),
        name="reduce",
    )(partial_d, partial_g, partial_s)


def small_step(small_params, small_moment_one, small_moment_two, small_average, small_grad):
    first, second, direction = adam_part(small_moment_one, small_moment_two, small_grad)
    fresh = small_params - rate_small * direction
    return first, second, fresh, ema_decay * small_average + (1.0 - ema_decay) * fresh


def line_body(
    features,
    counts,
    weights,
    small_params,
    out_grad,
    moment_one,
    moment_two,
    average,
    basis_left,
    basis_right,
    small_moment_one,
    small_moment_two,
    small_average,
):
    cores = lax.axis_size("mp")
    chips = cores // 2
    cols = weights.shape[2]
    swap = [(i, i ^ 1) for i in range(cores)]
    slot_count = features.shape[1]
    total = jnp.sum(counts)
    live_rows = (jnp.arange(slot_count, dtype=jnp.int32) < total).astype(jnp.float32)
    wide_f, wide_w = gather(features, weights.astype(jnp.bfloat16), chips, 2, 1)
    partial = jnp.einsum("tri,tio->tro", wide_f, wide_w, preferred_element_type=jnp.float32)
    product = partial[:, :, :cols] + lax.ppermute(partial[:, :, cols:], "mp", swap)
    result, back = jax.vjp(lambda a, b: stitch_local(a, b, live_rows), product, small_params)
    stitched = lax.all_gather(result.astype(jnp.bfloat16), "mp", axis=2, tiled=True)
    dz, small_part = back(out_grad.astype(jnp.float32))
    dz_low = dz.astype(jnp.bfloat16)
    wide_dz = jnp.concatenate([dz_low, lax.ppermute(dz_low, "mp", swap)], axis=2)
    partial_d = jnp.einsum("tro,tio->tri", wide_dz, wide_w, preferred_element_type=jnp.float32)
    partial_g = jnp.einsum("tri,tro->tio", wide_f, wide_dz, preferred_element_type=jnp.float32)
    small_part = jnp.pad(small_part, ((0, 2), (0, 0)))
    d_feat, parts, small_parts = reduce(
        partial_d.astype(jnp.bfloat16), partial_g.astype(jnp.bfloat16), small_part, chips, 2, 2
    )
    states = soap(parts, weights, moment_one, moment_two, average, basis_left, basis_right)
    small_states = small_step(
        small_params, small_moment_one, small_moment_two, small_average, jnp.sum(small_parts, 0)[:6]
    )
    return (stitched, d_feat) + tuple(states) + small_states


def plain_body(
    features,
    counts,
    weights,
    small_params,
    out_grad,
    moment_one,
    moment_two,
    average,
    basis_left,
    basis_right,
    small_moment_one,
    small_moment_two,
    small_average,
):
    slot_count = features.shape[1]
    total = jnp.sum(counts)
    live_rows = (jnp.arange(slot_count, dtype=jnp.int32) < total).astype(jnp.float32)
    weights_low = lax.all_gather(weights.astype(jnp.bfloat16), "dp", axis=1, tiled=True)
    feats_full = lax.all_gather(features, "mp", axis=2, tiled=True)
    product = jnp.einsum(
        "tri,tio->tro", feats_full, weights_low, preferred_element_type=jnp.float32
    )
    result, back = jax.vjp(lambda a, b: stitch_local(a, b, live_rows), product, small_params)
    stitched = lax.all_gather(result.astype(jnp.bfloat16), "mp", axis=2, tiled=True)
    dz, small_part = back(out_grad.astype(jnp.float32))
    dz_low = dz.astype(jnp.bfloat16)
    grad_part = jnp.einsum("tri,tro->tio", feats_full, dz_low, preferred_element_type=jnp.float32)
    partial_sums = jnp.einsum(
        "tro,tio->tri", dz_low, weights_low, preferred_element_type=jnp.float32
    )
    d_feat = lax.psum_scatter(
        partial_sums.astype(jnp.float32), "mp", scatter_dimension=2, tiled=True
    )
    grad = lax.psum_scatter(grad_part, "dp", scatter_dimension=1, tiled=True)
    small_grad = lax.psum(small_part, "dp")
    towers, n_in, n_out = grad.shape
    blocks = grad.reshape(towers, n_in // BLOCK, BLOCK, n_out // BLOCK, BLOCK)
    rotated = jnp.einsum(
        "trcai,tracb,trcbj->tricj", basis_left, blocks, basis_right, precision=lax.Precision.HIGHEST
    ).reshape(towers, n_in, n_out)
    first, second, direction = adam_part(moment_one, moment_two, rotated)
    turned = direction.reshape(towers, n_in // BLOCK, BLOCK, n_out // BLOCK, BLOCK)
    step_back = jnp.einsum(
        "trcai,tricj,trcbj->tracb", basis_left, turned, basis_right, precision=lax.Precision.HIGHEST
    ).reshape(towers, n_in, n_out)
    new_weights = weights - rate_main * (step_back + decay_weight * weights)
    new_average = ema_decay * average + (1.0 - ema_decay) * new_weights
    return (
        stitched,
        d_feat.astype(jnp.bfloat16),
        first,
        second,
        new_weights,
        new_average,
        new_weights.astype(jnp.bfloat16),
    ) + small_step(small_params, small_moment_one, small_moment_two, small_average, small_grad)


def solution(mesh):
    def body(features, counts, weights, *rest):
        dp, mp = mesh.shape["dp"], mesh.shape["mp"]
        tiles = features.shape[2] % 128 == 0 and weights.shape[2] % 128 == 0
        suits = dp == 4 and mp == 2 * dp and tiles and features.shape[1] % 64 == 0
        return (line_body if suits else plain_body)(features, counts, weights, *rest)

    return jax.shard_map(
        body,
        mesh=mesh,
        in_specs=(
            P(None, "dp", "mp"),
            P("dp"),
            P(None, "dp", "mp"),
            P(None, "mp"),
            P(None, "dp", "mp"),
            P(None, "dp", "mp"),
            P(None, "dp", "mp"),
            P(None, "dp", "mp"),
            P(None, "dp", "mp", None, None),
            P(None, "dp", "mp", None, None),
            P(None, "mp"),
            P(None, "mp"),
            P(None, "mp"),
        ),
        out_specs=(
            P(None, "dp", None),
            P(None, "dp", "mp"),
            P(None, "dp", "mp"),
            P(None, "dp", "mp"),
            P(None, "dp", "mp"),
            P(None, "dp", "mp"),
            P(None, "dp", "mp"),
            P(None, "mp"),
            P(None, "mp"),
            P(None, "mp"),
            P(None, "mp"),
        ),
        check_vma=False,
    )
```

```python
import functools

import jax
import jax.numpy as jnp
from jax import lax
from jax.experimental import pallas as pl
from jax.experimental.pallas import tpu as pltpu
from jax.sharding import PartitionSpec as P

BLOCK = 64
STEP = 5


beta_one = 0.5
beta_two = 0.5
ema_decay = 0.5
rate_main = 0.01
rate_small = 0.05
decay_weight = 0.01
eps = 1e-08


def stitch_local(product, small, live_rows):
    pre_act = product + small[0:2][:, None, :]
    activated = jax.nn.gelu(pre_act, approximate=True)
    first = small[2] * activated[0] + small[3] * activated[1]
    second = small[4] * activated[0] + small[5] * activated[1]
    return jnp.stack([first, second]) * live_rows[None, :, None]


def adam_part(moment_a, moment_b, grad):
    first = beta_one * moment_a + (1.0 - beta_one) * grad
    second = beta_two * moment_b + (1.0 - beta_two) * grad * grad
    direction = first / (1.0 - beta_one**STEP) / (jnp.sqrt(second / (1.0 - beta_two**STEP)) + eps)
    return (first, second, direction)

def split(v):
    high = v.astype(jnp.bfloat16)
    return high, (v - high.astype(jnp.float32)).astype(jnp.bfloat16)

def soap_pair(grad, left, right, moment_a, moment_b):
    row = lax.broadcasted_iota(jnp.int32, (2 * BLOCK, 2 * BLOCK), 0) // BLOCK
    lane = lax.broadcasted_iota(jnp.int32, (2 * BLOCK, 2 * BLOCK), 1) // BLOCK
    own = row == lane
    def diagonal(v):
        return jnp.where(own, jnp.concatenate([v, v], axis=0), 0.0)
    def beside(v):
        return jnp.concatenate([v[0], v[1]], axis=1)
    def dot(a, b, ca, cb):
        return lax.dot_general(a, b, (((ca,), (cb,)), ((), ())), preferred_element_type=jnp.float32)
    right_high, right_low = split(diagonal(beside(right)))
    left_high, left_low = split(beside(left))
    up_high, up_low = split(left.reshape(2 * BLOCK, BLOCK))
    def turn(v, cb):
        high, low = split(v)
        return (dot(jnp.concatenate([high, low], axis=1), jnp.concatenate([right_high, right_high], axis=cb), 1, cb)
                + dot(high, right_low, 1, cb))
    high, low = split(diagonal(turn(grad, 0)))
    rotated = dot(jnp.concatenate([up_high, up_high, up_low], axis=0), jnp.concatenate([high, low, high], axis=0), 0, 0)
    first, second, direction = adam_part(moment_a, moment_b, rotated)
    high, low = split(diagonal(turn(direction, 1)))
    step = dot(jnp.concatenate([left_high, left_high, left_low], axis=1), jnp.concatenate([high, low, high], axis=0), 1, 0)
    return first, second, step

def soap_body(parts, weights, moment_a, moment_b, average, left, right, first, second, new_weights, new_average, copy):
    groups, pairs = left.shape[1], left.shape[2] // 2
    def strip(g, _):
        rows = pl.ds(pl.multiple_of(g * BLOCK, BLOCK), BLOCK)
        for q in range(pairs):
            cols = pl.ds(2 * BLOCK * q, 2 * BLOCK)
            at = (0, rows, cols)
            grad = parts[(0, 0) + at].astype(jnp.float32)
            for k in range(1, parts.shape[0]):
                grad = grad + parts[(k, 0) + at].astype(jnp.float32)
            one, two, step = soap_pair(grad, left[0, g, 2 * q:2 * q + 2], right[0, g, 2 * q:2 * q + 2], moment_a[at], moment_b[at])
            first[at] = one
            second[at] = two
            held = weights[at]
            fresh = held - rate_main * (step + decay_weight * held)
            new_weights[at] = fresh
            new_average[at] = ema_decay * average[at] + (1.0 - ema_decay) * fresh
            copy[at] = fresh.astype(jnp.bfloat16)
        return 0
    lax.fori_loop(0, groups, strip, 0)

def soap(parts, weights, moment_a, moment_b, average, left, right, group=3):
    towers, rows, cols = weights.shape
    half = parts.shape[3]
    steps = half // (BLOCK * group)
    flat = lambda t, p, g: (t, p * steps + g, 0)
    basis = lambda t, p, g: (t, p * steps + g, 0, 0, 0)
    state = pl.BlockSpec((1, BLOCK * group, cols), flat)
    base = pl.BlockSpec((1, group, cols // BLOCK, BLOCK, BLOCK), basis)
    full = jax.ShapeDtypeStruct(weights.shape, jnp.float32)
    return pl.pallas_call(
        soap_body,
        grid=(towers, 2, steps),
        in_specs=[pl.BlockSpec((parts.shape[0], 1, 1, BLOCK * group, cols), lambda t, p, g: (0, p, t, g, 0)),
                  state, state, state, state, base, base],
        out_specs=[state] * 5,
        out_shape=[full] * 4 + [jax.ShapeDtypeStruct(weights.shape, jnp.bfloat16)],
        compiler_params=pltpu.CompilerParams(vmem_limit_bytes=48 * 2**20),
        cost_estimate=pl.CostEstimate(flops=8 * 2 * towers * rows * cols * 64, bytes_accessed=130 * 2**20, transcendentals=0),
        name="soap",
    )(parts, weights, moment_a, moment_b, average, left, right)


MESH = pl.DeviceIdType.MESH


def place():
    mp = lax.axis_index("mp")
    return lax.axis_index("dp"), mp // 2, lax.rem(mp, 2)


def meet(devices):
    barrier = pltpu.get_barrier_semaphore()
    expected = 0
    for here, device in devices:
        @pl.when(here)
        def _():
            pl.semaphore_signal(barrier, inc=1, device_id=device, device_id_type=MESH)
        expected = expected + jnp.where(here, 1, 0)
    pl.semaphore_wait(barrier, expected)


def gather_kernel(chips, ranges, share, *refs):
    if share:
        (f_ref, w_ref, o_ref, pick_ref, fg_ref, wg_ref, og_ref, offer_f, offer_o, taken_f, taken_o,
         f_send, f_recv, w_send, w_recv, own_sem, x_send, x_recv, y_sem) = refs
    else:
        f_ref, w_ref, fg_ref, wg_ref, f_send, f_recv, w_send, w_recv, own_sem = refs
    dp, chip, core = place()
    towers, rows, depth = f_ref.shape
    cols = w_ref.shape[2]
    across, along = dp ^ 1, dp ^ 2
    others = (across, along, dp ^ 3)
    at = lambda c, k: (c, 2 * chip + k)

    meet([(chip > 0, (dp, 2 * (chip - 1) + core)), (chip < chips - 1, (dp, 2 * (chip + 1) + core)),
          (chip >= 0, at(dp, 1 - core))] + [(chip >= 0, at(c, k)) for c in (across, along) for k in (0, 1)]
         + ([(chip >= 0, at(others[2], core))] if share else []))

    def copies(step, way, t, k, shard, there):
        lanes = pl.ds(pl.multiple_of(shard * depth, 128), depth)
        rws = pl.ds(*ranges[k])
        src = fg_ref.at[t, rws, lanes]
        if step == 0:
            src = taken_f.at[t] if share and k == len(ranges) - 1 else f_ref.at[t, rws]
        n = ((way * (chips - 1) + step) * towers + t) * len(ranges) + k
        return pltpu.make_async_remote_copy(
            src_ref=src, dst_ref=fg_ref.at[t, rws, lanes], send_sem=f_send.at[n], recv_sem=f_recv.at[n],
            device_id=(dp, 2 * there + core), device_id_type=MESH)

    def feature(step, way, t, k):
        return copies(step, way, t, k, chip - step if way == 0 else chip + step, chip + 1 if way == 0 else chip - 1)

    def incoming(step, way, t, k):
        return copies(step, way, t, k, chip - 1 - step if way == 0 else chip + 1 + step, chip)

    def sends(step, way):
        return (chip < chips - 1) & (chip >= step) if way == 0 else (chip > 0) & (chip + step < chips)

    def receives(step, way):
        return chip > step if way == 0 else chip + step < chips - 1

    def launch(t, k):
        for way in (0, 1):
            @pl.when(sends(0, way))
            def _():
                feature(0, way, t, k).start()

    def block(owner, slot, t):
        return wg_ref.at[t, pl.ds(pl.multiple_of(owner * depth, 128), depth), pl.ds(pl.multiple_of(slot * cols, 128), cols)]

    def weight(kind, k, t):
        to = at((across, along, dp)[kind], k)
        n = (kind * 2 + core) * 2 + t
        return pltpu.make_async_remote_copy(
            src_ref=w_ref.at[t, pl.ds(pl.multiple_of(k * depth, 128), depth)], dst_ref=block(dp, k ^ core, t),
            send_sem=w_send.at[(kind * 2 + k) * 2 + t], recv_sem=w_recv.at[n], device_id=to, device_id_type=MESH)

    def forward(kind, slot):
        owner, to, t = ((across, along, 0), (along, across, 1))[kind]
        n = 12 + kind * 2 + slot
        return pltpu.make_async_remote_copy(
            src_ref=block(owner, slot, t), dst_ref=block(owner, slot, t),
            send_sem=w_send.at[n], recv_sem=w_recv.at[n], device_id=at(to, core), device_id_type=MESH)

    def arrived(kind, slot, t):
        owner = (across, along, dp)[kind]
        n = (kind * 2 + (slot ^ core)) * 2 + t
        pltpu.make_async_remote_copy(
            src_ref=block(owner, slot, t), dst_ref=block(owner, slot, t), send_sem=w_send.at[n], recv_sem=w_recv.at[n],
            device_id=at(dp, core), device_id_type=MESH).wait_recv()

    def offer(kind, what):
        first, size = share[1 + kind]
        src, dst = ((f_ref, offer_f), (o_ref, offer_o))[what]
        n = kind * 2 + what
        return pltpu.make_async_remote_copy(
            src_ref=src.at[:, pl.ds(first, size)], dst_ref=dst.at[1 + kind], send_sem=x_send.at[n], recv_sem=x_recv.at[n],
            device_id=at(others[kind], core), device_id_type=MESH)

    def choose(offers, taken):
        def strip(i, _):
            rws = pl.ds(pl.multiple_of(i * 16, 16), 16)
            for t in range(towers):
                value = offers[0, t, rws].astype(jnp.float32) * pick_ref[0]
                for kind in range(3):
                    value = value + offers[1 + kind, t, rws].astype(jnp.float32) * pick_ref[1 + kind]
                taken[t, rws] = value.astype(jnp.bfloat16)
            return 0
        lax.fori_loop(0, taken.shape[1] // 16, strip, 0)

    fixed = len(ranges) - 1 if share else len(ranges)
    kept = ranges[fixed][0] if share else rows
    mine = pl.ds(pl.multiple_of(chip * depth, 128), depth)
    own = [pltpu.make_async_copy(f_ref.at[t, pl.ds(0, kept)], fg_ref.at[t, pl.ds(0, kept), mine], own_sem.at[t]) for t in range(towers)]
    own += [pltpu.make_async_copy(w_ref.at[t, pl.ds(pl.multiple_of(core * depth, 128), depth)], block(dp, 0, t), own_sem.at[2 + t])
            for t in range(towers)]

    pieces = [(t, k) for k in range(len(ranges)) for t in range(towers)]
    if share:
        for kind in (2, 0, 1):
            offer(kind, 0).start()
        keep = [pltpu.make_async_copy(src.at[:, pl.ds(*share[0])], dst.at[0], y_sem.at[n])
                for n, (src, dst) in enumerate(((f_ref, offer_f), (o_ref, offer_o)))]
        for copy in keep:
            copy.start()
    for t, k in pieces:
        if k < fixed:
            launch(t, k)
    for copy in own:
        copy.start()
    if share:
        for kind in range(3):
            offer(kind, 0).wait_recv()
        keep[0].wait()
        choose(offer_f, taken_f)
        own_share = [pltpu.make_async_copy(taken_f.at[t], fg_ref.at[t, pl.ds(*ranges[fixed]), mine], y_sem.at[2 + t]) for t in range(towers)]
        for t in range(towers):
            launch(t, fixed)
            own_share[t].start()
    for t in (0, 1):
        for k in (0, 1):
            weight(0, k, t).start()
            weight(1, k, 1 - t).start()
    for t in (0, 1):
        weight(2, 1 - core, t).start()
    if share:
        for kind in (2, 0, 1):
            offer(kind, 1).start()

    for step in range(chips - 1):
        for t, k in pieces:
            for way in (0, 1):
                @pl.when(receives(step, way))
                def _():
                    incoming(step, way, t, k).wait_recv()
                if step + 1 < chips - 1:
                    @pl.when(sends(step + 1, way))
                    def _():
                        feature(step + 1, way, t, k).start()
            if step == 0 and (t, k) == pieces[-1]:
                for slot in (0, 1):
                    arrived(0, slot, 0)
                    forward(0, slot).start()
                    arrived(1, slot, 1)
                    forward(1, slot).start()

    for slot in (0, 1):
        arrived(0, slot, 1)
        arrived(1, slot, 0)
        forward(0, slot).wait_recv()
        forward(1, slot).wait_recv()
    for t in (0, 1):
        arrived(2, 1, t)
    if share:
        for kind in range(3):
            offer(kind, 1).wait_recv()
        keep[1].wait()
        choose(offer_o, taken_o)
        store = pltpu.make_async_copy(taken_o, og_ref, y_sem.at[1])
        store.start()
        store.wait()
        for copy in own_share:
            copy.wait()
        for kind in range(3):
            offer(kind, 0).wait_send()
            offer(kind, 1).wait_send()
    for t in (0, 1):
        for k in (0, 1):
            weight(0, k, t).wait_send()
            weight(1, k, t).wait_send()
        weight(2, 1 - core, t).wait_send()
    for slot in (0, 1):
        forward(0, slot).wait_send()
        forward(1, slot).wait_send()
    for step in range(chips - 1):
        for t, k in pieces:
            for way in (0, 1):
                @pl.when(sends(step, way))
                def _():
                    feature(step, way, t, k).wait_send()
    for copy in own:
        copy.wait()


def gather(features, weights_low, chips, ranges, ident, share=None, out_grad=None, pick=None):
    towers, _, depth = features.shape
    cols = weights_low.shape[2]
    rows = sum(ranges[-1])
    count = 2 * (chips - 1) * towers * len(ranges)
    dma = pltpu.SemaphoreType.DMA
    bf16 = jnp.bfloat16
    anywhere = pl.BlockSpec(memory_space=pl.ANY)
    out_shape = [jax.ShapeDtypeStruct((towers, rows, chips * depth), bf16),
                 jax.ShapeDtypeStruct((towers, chips * depth, 2 * cols), bf16)]
    scratch = [dma((count,)), dma((count,)), dma((16,)), dma((16,)), dma((4,))]
    operands, in_specs = [features, weights_low], [anywhere] * 2
    if share:
        size = share[0][1]
        out_shape.append(jax.ShapeDtypeStruct((towers, size, cols), bf16))
        scratch = ([pltpu.VMEM((n + (towers, size, w)), bf16) for n in ((4,), ()) for w in (depth, cols)]
                   + scratch + [dma((6,)), dma((6,)), dma((4,))])
        operands += [out_grad, pick]
        in_specs += [anywhere, pl.BlockSpec(memory_space=pltpu.SMEM)]
    return pl.pallas_call(
        functools.partial(gather_kernel, chips, ranges, share),
        out_shape=out_shape,
        in_specs=in_specs,
        out_specs=[anywhere] * len(out_shape),
        scratch_shapes=scratch,
        compiler_params=pltpu.CompilerParams(collective_id=ident, has_side_effects=True, vmem_limit_bytes=32 * 2**20),
        cost_estimate=pl.CostEstimate(flops=0, bytes_accessed=800 * 2**20, transcendentals=0),
        name="gather",
    )(*operands)


def reduce_kernel(chips, ranges, share, pd_ref, pg_ref, ps_ref, d_ref, gr_ref, sr_ref, *refs):
    if share:
        back_ref, refs = refs[0], refs[1:]
        held, term, total, d_send, d_recv, t_sem, o_sem, g_send, g_recv, s_send, s_recv, own_sem, b_send, b_recv = refs
    else:
        held, term, total, d_send, d_recv, t_sem, o_sem, g_send, g_recv, s_send, s_recv, own_sem = refs
    dp, chip, core = place()
    towers, rows, depth = d_ref.shape
    cols = pg_ref.shape[2] // 2
    across, along = dp ^ 1, dp ^ 2
    others = (across, along, dp ^ 3)
    at = lambda c, k: (c, 2 * chip + k)

    meet([(chip > 0, (dp, 2 * (chip - 1) + core)), (chip < chips - 1, (dp, 2 * (chip + 1) + core)),
          (chip >= 0, at(dp, 1 - core))] + [(chip >= 0, at(c, k)) for c in others for k in (0, 1)])

    def grad(kind, k, t):
        owner = (others + (dp,))[kind]
        return pltpu.make_async_remote_copy(
            src_ref=pg_ref.at[t, pl.ds(pl.multiple_of(owner * depth, 128), depth), pl.ds(pl.multiple_of((k ^ core) * cols, 128), cols)],
            dst_ref=gr_ref.at[dp, core, t], send_sem=g_send.at[(kind * 2 + k) * 2 + t],
            recv_sem=g_recv.at[(kind * 2 + core) * 2 + t], device_id=at(owner, k), device_id_type=MESH)

    def grad_arrived(kind, k, t):
        owner = (others + (dp,))[kind]
        pltpu.make_async_remote_copy(
            src_ref=gr_ref.at[owner, k, t], dst_ref=gr_ref.at[owner, k, t], send_sem=g_send.at[0],
            recv_sem=g_recv.at[(kind * 2 + k) * 2 + t], device_id=at(dp, core), device_id_type=MESH).wait_recv()

    def small(kind):
        return pltpu.make_async_remote_copy(
            src_ref=ps_ref, dst_ref=sr_ref.at[dp], send_sem=s_send.at[kind], recv_sem=s_recv.at[kind],
            device_id=at(others[kind], core), device_id_type=MESH)

    def target(step, way):
        return chip + chips - 1 - step if way == 0 else chip - (chips - 1 - step)

    def sends(step, way):
        return (chip < chips - 1) & (chip <= step) if way == 0 else (chip > 0) & (chips - 1 - chip <= step)

    def receives(step, way):
        return (chip > 0) & (chip <= step + 1) if way == 0 else (chip < chips - 1) & (chips - 1 - chip <= step + 1)

    def own_term(goal, t, k):
        return pd_ref.at[t, pl.ds(*ranges[k]), pl.ds(pl.multiple_of(goal * depth, 128), depth)]

    def partial(step, way, t, k, first):
        n = ((way * (chips - 1) + step) * towers + t) * len(ranges) + k
        src = own_term(target(step, way), t, k) if first else held.at[way, step - 1, t, pl.ds(*ranges[k])]
        there = chip + 1 if way == 0 else chip - 1
        return pltpu.make_async_remote_copy(
            src_ref=src, dst_ref=held.at[way, step, t, pl.ds(*ranges[k])], send_sem=d_send.at[n], recv_sem=d_recv.at[n],
            device_id=(dp, 2 * there + core), device_id_type=MESH)

    def landed(step, way, t, k):
        n = ((way * (chips - 1) + step) * towers + t) * len(ranges) + k
        ref = held.at[way, step, t, pl.ds(*ranges[k])]
        pltpu.make_async_remote_copy(src_ref=ref, dst_ref=ref, send_sem=d_send.at[n], recv_sem=d_recv.at[n],
                                     device_id=(dp, 2 * chip + core), device_id_type=MESH).wait_recv()

    order = range(len(ranges))
    if share:
        order = [len(ranges) - 1] + list(range(len(ranges) - 1))
    pieces = [(t, k) for k in order for t in range(towers)]
    ends = (chip == 0, chip == chips - 1)
    for t, k in pieces:
        for way in (0, 1):
            @pl.when(ends[way])
            def _():
                partial(0, way, t, k, True).start()
    own = [pltpu.make_async_copy(
        pg_ref.at[t, pl.ds(pl.multiple_of(dp * depth, 128), depth), pl.ds(0, cols)], gr_ref.at[dp, core, t], own_sem.at[t])
        for t in range(towers)]
    own.append(pltpu.make_async_copy(ps_ref, sr_ref.at[dp], own_sem.at[towers]))
    for copy in own:
        copy.start()
    for kind in range(3):
        small(kind).start()
    for t in range(towers):
        for kind in (2, 0, 1):
            for k in (0, 1):
                grad(kind, k, t).start()
        grad(3, 1 - core, t).start()

    strip = 16

    for step in range(1, chips - 1):
        for t, k in pieces:
            for way in (0, 1):
                @pl.when(sends(step, way) & ends[way])
                def _():
                    partial(step, way, t, k, True).start()

                @pl.when(sends(step, way) & jnp.logical_not(ends[way]))
                def _():
                    start, size = ranges[k]
                    load = pltpu.make_async_copy(own_term(target(step, way), t, k), term.at[way, pl.ds(0, size)], t_sem.at[way])
                    load.start()
                    landed(step - 1, way, t, k)
                    load.wait()

                    def add(i, _):
                        rws = pl.ds(pl.multiple_of(i * strip, strip), strip)
                        all_rows = pl.ds(pl.multiple_of(start + i * strip, strip), strip)
                        held[way, step - 1, t, all_rows] = (
                            held[way, step - 1, t, all_rows].astype(jnp.float32) + term[way, rws].astype(jnp.float32)
                        ).astype(jnp.bfloat16)
                        return 0
                    lax.fori_loop(0, size // strip, add, 0)
                    partial(step, way, t, k, False).start()

    stores = []
    handed = towers if share else 0

    def hand(kind, n):
        t, k = pieces[n]
        return pltpu.make_async_remote_copy(
            src_ref=total.at[n % 2, pl.ds(0, ranges[k][1])], dst_ref=back_ref.at[kind, t], send_sem=b_send.at[kind * 2 + t],
            recv_sem=b_recv.at[kind * 2 + t], device_id=at(others[kind], core), device_id_type=MESH)

    for n, (t, k) in enumerate(pieces):
        s = n % 2
        start, size = ranges[k]
        load = pltpu.make_async_copy(own_term(chip, t, k), term.at[s, pl.ds(0, size)], t_sem.at[s])
        load.start()
        for way in (0, 1):
            @pl.when(receives(chips - 2, way))
            def _():
                landed(chips - 2, way, t, k)
        load.wait()
        if n >= 2:
            stores[n - 2].wait()
            for kind in range(3 if n - 2 < handed else 0):
                hand(kind, n - 2).wait_send()

        def finish(i, _):
            rws = pl.ds(pl.multiple_of(i * strip, strip), strip)
            all_rows = pl.ds(pl.multiple_of(start + i * strip, strip), strip)
            value = term[s, rws].astype(jnp.float32)
            for way in (0, 1):
                here = receives(chips - 2, way)
                value = value + jnp.where(here, held[way, chips - 2, t, all_rows].astype(jnp.float32), 0.0)
            total[s, rws] = value.astype(jnp.bfloat16)
            return 0
        lax.fori_loop(0, size // strip, finish, 0)
        stores.append(pltpu.make_async_copy(total.at[s, pl.ds(0, size)], d_ref.at[t, pl.ds(start, size)], o_sem.at[s]))
        stores[n].start()
        if n < handed:
            for kind in (2, 0, 1):
                hand(kind, n).start()
    for store in stores[-2:]:
        store.wait()
    for n in range(handed):
        for kind in range(3):
            hand(kind, n).wait_recv()

    for t in range(towers):
        for kind in range(3):
            for k in (0, 1):
                grad_arrived(kind, k, t)
        grad_arrived(3, 1 - core, t)
    for kind in range(3):
        small(kind).wait()
    for t in range(towers):
        for kind in range(3):
            for k in (0, 1):
                grad(kind, k, t).wait_send()
        grad(3, 1 - core, t).wait_send()
    for step in range(chips - 1):
        for t, k in pieces:
            for way in (0, 1):
                @pl.when(sends(step, way))
                def _():
                    partial(step, way, t, k, True).wait_send()
    for copy in own:
        copy.wait()


def reduce(partial_d, partial_g, partial_s, chips, ranges, ident, share=None):
    towers, rows, wide = partial_d.shape
    depth, cols = wide // chips, partial_g.shape[2] // 2
    count = 2 * (chips - 1) * towers * len(ranges)
    part = max(size for _, size in ranges)
    dma = pltpu.SemaphoreType.DMA
    bf16 = jnp.bfloat16
    out_shape = [jax.ShapeDtypeStruct((towers, rows, depth), bf16),
                 jax.ShapeDtypeStruct((4, 2, towers, depth, cols), bf16),
                 jax.ShapeDtypeStruct((4,) + partial_s.shape, jnp.float32)]
    more = []
    if share:
        out_shape.append(jax.ShapeDtypeStruct((3, towers, ranges[-1][1], depth), bf16))
        more = [dma((6,)), dma((6,))]
    return pl.pallas_call(
        functools.partial(reduce_kernel, chips, ranges, share),
        out_shape=out_shape,
        in_specs=[pl.BlockSpec(memory_space=pl.ANY)] * 3,
        out_specs=[pl.BlockSpec(memory_space=pl.ANY)] * len(out_shape),
        scratch_shapes=[pltpu.VMEM((2, chips - 1, towers, rows, depth), bf16),
                        pltpu.VMEM((2, part, depth), bf16), pltpu.VMEM((2, part, depth), bf16),
                        dma((count,)), dma((count,)), dma((2,)), dma((2,)), dma((16,)), dma((16,)), dma((3,)), dma((3,)), dma((towers + 1,))] + more,
        compiler_params=pltpu.CompilerParams(collective_id=ident, has_side_effects=True, vmem_limit_bytes=56 * 2**20),
        cost_estimate=pl.CostEstimate(flops=0, bytes_accessed=800 * 2**20, transcendentals=0),
        name="reduce",
    )(partial_d, partial_g, partial_s)


def small_step(small_params, small_moment_one, small_moment_two, small_average, small_grad):
    first, second, direction = adam_part(small_moment_one, small_moment_two, small_grad)
    fresh = small_params - rate_small * direction
    return first, second, fresh, ema_decay * small_average + (1.0 - ema_decay) * fresh


def towers_pass(wide_f, wide_w, small_params, out_grad, live_rows):
    cols = out_grad.shape[2]
    swap = [(i, i ^ 1) for i in range(lax.axis_size("mp"))]
    partial = jnp.einsum("tri,tio->tro", wide_f, wide_w, preferred_element_type=jnp.float32)
    product = partial[:, :, :cols] + lax.ppermute(partial[:, :, cols:], "mp", swap)
    result, back = jax.vjp(lambda a, b: stitch_local(a, b, live_rows), product, small_params)
    dz, small_part = back(out_grad.astype(jnp.float32))
    dz_low = dz.astype(jnp.bfloat16)
    wide_dz = jnp.concatenate([dz_low, lax.ppermute(dz_low, "mp", swap)], axis=2)
    partial_d = jnp.einsum("tro,tio->tri", wide_dz, wide_w, preferred_element_type=jnp.float32)
    partial_g = jnp.einsum("tri,tro->tio", wide_f, wide_dz, preferred_element_type=jnp.float32)
    small_part = jnp.pad(small_part, ((0, 2), (0, 0)))
    return result.astype(jnp.bfloat16), partial_d.astype(jnp.bfloat16), partial_g.astype(jnp.bfloat16), small_part


def update(d_feat, stitched, parts, small_parts, states, small_states):
    small_grad = jnp.sum(small_parts, 0)[: small_states[0].shape[0]]
    return (stitched, d_feat) + tuple(soap(parts, *states)) + small_step(*small_states, small_grad)


def own_rows(features, weights_low, small_params, out_grad, totals, states, small_states):
    rows = features.shape[1]
    chips = lax.axis_size("mp") // 2
    ranges = ((0, rows // 2), (rows // 2, rows // 2))
    live_rows = (jnp.arange(rows, dtype=jnp.int32) < totals[lax.axis_index("dp")]).astype(jnp.float32)
    wide_f, wide_w = gather(features, weights_low, chips, ranges, 1)
    result, partial_d, partial_g, small_part = towers_pass(wide_f, wide_w, small_params, out_grad, live_rows)
    stitched = lax.all_gather(result, "mp", axis=2, tiled=True)
    d_feat, parts, small_parts = reduce(partial_d, partial_g, small_part, chips, ranges, 2)
    return update(d_feat, stitched, parts, small_parts, states, small_states)


def shares(rows):
    keep = rows * 15 // 32 // 16 * 16
    size = -(-(rows - keep) // 64) * 16
    return keep, ((keep, size), (keep + size, size), (keep + 2 * size, size), (rows - size, size))


def shared_rows(features, weights_low, small_params, out_grad, totals, states, small_states):
    rows = features.shape[1]
    chips = lax.axis_size("mp") // 2
    keep, share = shares(rows)
    size = share[0][1]
    again = share[2][0] + size - share[3][0]
    half = keep // 32 * 16
    ranges = ((0, half), (half, keep - half), share[0])
    dp = lax.axis_index("dp")
    giver = jnp.argmax(totals).astype(jnp.int32)
    which = dp ^ giver
    pick = (jnp.arange(4, dtype=jnp.int32) == which).astype(jnp.float32)
    starts = jnp.array([first for first, _ in share], jnp.int32)
    slot = starts[which] + jnp.arange(size, dtype=jnp.int32)
    fresh = (jnp.arange(size, dtype=jnp.int32) >= again) | (which != 3)
    live = jnp.concatenate([jnp.arange(keep, dtype=jnp.int32) < totals[dp], (slot < totals[giver]) & fresh])
    wide_f, wide_w, taken = gather(features, weights_low, chips, ranges, 3, share, out_grad, pick)
    out_grad = jnp.concatenate([out_grad[:, :keep], taken], axis=1)
    result, partial_d, partial_g, small_part = towers_pass(
        wide_f, wide_w, small_params, out_grad, live.astype(jnp.float32)
    )

    def whole(here, back):
        rest = jnp.concatenate([here[:, keep:], back[0], back[1], back[2][:, again:]], axis=1)
        return jnp.concatenate([here[:, :keep], jnp.where(which == 0, rest, 0)], axis=1)

    perms = [[(i, i ^ k) for i in range(4)] for k in (1, 2, 3)]
    stitched = lax.all_gather(
        whole(result, [lax.ppermute(result[:, keep:], "dp", p) for p in perms]), "mp", axis=2, tiled=True
    )
    d_feat, parts, small_parts, back = reduce(partial_d, partial_g, small_part, chips, ranges, 4, share)
    return update(whole(d_feat, back), stitched, parts, small_parts, states, small_states)


def line_body(
    features,
    counts,
    weights,
    small_params,
    out_grad,
    moment_one,
    moment_two,
    average,
    basis_left,
    basis_right,
    small_moment_one,
    small_moment_two,
    small_average,
):
    totals = lax.all_gather(jnp.sum(counts), "dp")
    keep, _ = shares(features.shape[1])
    return lax.cond(
        jnp.sum(totals > keep) == 1,
        shared_rows,
        own_rows,
        features,
        weights.astype(jnp.bfloat16),
        small_params,
        out_grad,
        totals,
        (weights, moment_one, moment_two, average, basis_left, basis_right),
        (small_params, small_moment_one, small_moment_two, small_average),
    )


def plain_body(
    features,
    counts,
    weights,
    small_params,
    out_grad,
    moment_one,
    moment_two,
    average,
    basis_left,
    basis_right,
    small_moment_one,
    small_moment_two,
    small_average,
):
    slot_count = features.shape[1]
    total = jnp.sum(counts)
    live_rows = (jnp.arange(slot_count, dtype=jnp.int32) < total).astype(jnp.float32)
    weights_low = lax.all_gather(weights.astype(jnp.bfloat16), "dp", axis=1, tiled=True)
    feats_full = lax.all_gather(features, "mp", axis=2, tiled=True)
    product = jnp.einsum(
        "tri,tio->tro", feats_full, weights_low, preferred_element_type=jnp.float32
    )
    result, back = jax.vjp(lambda a, b: stitch_local(a, b, live_rows), product, small_params)
    stitched = lax.all_gather(result.astype(jnp.bfloat16), "mp", axis=2, tiled=True)
    dz, small_part = back(out_grad.astype(jnp.float32))
    dz_low = dz.astype(jnp.bfloat16)
    grad_part = jnp.einsum("tri,tro->tio", feats_full, dz_low, preferred_element_type=jnp.float32)
    partial_sums = jnp.einsum(
        "tro,tio->tri", dz_low, weights_low, preferred_element_type=jnp.float32
    )
    d_feat = lax.psum_scatter(
        partial_sums.astype(jnp.float32), "mp", scatter_dimension=2, tiled=True
    )
    grad = lax.psum_scatter(grad_part, "dp", scatter_dimension=1, tiled=True)
    small_grad = lax.psum(small_part, "dp")
    towers, n_in, n_out = grad.shape
    blocks = grad.reshape(towers, n_in // BLOCK, BLOCK, n_out // BLOCK, BLOCK)
    rotated = jnp.einsum(
        "trcai,tracb,trcbj->tricj", basis_left, blocks, basis_right, precision=lax.Precision.HIGHEST
    ).reshape(towers, n_in, n_out)
    first, second, direction = adam_part(moment_one, moment_two, rotated)
    turned = direction.reshape(towers, n_in // BLOCK, BLOCK, n_out // BLOCK, BLOCK)
    step_back = jnp.einsum(
        "trcai,tricj,trcbj->tracb", basis_left, turned, basis_right, precision=lax.Precision.HIGHEST
    ).reshape(towers, n_in, n_out)
    new_weights = weights - rate_main * (step_back + decay_weight * weights)
    new_average = ema_decay * average + (1.0 - ema_decay) * new_weights
    return (
        stitched,
        d_feat.astype(jnp.bfloat16),
        first,
        second,
        new_weights,
        new_average,
        new_weights.astype(jnp.bfloat16),
    ) + small_step(small_params, small_moment_one, small_moment_two, small_average, small_grad)


def solution(mesh):
    def body(features, counts, weights, *rest):
        dp, mp = mesh.shape["dp"], mesh.shape["mp"]
        tiles = features.shape[2] % 128 == 0 and weights.shape[2] % 128 == 0
        suits = dp == 4 and mp == 2 * dp and tiles and features.shape[1] % 64 == 0
        return (line_body if suits else plain_body)(features, counts, weights, *rest)

    return jax.shard_map(
        body,
        mesh=mesh,
        in_specs=(
            P(None, "dp", "mp"),
            P("dp"),
            P(None, "dp", "mp"),
            P(None, "mp"),
            P(None, "dp", "mp"),
            P(None, "dp", "mp"),
            P(None, "dp", "mp"),
            P(None, "dp", "mp"),
            P(None, "dp", "mp", None, None),
            P(None, "dp", "mp", None, None),
            P(None, "mp"),
            P(None, "mp"),
            P(None, "mp"),
        ),
        out_specs=(
            P(None, "dp", None),
            P(None, "dp", "mp"),
            P(None, "dp", "mp"),
            P(None, "dp", "mp"),
            P(None, "dp", "mp"),
            P(None, "dp", "mp"),
            P(None, "dp", "mp"),
            P(None, "mp"),
            P(None, "mp"),
            P(None, "mp"),
            P(None, "mp"),
        ),
        check_vma=False,
    )
```

```python
import functools
import math

import jax
import jax.numpy as jnp
from jax import lax
from jax.experimental import pallas as pl
from jax.experimental.pallas import tpu as pltpu
from jax.sharding import PartitionSpec as P

BLOCK = 64
STEP = 5


beta_one = 0.5
beta_two = 0.5
ema_decay = 0.5
rate_main = 0.01
rate_small = 0.05
decay_weight = 0.01
eps = 1e-08


def stitch_local(product, small, live_rows):
    pre_act = product + small[0:2][:, None, :]
    activated = jax.nn.gelu(pre_act, approximate=True)
    first = small[2] * activated[0] + small[3] * activated[1]
    second = small[4] * activated[0] + small[5] * activated[1]
    return jnp.stack([first, second]) * live_rows[None, :, None]


def adam_part(moment_a, moment_b, grad):
    first = beta_one * moment_a + (1.0 - beta_one) * grad
    second = beta_two * moment_b + (1.0 - beta_two) * grad * grad
    direction = first / (1.0 - beta_one**STEP) / (jnp.sqrt(second / (1.0 - beta_two**STEP)) + eps)
    return (first, second, direction)

def split(v):
    high = v.astype(jnp.bfloat16)
    return high, (v - high.astype(jnp.float32)).astype(jnp.bfloat16)

def soap_blocks(grads, lefts, rights, moments):
    row = lax.broadcasted_iota(jnp.int32, (2 * BLOCK, 2 * BLOCK), 0) // BLOCK
    lane = lax.broadcasted_iota(jnp.int32, (2 * BLOCK, 2 * BLOCK), 1) // BLOCK
    own = row == lane

    def diagonal(v):
        return jnp.where(own, jnp.concatenate([v, v], axis=0), 0.0)

    def beside(v):
        return jnp.concatenate([v[0], v[1]], axis=1)

    def stationary(v, axis):
        high, low = split(v)
        return jnp.concatenate([high, high, low], axis=axis)

    def moving(v, axis):
        high, low = split(v)
        return jnp.concatenate([high, low, high], axis=axis)

    def dots(a, b, ca, cb):
        dims = (((ca,), (cb,)), ((), ()))
        return [lax.dot_general(x, y, dims, preferred_element_type=jnp.float32) for x, y in zip(a, b)]

    right = [diagonal(beside(v)) for v in rights]
    values = dots([moving(v, 1) for v in grads], [stationary(v, 0) for v in right], 1, 0)
    values = dots([stationary(v.reshape(2 * BLOCK, BLOCK), 0) for v in lefts], [moving(diagonal(v), 0) for v in values], 0, 0)
    states = [adam_part(a, b, v) for (a, b), v in zip(moments, values)]
    values = dots([moving(v[2], 1) for v in states], [stationary(v, 1) for v in right], 1, 1)
    values = dots([stationary(beside(v), 1) for v in lefts], [moving(diagonal(v), 0) for v in values], 1, 0)
    return [(first, second, step) for (first, second, _), step in zip(states, values)]


def soap_body(together, parts, stitched, d_feat, weights, moment_a, moment_b, average, left, right,
              first, second, new_weights, new_average, copy, stitched_out, d_feat_out):
    groups, pairs = left.shape[1], left.shape[2] // 2
    stitched_out[...] = stitched[...]
    d_feat_out[...] = d_feat[...]

    def strips(g, _):
        places = [(g * together + s, q) for s in range(together) for q in range(pairs)]
        ats = [(0, pl.ds(pl.multiple_of(r * BLOCK, BLOCK), BLOCK), pl.ds(2 * BLOCK * q, 2 * BLOCK)) for r, q in places]
        grads = []
        for at in ats:
            grad = parts[(0, 0) + at].astype(jnp.float32)
            for k in range(1, parts.shape[0]):
                grad = grad + parts[(k, 0) + at].astype(jnp.float32)
            grads.append(grad)
        done = soap_blocks(grads, [left[0, r, 2 * q : 2 * q + 2] for r, q in places],
                           [right[0, r, 2 * q : 2 * q + 2] for r, q in places], [(moment_a[at], moment_b[at]) for at in ats])
        olds = [(weights[at], average[at]) for at in ats]
        for at, (one, two, step), (held, mean) in zip(ats, done, olds):
            first[at] = one
            second[at] = two
            fresh = held - rate_main * (step + decay_weight * held)
            new_weights[at] = fresh
            new_average[at] = ema_decay * mean + (1.0 - ema_decay) * fresh
            copy[at] = fresh.astype(jnp.bfloat16)
        return 0

    lax.fori_loop(0, groups // together, strips, 0)


def soap(parts, stitched, d_feat, weights, moment_a, moment_b, average, left, right, group=6):
    towers, rows, cols = weights.shape
    half = parts.shape[3]
    steps = half // (BLOCK * group)
    flat = lambda t, p, g: (t, p * steps + g, 0)
    basis = lambda t, p, g: (t, p * steps + g, 0, 0, 0)
    state = pl.BlockSpec((1, BLOCK * group, cols), flat)
    base = pl.BlockSpec((1, group, cols // BLOCK, BLOCK, BLOCK), basis)
    full = jax.ShapeDtypeStruct(weights.shape, jnp.float32)
    strips = max(n for n in range(1, 2 * steps + 1) if stitched.shape[1] % (16 * n) == 0)

    def through(v):
        return pl.BlockSpec((1, v.shape[1] // strips, v.shape[2]), lambda t, p, g: (t, jnp.minimum(p * steps + g, strips - 1), 0))

    return pl.pallas_call(
        functools.partial(soap_body, 2 - group % 2),
        grid=(towers, 2, steps),
        in_specs=[pl.BlockSpec((parts.shape[0], 1, 1, BLOCK * group, cols), lambda t, p, g: (0, p, t, g, 0)),
                  through(stitched), through(d_feat), state, state, state, state, base, base],
        out_specs=[state] * 5 + [through(stitched), through(d_feat)],
        out_shape=[full] * 4 + [jax.ShapeDtypeStruct(weights.shape, jnp.bfloat16)]
        + [jax.ShapeDtypeStruct(v.shape, v.dtype) for v in (stitched, d_feat)],
        compiler_params=pltpu.CompilerParams(vmem_limit_bytes=48 * 2**20),
        cost_estimate=pl.CostEstimate(flops=8 * 2 * towers * rows * cols * 64, bytes_accessed=130 * 2**20, transcendentals=0),
        name="soap",
    )(parts, stitched, d_feat, weights, moment_a, moment_b, average, left, right)


MESH = pl.DeviceIdType.MESH


def place():
    mp = lax.axis_index("mp")
    return lax.axis_index("dp"), mp // 2, lax.rem(mp, 2)


def meet(devices):
    barrier = pltpu.get_barrier_semaphore()
    expected = 0
    for here, device in devices:
        @pl.when(here)
        def _():
            pl.semaphore_signal(barrier, inc=1, device_id=device, device_id_type=MESH)
        expected = expected + jnp.where(here, 1, 0)
    pl.semaphore_wait(barrier, expected)


def gather_kernel(chips, ranges, f_ref, w_ref, fg_ref, wg_ref, f_send, f_recv, w_send, w_recv, own_sem):
    dp, chip, core = place()
    towers, rows, depth = f_ref.shape
    cols = w_ref.shape[2]
    across, along = dp ^ 1, dp ^ 2
    at = lambda c, k: (c, 2 * chip + k)

    meet([(chip > 0, (dp, 2 * (chip - 1) + core)), (chip < chips - 1, (dp, 2 * (chip + 1) + core)),
          (chip >= 0, at(dp, 1 - core))] + [(chip >= 0, at(c, k)) for c in (across, along) for k in (0, 1)])

    def copies(step, way, t, k, shard, there):
        lanes = pl.ds(pl.multiple_of(shard * depth, 128), depth)
        rws = pl.ds(*ranges[k])
        src = fg_ref.at[t, rws, lanes]
        if step == 0:
            src = f_ref.at[t, rws]
        n = ((way * (chips - 1) + step) * towers + t) * len(ranges) + k
        return pltpu.make_async_remote_copy(
            src_ref=src, dst_ref=fg_ref.at[t, rws, lanes], send_sem=f_send.at[n], recv_sem=f_recv.at[n],
            device_id=(dp, 2 * there + core), device_id_type=MESH)

    def feature(step, way, t, k):
        return copies(step, way, t, k, chip - step if way == 0 else chip + step, chip + 1 if way == 0 else chip - 1)

    def incoming(step, way, t, k):
        return copies(step, way, t, k, chip - 1 - step if way == 0 else chip + 1 + step, chip)

    def sends(step, way):
        return (chip < chips - 1) & (chip >= step) if way == 0 else (chip > 0) & (chip + step < chips)

    def receives(step, way):
        return chip > step if way == 0 else chip + step < chips - 1

    def launch(t, k):
        for way in (0, 1):
            @pl.when(sends(0, way))
            def _():
                feature(0, way, t, k).start()

    def block(owner, slot, t):
        return wg_ref.at[t, pl.ds(pl.multiple_of(owner * depth, 128), depth), pl.ds(pl.multiple_of(slot * cols, 128), cols)]

    def weight(kind, k, t):
        to = at((across, along, dp)[kind], k)
        n = (kind * 2 + core) * 2 + t
        return pltpu.make_async_remote_copy(
            src_ref=w_ref.at[t, pl.ds(pl.multiple_of(k * depth, 128), depth)], dst_ref=block(dp, k ^ core, t),
            send_sem=w_send.at[(kind * 2 + k) * 2 + t], recv_sem=w_recv.at[n], device_id=to, device_id_type=MESH)

    def forward(kind, slot):
        owner, to, t = ((across, along, 0), (along, across, 1))[kind]
        n = 12 + kind * 2 + slot
        return pltpu.make_async_remote_copy(
            src_ref=block(owner, slot, t), dst_ref=block(owner, slot, t),
            send_sem=w_send.at[n], recv_sem=w_recv.at[n], device_id=at(to, core), device_id_type=MESH)

    def arrived(kind, slot, t):
        owner = (across, along, dp)[kind]
        n = (kind * 2 + (slot ^ core)) * 2 + t
        pltpu.make_async_remote_copy(
            src_ref=block(owner, slot, t), dst_ref=block(owner, slot, t), send_sem=w_send.at[n], recv_sem=w_recv.at[n],
            device_id=at(dp, core), device_id_type=MESH).wait_recv()

    mine = pl.ds(pl.multiple_of(chip * depth, 128), depth)
    own = [pltpu.make_async_copy(f_ref.at[t], fg_ref.at[t, :, mine], own_sem.at[t]) for t in range(towers)]
    own += [pltpu.make_async_copy(w_ref.at[t, pl.ds(pl.multiple_of(core * depth, 128), depth)], block(dp, 0, t), own_sem.at[2 + t])
            for t in range(towers)]

    pieces = [(t, k) for k in range(len(ranges)) for t in range(towers)]
    for t, k in pieces:
        launch(t, k)
    for copy in own:
        copy.start()
    for t in (0, 1):
        for k in (0, 1):
            weight(0, k, t).start()
            weight(1, k, 1 - t).start()
    for t in (0, 1):
        weight(2, 1 - core, t).start()

    for step in range(chips - 1):
        for t, k in pieces:
            for way in (0, 1):
                @pl.when(receives(step, way))
                def _():
                    incoming(step, way, t, k).wait_recv()
                if step + 1 < chips - 1:
                    @pl.when(sends(step + 1, way))
                    def _():
                        feature(step + 1, way, t, k).start()
            if step == 0 and (t, k) == pieces[-1]:
                for slot in (0, 1):
                    arrived(0, slot, 0)
                    forward(0, slot).start()
                    arrived(1, slot, 1)
                    forward(1, slot).start()

    for slot in (0, 1):
        arrived(0, slot, 1)
        arrived(1, slot, 0)
        forward(0, slot).wait_recv()
        forward(1, slot).wait_recv()
    for t in (0, 1):
        arrived(2, 1, t)
    for t in (0, 1):
        for k in (0, 1):
            weight(0, k, t).wait_send()
            weight(1, k, t).wait_send()
        weight(2, 1 - core, t).wait_send()
    for slot in (0, 1):
        forward(0, slot).wait_send()
        forward(1, slot).wait_send()
    for step in range(chips - 1):
        for t, k in pieces:
            for way in (0, 1):
                @pl.when(sends(step, way))
                def _():
                    feature(step, way, t, k).wait_send()
    for copy in own:
        copy.wait()


def gather(features, weights_low, chips, ranges, ident):
    towers, rows, depth = features.shape
    cols = weights_low.shape[2]
    count = 2 * (chips - 1) * towers * len(ranges)
    dma = pltpu.SemaphoreType.DMA
    anywhere = pl.BlockSpec(memory_space=pl.ANY)
    return pl.pallas_call(
        functools.partial(gather_kernel, chips, ranges),
        out_shape=[jax.ShapeDtypeStruct((towers, rows, chips * depth), jnp.bfloat16),
                   jax.ShapeDtypeStruct((towers, chips * depth, 2 * cols), jnp.bfloat16)],
        in_specs=[anywhere] * 2,
        out_specs=[anywhere] * 2,
        scratch_shapes=[dma((count,)), dma((count,)), dma((16,)), dma((16,)), dma((4,))],
        compiler_params=pltpu.CompilerParams(collective_id=ident, has_side_effects=True),
        cost_estimate=pl.CostEstimate(flops=0, bytes_accessed=800 * 2**20, transcendentals=0),
        name="gather",
    )(features, weights_low)


def reduce_kernel(chips, ranges, pd_ref, pg_ref, ps_ref, d_ref, gr_ref, sr_ref, held, term, total,
                  d_send, d_recv, t_sem, o_sem, g_send, g_recv, s_send, s_recv, own_sem):
    dp, chip, core = place()
    towers, rows, depth = d_ref.shape
    cols = pg_ref.shape[2] // 2
    across, along = dp ^ 1, dp ^ 2
    others = (across, along, dp ^ 3)
    at = lambda c, k: (c, 2 * chip + k)

    meet([(chip > 0, (dp, 2 * (chip - 1) + core)), (chip < chips - 1, (dp, 2 * (chip + 1) + core)),
          (chip >= 0, at(dp, 1 - core))] + [(chip >= 0, at(c, k)) for c in others for k in (0, 1)])

    def grad(kind, k, t):
        owner = (others + (dp,))[kind]
        return pltpu.make_async_remote_copy(
            src_ref=pg_ref.at[t, pl.ds(pl.multiple_of(owner * depth, 128), depth), pl.ds(pl.multiple_of((k ^ core) * cols, 128), cols)],
            dst_ref=gr_ref.at[dp, core, t], send_sem=g_send.at[(kind * 2 + k) * 2 + t],
            recv_sem=g_recv.at[(kind * 2 + core) * 2 + t], device_id=at(owner, k), device_id_type=MESH)

    def grad_arrived(kind, k, t):
        owner = (others + (dp,))[kind]
        pltpu.make_async_remote_copy(
            src_ref=gr_ref.at[owner, k, t], dst_ref=gr_ref.at[owner, k, t], send_sem=g_send.at[0],
            recv_sem=g_recv.at[(kind * 2 + k) * 2 + t], device_id=at(dp, core), device_id_type=MESH).wait_recv()

    def small(kind):
        return pltpu.make_async_remote_copy(
            src_ref=ps_ref, dst_ref=sr_ref.at[dp], send_sem=s_send.at[kind], recv_sem=s_recv.at[kind],
            device_id=at(others[kind], core), device_id_type=MESH)

    def target(step, way):
        return chip + chips - 1 - step if way == 0 else chip - (chips - 1 - step)

    def sends(step, way):
        return (chip < chips - 1) & (chip <= step) if way == 0 else (chip > 0) & (chips - 1 - chip <= step)

    def receives(step, way):
        return (chip > 0) & (chip <= step + 1) if way == 0 else (chip < chips - 1) & (chips - 1 - chip <= step + 1)

    def own_term(goal, t, k):
        return pd_ref.at[t, pl.ds(*ranges[k]), pl.ds(pl.multiple_of(goal * depth, 128), depth)]

    def partial(step, way, t, k, first):
        n = ((way * (chips - 1) + step) * towers + t) * len(ranges) + k
        src = own_term(target(step, way), t, k) if first else held.at[way, step - 1, t, pl.ds(*ranges[k])]
        there = chip + 1 if way == 0 else chip - 1
        return pltpu.make_async_remote_copy(
            src_ref=src, dst_ref=held.at[way, step, t, pl.ds(*ranges[k])], send_sem=d_send.at[n], recv_sem=d_recv.at[n],
            device_id=(dp, 2 * there + core), device_id_type=MESH)

    def landed(step, way, t, k):
        n = ((way * (chips - 1) + step) * towers + t) * len(ranges) + k
        ref = held.at[way, step, t, pl.ds(*ranges[k])]
        pltpu.make_async_remote_copy(src_ref=ref, dst_ref=ref, send_sem=d_send.at[n], recv_sem=d_recv.at[n],
                                     device_id=(dp, 2 * chip + core), device_id_type=MESH).wait_recv()

    pieces = [(t, k) for t in range(towers) for k in range(len(ranges))]
    ends = (chip == 0, chip == chips - 1)
    for t, k in pieces:
        for way in (0, 1):
            @pl.when(ends[way])
            def _():
                partial(0, way, t, k, True).start()
    own = [pltpu.make_async_copy(
        pg_ref.at[t, pl.ds(pl.multiple_of(dp * depth, 128), depth), pl.ds(0, cols)], gr_ref.at[dp, core, t], own_sem.at[t])
        for t in range(towers)]
    own.append(pltpu.make_async_copy(ps_ref, sr_ref.at[dp], own_sem.at[towers]))
    for copy in own:
        copy.start()
    for kind in range(3):
        small(kind).start()
    for t in range(towers):
        for kind in (2, 0, 1):
            for k in (0, 1):
                grad(kind, k, t).start()
        grad(3, 1 - core, t).start()

    strip = 16

    for step in range(1, chips - 1):
        for t, k in pieces:
            for way in (0, 1):
                @pl.when(sends(step, way) & ends[way])
                def _():
                    partial(step, way, t, k, True).start()

                @pl.when(sends(step, way) & jnp.logical_not(ends[way]))
                def _():
                    start, size = ranges[k]
                    load = pltpu.make_async_copy(own_term(target(step, way), t, k), term.at[way, pl.ds(0, size)], t_sem.at[way])
                    load.start()
                    landed(step - 1, way, t, k)
                    load.wait()

                    def add(i, _):
                        rws = pl.ds(pl.multiple_of(i * strip, strip), strip)
                        all_rows = pl.ds(pl.multiple_of(start + i * strip, strip), strip)
                        held[way, step - 1, t, all_rows] = (
                            held[way, step - 1, t, all_rows].astype(jnp.float32) + term[way, rws].astype(jnp.float32)
                        ).astype(jnp.bfloat16)
                        return 0
                    lax.fori_loop(0, size // strip, add, 0)
                    partial(step, way, t, k, False).start()

    stores = []
    for n, (t, k) in enumerate(pieces):
        s = n % 2
        start, size = ranges[k]
        load = pltpu.make_async_copy(own_term(chip, t, k), term.at[s, pl.ds(0, size)], t_sem.at[s])
        load.start()
        for way in (0, 1):
            @pl.when(receives(chips - 2, way))
            def _():
                landed(chips - 2, way, t, k)
        load.wait()
        if n >= 2:
            stores[n - 2].wait()

        def finish(i, _):
            rws = pl.ds(pl.multiple_of(i * strip, strip), strip)
            all_rows = pl.ds(pl.multiple_of(start + i * strip, strip), strip)
            value = term[s, rws].astype(jnp.float32)
            for way in (0, 1):
                here = receives(chips - 2, way)
                value = value + jnp.where(here, held[way, chips - 2, t, all_rows].astype(jnp.float32), 0.0)
            total[s, rws] = value.astype(jnp.bfloat16)
            return 0
        lax.fori_loop(0, size // strip, finish, 0)
        stores.append(pltpu.make_async_copy(total.at[s, pl.ds(0, size)], d_ref.at[t, pl.ds(start, size)], o_sem.at[s]))
        stores[n].start()
    for store in stores[-2:]:
        store.wait()

    for t in range(towers):
        for kind in range(3):
            for k in (0, 1):
                grad_arrived(kind, k, t)
        grad_arrived(3, 1 - core, t)
    for kind in range(3):
        small(kind).wait()
    for t in range(towers):
        for kind in range(3):
            for k in (0, 1):
                grad(kind, k, t).wait_send()
        grad(3, 1 - core, t).wait_send()
    for step in range(chips - 1):
        for t, k in pieces:
            for way in (0, 1):
                @pl.when(sends(step, way))
                def _():
                    partial(step, way, t, k, True).wait_send()
    for copy in own:
        copy.wait()


def reduce(partial_d, partial_g, partial_s, chips, ranges, ident):
    towers, rows, wide = partial_d.shape
    depth, cols = wide // chips, partial_g.shape[2] // 2
    count = 2 * (chips - 1) * towers * len(ranges)
    part = max(size for _, size in ranges)
    dma = pltpu.SemaphoreType.DMA
    bf16 = jnp.bfloat16
    out_shape = [jax.ShapeDtypeStruct((towers, rows, depth), bf16),
                 jax.ShapeDtypeStruct((4, 2, towers, depth, cols), bf16),
                 jax.ShapeDtypeStruct((4,) + partial_s.shape, jnp.float32)]
    return pl.pallas_call(
        functools.partial(reduce_kernel, chips, ranges),
        out_shape=out_shape,
        in_specs=[pl.BlockSpec(memory_space=pl.ANY)] * 3,
        out_specs=[pl.BlockSpec(memory_space=pl.ANY)] * len(out_shape),
        scratch_shapes=[pltpu.VMEM((2, chips - 1, towers, rows, depth), bf16),
                        pltpu.VMEM((2, part, depth), bf16), pltpu.VMEM((2, part, depth), bf16),
                        dma((count,)), dma((count,)), dma((2,)), dma((2,)), dma((16,)), dma((16,)), dma((3,)), dma((3,)), dma((towers + 1,))],
        compiler_params=pltpu.CompilerParams(collective_id=ident, has_side_effects=True, vmem_limit_bytes=56 * 2**20),
        cost_estimate=pl.CostEstimate(flops=0, bytes_accessed=800 * 2**20, transcendentals=0),
        name="reduce",
    )(partial_d, partial_g, partial_s)


def forward_kernel(chips, share, ranges, f_ref, w_ref, o_ref, n_ref, sp_ref, fg_ref, wg_ref, y_ref, dz_ref, sg_ref, tot_ref,
                   offer_f, taken, offer_o, og, w_wide, w_low, f_tile, w_tile, acc, theirs, live, y_here, dz_here, sums_here,
                   tot, f_send, f_recv, w_send, w_recv, own_sem, x_send, x_recv, k_sem, n_send, n_recv, l_sem, ft_sem, wt_sem,
                   a_send, a_recv, z_send, z_recv, out_sem):
    dp, chip, core = place()
    towers, _, depth = f_ref.shape
    cols = w_ref.shape[2]
    steps = chips - 1
    keep = share[0][0]
    fixed = len(ranges) - 1
    across, along = dp ^ 1, dp ^ 2
    others = (across, along, dp ^ 3)
    at = lambda c, k: (c, 2 * chip + k)
    ends = (chip == 0) | (chip == steps)

    meet([(chip > 0, (dp, 2 * (chip - 1) + core)), (chip < steps, (dp, 2 * (chip + 1) + core)),
          (chip >= 0, at(dp, 1 - core))] + [(chip >= 0, at(c, k)) for c in (across, along) for k in (0, 1)]
         + [(chip >= 0, at(others[2], core))])

    def shard_lanes(shard):
        return pl.ds(pl.multiple_of(shard * depth, 128), depth)

    def copies(step, way, t, k, shard, there):
        rws = pl.ds(*ranges[k])
        dst = fg_ref.at[t, rws, shard_lanes(shard)]
        src = dst
        if step == 0:
            src = taken.at[t] if k == fixed else f_ref.at[t, rws]
        n = t * len(ranges) + k
        return pltpu.make_async_remote_copy(
            src_ref=src, dst_ref=dst, send_sem=f_send.at[way, step, n], recv_sem=f_recv.at[way, step, n],
            device_id=(dp, 2 * there + core), device_id_type=MESH)

    def feature(step, way, t, k):
        return copies(step, way, t, k, chip - step if way == 0 else chip + step, chip + 1 if way == 0 else chip - 1)

    def incoming(step, way, t, k):
        return copies(step, way, t, k, chip - 1 - step if way == 0 else chip + 1 + step, chip)

    def sends(step, way):
        return (chip < steps) & (chip >= step) if way == 0 else (chip > 0) & (chip + step <= steps)

    def receives(step, way):
        return chip > step if way == 0 else chip + step < steps

    def launch(t, k):
        for way in (0, 1):
            @pl.when(sends(0, way))
            def _():
                feature(0, way, t, k).start()

    def block(owner, slot, t):
        return wg_ref.at[t, pl.ds(pl.multiple_of(owner * depth, 128), depth), pl.ds(pl.multiple_of(slot * cols, 128), cols)]

    def weight(kind, k, t):
        return pltpu.make_async_remote_copy(
            src_ref=w_low.at[t, k], dst_ref=block(dp, k ^ core, t),
            send_sem=w_send.at[(kind * 2 + k) * 2 + t], recv_sem=w_recv.at[(kind * 2 + core) * 2 + t],
            device_id=at((across, along, dp)[kind], k), device_id_type=MESH)

    def pass_on(kind, slot):
        owner, to, t = ((across, along, 0), (along, across, 1))[kind]
        n = 12 + kind * 2 + slot
        return pltpu.make_async_remote_copy(
            src_ref=block(owner, slot, t), dst_ref=block(owner, slot, t),
            send_sem=w_send.at[n], recv_sem=w_recv.at[n], device_id=at(to, core), device_id_type=MESH)

    def arrived(kind, slot, t):
        owner = (across, along, dp)[kind]
        n = (kind * 2 + (slot ^ core)) * 2 + t
        pltpu.make_async_remote_copy(
            src_ref=block(owner, slot, t), dst_ref=block(owner, slot, t), send_sem=w_send.at[n], recv_sem=w_recv.at[n],
            device_id=at(dp, core), device_id_type=MESH).wait_recv()

    def offer(kind, what):
        src, dst = ((f_ref, offer_f), (o_ref, offer_o))[what]
        n = kind * 2 + what
        return pltpu.make_async_remote_copy(
            src_ref=src.at[:, pl.ds(*share[1 + kind])], dst_ref=dst.at[1 + kind], send_sem=x_send.at[n], recv_sem=x_recv.at[n],
            device_id=at(others[kind], core), device_id_type=MESH)

    def tell(kind):
        return pltpu.make_async_remote_copy(
            src_ref=n_ref, dst_ref=tot.at[1 + kind], send_sem=n_send.at[kind], recv_sem=n_recv.at[kind],
            device_id=at(others[kind], core), device_id_type=MESH)

    def choose(offers, into):
        width = offers.shape[3]
        weigh = [jnp.broadcast_to(jnp.where(tot[kind, :1, :width] > keep, 1.0, 0.0), (16, width)) for kind in range(4)]

        def strip(i, _):
            rws = pl.ds(pl.multiple_of(i * 16, 16), 16)
            for t in range(towers):
                value = offers[0, t, rws].astype(jnp.float32) * weigh[0]
                for kind in range(1, 4):
                    value = value + offers[kind, t, rws].astype(jnp.float32) * weigh[kind]
                into(t, i, value.astype(jnp.bfloat16))
            return 0
        lax.fori_loop(0, share[0][1] // 16, strip, 0)

    for kind in range(3):
        tell(kind).start()
    for kind in (2, 0, 1):
        offer(kind, 0).start()
    pieces = [(t, k) for k in range(len(ranges)) for t in range(towers)]
    for t, k in pieces:
        if k < fixed:
            launch(t, k)
    local = [(n_ref, tot.at[0]), (f_ref.at[:, pl.ds(*share[0])], offer_f.at[0]), (o_ref.at[:, pl.ds(*share[0])], offer_o.at[0]),
             (o_ref.at[:, pl.ds(0, keep)], og.at[:, pl.ds(0, keep)])]
    local = [pltpu.make_async_copy(src, dst, l_sem.at[n]) for n, (src, dst) in enumerate(local)]
    for copy in local:
        copy.start()
    own = [pltpu.make_async_copy(f_ref.at[t, pl.ds(0, keep)], fg_ref.at[t, pl.ds(0, keep), shard_lanes(chip)], own_sem.at[t])
           for t in range(towers)]
    for copy in own:
        copy.start()

    halves = [(t, k) for t in range(towers) for k in (0, 1)]
    wide = [pltpu.make_async_copy(w_ref.at[t, pl.ds(k * depth, depth)], w_wide.at[n % 2], k_sem.at[n % 2]) for n, (t, k) in enumerate(halves)]
    wide[0].start()
    for n, (t, k) in enumerate(halves):
        wide[n].wait()
        if n + 1 < len(halves):
            wide[n + 1].start()

        def round_strip(i, _):
            rws = pl.ds(pl.multiple_of(i * 64, 64), 64)
            w_low[t, k, rws] = w_wide[n % 2, rws].astype(jnp.bfloat16)
            return 0
        lax.fori_loop(0, depth // 64, round_strip, 0)
    own_w = [pltpu.make_async_copy(w_low.at[t, core], block(dp, 0, t), own_sem.at[towers + t]) for t in range(towers)]
    for copy in own_w:
        copy.start()

    local[0].wait()
    local[1].wait()
    for kind in range(3):
        tell(kind).wait_recv()
    totals = pltpu.make_async_copy(tot, tot_ref, l_sem.at[4])
    totals.start()
    for kind in range(3):
        offer(kind, 0).wait_recv()

    def take(t, i, value):
        taken[t, pl.ds(pl.multiple_of(i * 16, 16), 16)] = value
    choose(offer_f, take)
    own_share = [pltpu.make_async_copy(taken.at[t], fg_ref.at[t, pl.ds(*ranges[fixed]), shard_lanes(chip)], own_sem.at[2 * towers + t])
                 for t in range(towers)]
    for t in range(towers):
        launch(t, fixed)
        own_share[t].start()
    for t in (0, 1):
        for k in (0, 1):
            weight(0, k, t).start()
            weight(1, k, 1 - t).start()
    for t in (0, 1):
        weight(2, 1 - core, t).start()
    for kind in (2, 0, 1):
        offer(kind, 1).start()

    def alive(i, _):
        rws = pl.ds(pl.multiple_of(i * 16, 16), 16)
        row = lax.broadcasted_iota(jnp.int32, (16, cols), 0).astype(jnp.float32) + (i * 16).astype(jnp.float32)
        here = jnp.where(row < tot[0, :1, :cols], 1.0, 0.0)
        there = jnp.zeros_like(here)
        for kind in range(4):
            count = tot[kind, :1, :cols]
            slot = row + float(share[kind][0] - keep)
            valid = (slot < count) & (count > keep)
            if kind == 3:
                valid = valid & (slot >= share[2][0] + share[2][1])
            there = there + jnp.where(valid, 1.0, 0.0)
        live[rws] = jnp.where(row < keep, here, there)
        return 0
    lax.fori_loop(0, sum(ranges[fixed]) // 16, alive, 0)

    for step in range(steps - 1):
        for t, k in pieces:
            for way in (0, 1):
                @pl.when(receives(step, way))
                def _():
                    incoming(step, way, t, k).wait_recv()

                @pl.when(sends(step + 1, way))
                def _():
                    feature(step + 1, way, t, k).start()
        if step == 0:
            for slot in (0, 1):
                arrived(0, slot, 0)
                pass_on(0, slot).start()
                arrived(1, slot, 1)
                pass_on(1, slot).start()

    for copy in local[2:]:
        copy.wait()
    for kind in range(3):
        offer(kind, 1).wait_recv()

    def take_grad(t, i, value):
        og[t, pl.ds(pl.multiple_of(keep + i * 16, 16), 16)] = value
    choose(offer_o, take_grad)
    for slot in (0, 1):
        arrived(0, slot, 1)
        arrived(1, slot, 0)
        pass_on(0, slot).wait_recv()
        pass_on(1, slot).wait_recv()
    for t in (0, 1):
        arrived(2, 1, t)
    for copy in own + own_w + own_share:
        copy.wait()

    units = [(j, t) for j in range(chips) for t in range(towers)]
    shard = lambda j: jnp.where(chip == steps, steps - j, j)

    def load_w(n):
        j, t = units[n]
        return pltpu.make_async_copy(wg_ref.at[t, pl.ds(pl.multiple_of(shard(j) * depth, 128), depth)], w_tile.at[n % 2], wt_sem.at[n % 2])

    def load_f(n):
        j, t = units[n]
        return pltpu.make_async_copy(fg_ref.at[t, :, shard_lanes(shard(j))], f_tile.at[n % 2], ft_sem.at[n % 2])

    def add(t, slot, start, size, first):
        for col in range(0, 2 * cols, cols):
            value = jnp.dot(f_tile[slot, pl.ds(start, size)], w_tile[slot, :, pl.ds(col, cols)], preferred_element_type=jnp.float32)
            where = (t, pl.ds(start, size), pl.ds(col, cols))
            acc[where] = value if first else acc[where] + value

    rows = sum(ranges[fixed])
    part = rows // 4
    load_w(0).start()
    load_f(0).start()
    for n, (j, t) in enumerate(units):
        if n + 1 < len(units):
            load_w(n + 1).start()
            if units[n + 1][0] < steps:
                load_f(n + 1).start()
            else:
                @pl.when(jnp.logical_not(ends))
                def _():
                    load_f(n + 1).start()
        load_w(n).wait()

        def multiply():
            load_f(n).wait()

            def one(i, _):
                add(t, n % 2, pl.multiple_of(i * part, 16), part, j == 0)
                return 0
            lax.fori_loop(0, 4, one, 0)
        if j < steps:
            multiply()
        else:
            pl.when(jnp.logical_not(ends))(multiply)

    def swap_sum(t, k):
        rws = pl.ds(*ranges[k])
        return pltpu.make_async_remote_copy(
            src_ref=acc.at[t, rws, pl.ds(cols, cols)], dst_ref=theirs.at[t, rws], send_sem=a_send.at[t, k],
            recv_sem=a_recv.at[t, k], device_id=at(dp, 1 - core), device_id_type=MESH)

    for t, k in pieces:
        slot = (len(units) - towers + t) % 2
        for way in (0, 1):
            @pl.when(receives(steps - 1, way))
            def _():
                incoming(steps - 1, way, t, k).wait_recv()
                piece = pltpu.make_async_copy(
                    fg_ref.at[t, pl.ds(*ranges[k]), shard_lanes(shard(steps))], f_tile.at[slot, pl.ds(*ranges[k])], ft_sem.at[slot])
                piece.start()
                piece.wait()
                add(t, slot, *ranges[k], False)
        swap_sum(t, k).start()

    def swap_dz(t, k):
        rws = pl.ds(*ranges[k])
        return pltpu.make_async_remote_copy(
            src_ref=dz_here.at[t, rws], dst_ref=dz_ref.at[t, rws, pl.ds(cols, cols)], send_sem=z_send.at[t, k],
            recv_sem=z_recv.at[t, k], device_id=at(dp, 1 - core), device_id_type=MESH)

    def keep_dz(t, k):
        rws = pl.ds(*ranges[k])
        return pltpu.make_async_copy(dz_here.at[t, rws], dz_ref.at[t, rws, pl.ds(0, cols)], out_sem.at[t, k])

    sums_here[...] = jnp.zeros_like(sums_here)
    factor, cubic = math.sqrt(2.0 / math.pi), 0.044715

    def both(i, start):
        rws = pl.ds(pl.multiple_of(start + i * 16, 16), 16)
        activated, slope = [], []
        for t in range(towers):
            v = acc[t, rws, :cols] + theirs[t, rws] + sp_ref[t : t + 1]
            square = v * v
            th = jnp.tanh(factor * (v + cubic * (square * v)))
            activated.append(0.5 * v * (1.0 + th))
            slope.append(0.5 * (1.0 + th) + 0.5 * v * (1.0 - th * th) * (factor * (1.0 + 3.0 * cubic * square)))
        mask = live[rws]
        dy = [og[t, rws].astype(jnp.float32) * mask for t in range(towers)]
        for t in range(towers):
            y_here[t, rws] = ((sp_ref[2 + 2 * t : 3 + 2 * t] * activated[0] + sp_ref[3 + 2 * t : 4 + 2 * t] * activated[1]) * mask).astype(jnp.bfloat16)
        dz = [slope[t] * (sp_ref[2 + t : 3 + t] * dy[0] + sp_ref[4 + t : 5 + t] * dy[1]) for t in range(towers)]
        for t in range(towers):
            dz_here[t, rws] = dz[t].astype(jnp.bfloat16)
        terms = dz + [activated[0] * dy[0], activated[1] * dy[0], activated[0] * dy[1], activated[1] * dy[1]]
        for n, term in enumerate(terms):
            sums_here[n] += term[:8] + term[8:]
        return start

    for k in range(len(ranges)):
        for t in range(towers):
            swap_sum(t, k).wait_recv()
        start, size = ranges[k]
        lax.fori_loop(0, size // 16, lambda i, c: both(i, c), start)
        for t in range(towers):
            swap_dz(t, k).start()
            keep_dz(t, k).start()
    keep_y = pltpu.make_async_copy(y_here, y_ref, l_sem.at[5])
    keep_y.start()
    sg_ref[...] = jnp.zeros_like(sg_ref)
    for n in range(6):
        sg_ref[n : n + 1] = jnp.sum(sums_here[n], axis=0, keepdims=True)

    for t, k in pieces:
        swap_dz(t, k).wait_recv()
    for t, k in pieces:
        swap_dz(t, k).wait_send()
        keep_dz(t, k).wait()
        swap_sum(t, k).wait_send()
    keep_y.wait()
    totals.wait()
    for kind in range(3):
        tell(kind).wait_send()
        offer(kind, 0).wait_send()
        offer(kind, 1).wait_send()
    for t in (0, 1):
        for k in (0, 1):
            weight(0, k, t).wait_send()
            weight(1, k, t).wait_send()
        weight(2, 1 - core, t).wait_send()
    for slot in (0, 1):
        pass_on(0, slot).wait_send()
        pass_on(1, slot).wait_send()
    for step in range(steps):
        for t, k in pieces:
            for way in (0, 1):
                @pl.when(sends(step, way))
                def _():
                    feature(step, way, t, k).wait_send()


def forward(features, weights, out_grad, count, small_params, chips, share, ident):
    towers, _, depth = features.shape
    cols = weights.shape[2]
    keep, size = share[0]
    rows = keep + size
    half = keep // 32 * 16
    ranges = ((0, half), (half, keep - half), share[0])
    steps = chips - 1
    dma, vmem = pltpu.SemaphoreType.DMA, pltpu.VMEM
    bf16, f32 = jnp.bfloat16, jnp.float32
    anywhere, here = pl.BlockSpec(memory_space=pl.ANY), pl.BlockSpec(memory_space=pltpu.VMEM)
    many = (2, steps, towers * len(ranges))
    told = jnp.broadcast_to(count.astype(f32), (8, depth))
    return pl.pallas_call(
        functools.partial(forward_kernel, chips, share, ranges),
        out_shape=[jax.ShapeDtypeStruct((towers, rows, chips * depth), bf16),
                   jax.ShapeDtypeStruct((towers, chips * depth, 2 * cols), bf16),
                   jax.ShapeDtypeStruct((towers, rows, cols), bf16),
                   jax.ShapeDtypeStruct((towers, rows, 2 * cols), bf16),
                   jax.ShapeDtypeStruct((8, cols), f32),
                   jax.ShapeDtypeStruct((4, 8, depth), f32)],
        in_specs=[anywhere] * 3 + [anywhere, here],
        out_specs=[anywhere] * 4 + [here, anywhere],
        scratch_shapes=[vmem((4, towers, size, depth), bf16), vmem((towers, size, depth), bf16), vmem((4, towers, size, cols), bf16),
                        vmem((towers, rows, cols), bf16), vmem((2, depth, cols), f32), vmem((towers, 2, depth, cols), bf16),
                        vmem((2, rows, depth), bf16), vmem((2, depth, 2 * cols), bf16), vmem((towers, rows, 2 * cols), f32),
                        vmem((towers, rows, cols), f32), vmem((rows, cols), f32), vmem((towers, rows, cols), bf16),
                        vmem((towers, rows, cols), bf16), vmem((6, 8, cols), f32), vmem((4, 8, depth), f32),
                        dma(many), dma(many), dma((16,)), dma((16,)), dma((3 * towers,)), dma((6,)), dma((6,)), dma((2,)),
                        dma((3,)), dma((3,)), dma((6,)), dma((2,)), dma((2,))]
        + [dma((towers, len(ranges)))] * 5,
        compiler_params=pltpu.CompilerParams(collective_id=ident, has_side_effects=True, vmem_limit_bytes=58 * 2**20),
        cost_estimate=pl.CostEstimate(flops=4 * towers * rows * cols * depth * chips, bytes_accessed=800 * 2**20, transcendentals=0),
        name="forward",
    )(features, weights, out_grad, told, small_params)


def sum_kernel(chips, parts, share, y_ref, full_ref, dz_ref, w_ref, pg_ref, ps_ref, st_ref, d_ref, gr_ref, sr_ref,
               given, rest, back, held, w_here, dz_here, total, d_send, d_recv, w_sem, o_sem, g_send, g_recv, s_send, s_recv, own_sem,
               b_send, b_recv, v_send, v_recv, v_sem, y_send, y_recv, p_send, p_recv, l_sem):
    dp, chip, core = place()
    towers, rows, _ = dz_ref.shape
    depth = d_ref.shape[2]
    cols = pg_ref.shape[2] // 2
    size = rows // parts
    pieces = towers * parts
    steps = chips - 1
    across, along = dp ^ 1, dp ^ 2
    others = (across, along, dp ^ 3)
    at = lambda c, k: (c, 2 * chip + k)

    meet([(chip > 0, (dp, 2 * (chip - 1) + core)), (chip < chips - 1, (dp, 2 * (chip + 1) + core)),
          (chip >= 0, at(dp, 1 - core))] + [(chip >= 0, at(c, k)) for c in others for k in (0, 1)])

    def grad(kind, k, t):
        owner = (others + (dp,))[kind]
        return pltpu.make_async_remote_copy(
            src_ref=pg_ref.at[t, pl.ds(pl.multiple_of(owner * depth, 128), depth), pl.ds(pl.multiple_of((k ^ core) * cols, 128), cols)],
            dst_ref=gr_ref.at[dp, core, t], send_sem=g_send.at[(kind * 2 + k) * 2 + t],
            recv_sem=g_recv.at[(kind * 2 + core) * 2 + t], device_id=at(owner, k), device_id_type=MESH)

    def grad_arrived(kind, k, t):
        owner = (others + (dp,))[kind]
        pltpu.make_async_remote_copy(
            src_ref=gr_ref.at[owner, k, t], dst_ref=gr_ref.at[owner, k, t], send_sem=g_send.at[0],
            recv_sem=g_recv.at[(kind * 2 + k) * 2 + t], device_id=at(dp, core), device_id_type=MESH).wait_recv()

    def small(kind):
        return pltpu.make_async_remote_copy(
            src_ref=ps_ref, dst_ref=sr_ref.at[dp], send_sem=s_send.at[kind], recv_sem=s_recv.at[kind],
            device_id=at(others[kind], core), device_id_type=MESH)

    keep = share[0][0]
    width = y_ref.shape[2]
    slots = st_ref.shape[1]
    again = share[2][0] + share[2][1] - share[3][0]
    bands = ((0, keep), (keep, slots - keep))

    def give(kind):
        return pltpu.make_async_remote_copy(
            src_ref=y_ref.at[:, pl.ds(*share[0])], dst_ref=given.at[1 + kind], send_sem=v_send.at[kind],
            recv_sem=v_recv.at[kind], device_id=at(others[kind], core), device_id_type=MESH)

    def channels(shard, k, t, b):
        lanes = pl.ds(pl.multiple_of((2 * shard + k) * width, 128), width)
        return st_ref.at[t, pl.ds(*bands[b]), lanes]

    def own_channels(t, b):
        return y_ref.at[t, pl.ds(*bands[b])] if b == 0 else rest.at[t]

    def along_line(step, way, t, b, shard, there):
        n = t * 2 + b
        dst = channels(shard, core, t, b)
        return pltpu.make_async_remote_copy(
            src_ref=own_channels(t, b) if step == 0 else dst, dst_ref=dst, send_sem=y_send.at[way, step, n],
            recv_sem=y_recv.at[way, step, n], device_id=(dp, 2 * there + core), device_id_type=MESH)

    def leaves(step, way):
        return (chip < steps) & (chip >= step) if way == 0 else (chip > 0) & (chip + step <= steps)

    def comes(step, way):
        return chip > step if way == 0 else chip + step < steps

    def leaving(step, way, t, b):
        return along_line(step, way, t, b, chip - step if way == 0 else chip + step, chip + 1 if way == 0 else chip - 1)

    def coming(step, way, t, b):
        return along_line(step, way, t, b, chip - 1 - step if way == 0 else chip + 1 + step, chip)

    def to_core(shard, t, b, own=False):
        dst = channels(shard, core, t, b)
        return pltpu.make_async_remote_copy(
            src_ref=own_channels(t, b) if own else dst, dst_ref=dst, send_sem=p_send.at[shard, t * 2 + b],
            recv_sem=p_recv.at[shard, t * 2 + b], device_id=at(dp, 1 - core), device_id_type=MESH)

    def from_core(shard, t, b):
        dst = channels(shard, 1 - core, t, b)
        return pltpu.make_async_remote_copy(
            src_ref=dst, dst_ref=dst, send_sem=p_send.at[shard, t * 2 + b], recv_sem=p_recv.at[shard, t * 2 + b],
            device_id=at(dp, core), device_id_type=MESH)

    def pass_on(event):
        step, t, b = event // 4, event % 4 // 2, event % 2
        for way in (0, 1):
            @pl.when(comes(step, way))
            def _():
                coming(step, way, t, b).wait_recv()
                to_core(chip - 1 - step if way == 0 else chip + 1 + step, t, b).start()
            if step + 1 < steps:
                @pl.when(leaves(step + 1, way))
                def _():
                    leaving(step + 1, way, t, b).start()

    def launch(b):
        for t in range(towers):
            for way in (0, 1):
                @pl.when(leaves(0, way))
                def _():
                    leaving(0, way, t, b).start()
            to_core(chip, t, b, True).start()
            pltpu.make_async_copy(own_channels(t, b), channels(chip, core, t, b), v_sem.at[1 + t * 2 + b]).start()

    ends = (chip == 0, chip == chips - 1)

    def target(step, way):
        return chip + steps - step if way == 0 else chip - (steps - step)

    def sends(step, way):
        return (chip < steps) & (chip <= step) if way == 0 else (chip > 0) & (steps - chip <= step)

    def where(piece):
        return lax.rem(piece, towers), pl.multiple_of(lax.rem(piece // towers + parts - 1, parts) * size, 16)

    def passing(m, way, turn):
        t, row = where(lax.rem(m, pieces))
        there = chip + 1 if way == 0 else chip - 1
        rws = pl.ds(row, size)
        return pltpu.make_async_remote_copy(
            src_ref=held.at[way, turn // pieces, t, rws], dst_ref=held.at[way, m // pieces, t, rws],
            send_sem=d_send.at[way, m], recv_sem=d_recv.at[way, m], device_id=(dp, 2 * there + core), device_id_type=MESH)

    def landed(m, way):
        t, row = where(lax.rem(m, pieces))
        ref = held.at[way, m // pieces, t, pl.ds(row, size)]
        pltpu.make_async_remote_copy(src_ref=ref, dst_ref=ref, send_sem=d_send.at[way, m], recv_sem=d_recv.at[way, m],
                                     device_id=(dp, 2 * chip + core), device_id_type=MESH).wait_recv()

    third = depth // 3 if depth % 384 == 0 else depth

    def product(goal, t, row, col):
        return lax.dot_general(dz_here[t, pl.ds(row, size)], w_here[goal, t, pl.ds(col, third)], (((1,), (1,)), ((), ())),
                               preferred_element_type=jnp.float32)

    loads = []
    for n in range(chips):
        loads.append(pltpu.make_async_copy(w_ref.at[:, pl.ds(n * depth, depth)], w_here.at[n], w_sem.at[n]))
    loads.append(pltpu.make_async_copy(dz_ref, dz_here, w_sem.at[chips]))
    for load in loads:
        load.start()
    own = [pltpu.make_async_copy(
        pg_ref.at[t, pl.ds(pl.multiple_of(dp * depth, 128), depth), pl.ds(0, cols)], gr_ref.at[dp, core, t], own_sem.at[t])
        for t in range(towers)]
    own.append(pltpu.make_async_copy(ps_ref, sr_ref.at[dp], own_sem.at[towers]))
    for kind in (2, 0, 1):
        give(kind).start()
    mine = pltpu.make_async_copy(y_ref.at[:, pl.ds(*share[0])], given.at[0], v_sem.at[0])
    mine.start()
    launch(0)
    for kind in range(3):
        small(kind).start()
    for t in range(towers):
        for kind in (2, 0, 1):
            for k in (0, 1):
                grad(kind, k, t).start()
        grad(3, 1 - core, t).start()
    for copy in own:
        copy.start()
    for load in loads:
        load.wait()

    mine.wait()
    for kind in range(3):
        give(kind).wait_recv()

    def fill(i, _):
        for kind in range(4):
            skip = again if kind == 3 else 0
            place_of = (share[kind][0] if kind < 3 else share[2][0] + share[2][1]) - keep

            @pl.when(i * 16 >= skip)
            def _():
                for t in range(towers):
                    value = given[kind, t, pl.ds(pl.multiple_of(i * 16, 16), 16)].astype(jnp.float32) * full_ref[0]
                    rest[t, pl.ds(pl.multiple_of(place_of - skip + i * 16, 16), 16)] = value.astype(jnp.bfloat16)
        return 0

    lax.fori_loop(0, share[0][1] // 16, fill, 0)
    launch(1)

    window = 3
    lag = 2
    turns = steps * pieces

    def finish(piece):
        t, row = where(piece)
        s = lax.rem(piece, 2)
        rws = pl.ds(row, size)

        @pl.when(piece >= 2)
        def _():
            store(piece - 2, False)

        @pl.when((piece >= 2) & (piece < 2 + towers))
        def _():
            for kind in range(3):
                hand(kind, piece - 2).wait_send()
        last = (steps - 1) * pieces + piece
        for way in (0, 1):
            @pl.when(jnp.logical_not(ends[way]))
            def _():
                landed(last, way)
        for col in range(0, depth, third):
            value = product(chip, t, row, col)
            lanes = pl.ds(col, third)

            @pl.when(ends[0])
            def _():
                total[s, :, lanes] = (value + held[1, steps - 1, t, rws, lanes].astype(jnp.float32)).astype(jnp.bfloat16)

            @pl.when(ends[1])
            def _():
                total[s, :, lanes] = (value + held[0, steps - 1, t, rws, lanes].astype(jnp.float32)).astype(jnp.bfloat16)

            @pl.when(jnp.logical_not(ends[0] | ends[1]))
            def _():
                total[s, :, lanes] = (value + held[0, steps - 1, t, rws, lanes].astype(jnp.float32)
                                      + held[1, steps - 1, t, rws, lanes].astype(jnp.float32)).astype(jnp.bfloat16)
        store(piece, True)

        @pl.when(piece < towers)
        def _():
            for kind in (2, 0, 1):
                hand(kind, piece).start()
            back[0, t] = total[s, pl.ds(skip, size - skip)]

    def store(piece, start):
        t, row = where(piece)
        s = lax.rem(piece, 2)
        for here, length in ((piece < towers, skip), (piece >= towers, size)):
            @pl.when(here)
            def _():
                copy = pltpu.make_async_copy(total.at[s, pl.ds(0, length)], d_ref.at[t, pl.ds(row, length)], o_sem.at[s])
                (copy.start if start else copy.wait)()

    skip = size - share[0][1]

    def hand(kind, piece):
        t, s = lax.rem(piece, towers), lax.rem(piece, 2)
        return pltpu.make_async_remote_copy(
            src_ref=total.at[s, pl.ds(skip, size - skip)], dst_ref=back.at[1 + kind, t], send_sem=b_send.at[kind, t],
            recv_sem=b_recv.at[kind, t], device_id=at(others[kind], core), device_id_type=MESH)

    def turn(m, _):
        step, piece = m // pieces, lax.rem(m, pieces)
        t, row = where(piece)
        rws = pl.ds(row, size)
        for way in (0, 1):
            goes = (m < turns) & sends(step, way)

            @pl.when(goes & ends[way])
            def _():
                for col in range(0, depth, third):
                    held[way, step, t, rws, pl.ds(col, third)] = product(target(step, way), t, row, col).astype(jnp.bfloat16)

                @pl.when(m >= window)
                def _():
                    passing(m - window, way, m - window).wait_send()
                passing(m, way, m).start()

            @pl.when(goes & jnp.logical_not(ends[way]))
            def _():
                landed(m - pieces, way)
                for col in range(0, depth, third):
                    lanes = pl.ds(col, third)
                    held[way, step - 1, t, rws, lanes] = (
                        product(target(step, way), t, row, col) + held[way, step - 1, t, rws, lanes].astype(jnp.float32)
                    ).astype(jnp.bfloat16)
                passing(m, way, m - pieces).start()

        for event in range(4 * steps):
            @pl.when(m == min(2 * event + 3, turns + lag - 1))
            def _():
                pass_on(event)

        @pl.when(m >= turns - pieces + lag)
        def _():
            finish(m - (turns - pieces + lag))
        return 0

    lax.fori_loop(0, turns + lag, turn, 0)

    def drain(m, _):
        for way in (0, 1):
            goes = sends(m // pieces, way)

            @pl.when(goes & (jnp.logical_not(ends[way]) | (m >= turns - window)))
            def _():
                passing(m, way, m).wait_send()
        return 0

    lax.fori_loop(0, turns, drain, 0)
    for t in range(towers):
        for b in (0, 1):
            pltpu.make_async_copy(own_channels(t, b), channels(chip, core, t, b), v_sem.at[1 + t * 2 + b]).wait()
            for shard in range(chips):
                from_core(shard, t, b).wait_recv()
                to_core(shard, t, b).wait_send()
            for step in range(steps):
                for way in (0, 1):
                    @pl.when(leaves(step, way))
                    def _():
                        leaving(step, way, t, b).wait_send()
    for kind in range(3):
        give(kind).wait_send()
    for piece in (pieces - 2, pieces - 1):
        store(piece, False)
    for t in range(towers):
        for kind in range(3):
            hand(kind, t).wait_recv()

    def mask(i, _):
        rws = pl.ds(pl.multiple_of(i * 16, 16), 16)
        for kind in range(4):
            for t in range(towers):
                back[kind, t, rws] = (back[kind, t, rws].astype(jnp.float32) * full_ref[0]).astype(jnp.bfloat16)
        return 0

    lax.fori_loop(0, share[0][1] // 16, mask, 0)
    last = []
    for kind in range(4):
        skipped = again if kind == 3 else 0
        first, length = share[kind][0] + skipped, share[kind][1] - skipped
        last += [pltpu.make_async_copy(back.at[kind, t, pl.ds(skipped, length)], d_ref.at[t, pl.ds(first, length)], l_sem.at[kind, t])
                 for t in range(towers)]
    for copy in last:
        copy.start()
    for copy in last:
        copy.wait()
    for t in range(towers):
        for kind in range(3):
            for k in (0, 1):
                grad_arrived(kind, k, t)
        grad_arrived(3, 1 - core, t)
    for kind in range(3):
        small(kind).wait()
    for t in range(towers):
        for kind in range(3):
            for k in (0, 1):
                grad(kind, k, t).wait_send()
        grad(3, 1 - core, t).wait_send()
    for copy in own:
        copy.wait()


def sums(result, full, slots, wide_dz, wide_w, partial_g, partial_s, chips, parts, ident, share):
    towers, rows, wide = wide_dz.shape
    depth, cols = wide_w.shape[1] // chips, partial_g.shape[2] // 2
    steps = chips - 1
    dma = pltpu.SemaphoreType.DMA
    bf16 = jnp.bfloat16
    anywhere = pl.BlockSpec(memory_space=pl.ANY)
    return pl.pallas_call(
        functools.partial(sum_kernel, chips, parts, share),
        out_shape=[jax.ShapeDtypeStruct((towers, slots, 2 * chips * cols), bf16),
                   jax.ShapeDtypeStruct((towers, slots, depth), bf16),
                   jax.ShapeDtypeStruct((4, 2, towers, depth, cols), bf16),
                   jax.ShapeDtypeStruct((4,) + partial_s.shape, jnp.float32)],
        in_specs=[anywhere, pl.BlockSpec(memory_space=pltpu.SMEM)] + [anywhere] * 4,
        out_specs=[anywhere] * 4,
        scratch_shapes=[pltpu.VMEM((4, towers, share[0][1], cols), bf16), pltpu.VMEM((towers, slots - share[0][0], cols), bf16),
                        pltpu.VMEM((4, towers, share[0][1], depth), bf16),
                        pltpu.VMEM((2, steps, towers, rows, depth), bf16), pltpu.VMEM((chips, towers, depth, wide), bf16),
                        pltpu.VMEM((towers, rows, wide), bf16), pltpu.VMEM((2, rows // parts, depth), bf16),
                        dma((2, steps * towers * parts)), dma((2, steps * towers * parts)), dma((chips + 1,)), dma((2,)),
                        dma((16,)), dma((16,)), dma((3,)), dma((3,)), dma((towers + 1,)), dma((3, towers)), dma((3, towers)), dma((3,)), dma((3,)), dma((5,)),
                        dma((2, steps, 4)), dma((2, steps, 4)), dma((chips, 4)), dma((chips, 4)), dma((4, towers))],
        compiler_params=pltpu.CompilerParams(collective_id=ident, has_side_effects=True, vmem_limit_bytes=58 * 2**20),
        cost_estimate=pl.CostEstimate(flops=2 * towers * rows * wide * depth * chips, bytes_accessed=800 * 2**20, transcendentals=0),
        name="sums",
    )(result, full, wide_dz, wide_w, partial_g, partial_s)


def small_step(small_params, small_moment_one, small_moment_two, small_average, small_grad):
    first, second, direction = adam_part(small_moment_one, small_moment_two, small_grad)
    fresh = small_params - rate_small * direction
    return first, second, fresh, ema_decay * small_average + (1.0 - ema_decay) * fresh


def update(d_feat, stitched, parts, small_parts, states, small_states):
    small_grad = jnp.sum(small_parts, 0)[: small_states[0].shape[0]]
    *fresh, stitched, d_feat = soap(parts, stitched, d_feat, *states)
    return (stitched, d_feat) + tuple(fresh) + small_step(*small_states, small_grad)


def own_rows(features, out_grad, totals, passed, states, small_states):
    _, rows, _ = features.shape
    weights, small_params = states[0], small_states[0]
    cols = weights.shape[2]
    cores = lax.axis_size("mp")
    swap = [(i, i ^ 1) for i in range(cores)]
    ranges = ((0, rows // 2), (rows // 2, rows // 2))
    live_rows = (jnp.arange(rows, dtype=jnp.float32) < totals[0]).astype(jnp.float32)
    wide_f, wide_w = gather(features, weights.astype(jnp.bfloat16), cores // 2, ranges, 1)
    partial = jnp.einsum("tri,tio->tro", wide_f, wide_w, preferred_element_type=jnp.float32)
    product = partial[:, :, :cols] + lax.ppermute(partial[:, :, cols:], "mp", swap)
    result, back = jax.vjp(lambda a, b: stitch_local(a, b, live_rows), product, small_params)
    stitched = lax.all_gather(result.astype(jnp.bfloat16), "mp", axis=2, tiled=True)
    dz, small_part = back(out_grad.astype(jnp.float32))
    dz_low = dz.astype(jnp.bfloat16)
    wide_dz = jnp.concatenate([dz_low, lax.ppermute(dz_low, "mp", swap)], axis=2)
    partial_d = jnp.einsum("tro,tio->tri", wide_dz, wide_w, preferred_element_type=jnp.float32)
    partial_g = jnp.einsum("tri,tro->tio", wide_f, wide_dz, preferred_element_type=jnp.float32)
    small_part = jnp.pad(small_part, ((0, 2), (0, 0)))
    d_feat, parts, small_parts = reduce(
        partial_d.astype(jnp.bfloat16), partial_g.astype(jnp.bfloat16), small_part, cores // 2, ranges, 2
    )
    return update(d_feat, stitched, parts, small_parts, states, small_states)


def shares(rows):
    keep = rows * 15 // 32 // 16 * 16
    size = -(-(rows - keep) // 64) * 16
    return keep, ((keep, size), (keep + size, size), (keep + 2 * size, size), (rows - size, size))


def shared_rows(features, out_grad, totals, passed, states, small_states):
    rows = features.shape[1]
    keep, share = shares(rows)
    wide_f, wide_w, result, wide_dz, small_part = passed
    full = (totals[:1] > keep).astype(jnp.float32)
    partial_g = jnp.einsum("tri,tro->tio", wide_f, wide_dz, preferred_element_type=jnp.float32)
    stitched, d_feat, parts, small_parts = sums(
        result, full, rows, wide_dz, wide_w, partial_g.astype(jnp.bfloat16), small_part, lax.axis_size("mp") // 2, 4, 4, share
    )
    return update(d_feat, stitched, parts, small_parts, states, small_states)


def line_body(
    features,
    counts,
    weights,
    small_params,
    out_grad,
    moment_one,
    moment_two,
    average,
    basis_left,
    basis_right,
    small_moment_one,
    small_moment_two,
    small_average,
):
    keep, share = shares(features.shape[1])
    *passed, told = forward(
        features, weights, out_grad, jnp.sum(counts), small_params, lax.axis_size("mp") // 2, share, 3
    )
    totals = told[:, 0, 0]
    return lax.cond(
        jnp.sum(totals > keep) == 1,
        shared_rows,
        own_rows,
        features,
        out_grad,
        totals,
        passed,
        (weights, moment_one, moment_two, average, basis_left, basis_right),
        (small_params, small_moment_one, small_moment_two, small_average),
    )


def plain_body(
    features,
    counts,
    weights,
    small_params,
    out_grad,
    moment_one,
    moment_two,
    average,
    basis_left,
    basis_right,
    small_moment_one,
    small_moment_two,
    small_average,
):
    slot_count = features.shape[1]
    total = jnp.sum(counts)
    live_rows = (jnp.arange(slot_count, dtype=jnp.int32) < total).astype(jnp.float32)
    weights_low = lax.all_gather(weights.astype(jnp.bfloat16), "dp", axis=1, tiled=True)
    feats_full = lax.all_gather(features, "mp", axis=2, tiled=True)
    product = jnp.einsum(
        "tri,tio->tro", feats_full, weights_low, preferred_element_type=jnp.float32
    )
    result, back = jax.vjp(lambda a, b: stitch_local(a, b, live_rows), product, small_params)
    stitched = lax.all_gather(result.astype(jnp.bfloat16), "mp", axis=2, tiled=True)
    dz, small_part = back(out_grad.astype(jnp.float32))
    dz_low = dz.astype(jnp.bfloat16)
    grad_part = jnp.einsum("tri,tro->tio", feats_full, dz_low, preferred_element_type=jnp.float32)
    partial_sums = jnp.einsum(
        "tro,tio->tri", dz_low, weights_low, preferred_element_type=jnp.float32
    )
    d_feat = lax.psum_scatter(
        partial_sums.astype(jnp.float32), "mp", scatter_dimension=2, tiled=True
    )
    grad = lax.psum_scatter(grad_part, "dp", scatter_dimension=1, tiled=True)
    small_grad = lax.psum(small_part, "dp")
    towers, n_in, n_out = grad.shape
    blocks = grad.reshape(towers, n_in // BLOCK, BLOCK, n_out // BLOCK, BLOCK)
    rotated = jnp.einsum(
        "trcai,tracb,trcbj->tricj", basis_left, blocks, basis_right, precision=lax.Precision.HIGHEST
    ).reshape(towers, n_in, n_out)
    first, second, direction = adam_part(moment_one, moment_two, rotated)
    turned = direction.reshape(towers, n_in // BLOCK, BLOCK, n_out // BLOCK, BLOCK)
    step_back = jnp.einsum(
        "trcai,tricj,trcbj->tracb", basis_left, turned, basis_right, precision=lax.Precision.HIGHEST
    ).reshape(towers, n_in, n_out)
    new_weights = weights - rate_main * (step_back + decay_weight * weights)
    new_average = ema_decay * average + (1.0 - ema_decay) * new_weights
    return (
        stitched,
        d_feat.astype(jnp.bfloat16),
        first,
        second,
        new_weights,
        new_average,
        new_weights.astype(jnp.bfloat16),
    ) + small_step(small_params, small_moment_one, small_moment_two, small_average, small_grad)


def solution(mesh):
    def body(features, counts, weights, *rest):
        dp, mp = mesh.shape["dp"], mesh.shape["mp"]
        tiles = features.shape[2] % 128 == 0 and weights.shape[2] % 128 == 0
        suits = dp == 4 and mp == 2 * dp and tiles and features.shape[1] % 64 == 0
        return (line_body if suits else plain_body)(features, counts, weights, *rest)

    return jax.shard_map(
        body,
        mesh=mesh,
        in_specs=(
            P(None, "dp", "mp"),
            P("dp"),
            P(None, "dp", "mp"),
            P(None, "mp"),
            P(None, "dp", "mp"),
            P(None, "dp", "mp"),
            P(None, "dp", "mp"),
            P(None, "dp", "mp"),
            P(None, "dp", "mp", None, None),
            P(None, "dp", "mp", None, None),
            P(None, "mp"),
            P(None, "mp"),
            P(None, "mp"),
        ),
        out_specs=(
            P(None, "dp", None),
            P(None, "dp", "mp"),
            P(None, "dp", "mp"),
            P(None, "dp", "mp"),
            P(None, "dp", "mp"),
            P(None, "dp", "mp"),
            P(None, "dp", "mp"),
            P(None, "mp"),
            P(None, "mp"),
            P(None, "mp"),
            P(None, "mp"),
        ),
        check_vma=False,
    )
```

```python
import functools
import math

import jax
import jax.numpy as jnp
from jax import lax
from jax.experimental import pallas as pl
from jax.experimental.pallas import tpu as pltpu
from jax.sharding import PartitionSpec as P

BLOCK = 64
STEP = 5


beta_one = 0.5
beta_two = 0.5
ema_decay = 0.5
rate_main = 0.01
rate_small = 0.05
decay_weight = 0.01
eps = 1e-08


def stitch_local(product, small, live_rows):
    pre_act = product + small[0:2][:, None, :]
    activated = jax.nn.gelu(pre_act, approximate=True)
    first = small[2] * activated[0] + small[3] * activated[1]
    second = small[4] * activated[0] + small[5] * activated[1]
    return jnp.stack([first, second]) * live_rows[None, :, None]


def adam_part(moment_a, moment_b, grad):
    first = beta_one * moment_a + (1.0 - beta_one) * grad
    second = beta_two * moment_b + (1.0 - beta_two) * grad * grad
    direction = first / (1.0 - beta_one**STEP) / (jnp.sqrt(second / (1.0 - beta_two**STEP)) + eps)
    return (first, second, direction)

def split(v):
    high = v.astype(jnp.bfloat16)
    return high, (v - high.astype(jnp.float32)).astype(jnp.bfloat16)

def soap_blocks(grads, lefts, rights, moments):
    row = lax.broadcasted_iota(jnp.int32, (2 * BLOCK, 2 * BLOCK), 0) // BLOCK
    lane = lax.broadcasted_iota(jnp.int32, (2 * BLOCK, 2 * BLOCK), 1) // BLOCK
    own = row == lane

    def diagonal(v):
        return jnp.where(own, jnp.concatenate([v, v], axis=0), 0.0)

    def beside(v):
        return jnp.concatenate([v[0], v[1]], axis=1)

    def stationary(v, axis):
        high, low = split(v)
        return jnp.concatenate([high, high, low], axis=axis)

    def moving(v, axis):
        high, low = split(v)
        return jnp.concatenate([high, low, high], axis=axis)

    def dots(a, b, ca, cb):
        dims = (((ca,), (cb,)), ((), ()))
        return [lax.dot_general(x, y, dims, preferred_element_type=jnp.float32) for x, y in zip(a, b)]

    right = [diagonal(beside(v)) for v in rights]
    values = dots([moving(v, 1) for v in grads], [stationary(v, 0) for v in right], 1, 0)
    values = dots([stationary(v.reshape(2 * BLOCK, BLOCK), 0) for v in lefts], [moving(diagonal(v), 0) for v in values], 0, 0)
    states = [adam_part(a, b, v) for (a, b), v in zip(moments, values)]
    values = dots([moving(v[2], 1) for v in states], [stationary(v, 1) for v in right], 1, 1)
    values = dots([stationary(beside(v), 1) for v in lefts], [moving(diagonal(v), 0) for v in values], 1, 0)
    return [(first, second, step) for (first, second, _), step in zip(states, values)]


def soap_body(together, strips, full, parts, stitched, d_feat, weights, moment_a, moment_b, average, left, right,
              first, second, new_weights, new_average, copy, stitched_out, d_feat_out):
    groups, pairs = left.shape[1], left.shape[2] // 2
    length = stitched.shape[1]
    row = jnp.minimum(pl.program_id(1) * pl.num_programs(2) + pl.program_id(2), strips - 1) * length

    @pl.when(row + length <= full[0])
    def _():
        stitched_out[...] = stitched[...]
        d_feat_out[...] = d_feat[...]

    @pl.when(row + length > full[0])
    def _():
        for source, target in ((stitched, stitched_out), (d_feat, d_feat_out)):
            def clear(i, _):
                rows = pl.ds(pl.multiple_of(i * 16, 16), 16)
                target[0, rows] = jnp.where(row + i * 16 < full[0], source[0, rows], 0)
                return 0
            lax.fori_loop(0, length // 16, clear, 0)

    def blocks(g, _):
        places = [(g * together + s, q) for s in range(together) for q in range(pairs)]
        ats = [(0, pl.ds(pl.multiple_of(r * BLOCK, BLOCK), BLOCK), pl.ds(2 * BLOCK * q, 2 * BLOCK)) for r, q in places]
        grads = []
        for at in ats:
            grad = parts[(0, 0) + at].astype(jnp.float32)
            for k in range(1, parts.shape[0]):
                grad = grad + parts[(k, 0) + at].astype(jnp.float32)
            grads.append(grad)
        done = soap_blocks(grads, [left[0, r, 2 * q : 2 * q + 2] for r, q in places],
                           [right[0, r, 2 * q : 2 * q + 2] for r, q in places], [(moment_a[at], moment_b[at]) for at in ats])
        olds = [(weights[at], average[at]) for at in ats]
        for at, (one, two, step), (held, mean) in zip(ats, done, olds):
            first[at] = one
            second[at] = two
            fresh = held - rate_main * (step + decay_weight * held)
            new_weights[at] = fresh
            new_average[at] = ema_decay * mean + (1.0 - ema_decay) * fresh
            copy[at] = fresh.astype(jnp.bfloat16)
        return 0

    lax.fori_loop(0, groups // together, blocks, 0)


def soap(parts, wanted, stitched, d_feat, weights, moment_a, moment_b, average, left, right, group=6):
    towers, rows, cols = weights.shape
    half = parts.shape[3]
    steps = half // (BLOCK * group)
    flat = lambda t, p, g: (t, p * steps + g, 0)
    basis = lambda t, p, g: (t, p * steps + g, 0, 0, 0)
    state = pl.BlockSpec((1, BLOCK * group, cols), flat)
    base = pl.BlockSpec((1, group, cols // BLOCK, BLOCK, BLOCK), basis)
    full = jax.ShapeDtypeStruct(weights.shape, jnp.float32)
    strips = max(n for n in range(1, 2 * steps + 1) if stitched.shape[1] % (16 * n) == 0)

    def through(v):
        return pl.BlockSpec((1, v.shape[1] // strips, v.shape[2]), lambda t, p, g: (t, jnp.minimum(p * steps + g, strips - 1), 0))

    return pl.pallas_call(
        functools.partial(soap_body, 2 - group % 2, strips),
        grid=(towers, 2, steps),
        in_specs=[pl.BlockSpec(memory_space=pltpu.SMEM),
                  pl.BlockSpec((parts.shape[0], 1, 1, BLOCK * group, cols), lambda t, p, g: (0, p, t, g, 0)),
                  through(stitched), through(d_feat), state, state, state, state, base, base],
        out_specs=[state] * 5 + [through(stitched), through(d_feat)],
        out_shape=[full] * 4 + [jax.ShapeDtypeStruct(weights.shape, jnp.bfloat16)]
        + [jax.ShapeDtypeStruct(v.shape, v.dtype) for v in (stitched, d_feat)],
        compiler_params=pltpu.CompilerParams(vmem_limit_bytes=48 * 2**20),
        cost_estimate=pl.CostEstimate(flops=8 * 2 * towers * rows * cols * 64, bytes_accessed=130 * 2**20, transcendentals=0),
        name="soap",
    )(wanted, parts, stitched, d_feat, weights, moment_a, moment_b, average, left, right)


MESH = pl.DeviceIdType.MESH


def place():
    mp = lax.axis_index("mp")
    return lax.axis_index("dp"), mp // 2, lax.rem(mp, 2)


def meet(devices):
    barrier = pltpu.get_barrier_semaphore()
    expected = 0
    for here, device in devices:
        @pl.when(here)
        def _():
            pl.semaphore_signal(barrier, inc=1, device_id=device, device_id_type=MESH)
        expected = expected + jnp.where(here, 1, 0)
    pl.semaphore_wait(barrier, expected)


def gather_kernel(chips, ranges, f_ref, w_ref, fg_ref, wg_ref, f_send, f_recv, w_send, w_recv, own_sem):
    dp, chip, core = place()
    towers, rows, depth = f_ref.shape
    cols = w_ref.shape[2]
    across, along = dp ^ 1, dp ^ 2
    at = lambda c, k: (c, 2 * chip + k)

    meet([(chip > 0, (dp, 2 * (chip - 1) + core)), (chip < chips - 1, (dp, 2 * (chip + 1) + core)),
          (chip >= 0, at(dp, 1 - core))] + [(chip >= 0, at(c, k)) for c in (across, along) for k in (0, 1)])

    def copies(step, way, t, k, shard, there):
        lanes = pl.ds(pl.multiple_of(shard * depth, 128), depth)
        rws = pl.ds(*ranges[k])
        src = fg_ref.at[t, rws, lanes]
        if step == 0:
            src = f_ref.at[t, rws]
        n = ((way * (chips - 1) + step) * towers + t) * len(ranges) + k
        return pltpu.make_async_remote_copy(
            src_ref=src, dst_ref=fg_ref.at[t, rws, lanes], send_sem=f_send.at[n], recv_sem=f_recv.at[n],
            device_id=(dp, 2 * there + core), device_id_type=MESH)

    def feature(step, way, t, k):
        return copies(step, way, t, k, chip - step if way == 0 else chip + step, chip + 1 if way == 0 else chip - 1)

    def incoming(step, way, t, k):
        return copies(step, way, t, k, chip - 1 - step if way == 0 else chip + 1 + step, chip)

    def sends(step, way):
        return (chip < chips - 1) & (chip >= step) if way == 0 else (chip > 0) & (chip + step < chips)

    def receives(step, way):
        return chip > step if way == 0 else chip + step < chips - 1

    def launch(t, k):
        for way in (0, 1):
            @pl.when(sends(0, way))
            def _():
                feature(0, way, t, k).start()

    def block(owner, slot, t):
        return wg_ref.at[t, pl.ds(pl.multiple_of(owner * depth, 128), depth), pl.ds(pl.multiple_of(slot * cols, 128), cols)]

    def weight(kind, k, t):
        to = at((across, along, dp)[kind], k)
        n = (kind * 2 + core) * 2 + t
        return pltpu.make_async_remote_copy(
            src_ref=w_ref.at[t, pl.ds(pl.multiple_of(k * depth, 128), depth)], dst_ref=block(dp, k ^ core, t),
            send_sem=w_send.at[(kind * 2 + k) * 2 + t], recv_sem=w_recv.at[n], device_id=to, device_id_type=MESH)

    def forward(kind, slot):
        owner, to, t = ((across, along, 0), (along, across, 1))[kind]
        n = 12 + kind * 2 + slot
        return pltpu.make_async_remote_copy(
            src_ref=block(owner, slot, t), dst_ref=block(owner, slot, t),
            send_sem=w_send.at[n], recv_sem=w_recv.at[n], device_id=at(to, core), device_id_type=MESH)

    def arrived(kind, slot, t):
        owner = (across, along, dp)[kind]
        n = (kind * 2 + (slot ^ core)) * 2 + t
        pltpu.make_async_remote_copy(
            src_ref=block(owner, slot, t), dst_ref=block(owner, slot, t), send_sem=w_send.at[n], recv_sem=w_recv.at[n],
            device_id=at(dp, core), device_id_type=MESH).wait_recv()

    mine = pl.ds(pl.multiple_of(chip * depth, 128), depth)
    own = [pltpu.make_async_copy(f_ref.at[t], fg_ref.at[t, :, mine], own_sem.at[t]) for t in range(towers)]
    own += [pltpu.make_async_copy(w_ref.at[t, pl.ds(pl.multiple_of(core * depth, 128), depth)], block(dp, 0, t), own_sem.at[2 + t])
            for t in range(towers)]

    pieces = [(t, k) for k in range(len(ranges)) for t in range(towers)]
    for t, k in pieces:
        launch(t, k)
    for copy in own:
        copy.start()
    for t in (0, 1):
        for k in (0, 1):
            weight(0, k, t).start()
            weight(1, k, 1 - t).start()
    for t in (0, 1):
        weight(2, 1 - core, t).start()

    for step in range(chips - 1):
        for t, k in pieces:
            for way in (0, 1):
                @pl.when(receives(step, way))
                def _():
                    incoming(step, way, t, k).wait_recv()
                if step + 1 < chips - 1:
                    @pl.when(sends(step + 1, way))
                    def _():
                        feature(step + 1, way, t, k).start()
            if step == 0 and (t, k) == pieces[-1]:
                for slot in (0, 1):
                    arrived(0, slot, 0)
                    forward(0, slot).start()
                    arrived(1, slot, 1)
                    forward(1, slot).start()

    for slot in (0, 1):
        arrived(0, slot, 1)
        arrived(1, slot, 0)
        forward(0, slot).wait_recv()
        forward(1, slot).wait_recv()
    for t in (0, 1):
        arrived(2, 1, t)
    for t in (0, 1):
        for k in (0, 1):
            weight(0, k, t).wait_send()
            weight(1, k, t).wait_send()
        weight(2, 1 - core, t).wait_send()
    for slot in (0, 1):
        forward(0, slot).wait_send()
        forward(1, slot).wait_send()
    for step in range(chips - 1):
        for t, k in pieces:
            for way in (0, 1):
                @pl.when(sends(step, way))
                def _():
                    feature(step, way, t, k).wait_send()
    for copy in own:
        copy.wait()


def gather(features, weights_low, chips, ranges, ident):
    towers, rows, depth = features.shape
    cols = weights_low.shape[2]
    count = 2 * (chips - 1) * towers * len(ranges)
    dma = pltpu.SemaphoreType.DMA
    anywhere = pl.BlockSpec(memory_space=pl.ANY)
    return pl.pallas_call(
        functools.partial(gather_kernel, chips, ranges),
        out_shape=[jax.ShapeDtypeStruct((towers, rows, chips * depth), jnp.bfloat16),
                   jax.ShapeDtypeStruct((towers, chips * depth, 2 * cols), jnp.bfloat16)],
        in_specs=[anywhere] * 2,
        out_specs=[anywhere] * 2,
        scratch_shapes=[dma((count,)), dma((count,)), dma((16,)), dma((16,)), dma((4,))],
        compiler_params=pltpu.CompilerParams(collective_id=ident, has_side_effects=True),
        cost_estimate=pl.CostEstimate(flops=0, bytes_accessed=800 * 2**20, transcendentals=0),
        name="gather",
    )(features, weights_low)


def reduce_kernel(chips, ranges, pd_ref, pg_ref, ps_ref, d_ref, gr_ref, sr_ref, held, term, total,
                  d_send, d_recv, t_sem, o_sem, g_send, g_recv, s_send, s_recv, own_sem):
    dp, chip, core = place()
    towers, rows, depth = d_ref.shape
    cols = pg_ref.shape[2] // 2
    across, along = dp ^ 1, dp ^ 2
    others = (across, along, dp ^ 3)
    at = lambda c, k: (c, 2 * chip + k)

    meet([(chip > 0, (dp, 2 * (chip - 1) + core)), (chip < chips - 1, (dp, 2 * (chip + 1) + core)),
          (chip >= 0, at(dp, 1 - core))] + [(chip >= 0, at(c, k)) for c in others for k in (0, 1)])

    def grad(kind, k, t):
        owner = (others + (dp,))[kind]
        return pltpu.make_async_remote_copy(
            src_ref=pg_ref.at[t, pl.ds(pl.multiple_of(owner * depth, 128), depth), pl.ds(pl.multiple_of((k ^ core) * cols, 128), cols)],
            dst_ref=gr_ref.at[dp, core, t], send_sem=g_send.at[(kind * 2 + k) * 2 + t],
            recv_sem=g_recv.at[(kind * 2 + core) * 2 + t], device_id=at(owner, k), device_id_type=MESH)

    def grad_arrived(kind, k, t):
        owner = (others + (dp,))[kind]
        pltpu.make_async_remote_copy(
            src_ref=gr_ref.at[owner, k, t], dst_ref=gr_ref.at[owner, k, t], send_sem=g_send.at[0],
            recv_sem=g_recv.at[(kind * 2 + k) * 2 + t], device_id=at(dp, core), device_id_type=MESH).wait_recv()

    def small(kind):
        return pltpu.make_async_remote_copy(
            src_ref=ps_ref, dst_ref=sr_ref.at[dp], send_sem=s_send.at[kind], recv_sem=s_recv.at[kind],
            device_id=at(others[kind], core), device_id_type=MESH)

    def target(step, way):
        return chip + chips - 1 - step if way == 0 else chip - (chips - 1 - step)

    def sends(step, way):
        return (chip < chips - 1) & (chip <= step) if way == 0 else (chip > 0) & (chips - 1 - chip <= step)

    def receives(step, way):
        return (chip > 0) & (chip <= step + 1) if way == 0 else (chip < chips - 1) & (chips - 1 - chip <= step + 1)

    def own_term(goal, t, k):
        return pd_ref.at[t, pl.ds(*ranges[k]), pl.ds(pl.multiple_of(goal * depth, 128), depth)]

    def partial(step, way, t, k, first):
        n = ((way * (chips - 1) + step) * towers + t) * len(ranges) + k
        src = own_term(target(step, way), t, k) if first else held.at[way, step - 1, t, pl.ds(*ranges[k])]
        there = chip + 1 if way == 0 else chip - 1
        return pltpu.make_async_remote_copy(
            src_ref=src, dst_ref=held.at[way, step, t, pl.ds(*ranges[k])], send_sem=d_send.at[n], recv_sem=d_recv.at[n],
            device_id=(dp, 2 * there + core), device_id_type=MESH)

    def landed(step, way, t, k):
        n = ((way * (chips - 1) + step) * towers + t) * len(ranges) + k
        ref = held.at[way, step, t, pl.ds(*ranges[k])]
        pltpu.make_async_remote_copy(src_ref=ref, dst_ref=ref, send_sem=d_send.at[n], recv_sem=d_recv.at[n],
                                     device_id=(dp, 2 * chip + core), device_id_type=MESH).wait_recv()

    pieces = [(t, k) for t in range(towers) for k in range(len(ranges))]
    ends = (chip == 0, chip == chips - 1)
    for t, k in pieces:
        for way in (0, 1):
            @pl.when(ends[way])
            def _():
                partial(0, way, t, k, True).start()
    own = [pltpu.make_async_copy(
        pg_ref.at[t, pl.ds(pl.multiple_of(dp * depth, 128), depth), pl.ds(0, cols)], gr_ref.at[dp, core, t], own_sem.at[t])
        for t in range(towers)]
    own.append(pltpu.make_async_copy(ps_ref, sr_ref.at[dp], own_sem.at[towers]))
    for copy in own:
        copy.start()
    for kind in range(3):
        small(kind).start()
    for t in range(towers):
        for kind in (2, 0, 1):
            for k in (0, 1):
                grad(kind, k, t).start()
        grad(3, 1 - core, t).start()

    strip = 16

    for step in range(1, chips - 1):
        for t, k in pieces:
            for way in (0, 1):
                @pl.when(sends(step, way) & ends[way])
                def _():
                    partial(step, way, t, k, True).start()

                @pl.when(sends(step, way) & jnp.logical_not(ends[way]))
                def _():
                    start, size = ranges[k]
                    load = pltpu.make_async_copy(own_term(target(step, way), t, k), term.at[way, pl.ds(0, size)], t_sem.at[way])
                    load.start()
                    landed(step - 1, way, t, k)
                    load.wait()

                    def add(i, _):
                        rws = pl.ds(pl.multiple_of(i * strip, strip), strip)
                        all_rows = pl.ds(pl.multiple_of(start + i * strip, strip), strip)
                        held[way, step - 1, t, all_rows] = (
                            held[way, step - 1, t, all_rows].astype(jnp.float32) + term[way, rws].astype(jnp.float32)
                        ).astype(jnp.bfloat16)
                        return 0
                    lax.fori_loop(0, size // strip, add, 0)
                    partial(step, way, t, k, False).start()

    stores = []
    for n, (t, k) in enumerate(pieces):
        s = n % 2
        start, size = ranges[k]
        load = pltpu.make_async_copy(own_term(chip, t, k), term.at[s, pl.ds(0, size)], t_sem.at[s])
        load.start()
        for way in (0, 1):
            @pl.when(receives(chips - 2, way))
            def _():
                landed(chips - 2, way, t, k)
        load.wait()
        if n >= 2:
            stores[n - 2].wait()

        def finish(i, _):
            rws = pl.ds(pl.multiple_of(i * strip, strip), strip)
            all_rows = pl.ds(pl.multiple_of(start + i * strip, strip), strip)
            value = term[s, rws].astype(jnp.float32)
            for way in (0, 1):
                here = receives(chips - 2, way)
                value = value + jnp.where(here, held[way, chips - 2, t, all_rows].astype(jnp.float32), 0.0)
            total[s, rws] = value.astype(jnp.bfloat16)
            return 0
        lax.fori_loop(0, size // strip, finish, 0)
        stores.append(pltpu.make_async_copy(total.at[s, pl.ds(0, size)], d_ref.at[t, pl.ds(start, size)], o_sem.at[s]))
        stores[n].start()
    for store in stores[-2:]:
        store.wait()

    for t in range(towers):
        for kind in range(3):
            for k in (0, 1):
                grad_arrived(kind, k, t)
        grad_arrived(3, 1 - core, t)
    for kind in range(3):
        small(kind).wait()
    for t in range(towers):
        for kind in range(3):
            for k in (0, 1):
                grad(kind, k, t).wait_send()
        grad(3, 1 - core, t).wait_send()
    for step in range(chips - 1):
        for t, k in pieces:
            for way in (0, 1):
                @pl.when(sends(step, way))
                def _():
                    partial(step, way, t, k, True).wait_send()
    for copy in own:
        copy.wait()


def reduce(partial_d, partial_g, partial_s, chips, ranges, ident):
    towers, rows, wide = partial_d.shape
    depth, cols = wide // chips, partial_g.shape[2] // 2
    count = 2 * (chips - 1) * towers * len(ranges)
    part = max(size for _, size in ranges)
    dma = pltpu.SemaphoreType.DMA
    bf16 = jnp.bfloat16
    out_shape = [jax.ShapeDtypeStruct((towers, rows, depth), bf16),
                 jax.ShapeDtypeStruct((4, 2, towers, depth, cols), bf16),
                 jax.ShapeDtypeStruct((4,) + partial_s.shape, jnp.float32)]
    return pl.pallas_call(
        functools.partial(reduce_kernel, chips, ranges),
        out_shape=out_shape,
        in_specs=[pl.BlockSpec(memory_space=pl.ANY)] * 3,
        out_specs=[pl.BlockSpec(memory_space=pl.ANY)] * len(out_shape),
        scratch_shapes=[pltpu.VMEM((2, chips - 1, towers, rows, depth), bf16),
                        pltpu.VMEM((2, part, depth), bf16), pltpu.VMEM((2, part, depth), bf16),
                        dma((count,)), dma((count,)), dma((2,)), dma((2,)), dma((16,)), dma((16,)), dma((3,)), dma((3,)), dma((towers + 1,))],
        compiler_params=pltpu.CompilerParams(collective_id=ident, has_side_effects=True, vmem_limit_bytes=56 * 2**20),
        cost_estimate=pl.CostEstimate(flops=0, bytes_accessed=800 * 2**20, transcendentals=0),
        name="reduce",
    )(partial_d, partial_g, partial_s)


def forward_kernel(chips, parts, share, f_ref, w_ref, o_ref, n_ref, sp_ref, fg_ref, wg_ref, y_ref, dz_ref, sg_ref, tot_ref,
                   offer_f, taken, offer_o, og, w_wide, w_low, f_tile, w_tile, acc, theirs, live, y_here, dz_here, sums_here,
                   tot, f_send, f_recv, w_send, w_recv, own_sem, x_send, x_recv, k_sem, n_send, n_recv, l_sem, ft_sem, wt_sem,
                   a_send, a_recv, z_send, z_recv, out_sem):
    dp, chip, core = place()
    towers, _, depth = f_ref.shape
    cols = w_ref.shape[2]
    steps = chips - 1
    keep, rows = share[0][0], sum(share[0])
    size = rows // parts
    pieces = towers * parts
    fixed = rows - size
    spare = keep - fixed
    across, along = dp ^ 1, dp ^ 2
    others = (across, along, dp ^ 3)
    at = lambda c, k: (c, 2 * chip + k)
    ends = (chip == 0) | (chip == steps)

    meet([(chip > 0, (dp, 2 * (chip - 1) + core)), (chip < steps, (dp, 2 * (chip + 1) + core)),
          (chip >= 0, at(dp, 1 - core))] + [(chip >= 0, at(c, k)) for c in (across, along) for k in (0, 1)]
         + [(chip >= 0, at(others[2], core))])

    def shard_lanes(shard):
        return pl.ds(pl.multiple_of(shard * depth, 128), depth)

    def piece_of(p):
        return lax.rem(p, towers), pl.ds(pl.multiple_of(p // towers * size, 16), size)

    def copies(step, way, p, shard, there, last):
        t, rws = piece_of(p)
        dst = fg_ref.at[t, rws, shard_lanes(shard)]
        src = dst
        if step == 0:
            src = taken.at[t] if last else f_ref.at[t, rws]
        return pltpu.make_async_remote_copy(
            src_ref=src, dst_ref=dst, send_sem=f_send.at[way, step, p], recv_sem=f_recv.at[way, step, p],
            device_id=(dp, 2 * there + core), device_id_type=MESH)

    def feature(step, way, p, last=False):
        return copies(step, way, p, chip - step if way == 0 else chip + step, chip + 1 if way == 0 else chip - 1, last)

    def incoming(step, way, p):
        return copies(step, way, p, chip - 1 - step if way == 0 else chip + 1 + step, chip, False)

    def sends(step, way):
        return (chip < steps) & (chip >= step) if way == 0 else (chip > 0) & (chip + step <= steps)

    def receives(step, way):
        return chip > step if way == 0 else chip + step < steps

    def launch(p, last):
        for way in (0, 1):
            @pl.when(sends(0, way))
            def _():
                feature(0, way, p, last).start()

    def block(owner, slot, t):
        return wg_ref.at[t, pl.ds(pl.multiple_of(owner * depth, 128), depth), pl.ds(pl.multiple_of(slot * cols, 128), cols)]

    def weight(kind, k, t):
        return pltpu.make_async_remote_copy(
            src_ref=w_low.at[t, k], dst_ref=block(dp, k ^ core, t),
            send_sem=w_send.at[(kind * 2 + k) * 2 + t], recv_sem=w_recv.at[(kind * 2 + core) * 2 + t],
            device_id=at((across, along, dp)[kind], k), device_id_type=MESH)

    def pass_on(kind, slot):
        owner, to, t = ((across, along, 0), (along, across, 1))[kind]
        n = 12 + kind * 2 + slot
        return pltpu.make_async_remote_copy(
            src_ref=block(owner, slot, t), dst_ref=block(owner, slot, t),
            send_sem=w_send.at[n], recv_sem=w_recv.at[n], device_id=at(to, core), device_id_type=MESH)

    def arrived(kind, slot, t):
        owner = (across, along, dp)[kind]
        n = (kind * 2 + (slot ^ core)) * 2 + t
        pltpu.make_async_remote_copy(
            src_ref=block(owner, slot, t), dst_ref=block(owner, slot, t), send_sem=w_send.at[n], recv_sem=w_recv.at[n],
            device_id=at(dp, core), device_id_type=MESH).wait_recv()

    def offer(kind, what):
        src, dst = ((f_ref, offer_f), (o_ref, offer_o))[what]
        n = kind * 2 + what
        return pltpu.make_async_remote_copy(
            src_ref=src.at[:, pl.ds(*share[1 + kind])], dst_ref=dst.at[1 + kind], send_sem=x_send.at[n], recv_sem=x_recv.at[n],
            device_id=at(others[kind], core), device_id_type=MESH)

    def tell(kind):
        return pltpu.make_async_remote_copy(
            src_ref=n_ref, dst_ref=tot.at[1 + kind], send_sem=n_send.at[kind], recv_sem=n_recv.at[kind],
            device_id=at(others[kind], core), device_id_type=MESH)

    def choose(offers, into, first):
        width = offers.shape[3]
        weigh = [jnp.broadcast_to(jnp.where(tot[kind, :1, :width] > keep, 1.0, 0.0), (16, width)) for kind in range(4)]

        def strip(i, _):
            rws = pl.ds(pl.multiple_of(i * 16, 16), 16)
            for t in range(towers):
                value = offers[0, t, rws].astype(jnp.float32) * weigh[0]
                for kind in range(1, 4):
                    value = value + offers[kind, t, rws].astype(jnp.float32) * weigh[kind]
                into[t, pl.ds(pl.multiple_of(first + i * 16, 16), 16)] = value.astype(jnp.bfloat16)
            return 0
        lax.fori_loop(0, share[0][1] // 16, strip, 0)

    def loop(count, body):
        def step(i, _):
            body(i)
            return 0
        lax.fori_loop(0, count, step, 0)

    for kind in range(3):
        tell(kind).start()
    for kind in (2, 0, 1):
        offer(kind, 0).start()
    loop(pieces - towers, lambda p: launch(p, False))
    local = [(n_ref, tot.at[0]), (f_ref.at[:, pl.ds(*share[0])], offer_f.at[0]), (f_ref.at[:, pl.ds(fixed, spare)], taken.at[:, pl.ds(0, spare)]),
             (o_ref.at[:, pl.ds(*share[0])], offer_o.at[0]), (o_ref.at[:, pl.ds(0, keep)], og.at[:, pl.ds(0, keep)])]
    local = [pltpu.make_async_copy(src, dst, l_sem.at[n]) for n, (src, dst) in enumerate(local)]
    for copy in local:
        copy.start()
    own = [pltpu.make_async_copy(f_ref.at[t, pl.ds(0, fixed)], fg_ref.at[t, pl.ds(0, fixed), shard_lanes(chip)], own_sem.at[t])
           for t in range(towers)]
    for copy in own:
        copy.start()

    def wide(n):
        return pltpu.make_async_copy(w_ref.at[n // 2, pl.ds(pl.multiple_of(lax.rem(n, 2) * depth, 128), depth)], w_wide.at[lax.rem(n, 2)],
                                     k_sem.at[lax.rem(n, 2)])

    def round_half(n):
        @pl.when(n + 1 < 2 * towers)
        def _():
            wide(n + 1).start()
        wide(n).wait()

        def strip(i):
            rws = pl.ds(pl.multiple_of(i * 64, 64), 64)
            w_low[n // 2, lax.rem(n, 2), rws] = w_wide[lax.rem(n, 2), rws].astype(jnp.bfloat16)
        loop(depth // 64, strip)
    wide(jnp.int32(0)).start()
    loop(2 * towers, round_half)
    own_w = [pltpu.make_async_copy(w_low.at[t, core], block(dp, 0, t), own_sem.at[towers + t]) for t in range(towers)]
    for copy in own_w:
        copy.start()

    for copy in local[:3]:
        copy.wait()
    for kind in range(3):
        tell(kind).wait_recv()
    totals = pltpu.make_async_copy(tot, tot_ref, l_sem.at[5])
    totals.start()
    for kind in range(3):
        offer(kind, 0).wait_recv()
    choose(offer_f, taken, spare)
    own_share = [pltpu.make_async_copy(taken.at[t], fg_ref.at[t, pl.ds(fixed, size), shard_lanes(chip)], own_sem.at[2 * towers + t])
                 for t in range(towers)]
    for t in range(towers):
        launch(pieces - towers + t, True)
    for copy in own_share:
        copy.start()
    for t in (0, 1):
        for k in (0, 1):
            weight(0, k, t).start()
            weight(1, k, 1 - t).start()
    for t in (0, 1):
        weight(2, 1 - core, t).start()
    for kind in (2, 0, 1):
        offer(kind, 1).start()

    def alive(i):
        rws = pl.ds(pl.multiple_of(i * 16, 16), 16)
        row = lax.broadcasted_iota(jnp.int32, (16, cols), 0).astype(jnp.float32) + (i * 16).astype(jnp.float32)
        here = jnp.where(row < tot[0, :1, :cols], 1.0, 0.0)
        there = jnp.zeros_like(here)
        for kind in range(4):
            count = tot[kind, :1, :cols]
            slot = row + float(share[kind][0] - keep)
            valid = (slot < count) & (count > keep)
            if kind == 3:
                valid = valid & (slot >= share[2][0] + share[2][1])
            there = there + jnp.where(valid, 1.0, 0.0)
        live[rws] = jnp.where(row < keep, here, there)
        for t in range(towers):
            acc[t, rws] = jnp.zeros((16, 2 * cols), jnp.float32)
    loop(rows // 16, alive)

    for step in range(steps - 1):
        def serve(p):
            for way in (0, 1):
                @pl.when(receives(step, way))
                def _():
                    incoming(step, way, p).wait_recv()

                @pl.when(sends(step + 1, way))
                def _():
                    feature(step + 1, way, p).start()
        loop(pieces, serve)
        if step == 0:
            for slot in (0, 1):
                arrived(0, slot, 0)
                pass_on(0, slot).start()
                arrived(1, slot, 1)
                pass_on(1, slot).start()

    for copy in local[3:]:
        copy.wait()
    for kind in range(3):
        offer(kind, 1).wait_recv()
    choose(offer_o, og, keep)
    for slot in (0, 1):
        arrived(0, slot, 1)
        arrived(1, slot, 0)
        pass_on(0, slot).wait_recv()
        pass_on(1, slot).wait_recv()
    for t in (0, 1):
        arrived(2, 1, t)
    for copy in own + own_w + own_share:
        copy.wait()

    def shard(j):
        return jnp.where(chip == steps, steps - j, j)

    def load_w(n):
        rws = pl.ds(pl.multiple_of(shard(n // towers) * depth, 128), depth)
        return pltpu.make_async_copy(wg_ref.at[lax.rem(n, towers), rws], w_tile.at[lax.rem(n, 2)], wt_sem.at[lax.rem(n, 2)])

    def load_f(n):
        return pltpu.make_async_copy(fg_ref.at[lax.rem(n, towers), :, shard_lanes(shard(n // towers))], f_tile.at[lax.rem(n, 2)],
                                     ft_sem.at[lax.rem(n, 2)])

    def add(t, slot, rws):
        for col in range(0, 2 * cols, cols):
            lanes = pl.ds(col, cols)
            acc[t, rws, lanes] += jnp.dot(f_tile[slot, rws], w_tile[slot, :, lanes], preferred_element_type=jnp.float32)

    def here(n):
        return (n < steps * towers) | jnp.logical_not(ends)

    def unit(n):
        @pl.when(n + 1 < chips * towers)
        def _():
            load_w(n + 1).start()

        @pl.when((n + 1 < chips * towers) & here(n + 1))
        def _():
            load_f(n + 1).start()
        load_w(n).wait()

        @pl.when(here(n))
        def _():
            load_f(n).wait()
            loop(parts, lambda i: add(lax.rem(n, towers), lax.rem(n, 2), pl.ds(pl.multiple_of(i * size, 16), size)))
    load_w(jnp.int32(0)).start()
    load_f(jnp.int32(0)).start()
    loop(chips * towers, unit)

    def swap_sum(p):
        t, rws = piece_of(p)
        return pltpu.make_async_remote_copy(
            src_ref=acc.at[t, rws, pl.ds(cols, cols)], dst_ref=theirs.at[t, rws], send_sem=a_send.at[p],
            recv_sem=a_recv.at[p], device_id=at(dp, 1 - core), device_id_type=MESH)

    def complete(p):
        t, rws = piece_of(p)
        for way in (0, 1):
            @pl.when(receives(steps - 1, way))
            def _():
                incoming(steps - 1, way, p).wait_recv()

        @pl.when(ends)
        def _():
            copy = pltpu.make_async_copy(fg_ref.at[t, rws, shard_lanes(shard(steps))], f_tile.at[t, rws], ft_sem.at[t])
            copy.start()
            copy.wait()
            add(t, t, rws)
        swap_sum(p).start()

    def swap_dz(p):
        t, rws = piece_of(p)
        return pltpu.make_async_remote_copy(
            src_ref=dz_here.at[t, rws], dst_ref=dz_ref.at[t, rws, pl.ds(cols, cols)], send_sem=z_send.at[p],
            recv_sem=z_recv.at[p], device_id=at(dp, 1 - core), device_id_type=MESH)

    def keep_dz(p):
        t, rws = piece_of(p)
        return pltpu.make_async_copy(dz_here.at[t, rws], dz_ref.at[t, rws, pl.ds(0, cols)], out_sem.at[p])

    sums_here[...] = jnp.zeros_like(sums_here)
    factor, cubic = math.sqrt(2.0 / math.pi), 0.044715

    def both(rws):
        activated, slope = [], []
        for t in range(towers):
            v = acc[t, rws, :cols] + theirs[t, rws] + sp_ref[t : t + 1]
            square = v * v
            th = jnp.tanh(factor * (v + cubic * (square * v)))
            activated.append(0.5 * v * (1.0 + th))
            slope.append(0.5 * (1.0 + th) + 0.5 * v * (1.0 - th * th) * (factor * (1.0 + 3.0 * cubic * square)))
        mask = live[rws]
        dy = [og[t, rws].astype(jnp.float32) * mask for t in range(towers)]
        for t in range(towers):
            y_here[t, rws] = ((sp_ref[2 + 2 * t : 3 + 2 * t] * activated[0] + sp_ref[3 + 2 * t : 4 + 2 * t] * activated[1]) * mask).astype(jnp.bfloat16)
        dz = [slope[t] * (sp_ref[2 + t : 3 + t] * dy[0] + sp_ref[4 + t : 5 + t] * dy[1]) for t in range(towers)]
        for t in range(towers):
            dz_here[t, rws] = dz[t].astype(jnp.bfloat16)
        terms = dz + [activated[0] * dy[0], activated[1] * dy[0], activated[0] * dy[1], activated[1] * dy[1]]
        for n, term in enumerate(terms):
            sums_here[n] += term[:8] + term[8:]

    def backward(k):
        for t in range(towers):
            swap_sum(k * towers + t).wait_recv()
        loop(size // 16, lambda i: both(pl.ds(pl.multiple_of(k * size + i * 16, 16), 16)))
        for t in range(towers):
            swap_dz(k * towers + t).start()
            keep_dz(k * towers + t).start()

    def stage(k):
        @pl.when(k < parts)
        def _():
            loop(towers, lambda t: complete(k * towers + t))

        @pl.when(k > 0)
        def _():
            backward(k - 1)
    loop(parts + 1, stage)
    keep_y = pltpu.make_async_copy(y_here, y_ref, l_sem.at[6])
    keep_y.start()
    sg_ref[...] = jnp.zeros_like(sg_ref)
    for n in range(6):
        sg_ref[n : n + 1] = jnp.sum(sums_here[n], axis=0, keepdims=True)

    def settle(p):
        swap_dz(p).wait_recv()
        swap_dz(p).wait_send()
        keep_dz(p).wait()
        swap_sum(p).wait_send()
        for step in range(steps):
            for way in (0, 1):
                @pl.when(sends(step, way))
                def _():
                    feature(step, way, p).wait_send()
    loop(pieces, settle)
    keep_y.wait()
    totals.wait()
    for kind in range(3):
        tell(kind).wait_send()
        offer(kind, 0).wait_send()
        offer(kind, 1).wait_send()
    for t in (0, 1):
        for k in (0, 1):
            weight(0, k, t).wait_send()
            weight(1, k, t).wait_send()
        weight(2, 1 - core, t).wait_send()
    for slot in (0, 1):
        pass_on(0, slot).wait_send()
        pass_on(1, slot).wait_send()


def forward(features, weights, out_grad, count, small_params, chips, parts, share, ident):
    towers, _, depth = features.shape
    cols = weights.shape[2]
    keep, size = share[0]
    rows = keep + size
    steps = chips - 1
    dma, vmem = pltpu.SemaphoreType.DMA, pltpu.VMEM
    bf16, f32 = jnp.bfloat16, jnp.float32
    anywhere, here = pl.BlockSpec(memory_space=pl.ANY), pl.BlockSpec(memory_space=pltpu.VMEM)
    pieces = towers * parts
    told = jnp.broadcast_to(count.astype(f32), (8, depth))
    return pl.pallas_call(
        functools.partial(forward_kernel, chips, parts, share),
        out_shape=[jax.ShapeDtypeStruct((towers, rows, chips * depth), bf16),
                   jax.ShapeDtypeStruct((towers, chips * depth, 2 * cols), bf16),
                   jax.ShapeDtypeStruct((towers, rows, cols), bf16),
                   jax.ShapeDtypeStruct((towers, rows, 2 * cols), bf16),
                   jax.ShapeDtypeStruct((8, cols), f32),
                   jax.ShapeDtypeStruct((4, 8, depth), f32)],
        in_specs=[anywhere] * 3 + [anywhere, here],
        out_specs=[anywhere] * 4 + [here, anywhere],
        scratch_shapes=[vmem((4, towers, size, depth), bf16), vmem((towers, rows // parts, depth), bf16), vmem((4, towers, size, cols), bf16),
                        vmem((towers, rows, cols), bf16), vmem((2, depth, cols), f32), vmem((towers, 2, depth, cols), bf16),
                        vmem((2, rows, depth), bf16), vmem((2, depth, 2 * cols), bf16), vmem((towers, rows, 2 * cols), f32),
                        vmem((towers, rows, cols), f32), vmem((rows, cols), f32), vmem((towers, rows, cols), bf16),
                        vmem((towers, rows, cols), bf16), vmem((6, 8, cols), f32), vmem((4, 8, depth), f32),
                        dma((2, steps, pieces)), dma((2, steps, pieces)), dma((16,)), dma((16,)), dma((3 * towers,)), dma((6,)), dma((6,)),
                        dma((2,)), dma((3,)), dma((3,)), dma((7,)), dma((2,)), dma((2,))] + [dma((pieces,))] * 5,
        compiler_params=pltpu.CompilerParams(collective_id=ident, has_side_effects=True, vmem_limit_bytes=58 * 2**20),
        cost_estimate=pl.CostEstimate(flops=4 * towers * rows * cols * depth * chips, bytes_accessed=800 * 2**20, transcendentals=0),
        name="forward",
    )(features, weights, out_grad, told, small_params)


def sum_kernel(chips, parts, share, y_ref, dz_ref, w_ref, f_ref, ps_ref, st_ref, d_ref, gr_ref, sr_ref, pg_ref, relay_ref,
               held, w_here, dz_here, total, f_part, g_part, r_part, d_send, d_recv, w_sem, o_sem, g_send, g_recv, s_send, s_recv,
               own_sem, b_send, b_recv, v_send, v_recv, y_send, y_recv, p_send, p_recv, y_sem, q_send, q_recv, f_sem, h_sem, r_sem,
               rs_send, rs_recv):
    dp, chip, core = place()
    towers, rows, _ = dz_ref.shape
    depth = d_ref.shape[2]
    cols = y_ref.shape[2]
    size = rows // parts
    pieces = towers * parts
    steps = chips - 1
    turns = steps * pieces
    across, along = dp ^ 1, dp ^ 2
    others = (across, along, dp ^ 3)
    at = lambda c, k: (c, 2 * chip + k)

    meet([(chip > 0, (dp, 2 * (chip - 1) + core)), (chip < chips - 1, (dp, 2 * (chip + 1) + core)),
          (chip >= 0, at(dp, 1 - core))] + [(chip >= 0, at(c, k)) for c in others for k in (0, 1)])

    def loop(count, body):
        def step(i, _):
            body(i)
            return 0
        lax.fori_loop(0, count, step, 0)

    blocks = 4 * towers
    thirds = 3

    def owner_of(m):
        return jnp.where(m < 2, 3, jnp.where((m == 4) | (m == 5), 0, jnp.where((m == 2) | (m == 7), 1, 2)))

    def third(n):
        return pl.ds(pl.multiple_of(lax.rem(n, thirds) * (depth // thirds), 128), depth // thirds)

    def f_load(n):
        m = n // thirds
        first = (dp ^ owner_of(m)) * depth + lax.rem(n, thirds) * (depth // thirds)
        lanes = pl.ds(pl.multiple_of(first, 128), depth // thirds)
        return pltpu.make_async_copy(f_ref.at[lax.rem(m, 2), :, lanes], f_part.at[lax.rem(n, 2)], f_sem.at[lax.rem(n, 2)])

    def g_store(n):
        return pltpu.make_async_copy(g_part.at[lax.rem(n, 2)], pg_ref.at[n // thirds, third(n)], h_sem.at[lax.rem(n, 2)])

    def relay(m):
        return pltpu.make_async_remote_copy(
            src_ref=pg_ref.at[m], dst_ref=relay_ref.at[m], send_sem=rs_send.at[m], recv_sem=rs_recv.at[m],
            device_id=at(dp ^ (m + 1), core), device_id_type=MESH)

    def r_load(n):
        return pltpu.make_async_copy(relay_ref.at[jnp.maximum(n // thirds - (blocks - 2), 0), third(n)], r_part.at[lax.rem(n, 2)],
                                     r_sem.at[lax.rem(n, 2)])

    def grad_block(m):
        joins = m >= blocks - 2

        @pl.when(joins)
        def _():
            relay(jnp.maximum(m - (blocks - 2), 0)).wait_recv()
            r_load(m * thirds).start()

        def part(c):
            n = m * thirds + c

            @pl.when(joins & (c + 1 < thirds))
            def _():
                r_load(n + 1).start()

            @pl.when(n + 1 < blocks * thirds)
            def _():
                f_load(n + 1).start()
            f_load(n).wait()

            @pl.when((n >= 2) & (n != (blocks - 2) * thirds) & (n != (blocks - 2) * thirds + 1))
            def _():
                g_store(n - 2).wait()

            @pl.when(joins)
            def _():
                r_load(n).wait()

            def half(h):
                lanes = pl.ds(pl.multiple_of(h * cols, 128), cols)
                value = lax.dot_general(
                    f_part[lax.rem(n, 2)], dz_here[lax.rem(m, 2), :, lanes], (((0,), (0,)), ((), ())),
                    preferred_element_type=jnp.float32)

                @pl.when(joins)
                def _():
                    g_part[lax.rem(n, 2), :, lanes] = (value + r_part[lax.rem(n, 2), :, lanes].astype(jnp.float32)).astype(jnp.bfloat16)

                @pl.when(jnp.logical_not(joins))
                def _():
                    g_part[lax.rem(n, 2), :, lanes] = value.astype(jnp.bfloat16)
            loop(2, half)
            g_store(n).start()
        loop(thirds, part)

    def grad(m, k):
        away = owner_of(m)
        return pltpu.make_async_remote_copy(
            src_ref=pg_ref.at[m, :, pl.ds(pl.multiple_of((k ^ core) * cols, 128), cols)],
            dst_ref=gr_ref.at[away, core, lax.rem(m, 2)], send_sem=g_send.at[m, k],
            recv_sem=g_recv.at[away, core, lax.rem(m, 2)], device_id=at(dp ^ away, k), device_id_type=MESH)

    def grad_own(t):
        return pltpu.make_async_copy(pg_ref.at[4 + t, :, pl.ds(0, cols)], gr_ref.at[0, core, t], own_sem.at[t])

    def grad_start(m):
        @pl.when(m < 2)
        def _():
            relay(jnp.minimum(m, 1)).start()

        @pl.when(m >= 2)
        def _():
            for k in (0, 1):
                @pl.when((owner_of(m) != 0) | (core != k))
                def _():
                    grad(m, k).start()

        @pl.when(owner_of(m) == 0)
        def _():
            grad_own(lax.rem(m, 2)).start()

    def grad_arrived(away, k, t):
        ref = gr_ref.at[away, k, t]
        pltpu.make_async_remote_copy(
            src_ref=ref, dst_ref=ref, send_sem=g_send.at[2, 0], recv_sem=g_recv.at[away, k, t], device_id=at(dp, core),
            device_id_type=MESH).wait_recv()

    early, late = blocks - 2, blocks + 3

    def block_at(m):
        return jnp.where(m < early, m, m - late + early)

    def small(kind):
        return pltpu.make_async_remote_copy(
            src_ref=ps_ref, dst_ref=sr_ref.at[dp], send_sem=s_send.at[kind], recv_sem=s_recv.at[kind],
            device_id=at(others[kind], core), device_id_type=MESH)

    bands = (share[0], (0, share[0][0]))

    def lanes_of(shard, k):
        return pl.ds(pl.multiple_of((2 * shard + k) * cols, 128), cols)

    def channels(shard, k, t, b):
        return st_ref.at[t, pl.ds(*bands[b]), lanes_of(shard, k)]

    def along_line(step, way, t, b, shard, there, own):
        dst = channels(shard, core, t, b)
        return pltpu.make_async_remote_copy(
            src_ref=y_ref.at[t, pl.ds(*bands[b])] if own else dst, dst_ref=dst, send_sem=y_send.at[way, step, b, t],
            recv_sem=y_recv.at[way, step, b, t], device_id=(dp, 2 * there + core), device_id_type=MESH)

    def leaves(step, way):
        return (chip < steps) & (chip >= step) if way == 0 else (chip > 0) & (chip + step <= steps)

    def comes(step, way):
        return chip > step if way == 0 else chip + step < steps

    def leaving(step, way, t, b, own=False):
        return along_line(step, way, t, b, chip - step if way == 0 else chip + step, chip + 1 if way == 0 else chip - 1, own)

    def coming(step, way, t, b):
        return along_line(step, way, t, b, chip - 1 - step if way == 0 else chip + 1 + step, chip, False)

    def to_core(shard, t, b, own=False):
        dst = channels(shard, core, t, b)
        return pltpu.make_async_remote_copy(
            src_ref=y_ref.at[t, pl.ds(*bands[b])] if own else dst, dst_ref=dst, send_sem=p_send.at[shard, b, t],
            recv_sem=p_recv.at[shard, b, t], device_id=at(dp, 1 - core), device_id_type=MESH)

    def from_core(shard, t, b):
        dst = channels(shard, 1 - core, t, b)
        return pltpu.make_async_remote_copy(
            src_ref=dst, dst_ref=dst, send_sem=p_send.at[shard, b, t], recv_sem=p_recv.at[shard, b, t],
            device_id=at(dp, core), device_id_type=MESH)

    def share_rows(kind):
        skip = share[2][0] + share[2][1] - share[3][0] if kind == 2 else 0
        first, length = share[1 + kind]
        return pl.ds(first + skip, length - skip), pl.ds(skip, length - skip)

    def give(kind, shard, t, own=False):
        to, taken = share_rows(kind)
        src = pl.ds(share[0][0] + taken.start, taken.size)
        return pltpu.make_async_remote_copy(
            src_ref=y_ref.at[t, src] if own else st_ref.at[t, src, lanes_of(shard, core)], dst_ref=st_ref.at[t, to, lanes_of(shard, core)],
            send_sem=v_send.at[kind, shard, t], recv_sem=v_recv.at[kind, shard, t], device_id=at(others[kind], core), device_id_type=MESH)

    def given_to_core(kind, shard, t, k):
        ref = st_ref.at[t, share_rows(kind)[0], lanes_of(shard, k)]
        return pltpu.make_async_remote_copy(
            src_ref=ref, dst_ref=ref, send_sem=q_send.at[kind, shard, t], recv_sem=q_recv.at[kind, shard, t],
            device_id=at(dp, 1 - core), device_id_type=MESH)

    def pass_on(event):
        step, t = event // (2 * towers), lax.rem(event, towers)
        for b in (0, 1):
            @pl.when(lax.rem(event, 2 * towers) // towers == b)
            def _():
                for way in (0, 1):
                    @pl.when(comes(step, way))
                    def _():
                        shard = chip - 1 - step if way == 0 else chip + 1 + step
                        coming(step, way, t, b).wait_recv()

                        @pl.when((step + 1 < steps) & leaves(step + 1, way))
                        def _():
                            leaving(jnp.minimum(step + 1, steps - 1), way, t, b).start()
                        to_core(shard, t, b).start()
                        if b == 0:
                            for kind in (2, 0, 1):
                                give(kind, shard, t).start()

    ends = (chip == 0) | (chip == steps)
    skip = size - share[0][1]

    def where(piece):
        row = pl.multiple_of(lax.rem(piece // towers + parts - 1, parts) * size, 16)
        return lax.rem(piece, towers), pl.ds(row, size)

    def passed(way):
        return jnp.where(way == 0, chip, steps - chip)

    def sends(step, way):
        return (passed(way) < steps) & (passed(way) <= step)

    def onward(way, n):
        return jnp.where(way == 0, chip + n, chip - n)

    def passing(m, way, turn):
        t, rws = where(lax.rem(m, pieces))
        return pltpu.make_async_remote_copy(
            src_ref=held.at[way, turn // pieces, t, rws], dst_ref=held.at[way, m // pieces, t, rws],
            send_sem=d_send.at[way, m], recv_sem=d_recv.at[way, m], device_id=(dp, 2 * onward(way, 1) + core), device_id_type=MESH)

    def landed(m, way):
        t, rws = where(lax.rem(m, pieces))
        ref = held.at[way, m // pieces, t, rws]
        pltpu.make_async_remote_copy(src_ref=ref, dst_ref=ref, send_sem=d_send.at[way, m], recv_sem=d_recv.at[way, m],
                                     device_id=(dp, 2 * chip + core), device_id_type=MESH).wait_recv()

    def product(goal, t, rws, col):
        return lax.dot_general(dz_here[t, rws], w_here[goal, t, third(col)], (((1,), (1,)), ((), ())),
                               preferred_element_type=jnp.float32)

    def store(piece):
        t, rws = where(piece)
        s = lax.rem(piece, 2)
        return pltpu.make_async_copy(total.at[s], d_ref.at[t, rws], o_sem.at[s])

    def hand(kind, piece):
        t, s = lax.rem(piece, towers), lax.rem(piece, 2)
        to, taken = share_rows(kind)
        return pltpu.make_async_remote_copy(
            src_ref=total.at[s, pl.ds(skip + taken.start, taken.size)], dst_ref=d_ref.at[t, to], send_sem=b_send.at[kind, t],
            recv_sem=b_recv.at[kind, t], device_id=at(others[kind], core), device_id_type=MESH)

    def finish(piece):
        t, rws = where(piece)
        s = lax.rem(piece, 2)

        @pl.when(piece >= 2)
        def _():
            store(piece - 2).wait()

        @pl.when((piece >= 2) & (piece < 2 + towers))
        def _():
            for kind in range(3):
                hand(kind, piece - 2).wait_send()
        for way in (0, 1):
            @pl.when(passed(way) > 0)
            def _():
                landed(turns - pieces + piece, way)

        def column(col):
            value = product(chip, t, rws, col)
            lanes = third(col)
            last = steps - 1

            @pl.when(ends)
            def _():
                way = jnp.where(chip == 0, 1, 0)
                total[s, :, lanes] = (value + held[way, last, t, rws, lanes].astype(jnp.float32)).astype(jnp.bfloat16)

            @pl.when(jnp.logical_not(ends))
            def _():
                total[s, :, lanes] = (value + held[0, last, t, rws, lanes].astype(jnp.float32)
                                      + held[1, last, t, rws, lanes].astype(jnp.float32)).astype(jnp.bfloat16)
        loop(thirds, column)
        store(piece).start()

        @pl.when(piece < towers)
        def _():
            for kind in (2, 0, 1):
                hand(kind, piece).start()

    window = 3
    lag = 2

    def send_sum(m, way):
        step = m // pieces
        t, rws = where(lax.rem(m, pieces))
        first = passed(way) == 0

        @pl.when(first & (m >= window))
        def _():
            passing(jnp.maximum(m - window, 0), way, 0).wait_send()

        @pl.when(jnp.logical_not(first))
        def _():
            landed(m - pieces, way)

        def column(col):
            lanes = third(col)
            value = product(onward(way, steps - step), t, rws, col)

            @pl.when(first)
            def _():
                held[way, step, t, rws, lanes] = value.astype(jnp.bfloat16)

            @pl.when(jnp.logical_not(first))
            def _():
                held[way, step - 1, t, rws, lanes] = (value + held[way, step - 1, t, rws, lanes].astype(jnp.float32)).astype(jnp.bfloat16)
        loop(thirds, column)
        passing(m, way, jnp.where(first, m, m - pieces)).start()

    def turn(m):
        def each_way(way):
            @pl.when((m < turns) & sends(m // pieces, way))
            def _():
                send_sum(m, way)
        loop(2, each_way)

        @pl.when((m == early) | (m == late + 2))
        def _():
            for c in (1, 2):
                g_store(block_at(m - 1) * thirds + c).wait()

        @pl.when((m < early) | (m == late) | (m == late + 1))
        def _():
            grad_block(block_at(m))

        @pl.when(((m > 0) & (m <= early)) | (m == late + 1) | (m == late + 2))
        def _():
            grad_start(block_at(m - 1))

        @pl.when((lax.rem(m, 2) == 1) & (m < 4 * towers * steps))
        def _():
            pass_on(m // 2)

        @pl.when(m >= turns - pieces + lag)
        def _():
            finish(m - (turns - pieces + lag))

    loads = [pltpu.make_async_copy(w_ref.at[:, pl.ds(n * depth, depth)], w_here.at[n], w_sem.at[n]) for n in range(chips)]
    loads.append(pltpu.make_async_copy(dz_ref, dz_here, w_sem.at[chips]))
    for load in reversed(loads):
        load.start()
    own = pltpu.make_async_copy(ps_ref, sr_ref.at[dp], own_sem.at[towers])
    own.start()
    f_load(jnp.int32(0)).start()
    own_y = [pltpu.make_async_copy(y_ref.at[t, pl.ds(*bands[b])], channels(chip, core, t, b), y_sem.at[t, b])
             for t in range(towers) for b in (0, 1)]
    for b in (0, 1):
        def start_y(t):
            for way in (0, 1):
                @pl.when(leaves(0, way))
                def _():
                    leaving(0, way, t, b, True).start()
            to_core(chip, t, b, True).start()
            if b == 0:
                for kind in (2, 0, 1):
                    give(kind, chip, t, True).start()
        loop(towers, start_y)
    for copy in own_y:
        copy.start()
    for kind in range(3):
        small(kind).start()
    for load in loads:
        load.wait()

    loop(turns + lag, turn)

    def receive_given(n):
        shard, t = n // towers, lax.rem(n, towers)
        for kind in range(3):
            give(kind, shard, t).wait_recv()
            given_to_core(kind, shard, t, core).start()
    loop(chips * towers, receive_given)

    def drain(m):
        def each_way(way):
            first = passed(way) == 0

            @pl.when(sends(m // pieces, way) & (jnp.logical_not(first) | (m >= turns - window)))
            def _():
                passing(m, way, 0).wait_send()
        loop(2, each_way)
    loop(turns, drain)
    for copy in own_y:
        copy.wait()

    def settle(n):
        shard, t = n // towers, lax.rem(n, towers)
        for b in (0, 1):
            from_core(shard, t, b).wait_recv()
            to_core(shard, t, b).wait_send()

            @pl.when(shard < steps)
            def _():
                for way in (0, 1):
                    @pl.when(leaves(shard, way))
                    def _():
                        leaving(jnp.minimum(shard, steps - 1), way, t, b).wait_send()
        for kind in range(3):
            give(kind, shard, t).wait_send()
            given_to_core(kind, shard, t, core).wait_send()
            given_to_core(kind, shard, t, 1 - core).wait_recv()
    loop(chips * towers, settle)
    for piece in (pieces - 2, pieces - 1):
        store(piece).wait()
    for t in range(towers):
        for kind in range(3):
            hand(kind, t).wait_recv()
        for away in range(3):
            for k in (0, 1):
                @pl.when((away != 0) | (core != k))
                def _():
                    grad_arrived(away, k, t)
        grad_own(t).wait()
        relay(t).wait_send()
    for kind in range(3):
        small(kind).wait()

    def sent(m):
        for k in (0, 1):
            @pl.when((owner_of(m) != 0) | (core != k))
            def _():
                grad(m, k).wait_send()
    loop(blocks - 2, lambda m: sent(m + 2))
    own.wait()


def sums(result, slots, wide_dz, wide_w, wide_f, partial_s, chips, parts, ident, share):
    towers, rows, wide = wide_dz.shape
    depth, cols = wide_w.shape[1] // chips, wide // 2
    steps = chips - 1
    dma, vmem = pltpu.SemaphoreType.DMA, pltpu.VMEM
    bf16 = jnp.bfloat16
    anywhere = pl.BlockSpec(memory_space=pl.ANY)
    pair = (2, steps * towers * parts)
    return pl.pallas_call(
        functools.partial(sum_kernel, chips, parts, share),
        out_shape=[jax.ShapeDtypeStruct((towers, slots, 2 * chips * cols), bf16),
                   jax.ShapeDtypeStruct((towers, slots, depth), bf16),
                   jax.ShapeDtypeStruct((3, 2, towers, depth, cols), bf16),
                   jax.ShapeDtypeStruct((4,) + partial_s.shape, jnp.float32),
                   jax.ShapeDtypeStruct((4 * towers, depth, wide), bf16),
                   jax.ShapeDtypeStruct((towers, depth, wide), bf16)],
        in_specs=[anywhere] * 5,
        out_specs=[anywhere] * 6,
        scratch_shapes=[vmem((2, steps, towers, rows, depth), bf16), vmem((chips, towers, depth, wide), bf16),
                        vmem((towers, rows, wide), bf16), vmem((2, rows // parts, depth), bf16), vmem((2, rows, depth // 3), bf16),
                        vmem((2, depth // 3, wide), bf16), vmem((2, depth // 3, wide), bf16),
                        dma(pair), dma(pair), dma((chips + 1,)), dma((2,)), dma((4 * towers, 2)), dma((3, 2, towers)), dma((3,)), dma((3,)),
                        dma((towers + 1,)), dma((3, towers)), dma((3, towers)), dma((3, chips, towers)), dma((3, chips, towers)),
                        dma((2, steps, 2, towers)), dma((2, steps, 2, towers)), dma((chips, 2, towers)), dma((chips, 2, towers)),
                        dma((towers, 2)), dma((3, chips, towers)), dma((3, chips, towers)), dma((2,)), dma((2,)), dma((2,)), dma((2,)), dma((2,))],
        compiler_params=pltpu.CompilerParams(collective_id=ident, has_side_effects=True, vmem_limit_bytes=58 * 2**20),
        cost_estimate=pl.CostEstimate(flops=4 * towers * rows * wide * depth * chips, bytes_accessed=800 * 2**20, transcendentals=0),
        name="sums",
    )(result, wide_dz, wide_w, wide_f, partial_s)


def small_step(small_params, small_moment_one, small_moment_two, small_average, small_grad):
    first, second, direction = adam_part(small_moment_one, small_moment_two, small_grad)
    fresh = small_params - rate_small * direction
    return first, second, fresh, ema_decay * small_average + (1.0 - ema_decay) * fresh


def update(d_feat, stitched, full, parts, small_parts, states, small_states):
    small_grad = jnp.sum(small_parts, 0)[: small_states[0].shape[0]]
    *fresh, stitched, d_feat = soap(parts, full, stitched, d_feat, *states)
    return (stitched, d_feat) + tuple(fresh) + small_step(*small_states, small_grad)


def own_rows(features, out_grad, totals, passed, states, small_states):
    _, rows, _ = features.shape
    weights, small_params = states[0], small_states[0]
    cols = weights.shape[2]
    cores = lax.axis_size("mp")
    swap = [(i, i ^ 1) for i in range(cores)]
    ranges = ((0, rows // 2), (rows // 2, rows // 2))
    live_rows = (jnp.arange(rows, dtype=jnp.float32) < totals[0]).astype(jnp.float32)
    wide_f, wide_w = gather(features, weights.astype(jnp.bfloat16), cores // 2, ranges, 1)
    partial = jnp.einsum("tri,tio->tro", wide_f, wide_w, preferred_element_type=jnp.float32)
    product = partial[:, :, :cols] + lax.ppermute(partial[:, :, cols:], "mp", swap)
    result, back = jax.vjp(lambda a, b: stitch_local(a, b, live_rows), product, small_params)
    stitched = lax.all_gather(result.astype(jnp.bfloat16), "mp", axis=2, tiled=True)
    dz, small_part = back(out_grad.astype(jnp.float32))
    dz_low = dz.astype(jnp.bfloat16)
    wide_dz = jnp.concatenate([dz_low, lax.ppermute(dz_low, "mp", swap)], axis=2)
    partial_d = jnp.einsum("tro,tio->tri", wide_dz, wide_w, preferred_element_type=jnp.float32)
    partial_g = jnp.einsum("tri,tro->tio", wide_f, wide_dz, preferred_element_type=jnp.float32)
    small_part = jnp.pad(small_part, ((0, 2), (0, 0)))
    d_feat, parts, small_parts = reduce(
        partial_d.astype(jnp.bfloat16), partial_g.astype(jnp.bfloat16), small_part, cores // 2, ranges, 2
    )
    full = jnp.full((1,), rows, jnp.int32)
    return update(d_feat, stitched, full, parts, small_parts, states, small_states)


def shares(rows):
    keep = rows * 15 // 32 // 16 * 16
    size = -(-(rows - keep) // 64) * 16
    return keep, ((keep, size), (keep + size, size), (keep + 2 * size, size), (rows - size, size))


def shared_rows(features, out_grad, totals, passed, states, small_states):
    rows = features.shape[1]
    keep, share = shares(rows)
    wide_f, wide_w, result, wide_dz, small_part = passed
    full = jnp.where(totals[:1] > keep, rows, keep)
    stitched, d_feat, parts, small_parts, *_ = sums(
        result, rows, wide_dz, wide_w, wide_f, small_part, lax.axis_size("mp") // 2, 4, 4, share
    )
    return update(d_feat, stitched, full, parts, small_parts, states, small_states)


def line_body(
    features,
    counts,
    weights,
    small_params,
    out_grad,
    moment_one,
    moment_two,
    average,
    basis_left,
    basis_right,
    small_moment_one,
    small_moment_two,
    small_average,
):
    keep, share = shares(features.shape[1])
    *passed, told = forward(
        features, weights, out_grad, jnp.sum(counts), small_params, lax.axis_size("mp") // 2, 4, share, 3
    )
    totals = told[:, 0, 0]
    return lax.cond(
        jnp.sum(totals > keep) == 1,
        shared_rows,
        own_rows,
        features,
        out_grad,
        totals,
        passed,
        (weights, moment_one, moment_two, average, basis_left, basis_right),
        (small_params, small_moment_one, small_moment_two, small_average),
    )


def plain_body(
    features,
    counts,
    weights,
    small_params,
    out_grad,
    moment_one,
    moment_two,
    average,
    basis_left,
    basis_right,
    small_moment_one,
    small_moment_two,
    small_average,
):
    slot_count = features.shape[1]
    total = jnp.sum(counts)
    live_rows = (jnp.arange(slot_count, dtype=jnp.int32) < total).astype(jnp.float32)
    weights_low = lax.all_gather(weights.astype(jnp.bfloat16), "dp", axis=1, tiled=True)
    feats_full = lax.all_gather(features, "mp", axis=2, tiled=True)
    product = jnp.einsum(
        "tri,tio->tro", feats_full, weights_low, preferred_element_type=jnp.float32
    )
    result, back = jax.vjp(lambda a, b: stitch_local(a, b, live_rows), product, small_params)
    stitched = lax.all_gather(result.astype(jnp.bfloat16), "mp", axis=2, tiled=True)
    dz, small_part = back(out_grad.astype(jnp.float32))
    dz_low = dz.astype(jnp.bfloat16)
    grad_part = jnp.einsum("tri,tro->tio", feats_full, dz_low, preferred_element_type=jnp.float32)
    partial_sums = jnp.einsum(
        "tro,tio->tri", dz_low, weights_low, preferred_element_type=jnp.float32
    )
    d_feat = lax.psum_scatter(
        partial_sums.astype(jnp.float32), "mp", scatter_dimension=2, tiled=True
    )
    grad = lax.psum_scatter(grad_part, "dp", scatter_dimension=1, tiled=True)
    small_grad = lax.psum(small_part, "dp")
    towers, n_in, n_out = grad.shape
    blocks = grad.reshape(towers, n_in // BLOCK, BLOCK, n_out // BLOCK, BLOCK)
    rotated = jnp.einsum(
        "trcai,tracb,trcbj->tricj", basis_left, blocks, basis_right, precision=lax.Precision.HIGHEST
    ).reshape(towers, n_in, n_out)
    first, second, direction = adam_part(moment_one, moment_two, rotated)
    turned = direction.reshape(towers, n_in // BLOCK, BLOCK, n_out // BLOCK, BLOCK)
    step_back = jnp.einsum(
        "trcai,tricj,trcbj->tracb", basis_left, turned, basis_right, precision=lax.Precision.HIGHEST
    ).reshape(towers, n_in, n_out)
    new_weights = weights - rate_main * (step_back + decay_weight * weights)
    new_average = ema_decay * average + (1.0 - ema_decay) * new_weights
    return (
        stitched,
        d_feat.astype(jnp.bfloat16),
        first,
        second,
        new_weights,
        new_average,
        new_weights.astype(jnp.bfloat16),
    ) + small_step(small_params, small_moment_one, small_moment_two, small_average, small_grad)


def solution(mesh):
    def body(features, counts, weights, *rest):
        dp, mp = mesh.shape["dp"], mesh.shape["mp"]
        tiles = features.shape[2] % 128 == 0 and weights.shape[2] % 128 == 0
        suits = dp == 4 and mp == 2 * dp and tiles and features.shape[1] % 64 == 0
        return (line_body if suits else plain_body)(features, counts, weights, *rest)

    return jax.shard_map(
        body,
        mesh=mesh,
        in_specs=(
            P(None, "dp", "mp"),
            P("dp"),
            P(None, "dp", "mp"),
            P(None, "mp"),
            P(None, "dp", "mp"),
            P(None, "dp", "mp"),
            P(None, "dp", "mp"),
            P(None, "dp", "mp"),
            P(None, "dp", "mp", None, None),
            P(None, "dp", "mp", None, None),
            P(None, "mp"),
            P(None, "mp"),
            P(None, "mp"),
        ),
        out_specs=(
            P(None, "dp", None),
            P(None, "dp", "mp"),
            P(None, "dp", "mp"),
            P(None, "dp", "mp"),
            P(None, "dp", "mp"),
            P(None, "dp", "mp"),
            P(None, "dp", "mp"),
            P(None, "mp"),
            P(None, "mp"),
            P(None, "mp"),
            P(None, "mp"),
        ),
        check_vma=False,
    )
```

```python
import functools
import math

import jax
import jax.numpy as jnp
from jax import lax
from jax.experimental import pallas as pl
from jax.experimental.pallas import tpu as pltpu
from jax.sharding import PartitionSpec as P

BLOCK = 64
STEP = 5


beta_one = 0.5
beta_two = 0.5
ema_decay = 0.5
rate_main = 0.01
rate_small = 0.05
decay_weight = 0.01
eps = 1e-08


def stitch_local(product, small, live_rows):
    pre_act = product + small[0:2][:, None, :]
    activated = jax.nn.gelu(pre_act, approximate=True)
    first = small[2] * activated[0] + small[3] * activated[1]
    second = small[4] * activated[0] + small[5] * activated[1]
    return jnp.stack([first, second]) * live_rows[None, :, None]


def adam_part(moment_a, moment_b, grad):
    first = beta_one * moment_a + (1.0 - beta_one) * grad
    second = beta_two * moment_b + (1.0 - beta_two) * grad * grad
    direction = first / (1.0 - beta_one**STEP) / (jnp.sqrt(second / (1.0 - beta_two**STEP)) + eps)
    return (first, second, direction)

def split(v):
    high = v.astype(jnp.bfloat16)
    return high, (v - high.astype(jnp.float32)).astype(jnp.bfloat16)

def soap_blocks(grads, lefts, rights, moments):
    row = lax.broadcasted_iota(jnp.int32, (2 * BLOCK, 2 * BLOCK), 0) // BLOCK
    lane = lax.broadcasted_iota(jnp.int32, (2 * BLOCK, 2 * BLOCK), 1) // BLOCK
    own = row == lane

    def diagonal(v):
        return jnp.where(own, jnp.concatenate([v, v], axis=0), 0.0)

    def beside(v):
        return jnp.concatenate([v[0], v[1]], axis=1)

    def stationary(v, axis):
        high, low = split(v)
        return jnp.concatenate([high, high, low], axis=axis)

    def moving(v, axis):
        high, low = split(v)
        return jnp.concatenate([high, low, high], axis=axis)

    def dots(a, b, ca, cb):
        dims = (((ca,), (cb,)), ((), ()))
        return [lax.dot_general(x, y, dims, preferred_element_type=jnp.float32) for x, y in zip(a, b)]

    right = [diagonal(beside(v)) for v in rights]
    values = dots([moving(v, 1) for v in grads], [stationary(v, 0) for v in right], 1, 0)
    values = dots([stationary(v.reshape(2 * BLOCK, BLOCK), 0) for v in lefts], [moving(diagonal(v), 0) for v in values], 0, 0)
    states = [adam_part(a, b, v) for (a, b), v in zip(moments, values)]
    values = dots([moving(v[2], 1) for v in states], [stationary(v, 1) for v in right], 1, 1)
    values = dots([stationary(beside(v), 1) for v in lefts], [moving(diagonal(v), 0) for v in values], 1, 0)
    return [(first, second, step) for (first, second, _), step in zip(states, values)]


def soap_body(together, strips, full, parts_a, parts_b, stitched, d_a, d_b, weights, moment_a, moment_b, average, left, right,
              first, second, new_weights, new_average, copy, stitched_out, d_feat_out):
    groups, pairs = left.shape[1], left.shape[2] // 2
    length = stitched.shape[1]
    row = jnp.minimum(pl.program_id(1) * pl.num_programs(2) + pl.program_id(2), strips - 1) * length

    first_tower = pl.program_id(0) == 0

    def clear(i, _):
        rows = pl.ds(pl.multiple_of(i * 16, 16), 16)
        wanted = row + i * 16 < full[0]
        stitched_out[0, rows] = jnp.where(wanted, stitched[0, rows], 0)
        d_feat_out[0, rows] = jnp.where(wanted, jnp.where(first_tower, d_a[rows], d_b[rows]), 0)
        return 0

    lax.fori_loop(0, length // 16, clear, 0)

    def blocks(g, _):
        places = [(g * together + s, q) for s in range(together) for q in range(pairs)]
        ats = [(0, pl.ds(pl.multiple_of(r * BLOCK, BLOCK), BLOCK), pl.ds(2 * BLOCK * q, 2 * BLOCK)) for r, q in places]
        grads = []
        for at in ats:
            grads.append(sum(jnp.where(first_tower, parts_a[(k,) + at], parts_b[(k,) + at]).astype(jnp.float32)
                             for k in range(parts_a.shape[0])))
        done = soap_blocks(grads, [left[0, r, 2 * q : 2 * q + 2] for r, q in places],
                           [right[0, r, 2 * q : 2 * q + 2] for r, q in places], [(moment_a[at], moment_b[at]) for at in ats])
        olds = [(weights[at], average[at]) for at in ats]
        for at, (one, two, step), (held, mean) in zip(ats, done, olds):
            first[at] = one
            second[at] = two
            fresh = held - rate_main * (step + decay_weight * held)
            new_weights[at] = fresh
            new_average[at] = ema_decay * mean + (1.0 - ema_decay) * fresh
            copy[at] = fresh.astype(jnp.bfloat16)
        return 0

    lax.fori_loop(0, groups // together, blocks, 0)


def soap(parts, wanted, stitched, d_feat, weights, moment_a, moment_b, average, left, right, group=6):
    towers, rows, cols = weights.shape
    half = parts[0].shape[2]
    steps = half // (BLOCK * group)
    flat = lambda t, p, g: (t, p * steps + g, 0)
    basis = lambda t, p, g: (t, p * steps + g, 0, 0, 0)
    state = pl.BlockSpec((1, BLOCK * group, cols), flat)
    base = pl.BlockSpec((1, group, cols // BLOCK, BLOCK, BLOCK), basis)
    full = jax.ShapeDtypeStruct(weights.shape, jnp.float32)
    strips = max(n for n in range(1, 2 * steps + 1) if stitched.shape[1] % (16 * n) == 0)

    def strip(p, g):
        return jnp.minimum(p * steps + g, strips - 1)

    def through(shape):
        return pl.BlockSpec((1, shape[1] // strips, shape[2]), lambda t, p, g: (t, strip(p, g), 0))

    def of_tower(n, shape, index, last):
        return pl.BlockSpec(shape, lambda t, p, g: tuple(jnp.where(t == n, a, b) for a, b in zip(index(p, g), last if n == 0 else index(0, 0))))

    pieces = [of_tower(n, (v.shape[0], 1, BLOCK * group, cols), lambda p, g: (0, p, g, 0), (0, 1, steps - 1, 0)) for n, v in enumerate(parts)]
    rows_of = [of_tower(n, (v.shape[0] // strips, v.shape[1]), lambda p, g: (strip(p, g), 0), (strips - 1, 0)) for n, v in enumerate(d_feat)]

    return pl.pallas_call(
        functools.partial(soap_body, 2 - group % 2, strips),
        grid=(towers, 2, steps),
        in_specs=[pl.BlockSpec(memory_space=pltpu.SMEM),
                  *pieces, through(stitched.shape), *rows_of, state, state, state, state, base, base],
        out_specs=[state] * 5 + [through(stitched.shape), through((towers,) + d_feat[0].shape)],
        out_shape=[full] * 4 + [jax.ShapeDtypeStruct(weights.shape, jnp.bfloat16)]
        + [jax.ShapeDtypeStruct(v, jnp.bfloat16) for v in (stitched.shape, (towers,) + d_feat[0].shape)],
        compiler_params=pltpu.CompilerParams(vmem_limit_bytes=48 * 2**20),
        cost_estimate=pl.CostEstimate(flops=8 * 2 * towers * rows * cols * 64, bytes_accessed=130 * 2**20, transcendentals=0),
        name="soap",
    )(wanted, *parts, stitched, *d_feat, weights, moment_a, moment_b, average, left, right)


MESH = pl.DeviceIdType.MESH


def place():
    mp = lax.axis_index("mp")
    return lax.axis_index("dp"), mp // 2, lax.rem(mp, 2)


def meet(devices):
    barrier = pltpu.get_barrier_semaphore()
    expected = 0
    for here, device in devices:
        @pl.when(here)
        def _():
            pl.semaphore_signal(barrier, inc=1, device_id=device, device_id_type=MESH)
        expected = expected + jnp.where(here, 1, 0)
    pl.semaphore_wait(barrier, expected)


def gather_kernel(chips, ranges, f_ref, w_ref, fg_ref, wg_ref, f_send, f_recv, w_send, w_recv, own_sem):
    dp, chip, core = place()
    towers, rows, depth = f_ref.shape
    cols = w_ref.shape[2]
    across, along = dp ^ 1, dp ^ 2
    at = lambda c, k: (c, 2 * chip + k)

    meet([(chip > 0, (dp, 2 * (chip - 1) + core)), (chip < chips - 1, (dp, 2 * (chip + 1) + core)),
          (chip >= 0, at(dp, 1 - core))] + [(chip >= 0, at(c, k)) for c in (across, along) for k in (0, 1)])

    def copies(step, way, t, k, shard, there):
        lanes = pl.ds(pl.multiple_of(shard * depth, 128), depth)
        rws = pl.ds(*ranges[k])
        src = fg_ref.at[t, rws, lanes]
        if step == 0:
            src = f_ref.at[t, rws]
        n = ((way * (chips - 1) + step) * towers + t) * len(ranges) + k
        return pltpu.make_async_remote_copy(
            src_ref=src, dst_ref=fg_ref.at[t, rws, lanes], send_sem=f_send.at[n], recv_sem=f_recv.at[n],
            device_id=(dp, 2 * there + core), device_id_type=MESH)

    def feature(step, way, t, k):
        return copies(step, way, t, k, chip - step if way == 0 else chip + step, chip + 1 if way == 0 else chip - 1)

    def incoming(step, way, t, k):
        return copies(step, way, t, k, chip - 1 - step if way == 0 else chip + 1 + step, chip)

    def sends(step, way):
        return (chip < chips - 1) & (chip >= step) if way == 0 else (chip > 0) & (chip + step < chips)

    def receives(step, way):
        return chip > step if way == 0 else chip + step < chips - 1

    def launch(t, k):
        for way in (0, 1):
            @pl.when(sends(0, way))
            def _():
                feature(0, way, t, k).start()

    def block(owner, slot, t):
        return wg_ref.at[t, pl.ds(pl.multiple_of(owner * depth, 128), depth), pl.ds(pl.multiple_of(slot * cols, 128), cols)]

    def weight(kind, k, t):
        to = at((across, along, dp)[kind], k)
        n = (kind * 2 + core) * 2 + t
        return pltpu.make_async_remote_copy(
            src_ref=w_ref.at[t, pl.ds(pl.multiple_of(k * depth, 128), depth)], dst_ref=block(dp, k ^ core, t),
            send_sem=w_send.at[(kind * 2 + k) * 2 + t], recv_sem=w_recv.at[n], device_id=to, device_id_type=MESH)

    def forward(kind, slot):
        owner, to, t = ((across, along, 0), (along, across, 1))[kind]
        n = 12 + kind * 2 + slot
        return pltpu.make_async_remote_copy(
            src_ref=block(owner, slot, t), dst_ref=block(owner, slot, t),
            send_sem=w_send.at[n], recv_sem=w_recv.at[n], device_id=at(to, core), device_id_type=MESH)

    def arrived(kind, slot, t):
        owner = (across, along, dp)[kind]
        n = (kind * 2 + (slot ^ core)) * 2 + t
        pltpu.make_async_remote_copy(
            src_ref=block(owner, slot, t), dst_ref=block(owner, slot, t), send_sem=w_send.at[n], recv_sem=w_recv.at[n],
            device_id=at(dp, core), device_id_type=MESH).wait_recv()

    mine = pl.ds(pl.multiple_of(chip * depth, 128), depth)
    own = [pltpu.make_async_copy(f_ref.at[t], fg_ref.at[t, :, mine], own_sem.at[t]) for t in range(towers)]
    own += [pltpu.make_async_copy(w_ref.at[t, pl.ds(pl.multiple_of(core * depth, 128), depth)], block(dp, 0, t), own_sem.at[2 + t])
            for t in range(towers)]

    pieces = [(t, k) for k in range(len(ranges)) for t in range(towers)]
    for t, k in pieces:
        launch(t, k)
    for copy in own:
        copy.start()
    for t in (0, 1):
        for k in (0, 1):
            weight(0, k, t).start()
            weight(1, k, 1 - t).start()
    for t in (0, 1):
        weight(2, 1 - core, t).start()

    for step in range(chips - 1):
        for t, k in pieces:
            for way in (0, 1):
                @pl.when(receives(step, way))
                def _():
                    incoming(step, way, t, k).wait_recv()
                if step + 1 < chips - 1:
                    @pl.when(sends(step + 1, way))
                    def _():
                        feature(step + 1, way, t, k).start()
            if step == 0 and (t, k) == pieces[-1]:
                for slot in (0, 1):
                    arrived(0, slot, 0)
                    forward(0, slot).start()
                    arrived(1, slot, 1)
                    forward(1, slot).start()

    for slot in (0, 1):
        arrived(0, slot, 1)
        arrived(1, slot, 0)
        forward(0, slot).wait_recv()
        forward(1, slot).wait_recv()
    for t in (0, 1):
        arrived(2, 1, t)
    for t in (0, 1):
        for k in (0, 1):
            weight(0, k, t).wait_send()
            weight(1, k, t).wait_send()
        weight(2, 1 - core, t).wait_send()
    for slot in (0, 1):
        forward(0, slot).wait_send()
        forward(1, slot).wait_send()
    for step in range(chips - 1):
        for t, k in pieces:
            for way in (0, 1):
                @pl.when(sends(step, way))
                def _():
                    feature(step, way, t, k).wait_send()
    for copy in own:
        copy.wait()


def gather(features, weights_low, chips, ranges, ident):
    towers, rows, depth = features.shape
    cols = weights_low.shape[2]
    count = 2 * (chips - 1) * towers * len(ranges)
    dma = pltpu.SemaphoreType.DMA
    anywhere = pl.BlockSpec(memory_space=pl.ANY)
    return pl.pallas_call(
        functools.partial(gather_kernel, chips, ranges),
        out_shape=[jax.ShapeDtypeStruct((towers, rows, chips * depth), jnp.bfloat16),
                   jax.ShapeDtypeStruct((towers, chips * depth, 2 * cols), jnp.bfloat16)],
        in_specs=[anywhere] * 2,
        out_specs=[anywhere] * 2,
        scratch_shapes=[dma((count,)), dma((count,)), dma((16,)), dma((16,)), dma((4,))],
        compiler_params=pltpu.CompilerParams(collective_id=ident, has_side_effects=True),
        cost_estimate=pl.CostEstimate(flops=0, bytes_accessed=800 * 2**20, transcendentals=0),
        name="gather",
    )(features, weights_low)


def reduce_kernel(chips, ranges, pd_ref, pg_ref, ps_ref, d_ref, gr_ref, sr_ref, held, term, total,
                  d_send, d_recv, t_sem, o_sem, g_send, g_recv, s_send, s_recv, own_sem):
    dp, chip, core = place()
    towers, rows, depth = d_ref.shape
    cols = pg_ref.shape[2] // 2
    across, along = dp ^ 1, dp ^ 2
    others = (across, along, dp ^ 3)
    at = lambda c, k: (c, 2 * chip + k)

    meet([(chip > 0, (dp, 2 * (chip - 1) + core)), (chip < chips - 1, (dp, 2 * (chip + 1) + core)),
          (chip >= 0, at(dp, 1 - core))] + [(chip >= 0, at(c, k)) for c in others for k in (0, 1)])

    def grad(kind, k, t):
        owner = (others + (dp,))[kind]
        return pltpu.make_async_remote_copy(
            src_ref=pg_ref.at[t, pl.ds(pl.multiple_of(owner * depth, 128), depth), pl.ds(pl.multiple_of((k ^ core) * cols, 128), cols)],
            dst_ref=gr_ref.at[dp, core, t], send_sem=g_send.at[(kind * 2 + k) * 2 + t],
            recv_sem=g_recv.at[(kind * 2 + core) * 2 + t], device_id=at(owner, k), device_id_type=MESH)

    def grad_arrived(kind, k, t):
        owner = (others + (dp,))[kind]
        pltpu.make_async_remote_copy(
            src_ref=gr_ref.at[owner, k, t], dst_ref=gr_ref.at[owner, k, t], send_sem=g_send.at[0],
            recv_sem=g_recv.at[(kind * 2 + k) * 2 + t], device_id=at(dp, core), device_id_type=MESH).wait_recv()

    def small(kind):
        return pltpu.make_async_remote_copy(
            src_ref=ps_ref, dst_ref=sr_ref.at[dp], send_sem=s_send.at[kind], recv_sem=s_recv.at[kind],
            device_id=at(others[kind], core), device_id_type=MESH)

    def target(step, way):
        return chip + chips - 1 - step if way == 0 else chip - (chips - 1 - step)

    def sends(step, way):
        return (chip < chips - 1) & (chip <= step) if way == 0 else (chip > 0) & (chips - 1 - chip <= step)

    def receives(step, way):
        return (chip > 0) & (chip <= step + 1) if way == 0 else (chip < chips - 1) & (chips - 1 - chip <= step + 1)

    def own_term(goal, t, k):
        return pd_ref.at[t, pl.ds(*ranges[k]), pl.ds(pl.multiple_of(goal * depth, 128), depth)]

    def partial(step, way, t, k, first):
        n = ((way * (chips - 1) + step) * towers + t) * len(ranges) + k
        src = own_term(target(step, way), t, k) if first else held.at[way, step - 1, t, pl.ds(*ranges[k])]
        there = chip + 1 if way == 0 else chip - 1
        return pltpu.make_async_remote_copy(
            src_ref=src, dst_ref=held.at[way, step, t, pl.ds(*ranges[k])], send_sem=d_send.at[n], recv_sem=d_recv.at[n],
            device_id=(dp, 2 * there + core), device_id_type=MESH)

    def landed(step, way, t, k):
        n = ((way * (chips - 1) + step) * towers + t) * len(ranges) + k
        ref = held.at[way, step, t, pl.ds(*ranges[k])]
        pltpu.make_async_remote_copy(src_ref=ref, dst_ref=ref, send_sem=d_send.at[n], recv_sem=d_recv.at[n],
                                     device_id=(dp, 2 * chip + core), device_id_type=MESH).wait_recv()

    pieces = [(t, k) for t in range(towers) for k in range(len(ranges))]
    ends = (chip == 0, chip == chips - 1)
    for t, k in pieces:
        for way in (0, 1):
            @pl.when(ends[way])
            def _():
                partial(0, way, t, k, True).start()
    own = [pltpu.make_async_copy(
        pg_ref.at[t, pl.ds(pl.multiple_of(dp * depth, 128), depth), pl.ds(0, cols)], gr_ref.at[dp, core, t], own_sem.at[t])
        for t in range(towers)]
    own.append(pltpu.make_async_copy(ps_ref, sr_ref.at[dp], own_sem.at[towers]))
    for copy in own:
        copy.start()
    for kind in range(3):
        small(kind).start()
    for t in range(towers):
        for kind in (2, 0, 1):
            for k in (0, 1):
                grad(kind, k, t).start()
        grad(3, 1 - core, t).start()

    strip = 16

    for step in range(1, chips - 1):
        for t, k in pieces:
            for way in (0, 1):
                @pl.when(sends(step, way) & ends[way])
                def _():
                    partial(step, way, t, k, True).start()

                @pl.when(sends(step, way) & jnp.logical_not(ends[way]))
                def _():
                    start, size = ranges[k]
                    load = pltpu.make_async_copy(own_term(target(step, way), t, k), term.at[way, pl.ds(0, size)], t_sem.at[way])
                    load.start()
                    landed(step - 1, way, t, k)
                    load.wait()

                    def add(i, _):
                        rws = pl.ds(pl.multiple_of(i * strip, strip), strip)
                        all_rows = pl.ds(pl.multiple_of(start + i * strip, strip), strip)
                        held[way, step - 1, t, all_rows] = (
                            held[way, step - 1, t, all_rows].astype(jnp.float32) + term[way, rws].astype(jnp.float32)
                        ).astype(jnp.bfloat16)
                        return 0
                    lax.fori_loop(0, size // strip, add, 0)
                    partial(step, way, t, k, False).start()

    stores = []
    for n, (t, k) in enumerate(pieces):
        s = n % 2
        start, size = ranges[k]
        load = pltpu.make_async_copy(own_term(chip, t, k), term.at[s, pl.ds(0, size)], t_sem.at[s])
        load.start()
        for way in (0, 1):
            @pl.when(receives(chips - 2, way))
            def _():
                landed(chips - 2, way, t, k)
        load.wait()
        if n >= 2:
            stores[n - 2].wait()

        def finish(i, _):
            rws = pl.ds(pl.multiple_of(i * strip, strip), strip)
            all_rows = pl.ds(pl.multiple_of(start + i * strip, strip), strip)
            value = term[s, rws].astype(jnp.float32)
            for way in (0, 1):
                here = receives(chips - 2, way)
                value = value + jnp.where(here, held[way, chips - 2, t, all_rows].astype(jnp.float32), 0.0)
            total[s, rws] = value.astype(jnp.bfloat16)
            return 0
        lax.fori_loop(0, size // strip, finish, 0)
        stores.append(pltpu.make_async_copy(total.at[s, pl.ds(0, size)], d_ref.at[t, pl.ds(start, size)], o_sem.at[s]))
        stores[n].start()
    for store in stores[-2:]:
        store.wait()

    for t in range(towers):
        for kind in range(3):
            for k in (0, 1):
                grad_arrived(kind, k, t)
        grad_arrived(3, 1 - core, t)
    for kind in range(3):
        small(kind).wait()
    for t in range(towers):
        for kind in range(3):
            for k in (0, 1):
                grad(kind, k, t).wait_send()
        grad(3, 1 - core, t).wait_send()
    for step in range(chips - 1):
        for t, k in pieces:
            for way in (0, 1):
                @pl.when(sends(step, way))
                def _():
                    partial(step, way, t, k, True).wait_send()
    for copy in own:
        copy.wait()


def reduce(partial_d, partial_g, partial_s, chips, ranges, ident):
    towers, rows, wide = partial_d.shape
    depth, cols = wide // chips, partial_g.shape[2] // 2
    count = 2 * (chips - 1) * towers * len(ranges)
    part = max(size for _, size in ranges)
    dma = pltpu.SemaphoreType.DMA
    bf16 = jnp.bfloat16
    out_shape = [jax.ShapeDtypeStruct((towers, rows, depth), bf16),
                 jax.ShapeDtypeStruct((4, 2, towers, depth, cols), bf16),
                 jax.ShapeDtypeStruct((4,) + partial_s.shape, jnp.float32)]
    return pl.pallas_call(
        functools.partial(reduce_kernel, chips, ranges),
        out_shape=out_shape,
        in_specs=[pl.BlockSpec(memory_space=pl.ANY)] * 3,
        out_specs=[pl.BlockSpec(memory_space=pl.ANY)] * len(out_shape),
        scratch_shapes=[pltpu.VMEM((2, chips - 1, towers, rows, depth), bf16),
                        pltpu.VMEM((2, part, depth), bf16), pltpu.VMEM((2, part, depth), bf16),
                        dma((count,)), dma((count,)), dma((2,)), dma((2,)), dma((16,)), dma((16,)), dma((3,)), dma((3,)), dma((towers + 1,))],
        compiler_params=pltpu.CompilerParams(collective_id=ident, has_side_effects=True, vmem_limit_bytes=56 * 2**20),
        cost_estimate=pl.CostEstimate(flops=0, bytes_accessed=800 * 2**20, transcendentals=0),
        name="reduce",
    )(partial_d, partial_g, partial_s)


def loop(count, body):
    def step(i, _):
        body(i)
        return 0
    lax.fori_loop(0, count, step, 0)


def wait_for(ref, sem, other):
    pltpu.make_async_remote_copy(src_ref=ref, dst_ref=ref, send_sem=other, recv_sem=sem, device_id=dict(dp=0, mp=0),
                                 device_id_type=MESH).wait_recv()


class Spot:
    def __init__(self, chips):
        self.dp, self.chip, self.core = place()
        self.chips, self.steps = chips, chips - 1
        self.others = (self.dp ^ 1, self.dp ^ 2, self.dp ^ 3)
        self.ends = (self.chip == 0) | (self.chip == self.steps)

    def at(self, dp, core):
        return dp, 2 * self.chip + core

    def on_line(self, chip):
        return self.dp, 2 * chip + self.core

    def passed(self, way):
        return jnp.where(way == 0, self.chip, self.steps - self.chip)

    def onward(self, way, n):
        return jnp.where(way == 0, self.chip + n, self.chip - n)

    def leaves(self, step, way):
        return (self.passed(way) < self.steps) & (self.passed(way) >= step)

    def comes(self, step, way):
        return self.passed(way) > step

    def greet(self):
        meet([(self.chip > 0, self.on_line(self.chip - 1)), (self.chip < self.steps, self.on_line(self.chip + 1)),
              (self.chip >= 0, self.at(self.dp, 1 - self.core))]
             + [(self.chip >= 0, self.at(c, k)) for c in self.others for k in (0, 1)])


class Features:
    def __init__(self, spot, f_ref, taken, fg, size, send, recv):
        self.spot, self.f_ref, self.taken, self.fg, self.size, self.send, self.recv = spot, f_ref, taken, fg, size, send, recv
        self.depth = f_ref.shape[1]

    def rows(self, q):
        return pl.ds(pl.multiple_of(q * self.size, 16), self.size)

    def lanes(self, shard):
        return pl.ds(pl.multiple_of(shard * self.depth, 128), self.depth)

    def copy(self, step, way, q, src=None):
        ref = self.fg.at[self.rows(q), self.lanes(self.spot.onward(way, -step))]
        return pltpu.make_async_remote_copy(
            src_ref=ref if src is None else src, dst_ref=ref, send_sem=self.send.at[way, step, q], recv_sem=self.recv.at[way, step, q],
            device_id=self.spot.on_line(self.spot.onward(way, 1)), device_id_type=MESH)

    def launch(self, q, last):
        def each(way):
            @pl.when(self.spot.leaves(0, way))
            def _():
                self.copy(0, way, q, self.taken if last else self.f_ref.at[self.rows(q)]).start()
        loop(2, each)

    def arrive(self, step, q):
        def each(way):
            @pl.when(self.spot.comes(step, way))
            def _():
                ref = self.fg.at[self.rows(q), self.lanes(self.spot.onward(way, -1 - step))]
                wait_for(ref, self.recv.at[way, step, q], self.send.at[way, step, q])
        loop(2, each)

    def serve(self, step, q):
        self.arrive(step, q)

        def each(way):
            @pl.when(self.spot.leaves(step + 1, way))
            def _():
                self.copy(step + 1, way, q).start()
        loop(2, each)

    def settle(self, q):
        for step in range(self.spot.steps):
            def each(way):
                @pl.when(self.spot.leaves(step, way))
                def _():
                    self.copy(step, way, q).wait_send()
            loop(2, each)


class Weights:
    def __init__(self, spot, w_ref, wide, low, wg, wide_sem, own_sem, send, recv):
        self.spot, self.w_ref, self.wide, self.low, self.wg = spot, w_ref, wide, low, wg
        self.wide_sem, self.own_sem, self.send, self.recv = wide_sem, own_sem, send, recv
        self.depth, self.cols = low.shape[1], low.shape[2]

    def block(self, owner, slot):
        return self.wg.at[pl.ds(pl.multiple_of(owner * self.depth, 128), self.depth), pl.ds(pl.multiple_of(slot * self.cols, 128), self.cols)]

    def round(self):
        part = self.wide.shape[1]
        parts = self.depth // part

        def load(n):
            return pltpu.make_async_copy(self.w_ref.at[pl.ds(pl.multiple_of(n * part, 16), part)], self.wide.at[lax.rem(n, 2)],
                                         self.wide_sem.at[lax.rem(n, 2)])

        def one(n):
            @pl.when(n + 1 < 2 * parts)
            def _():
                load(n + 1).start()
            load(n).wait()

            def strip(i):
                rows = pl.ds(pl.multiple_of(i * 32, 32), 32)
                to = pl.ds(pl.multiple_of(lax.rem(n, parts) * part + i * 32, 32), 32)
                self.low[n // parts, to] = self.wide[lax.rem(n, 2), rows].astype(jnp.bfloat16)
            loop(part // 32, strip)
        load(jnp.int32(0)).start()
        loop(2 * parts, one)

    def send_own(self, kind, slot):
        s = self.spot
        k = s.core ^ slot
        return pltpu.make_async_remote_copy(
            src_ref=self.low.at[k], dst_ref=self.block(s.dp, slot), send_sem=self.send.at[kind, slot], recv_sem=self.recv.at[kind, slot],
            device_id=s.at((s.others[0], s.others[1], s.dp)[kind], k), device_id_type=MESH)

    def send_on(self, kind):
        s = self.spot
        ref = self.block(s.others[kind], kind)
        return pltpu.make_async_remote_copy(
            src_ref=ref, dst_ref=ref, send_sem=self.send.at[3, kind], recv_sem=self.recv.at[3, kind],
            device_id=s.at(s.others[1 - kind], s.core), device_id_type=MESH)

    def arrive(self, kind, slot):
        owner = (self.spot.others[0], self.spot.others[1], self.spot.dp)[kind]
        wait_for(self.block(owner, slot), self.recv.at[kind, slot], self.send.at[kind, slot])

    def own(self):
        return pltpu.make_async_copy(self.low.at[self.spot.core], self.block(self.spot.dp, 0), self.own_sem)

    def start(self):
        self.own().start()
        for slot in (0, 1):
            self.send_own(0, slot).start()
            self.send_own(1, 1 - slot).start()
        self.send_own(2, 1).start()

    def relay(self):
        for kind in (0, 1):
            self.arrive(kind, kind)
            self.send_on(kind).start()

    def finish(self):
        for kind in (0, 1):
            self.arrive(kind, 1 - kind)
            wait_for(self.block(self.spot.others[2], kind), self.recv.at[3, kind], self.send.at[3, kind])
        self.arrive(2, 1)
        self.own().wait()

    def settle(self):
        for kind in (0, 1):
            for slot in (0, 1):
                self.send_own(kind, slot).wait_send()
            self.send_on(kind).wait_send()
        self.send_own(2, 1).wait_send()


class Products:
    def __init__(self, spot, features, wg, f_tile, w_tile, acc, theirs, f_sem, w_sem, send, recv):
        self.spot, self.features, self.wg, self.f_tile, self.w_tile, self.acc, self.theirs = spot, features, wg, f_tile, w_tile, acc, theirs
        self.f_sem, self.w_sem, self.send, self.recv = f_sem, w_sem, send, recv
        self.cols = theirs.shape[1]

    def shard(self, j):
        return jnp.where(self.spot.chip == self.spot.steps, self.spot.steps - j, j)

    def load_w(self, j):
        depth = self.features.depth
        rows = pl.ds(pl.multiple_of(self.shard(j) * depth, 128), depth)
        return pltpu.make_async_copy(self.wg.at[rows], self.w_tile.at[lax.rem(j, 2)], self.w_sem.at[lax.rem(j, 2)])

    def load_f(self, j):
        lanes = self.features.lanes(self.shard(j))
        return pltpu.make_async_copy(self.features.fg.at[:, lanes], self.f_tile.at[lax.rem(j, 2)], self.f_sem.at[lax.rem(j, 2)])

    def here(self, j):
        return (j < self.spot.steps) | jnp.logical_not(self.spot.ends)

    def add(self, slot, rows):
        for col in range(0, 2 * self.cols, self.cols):
            lanes = pl.ds(col, self.cols)
            self.acc[rows, lanes] += jnp.dot(self.f_tile[slot, rows], self.w_tile[slot, :, lanes], preferred_element_type=jnp.float32)

    def multiply(self):
        def unit(j):
            @pl.when(j < self.spot.steps)
            def _():
                self.load_w(j + 1).start()

            @pl.when((j < self.spot.steps) & self.here(j + 1))
            def _():
                self.load_f(j + 1).start()
            self.load_w(j).wait()

            @pl.when(self.here(j))
            def _():
                self.load_f(j).wait()
                loop(self.acc.shape[0] // self.features.size, lambda q: self.add(lax.rem(j, 2), self.features.rows(q)))
        self.load_w(jnp.int32(0)).start()
        self.load_f(jnp.int32(0)).start()
        loop(self.spot.chips, unit)

    def swap(self, q):
        rows = self.features.rows(q)
        return pltpu.make_async_remote_copy(
            src_ref=self.acc.at[rows, pl.ds(self.cols, self.cols)], dst_ref=self.theirs.at[rows], send_sem=self.send.at[q],
            recv_sem=self.recv.at[q], device_id=self.spot.at(self.spot.dp, 1 - self.spot.core), device_id_type=MESH)

    def complete(self, q):
        slot = self.spot.steps % 2
        self.features.arrive(self.spot.steps - 1, q)

        @pl.when(self.spot.ends)
        def _():
            rows = self.features.rows(q)
            copy = pltpu.make_async_copy(self.features.fg.at[rows, self.features.lanes(self.shard(self.spot.steps))],
                                         self.f_tile.at[slot, rows], self.f_sem.at[slot])
            copy.start()
            copy.wait()
            self.add(slot, rows)
        self.swap(q).start()


class Backward:
    def __init__(self, spot, size, dz_here, dz_ref, send, recv, out_sem):
        self.spot, self.size, self.dz_here, self.dz_ref, self.send, self.recv, self.out_sem = spot, size, dz_here, dz_ref, send, recv, out_sem
        self.cols = dz_here.shape[1]

    def rows(self, q):
        return pl.ds(pl.multiple_of(q * self.size, 16), self.size)

    def swap(self, q):
        return pltpu.make_async_remote_copy(
            src_ref=self.dz_here.at[self.rows(q)], dst_ref=self.dz_ref.at[self.rows(q), pl.ds(self.cols, self.cols)],
            send_sem=self.send.at[q], recv_sem=self.recv.at[q], device_id=self.spot.at(self.spot.dp, 1 - self.spot.core), device_id_type=MESH)

    def keep(self, q):
        return pltpu.make_async_copy(self.dz_here.at[self.rows(q)], self.dz_ref.at[self.rows(q), pl.ds(0, self.cols)], self.out_sem.at[q])

    def start(self, q):
        self.swap(q).start()
        self.keep(q).start()

    def settle(self, q):
        self.swap(q).wait_recv()
        self.swap(q).wait_send()
        self.keep(q).wait()


def gelu_and_slope(v):
    factor, cubic = math.sqrt(2.0 / math.pi), 0.044715
    square = v * v
    th = jnp.tanh(factor * (v + cubic * (square * v)))
    slope = 0.5 * (1.0 + th) + 0.5 * v * (1.0 - th * th) * (factor * (1.0 + 3.0 * cubic * square))
    return 0.5 * v * (1.0 + th), slope


def live_rows_of(tot, share, live):
    keep = share[0][0]
    cols = live.shape[1]

    def strip(i):
        row = lax.broadcasted_iota(jnp.int32, (16, cols), 0).astype(jnp.float32) + (i * 16).astype(jnp.float32)
        here = jnp.where(row < tot[0, :1, :cols], 1.0, 0.0)
        there = jnp.zeros_like(here)
        for kind in range(4):
            count = tot[kind, :1, :cols]
            slot = row + float(share[kind][0] - keep)
            valid = (slot < count) & (count > keep)
            if kind == 3:
                valid = valid & (slot >= share[2][0] + share[2][1])
            there = there + jnp.where(valid, 1.0, 0.0)
        live[pl.ds(pl.multiple_of(i * 16, 16), 16)] = jnp.where(row < keep, here, there)
    loop(live.shape[0] // 16, strip)


def clear(ref):
    def strip(i):
        ref[pl.ds(pl.multiple_of(i * 16, 16), 16)] = jnp.zeros((16, ref.shape[1]), ref.dtype)
    loop(ref.shape[0] // 16, strip)


def fold(term):
    return term[:8] + term[8:]


class Grads:
    jobs, thirds = 8, 3

    def __init__(self, spot, fg, dz_here, gr, pg, relay, f_part, g_part, r_part, f_sem, g_sem, r_sem, send, recv, relay_send, relay_recv, own_sem):
        self.spot, self.fg, self.dz_here, self.gr, self.pg, self.relay_ref = spot, fg, dz_here, gr, pg, relay
        self.f_part, self.g_part, self.r_part, self.f_sem, self.g_sem, self.r_sem = f_part, g_part, r_part, f_sem, g_sem, r_sem
        self.send, self.recv, self.relay_send, self.relay_recv, self.own_sem = send, recv, relay_send, relay_recv, own_sem
        self.depth, self.cols = pg.shape[1], pg.shape[2]
        self.part = self.depth // self.thirds

    def owner_of(self, m):
        return jnp.where(m < 2, 3, jnp.where((m == 4) | (m == 5), 0, jnp.where((m == 2) | (m == 7), 1, 2)))

    def third(self, n):
        return pl.ds(pl.multiple_of(lax.rem(n, self.thirds) * self.part, 128), self.part)

    def load(self, n):
        first = (self.spot.dp ^ self.owner_of(n // self.thirds)) * self.depth + lax.rem(n, self.thirds) * self.part
        return pltpu.make_async_copy(self.fg.at[:, pl.ds(pl.multiple_of(first, 128), self.part)], self.f_part.at[lax.rem(n, 2)],
                                     self.f_sem.at[lax.rem(n, 2)])

    def store(self, n):
        return pltpu.make_async_copy(self.g_part.at[lax.rem(n, 2)], self.pg.at[n // self.thirds, self.third(n)], self.g_sem.at[lax.rem(n, 2)])

    def relay(self, m):
        return pltpu.make_async_remote_copy(
            src_ref=self.pg.at[m], dst_ref=self.relay_ref.at[m], send_sem=self.relay_send.at[m], recv_sem=self.relay_recv.at[m],
            device_id=self.spot.at(self.spot.dp ^ (m + 1), self.spot.core), device_id_type=MESH)

    def relayed(self, n):
        return pltpu.make_async_copy(self.relay_ref.at[jnp.maximum(n // self.thirds - (self.jobs - 2), 0), self.third(n)],
                                     self.r_part.at[lax.rem(n, 2)], self.r_sem.at[lax.rem(n, 2)])

    def job(self, m):
        joins = m >= self.jobs - 2
        lanes = pl.ds(pl.multiple_of(lax.rem(m, 2) * self.cols, 128), self.cols)

        @pl.when(joins)
        def _():
            k = jnp.maximum(m - (self.jobs - 2), 0)
            wait_for(self.relay_ref.at[k], self.relay_recv.at[k], self.relay_send.at[k])
            self.relayed(m * self.thirds).start()

        def part(c):
            n = m * self.thirds + c

            @pl.when(joins & (c + 1 < self.thirds))
            def _():
                self.relayed(n + 1).start()

            @pl.when(n + 1 < self.jobs * self.thirds)
            def _():
                self.load(n + 1).start()
            self.load(n).wait()

            @pl.when((n >= 2) & (n != (self.jobs - 2) * self.thirds) & (n != (self.jobs - 2) * self.thirds + 1))
            def _():
                self.store(n - 2).wait()

            @pl.when(joins)
            def _():
                self.relayed(n).wait()
            value = lax.dot_general(self.f_part[lax.rem(n, 2)], self.dz_here[:, lanes], (((0,), (0,)), ((), ())),
                                    preferred_element_type=jnp.float32)

            @pl.when(joins)
            def _():
                self.g_part[lax.rem(n, 2)] = (value + self.r_part[lax.rem(n, 2)].astype(jnp.float32)).astype(jnp.bfloat16)

            @pl.when(jnp.logical_not(joins))
            def _():
                self.g_part[lax.rem(n, 2)] = value.astype(jnp.bfloat16)
            self.store(n).start()
        loop(self.thirds, part)

    def copy(self, m):
        away, k = self.owner_of(m), self.spot.core ^ lax.rem(m, 2)
        return pltpu.make_async_remote_copy(
            src_ref=self.pg.at[m], dst_ref=self.gr.at[away, self.spot.core], send_sem=self.send.at[m],
            recv_sem=self.recv.at[away, self.spot.core], device_id=self.spot.at(self.spot.dp ^ away, k), device_id_type=MESH)

    def own(self):
        return pltpu.make_async_copy(self.pg.at[4], self.gr.at[0, self.spot.core], self.own_sem)

    def start(self, m):
        @pl.when(m < 2)
        def _():
            self.relay(jnp.minimum(m, 1)).start()

        @pl.when((m >= 2) & (m != 4))
        def _():
            self.copy(m).start()

        @pl.when(m == 4)
        def _():
            self.own().start()

    def turn(self, m, late):
        early = self.jobs - 2

        def job_at(m):
            return jnp.where(m < early, m, m - late + early)

        @pl.when((m == early) | (m == late + 2))
        def _():
            for c in (1, 2):
                self.store(job_at(m - 1) * self.thirds + c).wait()

        @pl.when((m < early) | (m == late) | (m == late + 1))
        def _():
            self.job(job_at(m))

        @pl.when(((m > 0) & (m <= early)) | (m == late + 1) | (m == late + 2))
        def _():
            self.start(job_at(m - 1))

    def settle(self):
        for away in range(3):
            for k in (0, 1):
                @pl.when((away != 0) | (self.spot.core != k))
                def _():
                    wait_for(self.gr.at[away, k], self.recv.at[away, k], self.send.at[2])
        self.own().wait()
        for m in range(self.jobs):
            if m < 2:
                self.relay(m).wait_send()
            elif m != 4:
                self.copy(jnp.int32(m)).wait_send()


class Sums:
    window, lag = 3, 2

    def __init__(self, spot, parts, share, d_ref, dz_here, w_here, held, total, send, recv, out_sem, back_send, back_recv):
        self.spot, self.parts, self.share, self.d_ref, self.dz_here, self.w_here, self.held, self.total = spot, parts, share, d_ref, dz_here, w_here, held, total
        self.send, self.recv, self.out_sem, self.back_send, self.back_recv = send, recv, out_sem, back_send, back_recv
        self.size, self.depth = total.shape[1], total.shape[2]
        self.turns = spot.steps * parts
        self.skip = self.size - share[0][1]

    def rows(self, piece):
        return pl.ds(pl.multiple_of(lax.rem(piece + self.parts - 1, self.parts) * self.size, 16), self.size)

    def third(self, n):
        return pl.ds(pl.multiple_of(n * (self.depth // 3), 128), self.depth // 3)

    def sends(self, step, way):
        return (self.spot.passed(way) < self.spot.steps) & (self.spot.passed(way) <= step)

    def passing(self, m, way, turn):
        rows = self.rows(lax.rem(m, self.parts))
        return pltpu.make_async_remote_copy(
            src_ref=self.held.at[way, turn // self.parts, rows], dst_ref=self.held.at[way, m // self.parts, rows],
            send_sem=self.send.at[way, m], recv_sem=self.recv.at[way, m], device_id=self.spot.on_line(self.spot.onward(way, 1)),
            device_id_type=MESH)

    def landed(self, m, way):
        wait_for(self.held.at[way, m // self.parts, self.rows(lax.rem(m, self.parts))], self.recv.at[way, m], self.send.at[way, m])

    def product(self, goal, rows, col):
        return lax.dot_general(self.dz_here[rows], self.w_here[goal, self.third(col)], (((1,), (1,)), ((), ())),
                               preferred_element_type=jnp.float32)

    def store(self, piece):
        s = lax.rem(piece, 2)
        return pltpu.make_async_copy(self.total.at[s], self.d_ref.at[self.rows(piece)], self.out_sem.at[s])

    def hand(self, kind):
        to, taken = share_rows(self.share, kind)
        return pltpu.make_async_remote_copy(
            src_ref=self.total.at[0, pl.ds(self.skip + taken.start, taken.size)], dst_ref=self.d_ref.at[to], send_sem=self.back_send.at[kind],
            recv_sem=self.back_recv.at[kind], device_id=self.spot.at(self.spot.others[kind], self.spot.core), device_id_type=MESH)

    def send_sum(self, m, way):
        step, rows = m // self.parts, self.rows(lax.rem(m, self.parts))
        first = self.spot.passed(way) == 0
        held = self.held

        @pl.when(first & (m >= self.window))
        def _():
            self.passing(jnp.maximum(m - self.window, 0), way, 0).wait_send()

        @pl.when(jnp.logical_not(first))
        def _():
            self.landed(m - self.parts, way)

        def column(col):
            lanes = self.third(col)
            value = self.product(self.spot.onward(way, self.spot.steps - step), rows, col)

            @pl.when(first)
            def _():
                held[way, step, rows, lanes] = value.astype(jnp.bfloat16)

            @pl.when(jnp.logical_not(first))
            def _():
                held[way, step - 1, rows, lanes] = (value + held[way, step - 1, rows, lanes].astype(jnp.float32)).astype(jnp.bfloat16)
        loop(3, column)
        self.passing(m, way, jnp.where(first, m, m - self.parts)).start()

    def finish(self, piece):
        rows, s = self.rows(piece), lax.rem(piece, 2)
        held, total, last = self.held, self.total, self.spot.steps - 1

        @pl.when(piece >= 2)
        def _():
            self.store(piece - 2).wait()

        @pl.when(piece == 2)
        def _():
            for kind in range(3):
                self.hand(kind).wait_send()

        def each(way):
            @pl.when(self.spot.passed(way) > 0)
            def _():
                self.landed(self.turns - self.parts + piece, way)
        loop(2, each)

        def column(col):
            value = self.product(self.spot.chip, rows, col)
            lanes = self.third(col)

            @pl.when(self.spot.ends)
            def _():
                way = jnp.where(self.spot.chip == 0, 1, 0)
                total[s, :, lanes] = (value + held[way, last, rows, lanes].astype(jnp.float32)).astype(jnp.bfloat16)

            @pl.when(jnp.logical_not(self.spot.ends))
            def _():
                total[s, :, lanes] = (value + held[0, last, rows, lanes].astype(jnp.float32)
                                      + held[1, last, rows, lanes].astype(jnp.float32)).astype(jnp.bfloat16)
        loop(3, column)
        self.store(piece).start()

        @pl.when(piece == 0)
        def _():
            for kind in (2, 0, 1):
                self.hand(kind).start()

    def turn(self, m):
        def each(way):
            @pl.when((m < self.turns) & self.sends(m // self.parts, way))
            def _():
                self.send_sum(m, way)
        loop(2, each)

    def turn_end(self, m):
        first = self.turns - self.parts + self.lag

        @pl.when((m >= first) & (m < first + self.parts))
        def _():
            self.finish(m - first)

    def settle(self):
        def drain(m):
            def each(way):
                first = self.spot.passed(way) == 0

                @pl.when(self.sends(m // self.parts, way) & (jnp.logical_not(first) | (m >= self.turns - self.window)))
                def _():
                    self.passing(m, way, 0).wait_send()
            loop(2, each)
        loop(self.turns, drain)
        for piece in (self.parts - 2, self.parts - 1):
            self.store(piece).wait()
        for kind in range(3):
            self.hand(kind).wait_recv()


def share_rows(share, kind):
    skip = share[2][0] + share[2][1] - share[3][0] if kind == 2 else 0
    first, length = share[1 + kind]
    return pl.ds(first + skip, length - skip), pl.ds(skip, length - skip)


class Stitched:
    def __init__(self, spot, share, y_ref, st_ref, y_send, y_recv, core_send, core_recv, give_send, give_recv, given_send, given_recv, own_sem):
        self.spot, self.share, self.y_ref, self.st_ref = spot, share, y_ref, st_ref
        self.y_send, self.y_recv, self.core_send, self.core_recv = y_send, y_recv, core_send, core_recv
        self.give_send, self.give_recv, self.given_send, self.given_recv, self.own_sem = give_send, give_recv, given_send, given_recv, own_sem
        self.towers, self.cols = y_ref.shape[0], y_ref.shape[2]
        self.bands = (share[0], (0, share[0][0]))
        self.events = 2 * self.towers * spot.steps

    def lanes(self, shard, k):
        return pl.ds(pl.multiple_of((2 * shard + k) * self.cols, 128), self.cols)

    def place(self, shard, k, t, b):
        return self.st_ref.at[t, pl.ds(*self.bands[b]), self.lanes(shard, k)]

    def source(self, t, b):
        return self.y_ref.at[t, pl.ds(*self.bands[b])]

    def leave(self, step, way, t, b, own=False):
        s = self.spot
        dst = self.place(s.onward(way, -step), s.core, t, b)
        return pltpu.make_async_remote_copy(
            src_ref=self.source(t, b) if own else dst, dst_ref=dst, send_sem=self.y_send.at[way, step, b, t],
            recv_sem=self.y_recv.at[way, step, b, t], device_id=s.on_line(s.onward(way, 1)), device_id_type=MESH)

    def to_core(self, shard, t, b, own=False):
        s = self.spot
        dst = self.place(shard, s.core, t, b)
        return pltpu.make_async_remote_copy(
            src_ref=self.source(t, b) if own else dst, dst_ref=dst, send_sem=self.core_send.at[shard, b, t],
            recv_sem=self.core_recv.at[shard, b, t], device_id=s.at(s.dp, 1 - s.core), device_id_type=MESH)

    def give(self, kind, shard, t, own=False):
        s = self.spot
        to, taken = share_rows(self.share, kind)
        src = pl.ds(self.share[0][0] + taken.start, taken.size)
        return pltpu.make_async_remote_copy(
            src_ref=self.y_ref.at[t, src] if own else self.st_ref.at[t, src, self.lanes(shard, s.core)],
            dst_ref=self.st_ref.at[t, to, self.lanes(shard, s.core)], send_sem=self.give_send.at[kind, shard, t],
            recv_sem=self.give_recv.at[kind, shard, t], device_id=s.at(s.others[kind], s.core), device_id_type=MESH)

    def given_place(self, kind, shard, t, k):
        return self.st_ref.at[t, share_rows(self.share, kind)[0], self.lanes(shard, k)]

    def given(self, kind, shard, t):
        s = self.spot
        ref = self.given_place(kind, shard, t, s.core)
        return pltpu.make_async_remote_copy(
            src_ref=ref, dst_ref=ref, send_sem=self.given_send.at[kind, shard, t], recv_sem=self.given_recv.at[kind, shard, t],
            device_id=s.at(s.dp, 1 - s.core), device_id_type=MESH)

    def own(self, t, b):
        return pltpu.make_async_copy(self.source(t, b), self.place(self.spot.chip, self.spot.core, t, b), self.own_sem.at[b, t])

    def start(self):
        for b in (0, 1):
            def tower(t):
                def each(way):
                    @pl.when(self.spot.leaves(0, way))
                    def _():
                        self.leave(0, way, t, b, True).start()
                loop(2, each)
                self.to_core(self.spot.chip, t, b, True).start()
                if b == 0:
                    for kind in (2, 0, 1):
                        self.give(kind, self.spot.chip, t, True).start()
                self.own(t, b).start()
            loop(self.towers, tower)

    def event(self, n):
        step, t = n // (2 * self.towers), lax.rem(n, self.towers)
        for b in (0, 1):
            def each(way):
                @pl.when(self.spot.comes(step, way))
                def _():
                    shard = self.spot.onward(way, -1 - step)
                    wait_for(self.place(shard, self.spot.core, t, b), self.y_recv.at[way, step, b, t], self.y_send.at[way, step, b, t])

                    @pl.when((step + 1 < self.spot.steps) & self.spot.leaves(step + 1, way))
                    def _():
                        self.leave(jnp.minimum(step + 1, self.spot.steps - 1), way, t, b).start()
                    self.to_core(shard, t, b).start()
                    if b == 0:
                        for kind in (2, 0, 1):
                            self.give(kind, shard, t).start()

            @pl.when(lax.rem(n, 2 * self.towers) // self.towers == b)
            def _():
                loop(2, each)

    def receive(self):
        def one(n):
            shard, t = n // self.towers, lax.rem(n, self.towers)
            for kind in range(3):
                wait_for(self.given_place(kind, shard, t, self.spot.core), self.give_recv.at[kind, shard, t], self.give_send.at[kind, shard, t])
                self.given(kind, shard, t).start()
        loop(self.spot.chips * self.towers, one)

    def settle(self):
        def one(n):
            shard, t = n // self.towers, lax.rem(n, self.towers)
            for b in (0, 1):
                wait_for(self.place(shard, 1 - self.spot.core, t, b), self.core_recv.at[shard, b, t], self.core_send.at[shard, b, t])
                self.to_core(shard, t, b).wait_send()

                @pl.when(shard < self.spot.steps)
                def _():
                    def each(way):
                        @pl.when(self.spot.leaves(shard, way))
                        def _():
                            self.leave(jnp.minimum(shard, self.spot.steps - 1), way, t, b).wait_send()
                    loop(2, each)
            for kind in range(3):
                self.give(kind, shard, t).wait_send()
                self.given(kind, shard, t).wait_send()
                wait_for(self.given_place(kind, shard, t, 1 - self.spot.core), self.given_recv.at[kind, shard, t], self.given_send.at[kind, shard, t])
        loop(self.spot.chips * self.towers, one)
        for t in range(self.towers):
            for b in (0, 1):
                self.own(t, b).wait()


def first_kernel(chips, parts, share, f_ref, w_ref, o_ref, n_ref, sp_ref, fg_ref, wg_ref, next_ref, og_ref, dz_ref, act_ref, sg_ref, tot_ref,
                 offer_f, taken, offer_o, og, wide, low, f_tile, w_tile, acc, theirs, live, act, dz_here, sums_here, tot,
                 f_send, f_recv, w_send, w_recv, wide_sem, p_sem, a_send, a_recv, z_send, z_recv, out_sem, x_send, x_recv, l_sem):
    spot = Spot(chips)
    keep, rows = share[0][0], sum(share[0])
    size = rows // parts
    fixed = rows - size
    spare = keep - fixed
    cols = o_ref.shape[2]
    spot.greet()

    def offer(kind, what):
        src = (f_ref.at[0], f_ref.at[1], o_ref, n_ref)[what]
        dst = (offer_f.at[0, 1 + kind], offer_f.at[1, 1 + kind], offer_o.at[1 + kind], tot.at[1 + kind])[what]
        if what < 3:
            src = src.at[pl.ds(*share[1 + kind])] if what < 2 else src.at[:, pl.ds(*share[1 + kind])]
        return pltpu.make_async_remote_copy(
            src_ref=src, dst_ref=dst, send_sem=x_send.at[what, kind], recv_sem=x_recv.at[what, kind],
            device_id=spot.at(spot.others[kind], spot.core), device_id_type=MESH)

    def choose(width, read, write):
        weigh = [jnp.broadcast_to(jnp.where(tot[kind, :1, :width] > keep, 1.0, 0.0), (16, width)) for kind in range(4)]

        def strip(i):
            at = pl.ds(pl.multiple_of(i * 16, 16), 16)
            value = read(0, at).astype(jnp.float32) * weigh[0]
            for kind in range(1, 4):
                value = value + read(kind, at).astype(jnp.float32) * weigh[kind]
            write(i * 16, value.astype(jnp.bfloat16))
        loop(share[0][1] // 16, strip)

    features = Features(spot, f_ref.at[0], taken.at[0], fg_ref, size, f_send, f_recv)
    weights = Weights(spot, w_ref.at[0], wide, low, wg_ref, wide_sem, p_sem.at[4], w_send, w_recv)
    products = Products(spot, features, wg_ref, f_tile, w_tile, acc, theirs, p_sem.at[pl.ds(0, 2)], p_sem.at[pl.ds(2, 2)], a_send, a_recv)
    backward = Backward(spot, size, dz_here, dz_ref, z_send, z_recv, out_sem)

    for what in (3, 0):
        for kind in (2, 0, 1):
            offer(kind, what).start()
    loop(parts - 1, lambda q: features.launch(q, False))
    local = [(n_ref, tot.at[0])]
    for t in (0, 1):
        local += [(f_ref.at[t, pl.ds(*share[0])], offer_f.at[t, 0]), (f_ref.at[t, pl.ds(fixed, spare)], taken.at[t, pl.ds(0, spare)])]
    local += [(o_ref.at[:, pl.ds(*share[0])], offer_o.at[0]), (o_ref.at[:, pl.ds(0, keep)], og.at[:, pl.ds(0, keep)]),
              (f_ref.at[0, pl.ds(0, fixed)], fg_ref.at[pl.ds(0, fixed), features.lanes(spot.chip)])]
    local = [pltpu.make_async_copy(src, dst, l_sem.at[n]) for n, (src, dst) in enumerate(local)]
    for copy in local:
        copy.start()
    weights.round()
    weights.start()
    for copy in local[:3]:
        copy.wait()
    for what in (3, 0):
        for kind in range(3):
            offer(kind, what).wait_recv()

    def take(t):
        def write(row, value):
            taken[t, pl.ds(pl.multiple_of(spare + row, 16), 16)] = value
        choose(offer_f.shape[3], lambda kind, at: offer_f[t, kind, at], write)
    take(0)
    features.launch(parts - 1, True)
    more = [pltpu.make_async_copy(tot, tot_ref, l_sem.at[8]),
            pltpu.make_async_copy(taken.at[0], fg_ref.at[pl.ds(fixed, size), features.lanes(spot.chip)], l_sem.at[9])]
    for copy in more:
        copy.start()
    live_rows_of(tot, share, live)
    clear(acc)

    loop(parts, lambda q: features.serve(0, q))
    weights.relay()
    for what in (2, 1):
        for kind in (2, 0, 1):
            offer(kind, what).start()
    loop(parts, lambda q: features.serve(1, q))
    weights.finish()
    for copy in local[3:] + more:
        copy.wait()
    products.multiply()
    for kind in range(3):
        offer(kind, 2).wait_recv()
    for t in range(2):
        def write(row, value):
            og[t, pl.ds(pl.multiple_of(keep + row, 16), 16)] = value
        choose(cols, lambda kind, at: offer_o[kind, t, at], write)
    keeps = [pltpu.make_async_copy(og, og_ref, l_sem.at[0])]
    keeps[0].start()

    sums_here[...] = jnp.zeros_like(sums_here)

    def strip(at):
        activated, slope = gelu_and_slope(acc[at, :cols] + theirs[at] + sp_ref[0:1])
        mask = live[at]
        dy = [og[t, at].astype(jnp.float32) * mask for t in range(2)]
        dz = slope * (sp_ref[2:3] * dy[0] + sp_ref[4:5] * dy[1])
        act[at] = activated
        dz_here[at] = dz.astype(jnp.bfloat16)
        for n, term in enumerate((dz, activated * dy[0], activated * dy[1])):
            sums_here[n] += fold(term)

    def stage(k):
        @pl.when(k < parts)
        def _():
            products.complete(k)

        @pl.when(k > 0)
        def _():
            products.swap(k - 1).wait_recv()
            loop(size // 16, lambda i: strip(pl.ds(pl.multiple_of((k - 1) * size + i * 16, 16), 16)))
            backward.start(k - 1)
    loop(parts + 1, stage)
    for kind in range(3):
        offer(kind, 1).wait_recv()
    take(1)
    keeps += [pltpu.make_async_copy(act, act_ref, l_sem.at[1]), pltpu.make_async_copy(taken.at[1], next_ref, l_sem.at[2])]
    for copy in keeps[1:]:
        copy.start()
    sg_ref[...] = jnp.zeros_like(sg_ref)
    for n in range(3):
        sg_ref[2 * n : 2 * n + 1] = jnp.sum(sums_here[n], axis=0, keepdims=True)

    def settle(q):
        backward.settle(q)
        products.swap(q).wait_send()
        features.settle(q)
    loop(parts, settle)
    weights.settle()
    for copy in keeps:
        copy.wait()
    for what in range(4):
        for kind in range(3):
            offer(kind, what).wait_send()


def second_kernel(chips, parts, share, f_ref, w_ref, next_ref, og_ref, tot, act_ref, sp_ref, fg_first, wg_first, dz_first,
                  fg_ref, wg_ref, dz_ref, y_ref, sg_ref, d_ref, gr_ref, pg_ref, relay_ref,
                  og, wide, low, f_tile, w_tile, acc, theirs, live, act, dz_here, y_here, sums_here,
                  held, w_here, dz_wide, total, f_part, g_part, r_part,
                  f_send, f_recv, w_send, w_recv, wide_sem, p_sem, a_send, a_recv, z_send, z_recv, out_sem, l_sem,
                  d_send, d_recv, o_sem, b_send, b_recv, g_load, g_send, g_recv, rs_send, rs_recv, own_sem):
    spot = Spot(chips)
    rows = sum(share[0])
    size = rows // parts
    fixed = rows - size
    cols = og_ref.shape[2]
    spot.greet()
    features = Features(spot, f_ref.at[1], next_ref, fg_ref, size, f_send, f_recv)
    weights = Weights(spot, w_ref.at[1], wide, low, wg_ref, wide_sem, p_sem.at[4], w_send, w_recv)
    products = Products(spot, features, wg_ref, f_tile, w_tile, acc, theirs, p_sem.at[pl.ds(0, 2)], p_sem.at[pl.ds(2, 2)], a_send, a_recv)
    backward = Backward(spot, size, dz_here, dz_ref, z_send, z_recv, out_sem)
    gradients = Sums(spot, parts, share, d_ref, dz_wide, w_here, held, total, d_send, d_recv, o_sem, b_send, b_recv)
    grads = Grads(spot, fg_first, dz_wide, gr_ref, pg_ref, relay_ref, f_part, g_part, r_part, g_load.at[0], g_load.at[1], g_load.at[2],
                  g_send, g_recv, rs_send, rs_recv, own_sem)

    loop(parts - 1, lambda q: features.launch(q, False))
    features.launch(parts - 1, True)
    loads = first_loads(chips, wg_first, dz_first, w_here, dz_wide, l_sem)
    grads.load(jnp.int32(0)).start()
    weights.round()
    weights.start()
    local = [(og_ref, og), (act_ref, act), (f_ref.at[1, pl.ds(0, fixed)], fg_ref.at[pl.ds(0, fixed), features.lanes(spot.chip)]),
             (next_ref, fg_ref.at[pl.ds(fixed, size), features.lanes(spot.chip)])]
    local = [pltpu.make_async_copy(src, dst, l_sem.at[chips + 1 + n]) for n, (src, dst) in enumerate(local)]
    for copy in local:
        copy.start()
    for copy in loads:
        copy.wait()

    def turn(m):
        gradients.turn(m)
        grads.turn(m, 9)

        @pl.when(m == 4)
        def _():
            weights.relay()

        @pl.when((m >= 2) & (m < 2 + parts))
        def _():
            features.serve(0, m - 2)

        @pl.when((m >= 7) & (m < 7 + parts))
        def _():
            features.serve(1, m - 7)

        @pl.when(m == 0)
        def _():
            live_rows_of(tot, share, live)
            clear(acc)

        @pl.when(m == 11)
        def _():
            weights.finish()
            for copy in local:
                copy.wait()
            products.multiply()
        gradients.turn_end(m)
    loop(gradients.turns + gradients.lag, turn)

    sums_here[...] = jnp.zeros_like(sums_here)

    def strip(at):
        activated, slope = gelu_and_slope(acc[at, :cols] + theirs[at] + sp_ref[1:2])
        mask = live[at]
        other = act[at]
        dy = [og[t, at].astype(jnp.float32) * mask for t in range(2)]
        dz = slope * (sp_ref[3:4] * dy[0] + sp_ref[5:6] * dy[1])
        for t in range(2):
            y_here[t, at] = ((sp_ref[2 + 2 * t : 3 + 2 * t] * other + sp_ref[3 + 2 * t : 4 + 2 * t] * activated) * mask).astype(jnp.bfloat16)
        dz_here[at] = dz.astype(jnp.bfloat16)
        for n, term in enumerate((dz, activated * dy[0], activated * dy[1])):
            sums_here[n] += fold(term)

    def stage(k):
        @pl.when(k < parts)
        def _():
            products.complete(k)

        @pl.when(k > 0)
        def _():
            products.swap(k - 1).wait_recv()
            loop(size // 16, lambda i: strip(pl.ds(pl.multiple_of((k - 1) * size + i * 16, 16), 16)))
            backward.start(k - 1)
    loop(parts + 1, stage)
    keep_y = pltpu.make_async_copy(y_here, y_ref, l_sem.at[0])
    keep_y.start()
    sg_ref[...] = jnp.zeros_like(sg_ref)
    for n in range(3):
        sg_ref[2 * n + 1 : 2 * n + 2] = jnp.sum(sums_here[n], axis=0, keepdims=True)

    def settle(q):
        backward.settle(q)
        products.swap(q).wait_send()
        features.settle(q)
    loop(parts, settle)
    weights.settle()
    gradients.settle()
    grads.settle()
    keep_y.wait()


def first_loads(chips, wg, dz, w_here, dz_wide, sem):
    depth = w_here.shape[1]
    loads = [pltpu.make_async_copy(dz, dz_wide, sem.at[chips])]
    loads += [pltpu.make_async_copy(wg.at[pl.ds(n * depth, depth)], w_here.at[n], sem.at[n]) for n in range(chips)]
    for copy in loads:
        copy.start()
    return loads


def third_kernel(chips, parts, share, y_ref, fg_ref, wg_ref, dz_ref, ps_ref, st_ref, d_ref, gr_ref, sr_ref, pg_ref, relay_ref,
                 held, w_here, dz_wide, total, f_part, g_part, r_part, l_sem,
                 d_send, d_recv, o_sem, b_send, b_recv, g_load, g_send, g_recv, rs_send, rs_recv, own_sem, s_send, s_recv,
                 y_send, y_recv, core_send, core_recv, give_send, give_recv, given_send, given_recv, y_own):
    spot = Spot(chips)
    spot.greet()
    gradients = Sums(spot, parts, share, d_ref, dz_wide, w_here, held, total, d_send, d_recv, o_sem, b_send, b_recv)
    grads = Grads(spot, fg_ref, dz_wide, gr_ref, pg_ref, relay_ref, f_part, g_part, r_part, g_load.at[0], g_load.at[1], g_load.at[2],
                  g_send, g_recv, rs_send, rs_recv, own_sem)
    stitched = Stitched(spot, share, y_ref, st_ref, y_send, y_recv, core_send, core_recv, give_send, give_recv, given_send, given_recv, y_own)

    def small(kind):
        return pltpu.make_async_remote_copy(
            src_ref=ps_ref, dst_ref=sr_ref.at[spot.dp], send_sem=s_send.at[kind], recv_sem=s_recv.at[kind],
            device_id=spot.at(spot.others[kind], spot.core), device_id_type=MESH)

    loads = first_loads(chips, wg_ref, dz_ref, w_here, dz_wide, l_sem)
    grads.load(jnp.int32(0)).start()
    stitched.start()
    own = pltpu.make_async_copy(ps_ref, sr_ref.at[spot.dp], l_sem.at[chips + 1])
    own.start()
    for kind in range(3):
        small(kind).start()
    for copy in loads:
        copy.wait()

    def turn(m):
        gradients.turn(m)
        grads.turn(m, 8)

        @pl.when((m >= 1) & (m <= stitched.events))
        def _():
            stitched.event(m - 1)
        gradients.turn_end(m)
    loop(gradients.turns + gradients.lag, turn)
    stitched.receive()
    gradients.settle()
    stitched.settle()
    grads.settle()
    for kind in range(3):
        small(kind).wait()
    own.wait()


def call(kernel, name, ident, out, scratch, operands, small_in=(), small_out=(), flops=0):
    anywhere, here = pl.BlockSpec(memory_space=pl.ANY), pl.BlockSpec(memory_space=pltpu.VMEM)
    return pl.pallas_call(
        kernel,
        out_shape=out,
        in_specs=[here if n in small_in else anywhere for n in range(len(operands))],
        out_specs=[here if n in small_out else anywhere for n in range(len(out))],
        scratch_shapes=scratch,
        compiler_params=pltpu.CompilerParams(collective_id=ident, has_side_effects=True, vmem_limit_bytes=58 * 2**20),
        cost_estimate=pl.CostEstimate(flops=flops, bytes_accessed=500 * 2**20, transcendentals=0),
        name=name,
    )(*operands)


def shared_pass(features, weights, out_grad, count, small_params, chips, parts, share):
    towers, slots, depth = features.shape
    cols = weights.shape[2]
    keep, size = share[0]
    rows = keep + size
    steps = chips - 1
    piece = rows // parts
    dma, vmem = pltpu.SemaphoreType.DMA, pltpu.VMEM
    bf16, f32 = jnp.bfloat16, jnp.float32
    S = jax.ShapeDtypeStruct
    told = jnp.broadcast_to(count.astype(f32), (8, depth))
    flops = 2 * rows * 2 * cols * depth * chips
    line = [dma((2, steps, parts))] * 2 + [dma((4, 2))] * 2 + [dma((2,)), dma((5,))] + [dma((parts,))] * 5
    tiles = [vmem((2, depth // 4, cols), f32), vmem((2, depth, cols), bf16), vmem((2, rows, depth), bf16), vmem((2, depth, 2 * cols), bf16),
             vmem((rows, 2 * cols), f32), vmem((rows, cols), f32), vmem((rows, cols), f32), vmem((rows, cols), f32), vmem((rows, cols), bf16)]
    folded = vmem((3, 8, cols), f32)
    wide = [S((rows, chips * depth), bf16), S((chips * depth, 2 * cols), bf16)]
    *first, start, grad_here, dz, act, small_first, told = call(
        functools.partial(first_kernel, chips, parts, share), "first", 3,
        wide + [S((piece, depth), bf16), S((towers, rows, cols), bf16), S((rows, 2 * cols), bf16), S((rows, cols), f32), S((8, cols), f32),
                S((4, 8, depth), f32)],
        [vmem((towers, 4, size, depth), bf16), vmem((towers, piece, depth), bf16), vmem((4, towers, size, cols), bf16), vmem((towers, rows, cols), bf16)]
        + tiles + [folded, vmem((4, 8, depth), f32)] + line + [dma((4, 3)), dma((4, 3)), dma((10,))],
        (features, weights, out_grad, told, small_params), (4,), (6,), flops)
    *second, dz_second, result, small_second, d_first, gr_first, _, _ = call(
        functools.partial(second_kernel, chips, parts, share), "second", 5,
        wide + [S((rows, 2 * cols), bf16), S((towers, rows, cols), bf16), S((8, cols), f32)] + sums_out(slots, depth, cols),
        [vmem((towers, rows, cols), bf16)] + tiles + [vmem((towers, rows, cols), bf16), folded] + sums_scratch(chips, rows, parts, depth, cols)
        + line + [dma((chips + 5,))] + sums_dma(steps, parts),
        (features, weights, start, grad_here, told, act, small_params, *first, dz), (4, 6), (4,), 3 * flops)
    return told, (result, *second, dz_second, small_first + small_second), d_first, gr_first


def sums_out(slots, depth, cols):
    S, bf16 = jax.ShapeDtypeStruct, jnp.bfloat16
    return [S((slots, depth), bf16), S((3, 2, depth, cols), bf16), S((8, depth, cols), bf16), S((2, depth, cols), bf16)]


def sums_scratch(chips, rows, parts, depth, cols):
    vmem, bf16 = pltpu.VMEM, jnp.bfloat16
    return [vmem((2, chips - 1, rows, depth), bf16), vmem((chips, depth, 2 * cols), bf16), vmem((rows, 2 * cols), bf16),
            vmem((2, rows // parts, depth), bf16), vmem((2, rows, depth // 3), bf16)] + [vmem((2, depth // 3, cols), bf16)] * 2


def sums_dma(steps, parts):
    dma = pltpu.SemaphoreType.DMA
    return [dma((2, steps * parts))] * 2 + [dma((2,)), dma((3,)), dma((3,)), dma((3, 2)), dma((8,)), dma((3, 2)), dma((2,)), dma((2,)), dma(())]


def shared_sums(result, wide_f, wide_w, wide_dz, partial_s, slots, chips, parts, share):
    towers, rows, cols = result.shape
    depth, steps = wide_w.shape[0] // chips, chips - 1
    dma = pltpu.SemaphoreType.DMA
    S = jax.ShapeDtypeStruct
    stitched, d_feat, parts_of, smalls, _, _ = call(
        functools.partial(third_kernel, chips, parts, share), "third", 4,
        [S((towers, slots, 2 * chips * cols), jnp.bfloat16)] + sums_out(slots, depth, cols)[:2] + [S((4,) + partial_s.shape, jnp.float32)]
        + sums_out(slots, depth, cols)[2:],
        sums_scratch(chips, rows, parts, depth, cols) + [dma((chips + 2,))] + sums_dma(steps, parts) + [dma((3,))] * 2
        + [dma((2, steps, 2, towers))] * 2 + [dma((chips, 2, towers))] * 2 + [dma((3, chips, towers))] * 4 + [dma((2, towers))],
        (result, wide_f, wide_w, wide_dz, partial_s), flops=4 * rows * 2 * cols * depth * chips)
    return stitched, d_feat, parts_of, smalls


def small_step(small_params, small_moment_one, small_moment_two, small_average, small_grad):
    first, second, direction = adam_part(small_moment_one, small_moment_two, small_grad)
    fresh = small_params - rate_small * direction
    return first, second, fresh, ema_decay * small_average + (1.0 - ema_decay) * fresh


def update(d_feat, stitched, full, parts, small_parts, states, small_states):
    small_grad = jnp.sum(small_parts, 0)[: small_states[0].shape[0]]
    *fresh, stitched, d_feat = soap(parts, full, stitched, d_feat, *states)
    return (stitched, d_feat) + tuple(fresh) + small_step(*small_states, small_grad)


def own_rows(features, out_grad, totals, passed, first, states, small_states):
    _, rows, _ = features.shape
    weights, small_params = states[0], small_states[0]
    cols = weights.shape[2]
    cores = lax.axis_size("mp")
    swap = [(i, i ^ 1) for i in range(cores)]
    ranges = ((0, rows // 2), (rows // 2, rows // 2))
    live_rows = (jnp.arange(rows, dtype=jnp.float32) < totals[0]).astype(jnp.float32)
    wide_f, wide_w = gather(features, weights.astype(jnp.bfloat16), cores // 2, ranges, 1)
    partial = jnp.einsum("tri,tio->tro", wide_f, wide_w, preferred_element_type=jnp.float32)
    product = partial[:, :, :cols] + lax.ppermute(partial[:, :, cols:], "mp", swap)
    result, back = jax.vjp(lambda a, b: stitch_local(a, b, live_rows), product, small_params)
    stitched = lax.all_gather(result.astype(jnp.bfloat16), "mp", axis=2, tiled=True)
    dz, small_part = back(out_grad.astype(jnp.float32))
    dz_low = dz.astype(jnp.bfloat16)
    wide_dz = jnp.concatenate([dz_low, lax.ppermute(dz_low, "mp", swap)], axis=2)
    partial_d = jnp.einsum("tro,tio->tri", wide_dz, wide_w, preferred_element_type=jnp.float32)
    partial_g = jnp.einsum("tri,tro->tio", wide_f, wide_dz, preferred_element_type=jnp.float32)
    small_part = jnp.pad(small_part, ((0, 2), (0, 0)))
    d_feat, parts, small_parts = reduce(
        partial_d.astype(jnp.bfloat16), partial_g.astype(jnp.bfloat16), small_part, cores // 2, ranges, 2
    )
    full = jnp.full((1,), rows, jnp.int32)
    return update((d_feat[0], d_feat[1]), stitched, full, (parts[:, :, 0], parts[:, :, 1]), small_parts, states, small_states)


def shares(rows):
    keep = rows * 15 // 32 // 16 * 16
    size = -(-(rows - keep) // 64) * 16
    return keep, ((keep, size), (keep + size, size), (keep + 2 * size, size), (rows - size, size))


def shared_rows(features, out_grad, totals, passed, first, states, small_states):
    rows = features.shape[1]
    keep, share = shares(rows)
    d_first, gr_first = first
    full = jnp.where(totals[:1] > keep, rows, keep)
    stitched, d_second, gr_second, small_parts = shared_sums(*passed, rows, lax.axis_size("mp") // 2, 4, share)
    return update((d_first, d_second), stitched, full, (gr_first, gr_second), small_parts, states, small_states)


def line_body(
    features,
    counts,
    weights,
    small_params,
    out_grad,
    moment_one,
    moment_two,
    average,
    basis_left,
    basis_right,
    small_moment_one,
    small_moment_two,
    small_average,
):
    keep, share = shares(features.shape[1])
    told, passed, *first = shared_pass(
        features, weights, out_grad, jnp.sum(counts), small_params, lax.axis_size("mp") // 2, 4, share
    )
    totals = told[:, 0, 0]
    return lax.cond(
        jnp.sum(totals > keep) == 1,
        shared_rows,
        own_rows,
        features,
        out_grad,
        totals,
        passed,
        first,
        (weights, moment_one, moment_two, average, basis_left, basis_right),
        (small_params, small_moment_one, small_moment_two, small_average),
    )


def plain_body(
    features,
    counts,
    weights,
    small_params,
    out_grad,
    moment_one,
    moment_two,
    average,
    basis_left,
    basis_right,
    small_moment_one,
    small_moment_two,
    small_average,
):
    slot_count = features.shape[1]
    total = jnp.sum(counts)
    live_rows = (jnp.arange(slot_count, dtype=jnp.int32) < total).astype(jnp.float32)
    weights_low = lax.all_gather(weights.astype(jnp.bfloat16), "dp", axis=1, tiled=True)
    feats_full = lax.all_gather(features, "mp", axis=2, tiled=True)
    product = jnp.einsum(
        "tri,tio->tro", feats_full, weights_low, preferred_element_type=jnp.float32
    )
    result, back = jax.vjp(lambda a, b: stitch_local(a, b, live_rows), product, small_params)
    stitched = lax.all_gather(result.astype(jnp.bfloat16), "mp", axis=2, tiled=True)
    dz, small_part = back(out_grad.astype(jnp.float32))
    dz_low = dz.astype(jnp.bfloat16)
    grad_part = jnp.einsum("tri,tro->tio", feats_full, dz_low, preferred_element_type=jnp.float32)
    partial_sums = jnp.einsum(
        "tro,tio->tri", dz_low, weights_low, preferred_element_type=jnp.float32
    )
    d_feat = lax.psum_scatter(
        partial_sums.astype(jnp.float32), "mp", scatter_dimension=2, tiled=True
    )
    grad = lax.psum_scatter(grad_part, "dp", scatter_dimension=1, tiled=True)
    small_grad = lax.psum(small_part, "dp")
    towers, n_in, n_out = grad.shape
    blocks = grad.reshape(towers, n_in // BLOCK, BLOCK, n_out // BLOCK, BLOCK)
    rotated = jnp.einsum(
        "trcai,tracb,trcbj->tricj", basis_left, blocks, basis_right, precision=lax.Precision.HIGHEST
    ).reshape(towers, n_in, n_out)
    first, second, direction = adam_part(moment_one, moment_two, rotated)
    turned = direction.reshape(towers, n_in // BLOCK, BLOCK, n_out // BLOCK, BLOCK)
    step_back = jnp.einsum(
        "trcai,tricj,trcbj->tracb", basis_left, turned, basis_right, precision=lax.Precision.HIGHEST
    ).reshape(towers, n_in, n_out)
    new_weights = weights - rate_main * (step_back + decay_weight * weights)
    new_average = ema_decay * average + (1.0 - ema_decay) * new_weights
    return (
        stitched,
        d_feat.astype(jnp.bfloat16),
        first,
        second,
        new_weights,
        new_average,
        new_weights.astype(jnp.bfloat16),
    ) + small_step(small_params, small_moment_one, small_moment_two, small_average, small_grad)


def solution(mesh):
    def body(features, counts, weights, *rest):
        dp, mp = mesh.shape["dp"], mesh.shape["mp"]
        tiles = features.shape[2] % 128 == 0 and weights.shape[2] % 128 == 0
        suits = dp == 4 and mp == 2 * dp and tiles and features.shape[1] % 64 == 0
        return (line_body if suits else plain_body)(features, counts, weights, *rest)

    return jax.shard_map(
        body,
        mesh=mesh,
        in_specs=(
            P(None, "dp", "mp"),
            P("dp"),
            P(None, "dp", "mp"),
            P(None, "mp"),
            P(None, "dp", "mp"),
            P(None, "dp", "mp"),
            P(None, "dp", "mp"),
            P(None, "dp", "mp"),
            P(None, "dp", "mp", None, None),
            P(None, "dp", "mp", None, None),
            P(None, "mp"),
            P(None, "mp"),
            P(None, "mp"),
        ),
        out_specs=(
            P(None, "dp", None),
            P(None, "dp", "mp"),
            P(None, "dp", "mp"),
            P(None, "dp", "mp"),
            P(None, "dp", "mp"),
            P(None, "dp", "mp"),
            P(None, "dp", "mp"),
            P(None, "mp"),
            P(None, "mp"),
            P(None, "mp"),
            P(None, "mp"),
        ),
        check_vma=False,
    )
```

```python
import functools
import math

import jax
import jax.numpy as jnp
from jax import lax
from jax.experimental import pallas as pl
from jax.experimental.pallas import tpu as pltpu
from jax.sharding import PartitionSpec as P

BLOCK = 64
STEP = 5


beta_one = 0.5
beta_two = 0.5
ema_decay = 0.5
rate_main = 0.01
rate_small = 0.05
decay_weight = 0.01
eps = 1e-08


def stitch_local(product, small, live_rows):
    pre_act = product + small[0:2][:, None, :]
    activated = jax.nn.gelu(pre_act, approximate=True)
    first = small[2] * activated[0] + small[3] * activated[1]
    second = small[4] * activated[0] + small[5] * activated[1]
    return jnp.stack([first, second]) * live_rows[None, :, None]


def adam_part(moment_a, moment_b, grad):
    first = beta_one * moment_a + (1.0 - beta_one) * grad
    second = beta_two * moment_b + (1.0 - beta_two) * grad * grad
    direction = first / (1.0 - beta_one**STEP) / (jnp.sqrt(second / (1.0 - beta_two**STEP)) + eps)
    return (first, second, direction)

def split(v):
    high = v.astype(jnp.bfloat16)
    return high, (v - high.astype(jnp.float32)).astype(jnp.bfloat16)

def soap_blocks(grads, lefts, rights, moments):
    row = lax.broadcasted_iota(jnp.int32, (2 * BLOCK, 2 * BLOCK), 0) // BLOCK
    lane = lax.broadcasted_iota(jnp.int32, (2 * BLOCK, 2 * BLOCK), 1) // BLOCK
    own = row == lane

    def diagonal(v):
        return jnp.where(own, jnp.concatenate([v, v], axis=0), jnp.zeros((), v.dtype))

    def stationary(high, low, axis):
        return jnp.concatenate([high, high, low], axis=axis)

    def moving(v, axis):
        high, low = split(v)
        return jnp.concatenate([high, low, high], axis=axis)

    def dots(a, b, ca, cb):
        dims = (((ca,), (cb,)), ((), ()))
        return [lax.dot_general(x, y, dims, preferred_element_type=jnp.float32) for x, y in zip(a, b)]

    right = [(diagonal(high), diagonal(low)) for high, low in rights]
    values = dots([moving(v, 1) for v in grads], [stationary(*v, 0) for v in right], 1, 0)
    values = dots([stationary(*v, 0) for v in lefts], [moving(v, 0) for v in values], 0, 0)
    values = [jnp.where(lane[:BLOCK] == 0, v[:BLOCK], v[BLOCK:]) for v in values]
    states = [adam_part(a, b, v) for (a, b), v in zip(moments, values)]
    values = dots([moving(v[2], 1) for v in states], [stationary(*v, 1) for v in right], 1, 1)
    values = dots([stationary(*v, 1) for v in lefts], [moving(diagonal(v), 0) for v in values], 1, 0)
    return [(first, second, step) for (first, second, _), step in zip(states, values)]


def soap_body(together, strips, full, parts_a, parts_b, stitched, d_a, d_b, weights, moment_a, moment_b, average, left, right,
              first, second, new_weights, new_average, copy, stitched_out, d_feat_out):
    groups, pairs = left.shape[2], left.shape[4] // BLOCK
    length = stitched.shape[1]
    row = jnp.minimum(pl.program_id(1) * pl.num_programs(2) + pl.program_id(2), strips - 1) * length

    first_tower = pl.program_id(0) == 0

    def clear(i, _):
        rows = pl.ds(pl.multiple_of(i * 16, 16), 16)
        wanted = row + i * 16 < full[0]
        stitched_out[0, rows] = jnp.where(wanted, stitched[0, rows], 0)
        d_feat_out[0, rows] = jnp.where(wanted, jnp.where(first_tower, d_a[rows], d_b[rows]), 0)
        return 0

    lax.fori_loop(0, length // 16, clear, 0)

    def blocks(g, _):
        places = [(g * together + s, q) for s in range(together) for q in range(pairs)]
        ats = [(0, pl.ds(pl.multiple_of(r * BLOCK, BLOCK), BLOCK), pl.ds(2 * BLOCK * q, 2 * BLOCK)) for r, q in places]
        grads = []
        for at in ats:
            grads.append(sum(jnp.where(first_tower, parts_a[(k,) + at], parts_b[(k,) + at]).astype(jnp.float32)
                             for k in range(parts_a.shape[0])))
        def basis(ref, r, q):
            return tuple(ref[0, 0, r, k, BLOCK * q : BLOCK * (q + 1)] for k in (0, 1))

        done = soap_blocks(grads, [basis(left, *place) for place in places], [basis(right, *place) for place in places],
                           [(moment_a[at], moment_b[at]) for at in ats])
        olds = [(weights[at], average[at]) for at in ats]
        for at, (one, two, step), (held, mean) in zip(ats, done, olds):
            first[at] = one
            second[at] = two
            fresh = held - rate_main * (step + decay_weight * held)
            new_weights[at] = fresh
            new_average[at] = ema_decay * mean + (1.0 - ema_decay) * fresh
            copy[at] = fresh.astype(jnp.bfloat16)
        return 0

    lax.fori_loop(0, groups // together, blocks, 0)


def soap(parts, wanted, stitched, d_feat, weights, moment_a, moment_b, average, bases, group=6):
    towers, rows, cols = weights.shape
    half = parts[0].shape[2]
    steps = half // (BLOCK * group)
    flat = lambda t, p, g: (t, p * steps + g, 0)
    state = pl.BlockSpec((1, BLOCK * group, cols), flat)
    base = [pl.BlockSpec((1, 1, group) + bases.shape[3:], lambda t, p, g, n=n: (n, t, p * steps + g, 0, 0, 0)) for n in (0, 1)]
    full = jax.ShapeDtypeStruct(weights.shape, jnp.float32)
    strips = max(n for n in range(1, 2 * steps + 1) if stitched.shape[1] % (16 * n) == 0)

    def strip(p, g):
        return jnp.minimum(p * steps + g, strips - 1)

    def through(shape):
        return pl.BlockSpec((1, shape[1] // strips, shape[2]), lambda t, p, g: (t, strip(p, g), 0))

    def of_tower(n, shape, index, last):
        return pl.BlockSpec(shape, lambda t, p, g: tuple(jnp.where(t == n, a, b) for a, b in zip(index(p, g), last if n == 0 else index(0, 0))))

    pieces = [of_tower(n, (v.shape[0], 1, BLOCK * group, cols), lambda p, g: (0, p, g, 0), (0, 1, steps - 1, 0)) for n, v in enumerate(parts)]
    rows_of = [of_tower(n, (v.shape[0] // strips, v.shape[1]), lambda p, g: (strip(p, g), 0), (strips - 1, 0)) for n, v in enumerate(d_feat)]

    return pl.pallas_call(
        functools.partial(soap_body, 2 - group % 2, strips),
        grid=(towers, 2, steps),
        in_specs=[pl.BlockSpec(memory_space=pltpu.SMEM),
                  *pieces, through(stitched.shape), *rows_of, state, state, state, state, *base],
        out_specs=[state] * 5 + [through(stitched.shape), through((towers,) + d_feat[0].shape)],
        out_shape=[full] * 4 + [jax.ShapeDtypeStruct(weights.shape, jnp.bfloat16)]
        + [jax.ShapeDtypeStruct(v, jnp.bfloat16) for v in (stitched.shape, (towers,) + d_feat[0].shape)],
        compiler_params=pltpu.CompilerParams(vmem_limit_bytes=60 * 2**20),
        cost_estimate=pl.CostEstimate(flops=8 * 2 * towers * rows * cols * 64, bytes_accessed=130 * 2**20, transcendentals=0),
        name="soap",
    )(wanted, *parts, stitched, *d_feat, weights, moment_a, moment_b, average, bases, bases)


MESH = pl.DeviceIdType.MESH


def place():
    mp = lax.axis_index("mp")
    return lax.axis_index("dp"), mp // 2, lax.rem(mp, 2)


def meet(devices):
    barrier = pltpu.get_barrier_semaphore()
    expected = 0
    for here, device in devices:
        @pl.when(here)
        def _():
            pl.semaphore_signal(barrier, inc=1, device_id=device, device_id_type=MESH)
        expected = expected + jnp.where(here, 1, 0)
    pl.semaphore_wait(barrier, expected)


def gather_kernel(chips, ranges, f_ref, w_ref, fg_ref, wg_ref, f_send, f_recv, w_send, w_recv, own_sem):
    dp, chip, core = place()
    towers, rows, depth = f_ref.shape
    cols = w_ref.shape[2]
    across, along = dp ^ 1, dp ^ 2
    at = lambda c, k: (c, 2 * chip + k)

    meet([(chip > 0, (dp, 2 * (chip - 1) + core)), (chip < chips - 1, (dp, 2 * (chip + 1) + core)),
          (chip >= 0, at(dp, 1 - core))] + [(chip >= 0, at(c, k)) for c in (across, along) for k in (0, 1)])

    def copies(step, way, t, k, shard, there):
        lanes = pl.ds(pl.multiple_of(shard * depth, 128), depth)
        rws = pl.ds(*ranges[k])
        src = fg_ref.at[t, rws, lanes]
        if step == 0:
            src = f_ref.at[t, rws]
        n = ((way * (chips - 1) + step) * towers + t) * len(ranges) + k
        return pltpu.make_async_remote_copy(
            src_ref=src, dst_ref=fg_ref.at[t, rws, lanes], send_sem=f_send.at[n], recv_sem=f_recv.at[n],
            device_id=(dp, 2 * there + core), device_id_type=MESH)

    def feature(step, way, t, k):
        return copies(step, way, t, k, chip - step if way == 0 else chip + step, chip + 1 if way == 0 else chip - 1)

    def incoming(step, way, t, k):
        return copies(step, way, t, k, chip - 1 - step if way == 0 else chip + 1 + step, chip)

    def sends(step, way):
        return (chip < chips - 1) & (chip >= step) if way == 0 else (chip > 0) & (chip + step < chips)

    def receives(step, way):
        return chip > step if way == 0 else chip + step < chips - 1

    def launch(t, k):
        for way in (0, 1):
            @pl.when(sends(0, way))
            def _():
                feature(0, way, t, k).start()

    def block(owner, slot, t):
        return wg_ref.at[t, pl.ds(pl.multiple_of(owner * depth, 128), depth), pl.ds(pl.multiple_of(slot * cols, 128), cols)]

    def weight(kind, k, t):
        to = at((across, along, dp)[kind], k)
        n = (kind * 2 + core) * 2 + t
        return pltpu.make_async_remote_copy(
            src_ref=w_ref.at[t, pl.ds(pl.multiple_of(k * depth, 128), depth)], dst_ref=block(dp, k ^ core, t),
            send_sem=w_send.at[(kind * 2 + k) * 2 + t], recv_sem=w_recv.at[n], device_id=to, device_id_type=MESH)

    def forward(kind, slot):
        owner, to, t = ((across, along, 0), (along, across, 1))[kind]
        n = 12 + kind * 2 + slot
        return pltpu.make_async_remote_copy(
            src_ref=block(owner, slot, t), dst_ref=block(owner, slot, t),
            send_sem=w_send.at[n], recv_sem=w_recv.at[n], device_id=at(to, core), device_id_type=MESH)

    def arrived(kind, slot, t):
        owner = (across, along, dp)[kind]
        n = (kind * 2 + (slot ^ core)) * 2 + t
        pltpu.make_async_remote_copy(
            src_ref=block(owner, slot, t), dst_ref=block(owner, slot, t), send_sem=w_send.at[n], recv_sem=w_recv.at[n],
            device_id=at(dp, core), device_id_type=MESH).wait_recv()

    mine = pl.ds(pl.multiple_of(chip * depth, 128), depth)
    own = [pltpu.make_async_copy(f_ref.at[t], fg_ref.at[t, :, mine], own_sem.at[t]) for t in range(towers)]
    own += [pltpu.make_async_copy(w_ref.at[t, pl.ds(pl.multiple_of(core * depth, 128), depth)], block(dp, 0, t), own_sem.at[2 + t])
            for t in range(towers)]

    pieces = [(t, k) for k in range(len(ranges)) for t in range(towers)]
    for t, k in pieces:
        launch(t, k)
    for copy in own:
        copy.start()
    for t in (0, 1):
        for k in (0, 1):
            weight(0, k, t).start()
            weight(1, k, 1 - t).start()
    for t in (0, 1):
        weight(2, 1 - core, t).start()

    for step in range(chips - 1):
        for t, k in pieces:
            for way in (0, 1):
                @pl.when(receives(step, way))
                def _():
                    incoming(step, way, t, k).wait_recv()
                if step + 1 < chips - 1:
                    @pl.when(sends(step + 1, way))
                    def _():
                        feature(step + 1, way, t, k).start()
            if step == 0 and (t, k) == pieces[-1]:
                for slot in (0, 1):
                    arrived(0, slot, 0)
                    forward(0, slot).start()
                    arrived(1, slot, 1)
                    forward(1, slot).start()

    for slot in (0, 1):
        arrived(0, slot, 1)
        arrived(1, slot, 0)
        forward(0, slot).wait_recv()
        forward(1, slot).wait_recv()
    for t in (0, 1):
        arrived(2, 1, t)
    for t in (0, 1):
        for k in (0, 1):
            weight(0, k, t).wait_send()
            weight(1, k, t).wait_send()
        weight(2, 1 - core, t).wait_send()
    for slot in (0, 1):
        forward(0, slot).wait_send()
        forward(1, slot).wait_send()
    for step in range(chips - 1):
        for t, k in pieces:
            for way in (0, 1):
                @pl.when(sends(step, way))
                def _():
                    feature(step, way, t, k).wait_send()
    for copy in own:
        copy.wait()


def gather(features, weights_low, chips, ranges, ident):
    towers, rows, depth = features.shape
    cols = weights_low.shape[2]
    count = 2 * (chips - 1) * towers * len(ranges)
    dma = pltpu.SemaphoreType.DMA
    anywhere = pl.BlockSpec(memory_space=pl.ANY)
    return pl.pallas_call(
        functools.partial(gather_kernel, chips, ranges),
        out_shape=[jax.ShapeDtypeStruct((towers, rows, chips * depth), jnp.bfloat16),
                   jax.ShapeDtypeStruct((towers, chips * depth, 2 * cols), jnp.bfloat16)],
        in_specs=[anywhere] * 2,
        out_specs=[anywhere] * 2,
        scratch_shapes=[dma((count,)), dma((count,)), dma((16,)), dma((16,)), dma((4,))],
        compiler_params=pltpu.CompilerParams(collective_id=ident, has_side_effects=True),
        cost_estimate=pl.CostEstimate(flops=0, bytes_accessed=800 * 2**20, transcendentals=0),
        name="gather",
    )(features, weights_low)


def reduce_kernel(chips, ranges, pd_ref, pg_ref, ps_ref, d_ref, gr_ref, sr_ref, held, term, total,
                  d_send, d_recv, t_sem, o_sem, g_send, g_recv, s_send, s_recv, own_sem):
    dp, chip, core = place()
    towers, rows, depth = d_ref.shape
    cols = pg_ref.shape[2] // 2
    across, along = dp ^ 1, dp ^ 2
    others = (across, along, dp ^ 3)
    at = lambda c, k: (c, 2 * chip + k)

    meet([(chip > 0, (dp, 2 * (chip - 1) + core)), (chip < chips - 1, (dp, 2 * (chip + 1) + core)),
          (chip >= 0, at(dp, 1 - core))] + [(chip >= 0, at(c, k)) for c in others for k in (0, 1)])

    def grad(kind, k, t):
        owner = (others + (dp,))[kind]
        return pltpu.make_async_remote_copy(
            src_ref=pg_ref.at[t, pl.ds(pl.multiple_of(owner * depth, 128), depth), pl.ds(pl.multiple_of((k ^ core) * cols, 128), cols)],
            dst_ref=gr_ref.at[dp, core, t], send_sem=g_send.at[(kind * 2 + k) * 2 + t],
            recv_sem=g_recv.at[(kind * 2 + core) * 2 + t], device_id=at(owner, k), device_id_type=MESH)

    def grad_arrived(kind, k, t):
        owner = (others + (dp,))[kind]
        pltpu.make_async_remote_copy(
            src_ref=gr_ref.at[owner, k, t], dst_ref=gr_ref.at[owner, k, t], send_sem=g_send.at[0],
            recv_sem=g_recv.at[(kind * 2 + k) * 2 + t], device_id=at(dp, core), device_id_type=MESH).wait_recv()

    def small(kind):
        return pltpu.make_async_remote_copy(
            src_ref=ps_ref, dst_ref=sr_ref.at[dp], send_sem=s_send.at[kind], recv_sem=s_recv.at[kind],
            device_id=at(others[kind], core), device_id_type=MESH)

    def target(step, way):
        return chip + chips - 1 - step if way == 0 else chip - (chips - 1 - step)

    def sends(step, way):
        return (chip < chips - 1) & (chip <= step) if way == 0 else (chip > 0) & (chips - 1 - chip <= step)

    def receives(step, way):
        return (chip > 0) & (chip <= step + 1) if way == 0 else (chip < chips - 1) & (chips - 1 - chip <= step + 1)

    def own_term(goal, t, k):
        return pd_ref.at[t, pl.ds(*ranges[k]), pl.ds(pl.multiple_of(goal * depth, 128), depth)]

    def partial(step, way, t, k, first):
        n = ((way * (chips - 1) + step) * towers + t) * len(ranges) + k
        src = own_term(target(step, way), t, k) if first else held.at[way, step - 1, t, pl.ds(*ranges[k])]
        there = chip + 1 if way == 0 else chip - 1
        return pltpu.make_async_remote_copy(
            src_ref=src, dst_ref=held.at[way, step, t, pl.ds(*ranges[k])], send_sem=d_send.at[n], recv_sem=d_recv.at[n],
            device_id=(dp, 2 * there + core), device_id_type=MESH)

    def landed(step, way, t, k):
        n = ((way * (chips - 1) + step) * towers + t) * len(ranges) + k
        ref = held.at[way, step, t, pl.ds(*ranges[k])]
        pltpu.make_async_remote_copy(src_ref=ref, dst_ref=ref, send_sem=d_send.at[n], recv_sem=d_recv.at[n],
                                     device_id=(dp, 2 * chip + core), device_id_type=MESH).wait_recv()

    pieces = [(t, k) for t in range(towers) for k in range(len(ranges))]
    ends = (chip == 0, chip == chips - 1)
    for t, k in pieces:
        for way in (0, 1):
            @pl.when(ends[way])
            def _():
                partial(0, way, t, k, True).start()
    own = [pltpu.make_async_copy(
        pg_ref.at[t, pl.ds(pl.multiple_of(dp * depth, 128), depth), pl.ds(0, cols)], gr_ref.at[dp, core, t], own_sem.at[t])
        for t in range(towers)]
    own.append(pltpu.make_async_copy(ps_ref, sr_ref.at[dp], own_sem.at[towers]))
    for copy in own:
        copy.start()
    for kind in range(3):
        small(kind).start()
    for t in range(towers):
        for kind in (2, 0, 1):
            for k in (0, 1):
                grad(kind, k, t).start()
        grad(3, 1 - core, t).start()

    strip = 16

    for step in range(1, chips - 1):
        for t, k in pieces:
            for way in (0, 1):
                @pl.when(sends(step, way) & ends[way])
                def _():
                    partial(step, way, t, k, True).start()

                @pl.when(sends(step, way) & jnp.logical_not(ends[way]))
                def _():
                    start, size = ranges[k]
                    load = pltpu.make_async_copy(own_term(target(step, way), t, k), term.at[way, pl.ds(0, size)], t_sem.at[way])
                    load.start()
                    landed(step - 1, way, t, k)
                    load.wait()

                    def add(i, _):
                        rws = pl.ds(pl.multiple_of(i * strip, strip), strip)
                        all_rows = pl.ds(pl.multiple_of(start + i * strip, strip), strip)
                        held[way, step - 1, t, all_rows] = (
                            held[way, step - 1, t, all_rows].astype(jnp.float32) + term[way, rws].astype(jnp.float32)
                        ).astype(jnp.bfloat16)
                        return 0
                    lax.fori_loop(0, size // strip, add, 0)
                    partial(step, way, t, k, False).start()

    stores = []
    for n, (t, k) in enumerate(pieces):
        s = n % 2
        start, size = ranges[k]
        load = pltpu.make_async_copy(own_term(chip, t, k), term.at[s, pl.ds(0, size)], t_sem.at[s])
        load.start()
        for way in (0, 1):
            @pl.when(receives(chips - 2, way))
            def _():
                landed(chips - 2, way, t, k)
        load.wait()
        if n >= 2:
            stores[n - 2].wait()

        def finish(i, _):
            rws = pl.ds(pl.multiple_of(i * strip, strip), strip)
            all_rows = pl.ds(pl.multiple_of(start + i * strip, strip), strip)
            value = term[s, rws].astype(jnp.float32)
            for way in (0, 1):
                here = receives(chips - 2, way)
                value = value + jnp.where(here, held[way, chips - 2, t, all_rows].astype(jnp.float32), 0.0)
            total[s, rws] = value.astype(jnp.bfloat16)
            return 0
        lax.fori_loop(0, size // strip, finish, 0)
        stores.append(pltpu.make_async_copy(total.at[s, pl.ds(0, size)], d_ref.at[t, pl.ds(start, size)], o_sem.at[s]))
        stores[n].start()
    for store in stores[-2:]:
        store.wait()

    for t in range(towers):
        for kind in range(3):
            for k in (0, 1):
                grad_arrived(kind, k, t)
        grad_arrived(3, 1 - core, t)
    for kind in range(3):
        small(kind).wait()
    for t in range(towers):
        for kind in range(3):
            for k in (0, 1):
                grad(kind, k, t).wait_send()
        grad(3, 1 - core, t).wait_send()
    for step in range(chips - 1):
        for t, k in pieces:
            for way in (0, 1):
                @pl.when(sends(step, way))
                def _():
                    partial(step, way, t, k, True).wait_send()
    for copy in own:
        copy.wait()


def reduce(partial_d, partial_g, partial_s, chips, ranges, ident):
    towers, rows, wide = partial_d.shape
    depth, cols = wide // chips, partial_g.shape[2] // 2
    count = 2 * (chips - 1) * towers * len(ranges)
    part = max(size for _, size in ranges)
    dma = pltpu.SemaphoreType.DMA
    bf16 = jnp.bfloat16
    out_shape = [jax.ShapeDtypeStruct((towers, rows, depth), bf16),
                 jax.ShapeDtypeStruct((4, 2, towers, depth, cols), bf16),
                 jax.ShapeDtypeStruct((4,) + partial_s.shape, jnp.float32)]
    return pl.pallas_call(
        functools.partial(reduce_kernel, chips, ranges),
        out_shape=out_shape,
        in_specs=[pl.BlockSpec(memory_space=pl.ANY)] * 3,
        out_specs=[pl.BlockSpec(memory_space=pl.ANY)] * len(out_shape),
        scratch_shapes=[pltpu.VMEM((2, chips - 1, towers, rows, depth), bf16),
                        pltpu.VMEM((2, part, depth), bf16), pltpu.VMEM((2, part, depth), bf16),
                        dma((count,)), dma((count,)), dma((2,)), dma((2,)), dma((16,)), dma((16,)), dma((3,)), dma((3,)), dma((towers + 1,))],
        compiler_params=pltpu.CompilerParams(collective_id=ident, has_side_effects=True, vmem_limit_bytes=56 * 2**20),
        cost_estimate=pl.CostEstimate(flops=0, bytes_accessed=800 * 2**20, transcendentals=0),
        name="reduce",
    )(partial_d, partial_g, partial_s)


def loop(count, body):
    def step(i, _):
        body(i)
        return 0
    lax.fori_loop(0, count, step, 0)


def wait_for(ref, sem, other):
    pltpu.make_async_remote_copy(src_ref=ref, dst_ref=ref, send_sem=other, recv_sem=sem, device_id=dict(dp=0, mp=0),
                                 device_id_type=MESH).wait_recv()


class Spot:
    def __init__(self, chips):
        self.dp, self.chip, self.core = place()
        self.chips, self.steps = chips, chips - 1
        self.others = (self.dp ^ 1, self.dp ^ 2, self.dp ^ 3)
        self.ends = (self.chip == 0) | (self.chip == self.steps)

    def at(self, dp, core):
        return dp, 2 * self.chip + core

    def on_line(self, chip):
        return self.dp, 2 * chip + self.core

    def passed(self, way):
        return jnp.where(way == 0, self.chip, self.steps - self.chip)

    def onward(self, way, n):
        return jnp.where(way == 0, self.chip + n, self.chip - n)

    def leaves(self, step, way):
        return (self.passed(way) < self.steps) & (self.passed(way) >= step)

    def comes(self, step, way):
        return self.passed(way) > step

    def greet(self):
        meet([(self.chip > 0, self.on_line(self.chip - 1)), (self.chip < self.steps, self.on_line(self.chip + 1)),
              (self.chip >= 0, self.at(self.dp, 1 - self.core))]
             + [(self.chip >= 0, self.at(c, k)) for c in self.others for k in (0, 1)])


class Features:
    def __init__(self, spot, f_ref, taken, fg, size, send, recv):
        self.spot, self.f_ref, self.taken, self.fg, self.size, self.send, self.recv = spot, f_ref, taken, fg, size, send, recv
        self.depth = f_ref.shape[1]

    def rows(self, q):
        return pl.ds(pl.multiple_of(q * self.size, 16), self.size)

    def lanes(self, shard):
        return pl.ds(pl.multiple_of(shard * self.depth, 128), self.depth)

    def copy(self, step, way, q, src=None):
        ref = self.fg.at[self.rows(q), self.lanes(self.spot.onward(way, -step))]
        return pltpu.make_async_remote_copy(
            src_ref=ref if src is None else src, dst_ref=ref, send_sem=self.send.at[way, step, q], recv_sem=self.recv.at[way, step, q],
            device_id=self.spot.on_line(self.spot.onward(way, 1)), device_id_type=MESH)

    def launch(self, q, last):
        def each(way):
            @pl.when(self.spot.leaves(0, way))
            def _():
                self.copy(0, way, q, self.taken if last else self.f_ref.at[self.rows(q)]).start()
        loop(2, each)

    def arrive(self, step, q):
        def each(way):
            @pl.when(self.spot.comes(step, way))
            def _():
                ref = self.fg.at[self.rows(q), self.lanes(self.spot.onward(way, -1 - step))]
                wait_for(ref, self.recv.at[way, step, q], self.send.at[way, step, q])
        loop(2, each)

    def serve(self, step, q):
        self.arrive(step, q)

        def each(way):
            @pl.when(self.spot.leaves(step + 1, way))
            def _():
                self.copy(step + 1, way, q).start()
        loop(2, each)

    def settle(self, q):
        for step in range(self.spot.steps):
            def each(way):
                @pl.when(self.spot.leaves(step, way))
                def _():
                    self.copy(step, way, q).wait_send()
            loop(2, each)


class Weights:
    def __init__(self, spot, low, wg, own_sem, send, recv):
        self.spot, self.low, self.wg, self.own_sem, self.send, self.recv = spot, low, wg, own_sem, send, recv
        self.depth, self.cols = low.shape[1], low.shape[2]

    def block(self, owner, slot):
        return self.wg.at[pl.ds(pl.multiple_of(owner * self.depth, 128), self.depth), pl.ds(pl.multiple_of(slot * self.cols, 128), self.cols)]

    def round(self, w_ref, wide, sem):
        part = wide.shape[1]
        parts = self.depth // part

        def load(n):
            return pltpu.make_async_copy(w_ref.at[pl.ds(pl.multiple_of(n * part, 16), part)], wide.at[lax.rem(n, 2)], sem.at[lax.rem(n, 2)])

        def one(n):
            @pl.when(n + 1 < 2 * parts)
            def _():
                load(n + 1).start()
            load(n).wait()

            def strip(i):
                rows = pl.ds(pl.multiple_of(i * 32, 32), 32)
                to = pl.ds(pl.multiple_of(lax.rem(n, parts) * part + i * 32, 32), 32)
                self.low[n // parts, to] = wide[lax.rem(n, 2), rows].astype(jnp.bfloat16)
            loop(part // 32, strip)
        load(jnp.int32(0)).start()
        loop(2 * parts, one)

    def send_own(self, kind, slot):
        s = self.spot
        k = s.core ^ slot
        return pltpu.make_async_remote_copy(
            src_ref=self.low.at[k], dst_ref=self.block(s.dp, slot), send_sem=self.send.at[kind, slot], recv_sem=self.recv.at[kind, slot],
            device_id=s.at((s.others[0], s.others[1], s.dp)[kind], k), device_id_type=MESH)

    def send_on(self, kind):
        s = self.spot
        ref = self.block(s.others[kind], kind)
        return pltpu.make_async_remote_copy(
            src_ref=ref, dst_ref=ref, send_sem=self.send.at[3, kind], recv_sem=self.recv.at[3, kind],
            device_id=s.at(s.others[1 - kind], s.core), device_id_type=MESH)

    def arrive(self, kind, slot):
        owner = (self.spot.others[0], self.spot.others[1], self.spot.dp)[kind]
        wait_for(self.block(owner, slot), self.recv.at[kind, slot], self.send.at[kind, slot])

    def own(self):
        return pltpu.make_async_copy(self.low.at[self.spot.core], self.block(self.spot.dp, 0), self.own_sem)

    def start(self):
        self.own().start()
        for slot in (0, 1):
            self.send_own(0, slot).start()
            self.send_own(1, 1 - slot).start()
        self.send_own(2, 1).start()

    def relay(self):
        for kind in (0, 1):
            self.arrive(kind, kind)
            self.send_on(kind).start()

    def finish(self):
        for kind in (0, 1):
            self.arrive(kind, 1 - kind)
            wait_for(self.block(self.spot.others[2], kind), self.recv.at[3, kind], self.send.at[3, kind])
        self.arrive(2, 1)
        self.own().wait()

    def settle(self):
        for kind in (0, 1):
            for slot in (0, 1):
                self.send_own(kind, slot).wait_send()
            self.send_on(kind).wait_send()
        self.send_own(2, 1).wait_send()


class Products:
    def __init__(self, spot, features, wg, f_tile, w_tile, acc, theirs, f_sem, w_sem, send, recv):
        self.spot, self.features, self.wg, self.f_tile, self.w_tile, self.acc, self.theirs = spot, features, wg, f_tile, w_tile, acc, theirs
        self.f_sem, self.w_sem, self.send, self.recv = f_sem, w_sem, send, recv
        self.cols = theirs.shape[1]

    def shard(self, j):
        return jnp.where(self.spot.chip == self.spot.steps, self.spot.steps - j, j)

    def load_w(self, j):
        depth = self.features.depth
        rows = pl.ds(pl.multiple_of(self.shard(j) * depth, 128), depth)
        return pltpu.make_async_copy(self.wg.at[rows], self.w_tile.at[lax.rem(j, 2)], self.w_sem.at[lax.rem(j, 2)])

    def load_f(self, j):
        lanes = self.features.lanes(self.shard(j))
        return pltpu.make_async_copy(self.features.fg.at[:, lanes], self.f_tile.at[lax.rem(j, 2)], self.f_sem.at[lax.rem(j, 2)])

    def here(self, j):
        return (j < self.spot.steps) | jnp.logical_not(self.spot.ends)

    def add(self, slot, rows):
        for col in range(0, 2 * self.cols, self.cols):
            lanes = pl.ds(col, self.cols)
            self.acc[rows, lanes] += jnp.dot(self.f_tile[slot, rows], self.w_tile[slot, :, lanes], preferred_element_type=jnp.float32)

    def multiply(self):
        def unit(j):
            @pl.when(j < self.spot.steps)
            def _():
                self.load_w(j + 1).start()

            @pl.when((j < self.spot.steps) & self.here(j + 1))
            def _():
                self.load_f(j + 1).start()
            self.load_w(j).wait()

            @pl.when(self.here(j))
            def _():
                self.load_f(j).wait()
                loop(self.acc.shape[0] // self.features.size, lambda q: self.add(lax.rem(j, 2), self.features.rows(q)))
        self.load_w(jnp.int32(0)).start()
        self.load_f(jnp.int32(0)).start()
        loop(self.spot.chips, unit)

    def swap(self, q):
        rows = self.features.rows(q)
        return pltpu.make_async_remote_copy(
            src_ref=self.acc.at[rows, pl.ds(self.cols, self.cols)], dst_ref=self.theirs.at[rows], send_sem=self.send.at[q],
            recv_sem=self.recv.at[q], device_id=self.spot.at(self.spot.dp, 1 - self.spot.core), device_id_type=MESH)

    def complete(self, q):
        slot = self.spot.steps % 2
        self.features.arrive(self.spot.steps - 1, q)

        @pl.when(self.spot.ends)
        def _():
            rows = self.features.rows(q)
            copy = pltpu.make_async_copy(self.features.fg.at[rows, self.features.lanes(self.shard(self.spot.steps))],
                                         self.f_tile.at[slot, rows], self.f_sem.at[slot])
            copy.start()
            copy.wait()
            self.add(slot, rows)
        self.swap(q).start()


class Backward:
    def __init__(self, spot, size, dz_here, dz_ref, send, recv, out_sem):
        self.spot, self.size, self.dz_here, self.dz_ref, self.send, self.recv, self.out_sem = spot, size, dz_here, dz_ref, send, recv, out_sem
        self.cols = dz_here.shape[1]

    def rows(self, q):
        return pl.ds(pl.multiple_of(q * self.size, 16), self.size)

    def swap(self, q):
        return pltpu.make_async_remote_copy(
            src_ref=self.dz_here.at[self.rows(q)], dst_ref=self.dz_ref.at[self.rows(q), pl.ds(self.cols, self.cols)],
            send_sem=self.send.at[q], recv_sem=self.recv.at[q], device_id=self.spot.at(self.spot.dp, 1 - self.spot.core), device_id_type=MESH)

    def keep(self, q):
        return pltpu.make_async_copy(self.dz_here.at[self.rows(q)], self.dz_ref.at[self.rows(q), pl.ds(0, self.cols)], self.out_sem.at[q])

    def start(self, q):
        self.swap(q).start()
        self.keep(q).start()

    def settle(self, q):
        self.swap(q).wait_recv()
        self.swap(q).wait_send()
        self.keep(q).wait()


def gelu_and_slope(v):
    factor, cubic = math.sqrt(2.0 / math.pi), 0.044715
    square = v * v
    th = jnp.tanh(factor * (v + cubic * (square * v)))
    slope = 0.5 * (1.0 + th) + 0.5 * v * (1.0 - th * th) * (factor * (1.0 + 3.0 * cubic * square))
    return 0.5 * v * (1.0 + th), slope


def live_rows_of(tot, share, live):
    keep = share[0][0]
    cols = live.shape[1]

    def strip(i):
        row = lax.broadcasted_iota(jnp.int32, (16, cols), 0).astype(jnp.float32) + (i * 16).astype(jnp.float32)
        here = jnp.where(row < tot[0, :1, :cols], 1.0, 0.0)
        there = jnp.zeros_like(here)
        for kind in range(4):
            count = tot[kind, :1, :cols]
            slot = row + float(share[kind][0] - keep)
            valid = (slot < count) & (count > keep)
            if kind == 3:
                valid = valid & (slot >= share[2][0] + share[2][1])
            there = there + jnp.where(valid, 1.0, 0.0)
        live[pl.ds(pl.multiple_of(i * 16, 16), 16)] = jnp.where(row < keep, here, there)
    loop(live.shape[0] // 16, strip)


def clear(ref):
    def strip(i):
        ref[pl.ds(pl.multiple_of(i * 16, 16), 16)] = jnp.zeros((16, ref.shape[1]), ref.dtype)
    loop(ref.shape[0] // 16, strip)


def fold(term):
    return term[:8] + term[8:]


class Grads:
    jobs, thirds = 8, 3

    def __init__(self, spot, fg, dz_here, gr, pg, relay, f_part, g_part, r_part, f_sem, g_sem, r_sem, send, recv, relay_send, relay_recv, own_sem):
        self.spot, self.fg, self.dz_here, self.gr, self.pg, self.relay_ref = spot, fg, dz_here, gr, pg, relay
        self.f_part, self.g_part, self.r_part, self.f_sem, self.g_sem, self.r_sem = f_part, g_part, r_part, f_sem, g_sem, r_sem
        self.send, self.recv, self.relay_send, self.relay_recv, self.own_sem = send, recv, relay_send, relay_recv, own_sem
        self.depth, self.cols = pg.shape[1], pg.shape[2]
        self.part = self.depth // self.thirds

    def owner_of(self, m):
        return jnp.where(m < 2, 3, jnp.where((m == 4) | (m == 5), 0, jnp.where((m == 2) | (m == 7), 1, 2)))

    def third(self, n):
        return pl.ds(pl.multiple_of(lax.rem(n, self.thirds) * self.part, 128), self.part)

    def load(self, n):
        first = (self.spot.dp ^ self.owner_of(n // self.thirds)) * self.depth + lax.rem(n, self.thirds) * self.part
        return pltpu.make_async_copy(self.fg.at[:, pl.ds(pl.multiple_of(first, 128), self.part)], self.f_part.at[lax.rem(n, 2)],
                                     self.f_sem.at[lax.rem(n, 2)])

    def store(self, n):
        return pltpu.make_async_copy(self.g_part.at[lax.rem(n, 2)], self.pg.at[n // self.thirds, self.third(n)], self.g_sem.at[lax.rem(n, 2)])

    def relay(self, m):
        return pltpu.make_async_remote_copy(
            src_ref=self.pg.at[m], dst_ref=self.relay_ref.at[m], send_sem=self.relay_send.at[m], recv_sem=self.relay_recv.at[m],
            device_id=self.spot.at(self.spot.dp ^ (m + 1), self.spot.core), device_id_type=MESH)

    def relayed(self, n):
        return pltpu.make_async_copy(self.relay_ref.at[jnp.maximum(n // self.thirds - (self.jobs - 2), 0), self.third(n)],
                                     self.r_part.at[lax.rem(n, 2)], self.r_sem.at[lax.rem(n, 2)])

    def job(self, m):
        joins = m >= self.jobs - 2
        lanes = pl.ds(pl.multiple_of(lax.rem(m, 2) * self.cols, 128), self.cols)

        @pl.when(joins)
        def _():
            k = jnp.maximum(m - (self.jobs - 2), 0)
            wait_for(self.relay_ref.at[k], self.relay_recv.at[k], self.relay_send.at[k])
            self.relayed(m * self.thirds).start()

        def part(c):
            n = m * self.thirds + c

            @pl.when(joins & (c + 1 < self.thirds))
            def _():
                self.relayed(n + 1).start()

            @pl.when(n + 1 < self.jobs * self.thirds)
            def _():
                self.load(n + 1).start()
            self.load(n).wait()

            @pl.when((n >= 2) & (n != (self.jobs - 2) * self.thirds) & (n != (self.jobs - 2) * self.thirds + 1))
            def _():
                self.store(n - 2).wait()

            @pl.when(joins)
            def _():
                self.relayed(n).wait()
            value = lax.dot_general(self.f_part[lax.rem(n, 2)], self.dz_here[:, lanes], (((0,), (0,)), ((), ())),
                                    preferred_element_type=jnp.float32)

            @pl.when(joins)
            def _():
                self.g_part[lax.rem(n, 2)] = (value + self.r_part[lax.rem(n, 2)].astype(jnp.float32)).astype(jnp.bfloat16)

            @pl.when(jnp.logical_not(joins))
            def _():
                self.g_part[lax.rem(n, 2)] = value.astype(jnp.bfloat16)
            self.store(n).start()
        loop(self.thirds, part)

    def copy(self, m):
        away, k = self.owner_of(m), self.spot.core ^ lax.rem(m, 2)
        return pltpu.make_async_remote_copy(
            src_ref=self.pg.at[m], dst_ref=self.gr.at[away, self.spot.core], send_sem=self.send.at[m],
            recv_sem=self.recv.at[away, self.spot.core], device_id=self.spot.at(self.spot.dp ^ away, k), device_id_type=MESH)

    def own(self):
        return pltpu.make_async_copy(self.pg.at[4], self.gr.at[0, self.spot.core], self.own_sem)

    def start(self, m):
        @pl.when(m < 2)
        def _():
            self.relay(jnp.minimum(m, 1)).start()

        @pl.when((m >= 2) & (m != 4))
        def _():
            self.copy(m).start()

        @pl.when(m == 4)
        def _():
            self.own().start()

    def turn(self, m, begin, late):
        early = self.jobs - 2
        pause = begin + early

        def job_at(m):
            return jnp.where(m < pause, m - begin, m - late + early)

        @pl.when((m == pause) | (m == late + 2))
        def _():
            for c in (1, 2):
                self.store(job_at(m - 1) * self.thirds + c).wait()

        @pl.when(((m >= begin) & (m < pause)) | (m == late) | (m == late + 1))
        def _():
            self.job(job_at(m))

        @pl.when(((m > begin) & (m <= pause)) | (m == late + 1) | (m == late + 2))
        def _():
            self.start(job_at(m - 1))

    def settle(self):
        for away in range(3):
            for k in (0, 1):
                @pl.when((away != 0) | (self.spot.core != k))
                def _():
                    wait_for(self.gr.at[away, k], self.recv.at[away, k], self.send.at[2])
        self.own().wait()
        for m in range(self.jobs):
            if m < 2:
                self.relay(m).wait_send()
            elif m != 4:
                self.copy(jnp.int32(m)).wait_send()


class Sums:
    window, lag = 5, 1

    def __init__(self, spot, parts, share, d_ref, dz_here, w_here, held, total, send, recv, out_sem, back_send, back_recv):
        self.spot, self.parts, self.share, self.d_ref, self.dz_here, self.w_here, self.held, self.total = spot, parts, share, d_ref, dz_here, w_here, held, total
        self.send, self.recv, self.out_sem, self.back_send, self.back_recv = send, recv, out_sem, back_send, back_recv
        self.size, self.depth = total.shape[1], total.shape[2]
        self.turns = spot.steps * parts
        self.skip = self.size - share[0][1]

    def rows(self, piece):
        return pl.ds(pl.multiple_of(lax.rem(piece + self.parts - 1, self.parts) * self.size, 16), self.size)

    def third(self, n):
        return pl.ds(pl.multiple_of(n * (self.depth // 3), 128), self.depth // 3)

    def sends(self, step, way):
        return (self.spot.passed(way) < self.spot.steps) & (self.spot.passed(way) <= step)

    def passing(self, m, way, turn):
        rows = self.rows(lax.rem(m, self.parts))
        return pltpu.make_async_remote_copy(
            src_ref=self.held.at[way, turn // self.parts, rows], dst_ref=self.held.at[way, m // self.parts, rows],
            send_sem=self.send.at[way, m], recv_sem=self.recv.at[way, m], device_id=self.spot.on_line(self.spot.onward(way, 1)),
            device_id_type=MESH)

    def landed(self, m, way):
        wait_for(self.held.at[way, m // self.parts, self.rows(lax.rem(m, self.parts))], self.recv.at[way, m], self.send.at[way, m])

    def product(self, goal, rows, col):
        return lax.dot_general(self.dz_here[rows], self.w_here[goal, self.third(col)], (((1,), (1,)), ((), ())),
                               preferred_element_type=jnp.float32)

    def store(self, piece):
        s = lax.rem(piece, 2)
        return pltpu.make_async_copy(self.total.at[s], self.d_ref.at[self.rows(piece)], self.out_sem.at[s])

    def hand(self, kind):
        to, taken = share_rows(self.share, kind)
        return pltpu.make_async_remote_copy(
            src_ref=self.total.at[0, pl.ds(self.skip + taken.start, taken.size)], dst_ref=self.d_ref.at[to], send_sem=self.back_send.at[kind],
            recv_sem=self.back_recv.at[kind], device_id=self.spot.at(self.spot.others[kind], self.spot.core), device_id_type=MESH)

    def send_sum(self, m, way):
        step, rows = m // self.parts, self.rows(lax.rem(m, self.parts))
        first = self.spot.passed(way) == 0
        held = self.held

        @pl.when(first & (m >= self.window))
        def _():
            self.passing(jnp.maximum(m - self.window, 0), way, 0).wait_send()

        @pl.when(jnp.logical_not(first))
        def _():
            self.landed(m - self.parts, way)

        def column(col):
            lanes = self.third(col)
            value = self.product(self.spot.onward(way, self.spot.steps - step), rows, col)

            @pl.when(first)
            def _():
                held[way, step, rows, lanes] = value.astype(jnp.bfloat16)

            @pl.when(jnp.logical_not(first))
            def _():
                held[way, step - 1, rows, lanes] = (value + held[way, step - 1, rows, lanes].astype(jnp.float32)).astype(jnp.bfloat16)
        loop(3, column)
        self.passing(m, way, jnp.where(first, m, m - self.parts)).start()

    def finish(self, piece):
        rows, s = self.rows(piece), lax.rem(piece, 2)
        held, total, last = self.held, self.total, self.spot.steps - 1

        @pl.when(piece >= 2)
        def _():
            self.store(piece - 2).wait()

        @pl.when(piece == 2)
        def _():
            for kind in range(3):
                self.hand(kind).wait_send()

        def each(way):
            @pl.when(self.spot.passed(way) > 0)
            def _():
                self.landed(self.turns - self.parts + piece, way)
        loop(2, each)

        def column(col):
            value = self.product(self.spot.chip, rows, col)
            lanes = self.third(col)

            @pl.when(self.spot.ends)
            def _():
                way = jnp.where(self.spot.chip == 0, 1, 0)
                total[s, :, lanes] = (value + held[way, last, rows, lanes].astype(jnp.float32)).astype(jnp.bfloat16)

            @pl.when(jnp.logical_not(self.spot.ends))
            def _():
                total[s, :, lanes] = (value + held[0, last, rows, lanes].astype(jnp.float32)
                                      + held[1, last, rows, lanes].astype(jnp.float32)).astype(jnp.bfloat16)
        loop(3, column)
        self.store(piece).start()

        @pl.when(piece == 0)
        def _():
            for kind in (2, 0, 1):
                self.hand(kind).start()

    def turn(self, m):
        def each(way):
            @pl.when((m < self.turns) & self.sends(m // self.parts, way))
            def _():
                self.send_sum(m, way)
        loop(2, each)

    def turn_end(self, m):
        first = self.turns - self.parts + self.lag

        @pl.when((m >= first) & (m < first + self.parts))
        def _():
            self.finish(m - first)

    def settle(self):
        def drain(m):
            def each(way):
                first = self.spot.passed(way) == 0

                @pl.when(self.sends(m // self.parts, way) & (jnp.logical_not(first) | (m >= self.turns - self.window)))
                def _():
                    self.passing(m, way, 0).wait_send()
            loop(2, each)
        loop(self.turns, drain)
        for piece in (self.parts - 2, self.parts - 1):
            self.store(piece).wait()
        for kind in range(3):
            self.hand(kind).wait_recv()


def share_rows(share, kind):
    skip = share[2][0] + share[2][1] - share[3][0] if kind == 2 else 0
    first, length = share[1 + kind]
    return pl.ds(first + skip, length - skip), pl.ds(skip, length - skip)


class Bases:
    def __init__(self, left, right, out, held, parts, load_sem, store_sem):
        self.sources, self.out, self.held, self.parts, self.load_sem, self.store_sem = (left, right), out, held, parts, load_sem, store_sem
        self.groups, self.pairs = left.shape[1], left.shape[2] // 2
        self.units = left.shape[0] * self.groups

    def at(self, u):
        return u // self.groups, lax.rem(u, self.groups), lax.rem(u, 2)

    def load(self, u, start):
        t, r, slot = self.at(u)
        for n, source in enumerate(self.sources):
            copy = pltpu.make_async_copy(source.at[t, r], self.held.at[slot, n], self.load_sem.at[slot, n])
            (copy.start if start else copy.wait)()

    def store(self, u, start):
        t, r, slot = self.at(u)
        for n in (0, 1):
            copy = pltpu.make_async_copy(self.parts.at[slot, n], self.out.at[n, t, r], self.store_sem.at[slot, n])
            (copy.start if start else copy.wait)()

    def unit(self, u):
        @pl.when(u + 1 < self.units)
        def _():
            self.load(u + 1, True)
        self.load(u, False)

        @pl.when(u >= 2)
        def _():
            self.store(u - 2, False)
        slot = lax.rem(u, 2)
        for n in (0, 1):
            for q in range(self.pairs):
                both = jnp.concatenate([self.held[slot, n, 2 * q], self.held[slot, n, 2 * q + 1]], axis=1)
                high, low = split(both)
                rows = pl.ds(q * BLOCK, BLOCK)
                self.parts[slot, n, 0, rows] = high
                self.parts[slot, n, 1, rows] = low
        self.store(u, True)

    def some(self, first, count):
        def one(i):
            @pl.when(first + i < self.units)
            def _():
                self.unit(first + i)
        loop(count, one)

    def settle(self):
        for u in (self.units - 2, self.units - 1):
            self.store(jnp.int32(u), False)


class Stitched:
    def __init__(self, spot, share, y_ref, st_ref, y_send, y_recv, core_send, core_recv, give_send, give_recv, given_send, given_recv, own_sem):
        self.spot, self.share, self.y_ref, self.st_ref = spot, share, y_ref, st_ref
        self.y_send, self.y_recv, self.core_send, self.core_recv = y_send, y_recv, core_send, core_recv
        self.give_send, self.give_recv, self.given_send, self.given_recv, self.own_sem = give_send, give_recv, given_send, given_recv, own_sem
        self.towers, self.cols = y_ref.shape[0], y_ref.shape[2]
        self.bands = (share[0], (0, share[0][0]))
        self.events = 2 * self.towers * spot.steps

    def lanes(self, shard, k):
        return pl.ds(pl.multiple_of((2 * shard + k) * self.cols, 128), self.cols)

    def place(self, shard, k, t, b):
        return self.st_ref.at[t, pl.ds(*self.bands[b]), self.lanes(shard, k)]

    def source(self, t, b):
        return self.y_ref.at[t, pl.ds(*self.bands[b])]

    def leave(self, step, way, t, b, own=False):
        s = self.spot
        dst = self.place(s.onward(way, -step), s.core, t, b)
        return pltpu.make_async_remote_copy(
            src_ref=self.source(t, b) if own else dst, dst_ref=dst, send_sem=self.y_send.at[way, step, b, t],
            recv_sem=self.y_recv.at[way, step, b, t], device_id=s.on_line(s.onward(way, 1)), device_id_type=MESH)

    def to_core(self, shard, t, b, own=False):
        s = self.spot
        dst = self.place(shard, s.core, t, b)
        return pltpu.make_async_remote_copy(
            src_ref=self.source(t, b) if own else dst, dst_ref=dst, send_sem=self.core_send.at[shard, b, t],
            recv_sem=self.core_recv.at[shard, b, t], device_id=s.at(s.dp, 1 - s.core), device_id_type=MESH)

    def give(self, kind, shard, t, own=False):
        s = self.spot
        to, taken = share_rows(self.share, kind)
        src = pl.ds(self.share[0][0] + taken.start, taken.size)
        return pltpu.make_async_remote_copy(
            src_ref=self.y_ref.at[t, src] if own else self.st_ref.at[t, src, self.lanes(shard, s.core)],
            dst_ref=self.st_ref.at[t, to, self.lanes(shard, s.core)], send_sem=self.give_send.at[kind, shard, t],
            recv_sem=self.give_recv.at[kind, shard, t], device_id=s.at(s.others[kind], s.core), device_id_type=MESH)

    def given_place(self, kind, shard, t, k):
        return self.st_ref.at[t, share_rows(self.share, kind)[0], self.lanes(shard, k)]

    def given(self, kind, shard, t):
        s = self.spot
        ref = self.given_place(kind, shard, t, s.core)
        return pltpu.make_async_remote_copy(
            src_ref=ref, dst_ref=ref, send_sem=self.given_send.at[kind, shard, t], recv_sem=self.given_recv.at[kind, shard, t],
            device_id=s.at(s.dp, 1 - s.core), device_id_type=MESH)

    def own(self, t, b):
        return pltpu.make_async_copy(self.source(t, b), self.place(self.spot.chip, self.spot.core, t, b), self.own_sem.at[b, t])

    def start(self):
        for b in (0, 1):
            def tower(t):
                def each(way):
                    @pl.when(self.spot.leaves(0, way))
                    def _():
                        self.leave(0, way, t, b, True).start()
                loop(2, each)
                self.to_core(self.spot.chip, t, b, True).start()
                if b == 0:
                    for kind in (2, 0, 1):
                        self.give(kind, self.spot.chip, t, True).start()
                self.own(t, b).start()
            loop(self.towers, tower)

    def event(self, n):
        step, t = n // (2 * self.towers), lax.rem(n, self.towers)
        for b in (0, 1):
            def each(way):
                @pl.when(self.spot.comes(step, way))
                def _():
                    shard = self.spot.onward(way, -1 - step)
                    wait_for(self.place(shard, self.spot.core, t, b), self.y_recv.at[way, step, b, t], self.y_send.at[way, step, b, t])

                    @pl.when((step + 1 < self.spot.steps) & self.spot.leaves(step + 1, way))
                    def _():
                        self.leave(jnp.minimum(step + 1, self.spot.steps - 1), way, t, b).start()
                    self.to_core(shard, t, b).start()
                    if b == 0:
                        for kind in (2, 0, 1):
                            self.give(kind, shard, t).start()

            @pl.when(lax.rem(n, 2 * self.towers) // self.towers == b)
            def _():
                loop(2, each)

    def receive(self):
        def one(n):
            shard, t = n // self.towers, lax.rem(n, self.towers)
            for kind in range(3):
                wait_for(self.given_place(kind, shard, t, self.spot.core), self.give_recv.at[kind, shard, t], self.give_send.at[kind, shard, t])
                self.given(kind, shard, t).start()
        loop(self.spot.chips * self.towers, one)

    def settle(self):
        def one(n):
            shard, t = n // self.towers, lax.rem(n, self.towers)
            for b in (0, 1):
                wait_for(self.place(shard, 1 - self.spot.core, t, b), self.core_recv.at[shard, b, t], self.core_send.at[shard, b, t])
                self.to_core(shard, t, b).wait_send()

                @pl.when(shard < self.spot.steps)
                def _():
                    def each(way):
                        @pl.when(self.spot.leaves(shard, way))
                        def _():
                            self.leave(jnp.minimum(shard, self.spot.steps - 1), way, t, b).wait_send()
                    loop(2, each)
            for kind in range(3):
                self.give(kind, shard, t).wait_send()
                self.given(kind, shard, t).wait_send()
                wait_for(self.given_place(kind, shard, t, 1 - self.spot.core), self.given_recv.at[kind, shard, t], self.given_send.at[kind, shard, t])
        loop(self.spot.chips * self.towers, one)
        for t in range(self.towers):
            for b in (0, 1):
                self.own(t, b).wait()


def first_kernel(chips, parts, share, f_ref, w_ref, o_ref, n_ref, sp_ref, left_ref, right_ref,
                 fg_ref, wg_ref, low_ref, next_ref, og_ref, dz_ref, act_ref, sg_ref, tot_ref, bases_ref,
                 offer_f, taken, offer_o, og, wide, low, low_next, f_tile, w_tile, acc, theirs, live, act, dz_here, sums_here, tot, base_in, base_out,
                 f_send, f_recv, w_send, w_recv, wide_sem, p_sem, a_send, a_recv, z_send, z_recv, out_sem, x_send, x_recv, l_sem, base_load, base_store):
    spot = Spot(chips)
    keep, rows = share[0][0], sum(share[0])
    size = rows // parts
    fixed = rows - size
    spare = keep - fixed
    cols = o_ref.shape[2]
    spot.greet()

    def offer(kind, what):
        src = (f_ref.at[0], f_ref.at[1], o_ref, n_ref)[what]
        dst = (offer_f.at[0, 1 + kind], offer_f.at[1, 1 + kind], offer_o.at[1 + kind], tot.at[1 + kind])[what]
        if what < 3:
            src = src.at[pl.ds(*share[1 + kind])] if what < 2 else src.at[:, pl.ds(*share[1 + kind])]
        return pltpu.make_async_remote_copy(
            src_ref=src, dst_ref=dst, send_sem=x_send.at[what, kind], recv_sem=x_recv.at[what, kind],
            device_id=spot.at(spot.others[kind], spot.core), device_id_type=MESH)

    def choose(width, read, write):
        weigh = [jnp.broadcast_to(jnp.where(tot[kind, :1, :width] > keep, 1.0, 0.0), (16, width)) for kind in range(4)]

        def strip(i):
            at = pl.ds(pl.multiple_of(i * 16, 16), 16)
            value = read(0, at).astype(jnp.float32) * weigh[0]
            for kind in range(1, 4):
                value = value + read(kind, at).astype(jnp.float32) * weigh[kind]
            write(i * 16, value.astype(jnp.bfloat16))
        loop(share[0][1] // 16, strip)

    features = Features(spot, f_ref.at[0], taken.at[0], fg_ref, size, f_send, f_recv)
    weights = Weights(spot, low, wg_ref, p_sem.at[4], w_send, w_recv)
    products = Products(spot, features, wg_ref, f_tile, w_tile, acc, theirs, p_sem.at[pl.ds(0, 2)], p_sem.at[pl.ds(2, 2)], a_send, a_recv)
    backward = Backward(spot, size, dz_here, dz_ref, z_send, z_recv, out_sem)

    for what in (3, 0):
        for kind in (2, 0, 1):
            offer(kind, what).start()
    loop(parts - 1, lambda q: features.launch(q, False))
    local = [(n_ref, tot.at[0])]
    for t in (0, 1):
        local += [(f_ref.at[t, pl.ds(*share[0])], offer_f.at[t, 0])]
        if spare:
            local += [(f_ref.at[t, pl.ds(fixed, spare)], taken.at[t, pl.ds(0, spare)])]
    need = len(local) // 2 + 1
    local += [(o_ref.at[:, pl.ds(*share[0])], offer_o.at[0]), (o_ref.at[:, pl.ds(0, keep)], og.at[:, pl.ds(0, keep)]),
              (f_ref.at[0, pl.ds(0, fixed)], fg_ref.at[pl.ds(0, fixed), features.lanes(spot.chip)])]
    local = [pltpu.make_async_copy(src, dst, l_sem.at[n]) for n, (src, dst) in enumerate(local)]
    for copy in local:
        copy.start()
    weights.round(w_ref.at[0], wide, wide_sem)
    weights.start()
    for copy in local[:need]:
        copy.wait()
    for what in (3, 0):
        for kind in range(3):
            offer(kind, what).wait_recv()

    def take(t):
        def write(row, value):
            taken[t, pl.ds(pl.multiple_of(spare + row, 16), 16)] = value
        choose(offer_f.shape[3], lambda kind, at: offer_f[t, kind, at], write)
    take(0)
    features.launch(parts - 1, True)
    more = [pltpu.make_async_copy(tot, tot_ref, l_sem.at[8]),
            pltpu.make_async_copy(taken.at[0], fg_ref.at[pl.ds(fixed, size), features.lanes(spot.chip)], l_sem.at[9])]
    for copy in more:
        copy.start()
    live_rows_of(tot, share, live)
    clear(acc)
    Weights(spot, low_next, wg_ref, p_sem.at[4], w_send, w_recv).round(w_ref.at[1], wide, wide_sem)
    more.append(pltpu.make_async_copy(low_next, low_ref, l_sem.at[10]))
    more[2].start()

    bases = Bases(left_ref, right_ref, bases_ref, base_in, base_out, base_load, base_store)
    share_of = -(-bases.units // (2 * parts))

    def serve(step, q):
        features.serve(step, q)
        bases.some((step * parts + q) * share_of, share_of)
    bases.load(jnp.int32(0), True)
    loop(parts, lambda q: serve(0, q))
    weights.relay()
    for what in (2, 1):
        for kind in (2, 0, 1):
            offer(kind, what).start()
    loop(parts, lambda q: serve(1, q))
    weights.finish()
    for copy in local[need:] + more:
        copy.wait()
    products.multiply()
    for kind in range(3):
        offer(kind, 2).wait_recv()
    for t in range(2):
        def write(row, value):
            og[t, pl.ds(pl.multiple_of(keep + row, 16), 16)] = value
        choose(cols, lambda kind, at: offer_o[kind, t, at], write)
    keeps = [pltpu.make_async_copy(og, og_ref, l_sem.at[0])]
    keeps[0].start()

    sums_here[...] = jnp.zeros_like(sums_here)

    def strip(at):
        activated, slope = gelu_and_slope(acc[at, :cols] + theirs[at] + sp_ref[0:1])
        mask = live[at]
        dy = [og[t, at].astype(jnp.float32) * mask for t in range(2)]
        dz = slope * (sp_ref[2:3] * dy[0] + sp_ref[4:5] * dy[1])
        act[at] = activated
        dz_here[at] = dz.astype(jnp.bfloat16)
        for n, term in enumerate((dz, activated * dy[0], activated * dy[1])):
            sums_here[n] += fold(term)

    def stage(k):
        @pl.when(k < parts)
        def _():
            products.complete(k)

        @pl.when(k > 0)
        def _():
            products.swap(k - 1).wait_recv()
            loop(size // 16, lambda i: strip(pl.ds(pl.multiple_of((k - 1) * size + i * 16, 16), 16)))
            backward.start(k - 1)
    loop(parts + 1, stage)
    for kind in range(3):
        offer(kind, 1).wait_recv()
    take(1)
    keeps += [pltpu.make_async_copy(act, act_ref, l_sem.at[1]), pltpu.make_async_copy(taken.at[1], next_ref, l_sem.at[2])]
    for copy in keeps[1:]:
        copy.start()
    sg_ref[...] = jnp.zeros_like(sg_ref)
    for n in range(3):
        sg_ref[2 * n : 2 * n + 1] = jnp.sum(sums_here[n], axis=0, keepdims=True)

    def settle(q):
        backward.settle(q)
        products.swap(q).wait_send()
        features.settle(q)
    loop(parts, settle)
    weights.settle()
    bases.settle()
    for copy in keeps:
        copy.wait()
    for what in range(4):
        for kind in range(3):
            offer(kind, what).wait_send()


def second_kernel(chips, parts, share, f_ref, low_ref, next_ref, og_ref, tot, act_ref, sp_ref, fg_first, wg_first, dz_first,
                  fg_ref, wg_ref, dz_ref, y_ref, sg_ref, d_ref, gr_ref, pg_ref, relay_ref,
                  og, f_tile, w_tile, acc, theirs, live, act, dz_here, y_here, sums_here,
                  held, w_here, dz_wide, total, f_part, g_part, r_part,
                  f_send, f_recv, w_send, w_recv, p_sem, a_send, a_recv, z_send, z_recv, out_sem, l_sem,
                  d_send, d_recv, o_sem, b_send, b_recv, g_load, g_send, g_recv, rs_send, rs_recv, own_sem):
    spot = Spot(chips)
    rows = sum(share[0])
    size = rows // parts
    fixed = rows - size
    cols = og_ref.shape[2]
    spot.greet()
    features = Features(spot, f_ref.at[1], next_ref, fg_ref, size, f_send, f_recv)
    weights = Weights(spot, low_ref, wg_ref, p_sem.at[4], w_send, w_recv)
    products = Products(spot, features, wg_ref, f_tile, w_tile, acc, theirs, p_sem.at[pl.ds(0, 2)], p_sem.at[pl.ds(2, 2)], a_send, a_recv)
    backward = Backward(spot, size, dz_here, dz_ref, z_send, z_recv, out_sem)
    gradients = Sums(spot, parts, share, d_ref, dz_wide, w_here, held, total, d_send, d_recv, o_sem, b_send, b_recv)
    grads = Grads(spot, fg_first, dz_wide, gr_ref, pg_ref, relay_ref, f_part, g_part, r_part, g_load.at[0], g_load.at[1], g_load.at[2],
                  g_send, g_recv, rs_send, rs_recv, own_sem)

    loop(parts - 1, lambda q: features.launch(q, False))
    features.launch(parts - 1, True)
    weights.start()
    loads = first_loads(chips, wg_first, dz_first, w_here, dz_wide, l_sem)
    grads.load(jnp.int32(0)).start()
    local = [(og_ref, og), (act_ref, act), (f_ref.at[1, pl.ds(0, fixed)], fg_ref.at[pl.ds(0, fixed), features.lanes(spot.chip)]),
             (next_ref, fg_ref.at[pl.ds(fixed, size), features.lanes(spot.chip)])]
    local = [pltpu.make_async_copy(src, dst, l_sem.at[chips + 1 + n]) for n, (src, dst) in enumerate(local)]
    for copy in local:
        copy.start()
    for copy in loads:
        copy.wait()

    def turn(m):
        gradients.turn(m)
        grads.turn(m, 2, 10)

        @pl.when(m == 4)
        def _():
            weights.relay()

        @pl.when((m >= 2) & (m < 2 + parts))
        def _():
            features.serve(0, m - 2)

        @pl.when((m >= 4 + parts) & (m < 4 + 2 * parts))
        def _():
            features.serve(1, m - 4 - parts)

        @pl.when(m == 0)
        def _():
            live_rows_of(tot, share, live)
            clear(acc)

        @pl.when(m == 4 + 2 * parts)
        def _():
            weights.finish()
            for copy in local:
                copy.wait()
            products.multiply()
        gradients.turn_end(m)
    loop(gradients.turns + gradients.lag, turn)

    sums_here[...] = jnp.zeros_like(sums_here)

    def strip(at):
        activated, slope = gelu_and_slope(acc[at, :cols] + theirs[at] + sp_ref[1:2])
        mask = live[at]
        other = act[at]
        dy = [og[t, at].astype(jnp.float32) * mask for t in range(2)]
        dz = slope * (sp_ref[3:4] * dy[0] + sp_ref[5:6] * dy[1])
        for t in range(2):
            y_here[t, at] = ((sp_ref[2 + 2 * t : 3 + 2 * t] * other + sp_ref[3 + 2 * t : 4 + 2 * t] * activated) * mask).astype(jnp.bfloat16)
        dz_here[at] = dz.astype(jnp.bfloat16)
        for n, term in enumerate((dz, activated * dy[0], activated * dy[1])):
            sums_here[n] += fold(term)

    def stage(k):
        @pl.when(k < parts)
        def _():
            products.complete(k)

        @pl.when(k > 0)
        def _():
            products.swap(k - 1).wait_recv()
            loop(size // 16, lambda i: strip(pl.ds(pl.multiple_of((k - 1) * size + i * 16, 16), 16)))
            backward.start(k - 1)
    loop(parts + 1, stage)
    keep_y = pltpu.make_async_copy(y_here, y_ref, l_sem.at[0])
    keep_y.start()
    sg_ref[...] = jnp.zeros_like(sg_ref)
    for n in range(3):
        sg_ref[2 * n + 1 : 2 * n + 2] = jnp.sum(sums_here[n], axis=0, keepdims=True)

    def settle(q):
        backward.settle(q)
        products.swap(q).wait_send()
        features.settle(q)
    loop(parts, settle)
    weights.settle()
    gradients.settle()
    grads.settle()
    keep_y.wait()


def first_loads(chips, wg, dz, w_here, dz_wide, sem):
    depth = w_here.shape[1]
    loads = [pltpu.make_async_copy(dz, dz_wide, sem.at[chips])]
    loads += [pltpu.make_async_copy(wg.at[pl.ds(n * depth, depth)], w_here.at[n], sem.at[n]) for n in range(chips)]
    for copy in loads:
        copy.start()
    return loads


def third_kernel(chips, parts, share, y_ref, fg_ref, wg_ref, dz_ref, ps_ref, st_ref, d_ref, gr_ref, sr_ref, pg_ref, relay_ref,
                 held, w_here, dz_wide, total, f_part, g_part, r_part, l_sem,
                 d_send, d_recv, o_sem, b_send, b_recv, g_load, g_send, g_recv, rs_send, rs_recv, own_sem, s_send, s_recv,
                 y_send, y_recv, core_send, core_recv, give_send, give_recv, given_send, given_recv, y_own):
    spot = Spot(chips)
    spot.greet()
    gradients = Sums(spot, parts, share, d_ref, dz_wide, w_here, held, total, d_send, d_recv, o_sem, b_send, b_recv)
    grads = Grads(spot, fg_ref, dz_wide, gr_ref, pg_ref, relay_ref, f_part, g_part, r_part, g_load.at[0], g_load.at[1], g_load.at[2],
                  g_send, g_recv, rs_send, rs_recv, own_sem)
    stitched = Stitched(spot, share, y_ref, st_ref, y_send, y_recv, core_send, core_recv, give_send, give_recv, given_send, given_recv, y_own)

    def small(kind):
        return pltpu.make_async_remote_copy(
            src_ref=ps_ref, dst_ref=sr_ref.at[spot.dp], send_sem=s_send.at[kind], recv_sem=s_recv.at[kind],
            device_id=spot.at(spot.others[kind], spot.core), device_id_type=MESH)

    loads = first_loads(chips, wg_ref, dz_ref, w_here, dz_wide, l_sem)
    grads.load(jnp.int32(0)).start()
    stitched.start()
    own = pltpu.make_async_copy(ps_ref, sr_ref.at[spot.dp], l_sem.at[chips + 1])
    own.start()
    for kind in range(3):
        small(kind).start()
    for copy in loads:
        copy.wait()

    def turn(m):
        gradients.turn(m)
        grads.turn(m, 0, 8)

        @pl.when((m >= 1) & (m <= stitched.events))
        def _():
            stitched.event(m - 1)
        gradients.turn_end(m)
    loop(gradients.turns + gradients.lag, turn)
    stitched.receive()
    gradients.settle()
    stitched.settle()
    grads.settle()
    for kind in range(3):
        small(kind).wait()
    own.wait()


def call(kernel, name, ident, out, scratch, operands, small_in=(), small_out=(), flops=0):
    anywhere, here = pl.BlockSpec(memory_space=pl.ANY), pl.BlockSpec(memory_space=pltpu.VMEM)
    return pl.pallas_call(
        kernel,
        out_shape=out,
        in_specs=[here if n in small_in else anywhere for n in range(len(operands))],
        out_specs=[here if n in small_out else anywhere for n in range(len(out))],
        scratch_shapes=scratch,
        compiler_params=pltpu.CompilerParams(collective_id=ident, has_side_effects=True, vmem_limit_bytes=58 * 2**20),
        cost_estimate=pl.CostEstimate(flops=flops, bytes_accessed=500 * 2**20, transcendentals=0),
        name=name,
    )(*operands)


def parts_of(share):
    rows = sum(share[0])
    return max(n for n in range(1, rows // 16) if rows % (16 * n) == 0 and rows // n >= share[0][1])


def shared_pass(features, weights, out_grad, count, small_params, left, right, chips, share):
    parts = parts_of(share)
    towers, slots, depth = features.shape
    cols = weights.shape[2]
    keep, size = share[0]
    rows = keep + size
    steps = chips - 1
    piece = rows // parts
    dma, vmem = pltpu.SemaphoreType.DMA, pltpu.VMEM
    bf16, f32 = jnp.bfloat16, jnp.float32
    S = jax.ShapeDtypeStruct
    told = jnp.broadcast_to(count.astype(f32), (8, depth))
    flops = 2 * rows * 2 * cols * depth * chips
    gathers = [dma((2, steps, parts))] * 2 + [dma((4, 2))] * 2
    line = [dma((5,))] + [dma((parts,))] * 5
    tiles = [vmem((2, rows, depth), bf16), vmem((2, depth, 2 * cols), bf16),
             vmem((rows, 2 * cols), f32), vmem((rows, cols), f32), vmem((rows, cols), f32), vmem((rows, cols), f32), vmem((rows, cols), bf16)]
    folded = vmem((3, 8, cols), f32)
    wide = [S((rows, chips * depth), bf16), S((chips * depth, 2 * cols), bf16)]
    *first, low, start, grad_here, dz, act, small_first, told, bases = call(
        functools.partial(first_kernel, chips, parts, share), "first", 3,
        wide + [S((2, depth, cols), bf16), S((piece, depth), bf16), S((towers, rows, cols), bf16), S((rows, 2 * cols), bf16), S((rows, cols), f32), S((8, cols), f32),
                S((4, 8, depth), f32), S((2,) + left.shape[:2] + (2, left.shape[2] // 2 * BLOCK, 2 * BLOCK), bf16)],
        [vmem((towers, 4, size, depth), bf16), vmem((towers, piece, depth), bf16), vmem((4, towers, size, cols), bf16), vmem((towers, rows, cols), bf16), vmem((2, depth // 4, cols), f32)]
        + [vmem((2, depth, cols), bf16)] * 2 + tiles + [folded, vmem((4, 8, depth), f32), vmem((2, 2) + left.shape[2:], f32), vmem((2, 2, 2, left.shape[2] // 2 * BLOCK, 2 * BLOCK), bf16)] + gathers + [dma((2,))] + line
        + [dma((4, 3)), dma((4, 3)), dma((11,)), dma((2, 2)), dma((2, 2))],
        (features, weights, out_grad, told, small_params, left, right), (4,), (7,), flops)
    *second, dz_second, result, small_second, d_first, gr_first, _, _ = call(
        functools.partial(second_kernel, chips, parts, share), "second", 5,
        wide + [S((rows, 2 * cols), bf16), S((towers, rows, cols), bf16), S((8, cols), f32)] + sums_out(slots, depth, cols),
        [vmem((towers, rows, cols), bf16)] + tiles + [vmem((towers, rows, cols), bf16), folded] + sums_scratch(chips, rows, parts, depth, cols)
        + gathers + line + [dma((chips + 5,))] + sums_dma(steps, parts),
        (features, low, start, grad_here, told, act, small_params, *first, dz), (4, 6), (4,), 3 * flops)
    return told, bases, (result, *second, dz_second, small_first + small_second), d_first, gr_first


def sums_out(slots, depth, cols):
    S, bf16 = jax.ShapeDtypeStruct, jnp.bfloat16
    return [S((slots, depth), bf16), S((3, 2, depth, cols), bf16), S((8, depth, cols), bf16), S((2, depth, cols), bf16)]


def sums_scratch(chips, rows, parts, depth, cols):
    vmem, bf16 = pltpu.VMEM, jnp.bfloat16
    return [vmem((2, chips - 1, rows, depth), bf16), vmem((chips, depth, 2 * cols), bf16), vmem((rows, 2 * cols), bf16),
            vmem((2, rows // parts, depth), bf16), vmem((2, rows, depth // 3), bf16)] + [vmem((2, depth // 3, cols), bf16)] * 2


def sums_dma(steps, parts):
    dma = pltpu.SemaphoreType.DMA
    return [dma((2, steps * parts))] * 2 + [dma((2,)), dma((3,)), dma((3,)), dma((3, 2)), dma((8,)), dma((3, 2)), dma((2,)), dma((2,)), dma(())]


def shared_sums(result, wide_f, wide_w, wide_dz, partial_s, slots, chips, share):
    parts = parts_of(share)
    towers, rows, cols = result.shape
    depth, steps = wide_w.shape[0] // chips, chips - 1
    dma = pltpu.SemaphoreType.DMA
    S = jax.ShapeDtypeStruct
    stitched, d_feat, grad_parts, smalls, _, _ = call(
        functools.partial(third_kernel, chips, parts, share), "third", 4,
        [S((towers, slots, 2 * chips * cols), jnp.bfloat16)] + sums_out(slots, depth, cols)[:2] + [S((4,) + partial_s.shape, jnp.float32)]
        + sums_out(slots, depth, cols)[2:],
        sums_scratch(chips, rows, parts, depth, cols) + [dma((chips + 2,))] + sums_dma(steps, parts) + [dma((3,))] * 2
        + [dma((2, steps, 2, towers))] * 2 + [dma((chips, 2, towers))] * 2 + [dma((3, chips, towers))] * 4 + [dma((2, towers))],
        (result, wide_f, wide_w, wide_dz, partial_s), flops=4 * rows * 2 * cols * depth * chips)
    return stitched, d_feat, grad_parts, smalls


def small_step(small_params, small_moment_one, small_moment_two, small_average, small_grad):
    first, second, direction = adam_part(small_moment_one, small_moment_two, small_grad)
    fresh = small_params - rate_small * direction
    return first, second, fresh, ema_decay * small_average + (1.0 - ema_decay) * fresh


def update(d_feat, stitched, full, parts, small_parts, states, small_states):
    small_grad = jnp.sum(small_parts, 0)[: small_states[0].shape[0]]
    *fresh, stitched, d_feat = soap(parts, full, stitched, d_feat, *states)
    return (stitched, d_feat) + tuple(fresh) + small_step(*small_states, small_grad)


def own_rows(features, out_grad, totals, passed, first, states, small_states):
    _, rows, _ = features.shape
    weights, small_params = states[0], small_states[0]
    cols = weights.shape[2]
    cores = lax.axis_size("mp")
    swap = [(i, i ^ 1) for i in range(cores)]
    ranges = ((0, rows // 2), (rows // 2, rows // 2))
    live_rows = (jnp.arange(rows, dtype=jnp.float32) < totals[0]).astype(jnp.float32)
    wide_f, wide_w = gather(features, weights.astype(jnp.bfloat16), cores // 2, ranges, 1)
    partial = jnp.einsum("tri,tio->tro", wide_f, wide_w, preferred_element_type=jnp.float32)
    product = partial[:, :, :cols] + lax.ppermute(partial[:, :, cols:], "mp", swap)
    result, back = jax.vjp(lambda a, b: stitch_local(a, b, live_rows), product, small_params)
    stitched = lax.all_gather(result.astype(jnp.bfloat16), "mp", axis=2, tiled=True)
    dz, small_part = back(out_grad.astype(jnp.float32))
    dz_low = dz.astype(jnp.bfloat16)
    wide_dz = jnp.concatenate([dz_low, lax.ppermute(dz_low, "mp", swap)], axis=2)
    partial_d = jnp.einsum("tro,tio->tri", wide_dz, wide_w, preferred_element_type=jnp.float32)
    partial_g = jnp.einsum("tri,tro->tio", wide_f, wide_dz, preferred_element_type=jnp.float32)
    small_part = jnp.pad(small_part, ((0, 2), (0, 0)))
    d_feat, parts, small_parts = reduce(
        partial_d.astype(jnp.bfloat16), partial_g.astype(jnp.bfloat16), small_part, cores // 2, ranges, 2
    )
    full = jnp.full((1,), rows, jnp.int32)
    return update((d_feat[0], d_feat[1]), stitched, full, (parts[:, :, 0], parts[:, :, 1]), small_parts, states, small_states)


def shares(rows):
    keep = rows * 15 // 32 // 16 * 16
    size = -(-(rows - keep) // 64) * 16
    return keep, ((keep, size), (keep + size, size), (keep + 2 * size, size), (rows - size, size))


def shared_rows(features, out_grad, totals, passed, first, states, small_states):
    rows = features.shape[1]
    keep, share = shares(rows)
    d_first, gr_first = first
    full = jnp.where(totals[:1] > keep, rows, keep)
    stitched, d_second, gr_second, small_parts = shared_sums(*passed, rows, lax.axis_size("mp") // 2, share)
    return update((d_first, d_second), stitched, full, (gr_first, gr_second), small_parts, states, small_states)


def line_body(
    features,
    counts,
    weights,
    small_params,
    out_grad,
    moment_one,
    moment_two,
    average,
    basis_left,
    basis_right,
    small_moment_one,
    small_moment_two,
    small_average,
):
    keep, share = shares(features.shape[1])
    told, bases, passed, *first = shared_pass(
        features, weights, out_grad, jnp.sum(counts), small_params, basis_left, basis_right, lax.axis_size("mp") // 2, share
    )
    totals = told[:, 0, 0]
    return lax.cond(
        jnp.sum(totals > keep) == 1,
        shared_rows,
        own_rows,
        features,
        out_grad,
        totals,
        passed,
        first,
        (weights, moment_one, moment_two, average, bases),
        (small_params, small_moment_one, small_moment_two, small_average),
    )


def plain_body(
    features,
    counts,
    weights,
    small_params,
    out_grad,
    moment_one,
    moment_two,
    average,
    basis_left,
    basis_right,
    small_moment_one,
    small_moment_two,
    small_average,
):
    slot_count = features.shape[1]
    total = jnp.sum(counts)
    live_rows = (jnp.arange(slot_count, dtype=jnp.int32) < total).astype(jnp.float32)
    weights_low = lax.all_gather(weights.astype(jnp.bfloat16), "dp", axis=1, tiled=True)
    feats_full = lax.all_gather(features, "mp", axis=2, tiled=True)
    product = jnp.einsum(
        "tri,tio->tro", feats_full, weights_low, preferred_element_type=jnp.float32
    )
    result, back = jax.vjp(lambda a, b: stitch_local(a, b, live_rows), product, small_params)
    stitched = lax.all_gather(result.astype(jnp.bfloat16), "mp", axis=2, tiled=True)
    dz, small_part = back(out_grad.astype(jnp.float32))
    dz_low = dz.astype(jnp.bfloat16)
    grad_part = jnp.einsum("tri,tro->tio", feats_full, dz_low, preferred_element_type=jnp.float32)
    partial_sums = jnp.einsum(
        "tro,tio->tri", dz_low, weights_low, preferred_element_type=jnp.float32
    )
    d_feat = lax.psum_scatter(
        partial_sums.astype(jnp.float32), "mp", scatter_dimension=2, tiled=True
    )
    grad = lax.psum_scatter(grad_part, "dp", scatter_dimension=1, tiled=True)
    small_grad = lax.psum(small_part, "dp")
    towers, n_in, n_out = grad.shape
    blocks = grad.reshape(towers, n_in // BLOCK, BLOCK, n_out // BLOCK, BLOCK)
    rotated = jnp.einsum(
        "trcai,tracb,trcbj->tricj", basis_left, blocks, basis_right, precision=lax.Precision.HIGHEST
    ).reshape(towers, n_in, n_out)
    first, second, direction = adam_part(moment_one, moment_two, rotated)
    turned = direction.reshape(towers, n_in // BLOCK, BLOCK, n_out // BLOCK, BLOCK)
    step_back = jnp.einsum(
        "trcai,tricj,trcbj->tracb", basis_left, turned, basis_right, precision=lax.Precision.HIGHEST
    ).reshape(towers, n_in, n_out)
    new_weights = weights - rate_main * (step_back + decay_weight * weights)
    new_average = ema_decay * average + (1.0 - ema_decay) * new_weights
    return (
        stitched,
        d_feat.astype(jnp.bfloat16),
        first,
        second,
        new_weights,
        new_average,
        new_weights.astype(jnp.bfloat16),
    ) + small_step(small_params, small_moment_one, small_moment_two, small_average, small_grad)


def solution(mesh):
    def body(features, counts, weights, *rest):
        dp, mp = mesh.shape["dp"], mesh.shape["mp"]
        tiles = features.shape[2] % 128 == 0 and weights.shape[2] % 128 == 0
        suits = dp == 4 and mp == 2 * dp and tiles and features.shape[1] % 64 == 0
        return (line_body if suits else plain_body)(features, counts, weights, *rest)

    return jax.shard_map(
        body,
        mesh=mesh,
        in_specs=(
            P(None, "dp", "mp"),
            P("dp"),
            P(None, "dp", "mp"),
            P(None, "mp"),
            P(None, "dp", "mp"),
            P(None, "dp", "mp"),
            P(None, "dp", "mp"),
            P(None, "dp", "mp"),
            P(None, "dp", "mp", None, None),
            P(None, "dp", "mp", None, None),
            P(None, "mp"),
            P(None, "mp"),
            P(None, "mp"),
        ),
        out_specs=(
            P(None, "dp", None),
            P(None, "dp", "mp"),
            P(None, "dp", "mp"),
            P(None, "dp", "mp"),
            P(None, "dp", "mp"),
            P(None, "dp", "mp"),
            P(None, "dp", "mp"),
            P(None, "mp"),
            P(None, "mp"),
            P(None, "mp"),
            P(None, "mp"),
        ),
        check_vma=False,
    )
```

```python
import functools
import math

import jax
import jax.numpy as jnp
from jax import lax
from jax.experimental import pallas as pl
from jax.experimental.pallas import tpu as pltpu
from jax.sharding import PartitionSpec as P

BLOCK = 64
STEP = 5


beta_one = 0.5
beta_two = 0.5
ema_decay = 0.5
rate_main = 0.01
rate_small = 0.05
decay_weight = 0.01
eps = 1e-08


def stitch_local(product, small, live_rows):
    pre_act = product + small[0:2][:, None, :]
    activated = jax.nn.gelu(pre_act, approximate=True)
    first = small[2] * activated[0] + small[3] * activated[1]
    second = small[4] * activated[0] + small[5] * activated[1]
    return jnp.stack([first, second]) * live_rows[None, :, None]


def adam_part(moment_a, moment_b, grad):
    first = beta_one * moment_a + (1.0 - beta_one) * grad
    second = beta_two * moment_b + (1.0 - beta_two) * grad * grad
    direction = first / (1.0 - beta_one**STEP) / (jnp.sqrt(second / (1.0 - beta_two**STEP)) + eps)
    return (first, second, direction)

def split(v):
    high = v.astype(jnp.bfloat16)
    return high, (v - high.astype(jnp.float32)).astype(jnp.bfloat16)

def soap_blocks(grads, lefts, rights, moments):
    row = lax.broadcasted_iota(jnp.int32, (2 * BLOCK, 2 * BLOCK), 0) // BLOCK
    lane = lax.broadcasted_iota(jnp.int32, (2 * BLOCK, 2 * BLOCK), 1) // BLOCK
    own = row == lane

    def diagonal(v):
        return jnp.where(own, jnp.concatenate([v, v], axis=0), jnp.zeros((), v.dtype))

    def stationary(high, low, axis):
        return jnp.concatenate([high, high, low], axis=axis)

    def moving(v, axis):
        high, low = split(v)
        return jnp.concatenate([high, low, high], axis=axis)

    def dots(a, b, ca, cb):
        dims = (((ca,), (cb,)), ((), ()))
        return [lax.dot_general(x, y, dims, preferred_element_type=jnp.float32) for x, y in zip(a, b)]

    right = [(diagonal(high), diagonal(low)) for high, low in rights]
    values = dots([moving(v, 1) for v in grads], [stationary(*v, 0) for v in right], 1, 0)
    values = dots([stationary(*v, 0) for v in lefts], [moving(v, 0) for v in values], 0, 0)
    values = [jnp.where(lane[:BLOCK] == 0, v[:BLOCK], v[BLOCK:]) for v in values]
    states = [adam_part(a, b, v) for (a, b), v in zip(moments, values)]
    values = dots([moving(v[2], 1) for v in states], [stationary(*v, 1) for v in right], 1, 1)
    values = dots([stationary(*v, 1) for v in lefts], [moving(diagonal(v), 0) for v in values], 1, 0)
    return [(first, second, step) for (first, second, _), step in zip(states, values)]


def soap_body(together, strips, full, parts_a, parts_b, stitched, d_a, d_b, weights, moment_a, moment_b, average, left, right,
              first, second, new_weights, new_average, copy, stitched_out, d_feat_out):
    groups, pairs = left.shape[2], left.shape[4] // BLOCK
    length = stitched.shape[1]
    row = jnp.minimum(pl.program_id(1) * pl.num_programs(2) + pl.program_id(2), strips - 1) * length

    first_tower = pl.program_id(0) == 0

    def clear(i, _):
        rows = pl.ds(pl.multiple_of(i * 16, 16), 16)
        wanted = row + i * 16 < full[0]
        stitched_out[0, rows] = jnp.where(wanted, stitched[0, rows], 0)
        d_feat_out[0, rows] = jnp.where(wanted, jnp.where(first_tower, d_a[rows], d_b[rows]), 0)
        return 0

    lax.fori_loop(0, length // 16, clear, 0)

    def blocks(g, _):
        places = [(g * together + s, q) for s in range(together) for q in range(pairs)]
        ats = [(0, pl.ds(pl.multiple_of(r * BLOCK, BLOCK), BLOCK), pl.ds(2 * BLOCK * q, 2 * BLOCK)) for r, q in places]
        grads = []
        for at in ats:
            grads.append(sum(jnp.where(first_tower, parts_a[(k,) + at], parts_b[(k,) + at]).astype(jnp.float32)
                             for k in range(parts_a.shape[0])))
        def basis(ref, r, q):
            return tuple(ref[0, 0, r, k, BLOCK * q : BLOCK * (q + 1)] for k in (0, 1))

        done = soap_blocks(grads, [basis(left, *place) for place in places], [basis(right, *place) for place in places],
                           [(moment_a[at], moment_b[at]) for at in ats])
        olds = [(weights[at], average[at]) for at in ats]
        for at, (one, two, step), (held, mean) in zip(ats, done, olds):
            first[at] = one
            second[at] = two
            fresh = held - rate_main * (step + decay_weight * held)
            new_weights[at] = fresh
            new_average[at] = ema_decay * mean + (1.0 - ema_decay) * fresh
            copy[at] = fresh.astype(jnp.bfloat16)
        return 0

    lax.fori_loop(0, groups // together, blocks, 0)


def soap(parts, wanted, stitched, d_feat, weights, moment_a, moment_b, average, bases, group=6):
    towers, rows, cols = weights.shape
    half = parts[0].shape[2]
    steps = half // (BLOCK * group)
    flat = lambda t, p, g: (t, p * steps + g, 0)
    state = pl.BlockSpec((1, BLOCK * group, cols), flat)
    base = [pl.BlockSpec((1, 1, group) + bases.shape[3:], lambda t, p, g, n=n: (n, t, p * steps + g, 0, 0, 0)) for n in (0, 1)]
    full = jax.ShapeDtypeStruct(weights.shape, jnp.float32)
    strips = max(n for n in range(1, 2 * steps + 1) if stitched.shape[1] % (16 * n) == 0)

    def strip(p, g):
        return jnp.minimum(p * steps + g, strips - 1)

    def through(shape):
        return pl.BlockSpec((1, shape[1] // strips, shape[2]), lambda t, p, g: (t, strip(p, g), 0))

    def of_tower(n, shape, index, last):
        return pl.BlockSpec(shape, lambda t, p, g: tuple(jnp.where(t == n, a, b) for a, b in zip(index(p, g), last if n == 0 else index(0, 0))))

    pieces = [of_tower(n, (v.shape[0], 1, BLOCK * group, cols), lambda p, g: (0, p, g, 0), (0, 1, steps - 1, 0)) for n, v in enumerate(parts)]
    rows_of = [of_tower(n, (v.shape[0] // strips, v.shape[1]), lambda p, g: (strip(p, g), 0), (strips - 1, 0)) for n, v in enumerate(d_feat)]

    return pl.pallas_call(
        functools.partial(soap_body, group, strips),
        grid=(towers, 2, steps),
        in_specs=[pl.BlockSpec(memory_space=pltpu.SMEM),
                  *pieces, through(stitched.shape), *rows_of, state, state, state, state, *base],
        out_specs=[state] * 5 + [through(stitched.shape), through((towers,) + d_feat[0].shape)],
        out_shape=[full] * 4 + [jax.ShapeDtypeStruct(weights.shape, jnp.bfloat16)]
        + [jax.ShapeDtypeStruct(v, jnp.bfloat16) for v in (stitched.shape, (towers,) + d_feat[0].shape)],
        compiler_params=pltpu.CompilerParams(vmem_limit_bytes=60 * 2**20),
        cost_estimate=pl.CostEstimate(flops=8 * 2 * towers * rows * cols * 64, bytes_accessed=130 * 2**20, transcendentals=0),
        name="soap",
    )(wanted, *parts, stitched, *d_feat, weights, moment_a, moment_b, average, bases, bases)


MESH = pl.DeviceIdType.MESH


def place():
    mp = lax.axis_index("mp")
    return lax.axis_index("dp"), mp // 2, lax.rem(mp, 2)


def meet(devices):
    barrier = pltpu.get_barrier_semaphore()
    expected = 0
    for here, device in devices:
        @pl.when(here)
        def _():
            pl.semaphore_signal(barrier, inc=1, device_id=device, device_id_type=MESH)
        expected = expected + jnp.where(here, 1, 0)
    pl.semaphore_wait(barrier, expected)


def gather_kernel(chips, ranges, f_ref, w_ref, fg_ref, wg_ref, f_send, f_recv, w_send, w_recv, own_sem):
    dp, chip, core = place()
    towers, rows, depth = f_ref.shape
    cols = w_ref.shape[2]
    across, along = dp ^ 1, dp ^ 2
    at = lambda c, k: (c, 2 * chip + k)

    meet([(chip > 0, (dp, 2 * (chip - 1) + core)), (chip < chips - 1, (dp, 2 * (chip + 1) + core)),
          (chip >= 0, at(dp, 1 - core))] + [(chip >= 0, at(c, k)) for c in (across, along) for k in (0, 1)])

    def copies(step, way, t, k, shard, there):
        lanes = pl.ds(pl.multiple_of(shard * depth, 128), depth)
        rws = pl.ds(*ranges[k])
        src = fg_ref.at[t, rws, lanes]
        if step == 0:
            src = f_ref.at[t, rws]
        n = ((way * (chips - 1) + step) * towers + t) * len(ranges) + k
        return pltpu.make_async_remote_copy(
            src_ref=src, dst_ref=fg_ref.at[t, rws, lanes], send_sem=f_send.at[n], recv_sem=f_recv.at[n],
            device_id=(dp, 2 * there + core), device_id_type=MESH)

    def feature(step, way, t, k):
        return copies(step, way, t, k, chip - step if way == 0 else chip + step, chip + 1 if way == 0 else chip - 1)

    def incoming(step, way, t, k):
        return copies(step, way, t, k, chip - 1 - step if way == 0 else chip + 1 + step, chip)

    def sends(step, way):
        return (chip < chips - 1) & (chip >= step) if way == 0 else (chip > 0) & (chip + step < chips)

    def receives(step, way):
        return chip > step if way == 0 else chip + step < chips - 1

    def launch(t, k):
        for way in (0, 1):
            @pl.when(sends(0, way))
            def _():
                feature(0, way, t, k).start()

    def block(owner, slot, t):
        return wg_ref.at[t, pl.ds(pl.multiple_of(owner * depth, 128), depth), pl.ds(pl.multiple_of(slot * cols, 128), cols)]

    def weight(kind, k, t):
        to = at((across, along, dp)[kind], k)
        n = (kind * 2 + core) * 2 + t
        return pltpu.make_async_remote_copy(
            src_ref=w_ref.at[t, pl.ds(pl.multiple_of(k * depth, 128), depth)], dst_ref=block(dp, k ^ core, t),
            send_sem=w_send.at[(kind * 2 + k) * 2 + t], recv_sem=w_recv.at[n], device_id=to, device_id_type=MESH)

    def forward(kind, slot):
        owner, to, t = ((across, along, 0), (along, across, 1))[kind]
        n = 12 + kind * 2 + slot
        return pltpu.make_async_remote_copy(
            src_ref=block(owner, slot, t), dst_ref=block(owner, slot, t),
            send_sem=w_send.at[n], recv_sem=w_recv.at[n], device_id=at(to, core), device_id_type=MESH)

    def arrived(kind, slot, t):
        owner = (across, along, dp)[kind]
        n = (kind * 2 + (slot ^ core)) * 2 + t
        pltpu.make_async_remote_copy(
            src_ref=block(owner, slot, t), dst_ref=block(owner, slot, t), send_sem=w_send.at[n], recv_sem=w_recv.at[n],
            device_id=at(dp, core), device_id_type=MESH).wait_recv()

    mine = pl.ds(pl.multiple_of(chip * depth, 128), depth)
    own = [pltpu.make_async_copy(f_ref.at[t], fg_ref.at[t, :, mine], own_sem.at[t]) for t in range(towers)]
    own += [pltpu.make_async_copy(w_ref.at[t, pl.ds(pl.multiple_of(core * depth, 128), depth)], block(dp, 0, t), own_sem.at[2 + t])
            for t in range(towers)]

    pieces = [(t, k) for k in range(len(ranges)) for t in range(towers)]
    for t, k in pieces:
        launch(t, k)
    for copy in own:
        copy.start()
    for t in (0, 1):
        for k in (0, 1):
            weight(0, k, t).start()
            weight(1, k, 1 - t).start()
    for t in (0, 1):
        weight(2, 1 - core, t).start()

    for step in range(chips - 1):
        for t, k in pieces:
            for way in (0, 1):
                @pl.when(receives(step, way))
                def _():
                    incoming(step, way, t, k).wait_recv()
                if step + 1 < chips - 1:
                    @pl.when(sends(step + 1, way))
                    def _():
                        feature(step + 1, way, t, k).start()
            if step == 0 and (t, k) == pieces[-1]:
                for slot in (0, 1):
                    arrived(0, slot, 0)
                    forward(0, slot).start()
                    arrived(1, slot, 1)
                    forward(1, slot).start()

    for slot in (0, 1):
        arrived(0, slot, 1)
        arrived(1, slot, 0)
        forward(0, slot).wait_recv()
        forward(1, slot).wait_recv()
    for t in (0, 1):
        arrived(2, 1, t)
    for t in (0, 1):
        for k in (0, 1):
            weight(0, k, t).wait_send()
            weight(1, k, t).wait_send()
        weight(2, 1 - core, t).wait_send()
    for slot in (0, 1):
        forward(0, slot).wait_send()
        forward(1, slot).wait_send()
    for step in range(chips - 1):
        for t, k in pieces:
            for way in (0, 1):
                @pl.when(sends(step, way))
                def _():
                    feature(step, way, t, k).wait_send()
    for copy in own:
        copy.wait()


def gather(features, weights_low, chips, ranges, ident):
    towers, rows, depth = features.shape
    cols = weights_low.shape[2]
    count = 2 * (chips - 1) * towers * len(ranges)
    dma = pltpu.SemaphoreType.DMA
    anywhere = pl.BlockSpec(memory_space=pl.ANY)
    return pl.pallas_call(
        functools.partial(gather_kernel, chips, ranges),
        out_shape=[jax.ShapeDtypeStruct((towers, rows, chips * depth), jnp.bfloat16),
                   jax.ShapeDtypeStruct((towers, chips * depth, 2 * cols), jnp.bfloat16)],
        in_specs=[anywhere] * 2,
        out_specs=[anywhere] * 2,
        scratch_shapes=[dma((count,)), dma((count,)), dma((16,)), dma((16,)), dma((4,))],
        compiler_params=pltpu.CompilerParams(collective_id=ident, has_side_effects=True),
        cost_estimate=pl.CostEstimate(flops=0, bytes_accessed=800 * 2**20, transcendentals=0),
        name="gather",
    )(features, weights_low)


def reduce_kernel(chips, ranges, pd_ref, pg_ref, ps_ref, d_ref, gr_ref, sr_ref, held, term, total,
                  d_send, d_recv, t_sem, o_sem, g_send, g_recv, s_send, s_recv, own_sem):
    dp, chip, core = place()
    towers, rows, depth = d_ref.shape
    cols = pg_ref.shape[2] // 2
    across, along = dp ^ 1, dp ^ 2
    others = (across, along, dp ^ 3)
    at = lambda c, k: (c, 2 * chip + k)

    meet([(chip > 0, (dp, 2 * (chip - 1) + core)), (chip < chips - 1, (dp, 2 * (chip + 1) + core)),
          (chip >= 0, at(dp, 1 - core))] + [(chip >= 0, at(c, k)) for c in others for k in (0, 1)])

    def grad(kind, k, t):
        owner = (others + (dp,))[kind]
        return pltpu.make_async_remote_copy(
            src_ref=pg_ref.at[t, pl.ds(pl.multiple_of(owner * depth, 128), depth), pl.ds(pl.multiple_of((k ^ core) * cols, 128), cols)],
            dst_ref=gr_ref.at[dp, core, t], send_sem=g_send.at[(kind * 2 + k) * 2 + t],
            recv_sem=g_recv.at[(kind * 2 + core) * 2 + t], device_id=at(owner, k), device_id_type=MESH)

    def grad_arrived(kind, k, t):
        owner = (others + (dp,))[kind]
        pltpu.make_async_remote_copy(
            src_ref=gr_ref.at[owner, k, t], dst_ref=gr_ref.at[owner, k, t], send_sem=g_send.at[0],
            recv_sem=g_recv.at[(kind * 2 + k) * 2 + t], device_id=at(dp, core), device_id_type=MESH).wait_recv()

    def small(kind):
        return pltpu.make_async_remote_copy(
            src_ref=ps_ref, dst_ref=sr_ref.at[dp], send_sem=s_send.at[kind], recv_sem=s_recv.at[kind],
            device_id=at(others[kind], core), device_id_type=MESH)

    def target(step, way):
        return chip + chips - 1 - step if way == 0 else chip - (chips - 1 - step)

    def sends(step, way):
        return (chip < chips - 1) & (chip <= step) if way == 0 else (chip > 0) & (chips - 1 - chip <= step)

    def receives(step, way):
        return (chip > 0) & (chip <= step + 1) if way == 0 else (chip < chips - 1) & (chips - 1 - chip <= step + 1)

    def own_term(goal, t, k):
        return pd_ref.at[t, pl.ds(*ranges[k]), pl.ds(pl.multiple_of(goal * depth, 128), depth)]

    def partial(step, way, t, k, first):
        n = ((way * (chips - 1) + step) * towers + t) * len(ranges) + k
        src = own_term(target(step, way), t, k) if first else held.at[way, step - 1, t, pl.ds(*ranges[k])]
        there = chip + 1 if way == 0 else chip - 1
        return pltpu.make_async_remote_copy(
            src_ref=src, dst_ref=held.at[way, step, t, pl.ds(*ranges[k])], send_sem=d_send.at[n], recv_sem=d_recv.at[n],
            device_id=(dp, 2 * there + core), device_id_type=MESH)

    def landed(step, way, t, k):
        n = ((way * (chips - 1) + step) * towers + t) * len(ranges) + k
        ref = held.at[way, step, t, pl.ds(*ranges[k])]
        pltpu.make_async_remote_copy(src_ref=ref, dst_ref=ref, send_sem=d_send.at[n], recv_sem=d_recv.at[n],
                                     device_id=(dp, 2 * chip + core), device_id_type=MESH).wait_recv()

    pieces = [(t, k) for t in range(towers) for k in range(len(ranges))]
    ends = (chip == 0, chip == chips - 1)
    for t, k in pieces:
        for way in (0, 1):
            @pl.when(ends[way])
            def _():
                partial(0, way, t, k, True).start()
    own = [pltpu.make_async_copy(
        pg_ref.at[t, pl.ds(pl.multiple_of(dp * depth, 128), depth), pl.ds(0, cols)], gr_ref.at[dp, core, t], own_sem.at[t])
        for t in range(towers)]
    own.append(pltpu.make_async_copy(ps_ref, sr_ref.at[dp], own_sem.at[towers]))
    for copy in own:
        copy.start()
    for kind in range(3):
        small(kind).start()
    for t in range(towers):
        for kind in (2, 0, 1):
            for k in (0, 1):
                grad(kind, k, t).start()
        grad(3, 1 - core, t).start()

    strip = 16

    for step in range(1, chips - 1):
        for t, k in pieces:
            for way in (0, 1):
                @pl.when(sends(step, way) & ends[way])
                def _():
                    partial(step, way, t, k, True).start()

                @pl.when(sends(step, way) & jnp.logical_not(ends[way]))
                def _():
                    start, size = ranges[k]
                    load = pltpu.make_async_copy(own_term(target(step, way), t, k), term.at[way, pl.ds(0, size)], t_sem.at[way])
                    load.start()
                    landed(step - 1, way, t, k)
                    load.wait()

                    def add(i, _):
                        rws = pl.ds(pl.multiple_of(i * strip, strip), strip)
                        all_rows = pl.ds(pl.multiple_of(start + i * strip, strip), strip)
                        held[way, step - 1, t, all_rows] = (
                            held[way, step - 1, t, all_rows].astype(jnp.float32) + term[way, rws].astype(jnp.float32)
                        ).astype(jnp.bfloat16)
                        return 0
                    lax.fori_loop(0, size // strip, add, 0)
                    partial(step, way, t, k, False).start()

    stores = []
    for n, (t, k) in enumerate(pieces):
        s = n % 2
        start, size = ranges[k]
        load = pltpu.make_async_copy(own_term(chip, t, k), term.at[s, pl.ds(0, size)], t_sem.at[s])
        load.start()
        for way in (0, 1):
            @pl.when(receives(chips - 2, way))
            def _():
                landed(chips - 2, way, t, k)
        load.wait()
        if n >= 2:
            stores[n - 2].wait()

        def finish(i, _):
            rws = pl.ds(pl.multiple_of(i * strip, strip), strip)
            all_rows = pl.ds(pl.multiple_of(start + i * strip, strip), strip)
            value = term[s, rws].astype(jnp.float32)
            for way in (0, 1):
                here = receives(chips - 2, way)
                value = value + jnp.where(here, held[way, chips - 2, t, all_rows].astype(jnp.float32), 0.0)
            total[s, rws] = value.astype(jnp.bfloat16)
            return 0
        lax.fori_loop(0, size // strip, finish, 0)
        stores.append(pltpu.make_async_copy(total.at[s, pl.ds(0, size)], d_ref.at[t, pl.ds(start, size)], o_sem.at[s]))
        stores[n].start()
    for store in stores[-2:]:
        store.wait()

    for t in range(towers):
        for kind in range(3):
            for k in (0, 1):
                grad_arrived(kind, k, t)
        grad_arrived(3, 1 - core, t)
    for kind in range(3):
        small(kind).wait()
    for t in range(towers):
        for kind in range(3):
            for k in (0, 1):
                grad(kind, k, t).wait_send()
        grad(3, 1 - core, t).wait_send()
    for step in range(chips - 1):
        for t, k in pieces:
            for way in (0, 1):
                @pl.when(sends(step, way))
                def _():
                    partial(step, way, t, k, True).wait_send()
    for copy in own:
        copy.wait()


def reduce(partial_d, partial_g, partial_s, chips, ranges, ident):
    towers, rows, wide = partial_d.shape
    depth, cols = wide // chips, partial_g.shape[2] // 2
    count = 2 * (chips - 1) * towers * len(ranges)
    part = max(size for _, size in ranges)
    dma = pltpu.SemaphoreType.DMA
    bf16 = jnp.bfloat16
    out_shape = [jax.ShapeDtypeStruct((towers, rows, depth), bf16),
                 jax.ShapeDtypeStruct((4, 2, towers, depth, cols), bf16),
                 jax.ShapeDtypeStruct((4,) + partial_s.shape, jnp.float32)]
    return pl.pallas_call(
        functools.partial(reduce_kernel, chips, ranges),
        out_shape=out_shape,
        in_specs=[pl.BlockSpec(memory_space=pl.ANY)] * 3,
        out_specs=[pl.BlockSpec(memory_space=pl.ANY)] * len(out_shape),
        scratch_shapes=[pltpu.VMEM((2, chips - 1, towers, rows, depth), bf16),
                        pltpu.VMEM((2, part, depth), bf16), pltpu.VMEM((2, part, depth), bf16),
                        dma((count,)), dma((count,)), dma((2,)), dma((2,)), dma((16,)), dma((16,)), dma((3,)), dma((3,)), dma((towers + 1,))],
        compiler_params=pltpu.CompilerParams(collective_id=ident, has_side_effects=True, vmem_limit_bytes=56 * 2**20),
        cost_estimate=pl.CostEstimate(flops=0, bytes_accessed=800 * 2**20, transcendentals=0),
        name="reduce",
    )(partial_d, partial_g, partial_s)


def loop(count, body):
    def step(i, _):
        body(i)
        return 0
    lax.fori_loop(0, count, step, 0)


def wait_for(ref, sem, other):
    pltpu.make_async_remote_copy(src_ref=ref, dst_ref=ref, send_sem=other, recv_sem=sem, device_id=dict(dp=0, mp=0),
                                 device_id_type=MESH).wait_recv()


class Spot:
    def __init__(self, chips):
        self.dp, self.chip, self.core = place()
        self.chips, self.steps = chips, chips - 1
        self.others = (self.dp ^ 1, self.dp ^ 2, self.dp ^ 3)
        self.ends = (self.chip == 0) | (self.chip == self.steps)

    def at(self, dp, core):
        return dp, 2 * self.chip + core

    def on_line(self, chip):
        return self.dp, 2 * chip + self.core

    def passed(self, way):
        return jnp.where(way == 0, self.chip, self.steps - self.chip)

    def onward(self, way, n):
        return jnp.where(way == 0, self.chip + n, self.chip - n)

    def leaves(self, step, way):
        return (self.passed(way) < self.steps) & (self.passed(way) >= step)

    def comes(self, step, way):
        return self.passed(way) > step

    def greet(self):
        meet([(self.chip > 0, self.on_line(self.chip - 1)), (self.chip < self.steps, self.on_line(self.chip + 1)),
              (self.chip >= 0, self.at(self.dp, 1 - self.core))]
             + [(self.chip >= 0, self.at(c, k)) for c in self.others for k in (0, 1)])


class Features:
    def __init__(self, spot, f_ref, taken, fg, size, send, recv):
        self.spot, self.f_ref, self.taken, self.fg, self.size, self.send, self.recv = spot, f_ref, taken, fg, size, send, recv
        self.depth = f_ref.shape[1]

    def rows(self, q):
        return pl.ds(pl.multiple_of(q * self.size, 16), self.size)

    def lanes(self, shard):
        return pl.ds(pl.multiple_of(shard * self.depth, 128), self.depth)

    def copy(self, step, way, q, src=None):
        ref = self.fg.at[self.rows(q), self.lanes(self.spot.onward(way, -step))]
        return pltpu.make_async_remote_copy(
            src_ref=ref if src is None else src, dst_ref=ref, send_sem=self.send.at[way, step, q], recv_sem=self.recv.at[way, step, q],
            device_id=self.spot.on_line(self.spot.onward(way, 1)), device_id_type=MESH)

    def launch(self, q, last):
        def each(way):
            @pl.when(self.spot.leaves(0, way))
            def _():
                self.copy(0, way, q, self.taken if last else self.f_ref.at[self.rows(q)]).start()
        loop(2, each)

    def arrive(self, step, q):
        def each(way):
            @pl.when(self.spot.comes(step, way))
            def _():
                ref = self.fg.at[self.rows(q), self.lanes(self.spot.onward(way, -1 - step))]
                wait_for(ref, self.recv.at[way, step, q], self.send.at[way, step, q])
        loop(2, each)

    def serve(self, step, q):
        self.arrive(step, q)

        def each(way):
            @pl.when(self.spot.leaves(step + 1, way))
            def _():
                self.copy(step + 1, way, q).start()
        loop(2, each)

    def settle(self, q):
        for step in range(self.spot.steps):
            def each(way):
                @pl.when(self.spot.leaves(step, way))
                def _():
                    self.copy(step, way, q).wait_send()
            loop(2, each)


class Weights:
    def __init__(self, spot, low, wg, own_sem, send, recv):
        self.spot, self.low, self.wg, self.own_sem, self.send, self.recv = spot, low, wg, own_sem, send, recv
        self.depth, self.cols = low.shape[1], low.shape[2]

    def block(self, owner, slot):
        return self.wg.at[pl.ds(pl.multiple_of(owner * self.depth, 128), self.depth), pl.ds(pl.multiple_of(slot * self.cols, 128), self.cols)]

    def round(self, w_ref, wide, sem):
        part = wide.shape[1]
        parts = self.depth // part

        def load(n):
            return pltpu.make_async_copy(w_ref.at[pl.ds(pl.multiple_of(n * part, 16), part)], wide.at[lax.rem(n, 2)], sem.at[lax.rem(n, 2)])

        def one(n):
            @pl.when(n + 1 < 2 * parts)
            def _():
                load(n + 1).start()
            load(n).wait()

            def strip(i):
                rows = pl.ds(pl.multiple_of(i * 16, 16), 16)
                to = pl.ds(pl.multiple_of(lax.rem(n, parts) * part + i * 16, 16), 16)
                self.low[n // parts, to] = wide[lax.rem(n, 2), rows].astype(jnp.bfloat16)
            loop(part // 16, strip)
        load(jnp.int32(0)).start()
        loop(2 * parts, one)

    def send_own(self, kind, slot):
        s = self.spot
        k = s.core ^ slot
        return pltpu.make_async_remote_copy(
            src_ref=self.low.at[k], dst_ref=self.block(s.dp, slot), send_sem=self.send.at[kind, slot], recv_sem=self.recv.at[kind, slot],
            device_id=s.at((s.others[0], s.others[1], s.dp)[kind], k), device_id_type=MESH)

    def send_on(self, kind):
        s = self.spot
        ref = self.block(s.others[kind], kind)
        return pltpu.make_async_remote_copy(
            src_ref=ref, dst_ref=ref, send_sem=self.send.at[3, kind], recv_sem=self.recv.at[3, kind],
            device_id=s.at(s.others[1 - kind], s.core), device_id_type=MESH)

    def arrive(self, kind, slot):
        owner = (self.spot.others[0], self.spot.others[1], self.spot.dp)[kind]
        wait_for(self.block(owner, slot), self.recv.at[kind, slot], self.send.at[kind, slot])

    def own(self):
        return pltpu.make_async_copy(self.low.at[self.spot.core], self.block(self.spot.dp, 0), self.own_sem)

    def start(self):
        self.own().start()
        for slot in (0, 1):
            self.send_own(0, slot).start()
            self.send_own(1, 1 - slot).start()
        self.send_own(2, 1).start()

    def relay(self):
        for kind in (0, 1):
            self.arrive(kind, kind)
            self.send_on(kind).start()

    def finish(self):
        for kind in (0, 1):
            self.arrive(kind, 1 - kind)
            wait_for(self.block(self.spot.others[2], kind), self.recv.at[3, kind], self.send.at[3, kind])
        self.arrive(2, 1)
        self.own().wait()

    def settle(self):
        for kind in (0, 1):
            for slot in (0, 1):
                self.send_own(kind, slot).wait_send()
            self.send_on(kind).wait_send()
        self.send_own(2, 1).wait_send()


class Products:
    def __init__(self, spot, features, wg, f_tile, w_tile, acc, theirs, f_sem, w_sem, send, recv):
        self.spot, self.features, self.wg, self.f_tile, self.w_tile, self.acc, self.theirs = spot, features, wg, f_tile, w_tile, acc, theirs
        self.f_sem, self.w_sem, self.send, self.recv = f_sem, w_sem, send, recv
        self.cols = theirs.shape[1]

    def shard(self, j):
        return jnp.where(self.spot.chip == self.spot.steps, self.spot.steps - j, j)

    def load_w(self, j):
        depth = self.features.depth
        rows = pl.ds(pl.multiple_of(self.shard(j) * depth, 128), depth)
        return pltpu.make_async_copy(self.wg.at[rows], self.w_tile.at[lax.rem(j, 2)], self.w_sem.at[lax.rem(j, 2)])

    def load_f(self, j):
        lanes = self.features.lanes(self.shard(j))
        return pltpu.make_async_copy(self.features.fg.at[:, lanes], self.f_tile.at[lax.rem(j, 2)], self.f_sem.at[lax.rem(j, 2)])

    def here(self, j):
        return (j < self.spot.steps) | jnp.logical_not(self.spot.ends)

    def add(self, slot, rows):
        for col in range(0, 2 * self.cols, self.cols):
            lanes = pl.ds(col, self.cols)
            self.acc[rows, lanes] += jnp.dot(self.f_tile[slot, rows], self.w_tile[slot, :, lanes], preferred_element_type=jnp.float32)

    def multiply(self):
        def unit(j):
            @pl.when(j < self.spot.steps)
            def _():
                self.load_w(j + 1).start()

            @pl.when((j < self.spot.steps) & self.here(j + 1))
            def _():
                self.load_f(j + 1).start()
            self.load_w(j).wait()

            @pl.when(self.here(j))
            def _():
                self.load_f(j).wait()
                loop(self.acc.shape[0] // self.features.size, lambda q: self.add(lax.rem(j, 2), self.features.rows(q)))
        self.load_w(jnp.int32(0)).start()
        self.load_f(jnp.int32(0)).start()
        loop(self.spot.chips, unit)

    def swap(self, q):
        rows = self.features.rows(q)
        return pltpu.make_async_remote_copy(
            src_ref=self.acc.at[rows, pl.ds(self.cols, self.cols)], dst_ref=self.theirs.at[rows], send_sem=self.send.at[q],
            recv_sem=self.recv.at[q], device_id=self.spot.at(self.spot.dp, 1 - self.spot.core), device_id_type=MESH)

    def complete(self, q):
        slot = self.spot.steps % 2
        self.features.arrive(self.spot.steps - 1, q)

        @pl.when(self.spot.ends)
        def _():
            rows = self.features.rows(q)
            copy = pltpu.make_async_copy(self.features.fg.at[rows, self.features.lanes(self.shard(self.spot.steps))],
                                         self.f_tile.at[slot, rows], self.f_sem.at[slot])
            copy.start()
            copy.wait()
            self.add(slot, rows)
        self.swap(q).start()


class Backward:
    def __init__(self, spot, size, dz_here, dz_ref, send, recv, out_sem):
        self.spot, self.size, self.dz_here, self.dz_ref, self.send, self.recv, self.out_sem = spot, size, dz_here, dz_ref, send, recv, out_sem
        self.cols = dz_here.shape[1]

    def rows(self, q):
        return pl.ds(pl.multiple_of(q * self.size, 16), self.size)

    def swap(self, q):
        return pltpu.make_async_remote_copy(
            src_ref=self.dz_here.at[self.rows(q)], dst_ref=self.dz_ref.at[self.rows(q), pl.ds(self.cols, self.cols)],
            send_sem=self.send.at[q], recv_sem=self.recv.at[q], device_id=self.spot.at(self.spot.dp, 1 - self.spot.core), device_id_type=MESH)

    def keep(self, q):
        return pltpu.make_async_copy(self.dz_here.at[self.rows(q)], self.dz_ref.at[self.rows(q), pl.ds(0, self.cols)], self.out_sem.at[q])

    def start(self, q):
        self.swap(q).start()
        self.keep(q).start()

    def settle(self, q):
        self.swap(q).wait_recv()
        self.swap(q).wait_send()
        self.keep(q).wait()


def gelu_and_slope(v):
    factor, cubic = math.sqrt(2.0 / math.pi), 0.044715
    square = v * v
    th = jnp.tanh(factor * (v + cubic * (square * v)))
    slope = 0.5 * (1.0 + th) + 0.5 * v * (1.0 - th * th) * (factor * (1.0 + 3.0 * cubic * square))
    return 0.5 * v * (1.0 + th), slope


def live_rows_of(tot, share, live):
    keep = share[0][0]
    cols = live.shape[1]

    def strip(i):
        row = lax.broadcasted_iota(jnp.int32, (16, cols), 0).astype(jnp.float32) + (i * 16).astype(jnp.float32)
        here = jnp.where(row < tot[0, :1, :cols], 1.0, 0.0)
        there = jnp.zeros_like(here)
        for kind in range(4):
            count = tot[kind, :1, :cols]
            slot = row + float(share[kind][0] - keep)
            valid = (slot < count) & (count > keep)
            if kind == 3:
                valid = valid & (slot >= share[2][0] + share[2][1])
            there = there + jnp.where(valid, 1.0, 0.0)
        live[pl.ds(pl.multiple_of(i * 16, 16), 16)] = jnp.where(row < keep, here, there)
    loop(live.shape[0] // 16, strip)


def clear(ref):
    def strip(i):
        ref[pl.ds(pl.multiple_of(i * 16, 16), 16)] = jnp.zeros((16, ref.shape[1]), ref.dtype)
    loop(ref.shape[0] // 16, strip)


def fold(term):
    return term[:8] + term[8:]


class Grads:
    jobs, thirds = 8, 3

    def __init__(self, spot, fg, dz_here, gr, pg, relay, f_part, g_part, r_part, f_sem, g_sem, r_sem, send, recv, relay_send, relay_recv, own_sem):
        self.spot, self.fg, self.dz_here, self.gr, self.pg, self.relay_ref = spot, fg, dz_here, gr, pg, relay
        self.f_part, self.g_part, self.r_part, self.f_sem, self.g_sem, self.r_sem = f_part, g_part, r_part, f_sem, g_sem, r_sem
        self.send, self.recv, self.relay_send, self.relay_recv, self.own_sem = send, recv, relay_send, relay_recv, own_sem
        self.depth, self.cols = pg.shape[1], pg.shape[2]
        self.part = self.depth // self.thirds

    def owner_of(self, m):
        return jnp.where(m < 2, 3, jnp.where((m == 4) | (m == 5), 0, jnp.where((m == 2) | (m == 7), 1, 2)))

    def third(self, n):
        return pl.ds(pl.multiple_of(lax.rem(n, self.thirds) * self.part, 128), self.part)

    def load(self, n):
        first = (self.spot.dp ^ self.owner_of(n // self.thirds)) * self.depth + lax.rem(n, self.thirds) * self.part
        return pltpu.make_async_copy(self.fg.at[:, pl.ds(pl.multiple_of(first, 128), self.part)], self.f_part.at[lax.rem(n, 2)],
                                     self.f_sem.at[lax.rem(n, 2)])

    def store(self, n):
        return pltpu.make_async_copy(self.g_part.at[lax.rem(n, 2)], self.pg.at[n // self.thirds, self.third(n)], self.g_sem.at[lax.rem(n, 2)])

    def relay(self, m):
        return pltpu.make_async_remote_copy(
            src_ref=self.pg.at[m], dst_ref=self.relay_ref.at[m], send_sem=self.relay_send.at[m], recv_sem=self.relay_recv.at[m],
            device_id=self.spot.at(self.spot.dp ^ (m + 1), self.spot.core), device_id_type=MESH)

    def relayed(self, n):
        return pltpu.make_async_copy(self.relay_ref.at[jnp.maximum(n // self.thirds - (self.jobs - 2), 0), self.third(n)],
                                     self.r_part.at[lax.rem(n, 2)], self.r_sem.at[lax.rem(n, 2)])

    def job(self, m):
        joins = m >= self.jobs - 2
        lanes = pl.ds(pl.multiple_of(lax.rem(m, 2) * self.cols, 128), self.cols)

        @pl.when(joins)
        def _():
            k = jnp.maximum(m - (self.jobs - 2), 0)
            wait_for(self.relay_ref.at[k], self.relay_recv.at[k], self.relay_send.at[k])
            self.relayed(m * self.thirds).start()

        def part(c):
            n = m * self.thirds + c

            @pl.when(joins & (c + 1 < self.thirds))
            def _():
                self.relayed(n + 1).start()

            @pl.when(n + 1 < self.jobs * self.thirds)
            def _():
                self.load(n + 1).start()
            self.load(n).wait()

            @pl.when((n >= 2) & (n != (self.jobs - 2) * self.thirds) & (n != (self.jobs - 2) * self.thirds + 1))
            def _():
                self.store(n - 2).wait()

            @pl.when(joins)
            def _():
                self.relayed(n).wait()
            value = lax.dot_general(self.f_part[lax.rem(n, 2)], self.dz_here[:, lanes], (((0,), (0,)), ((), ())),
                                    preferred_element_type=jnp.float32)

            @pl.when(joins)
            def _():
                self.g_part[lax.rem(n, 2)] = (value + self.r_part[lax.rem(n, 2)].astype(jnp.float32)).astype(jnp.bfloat16)

            @pl.when(jnp.logical_not(joins))
            def _():
                self.g_part[lax.rem(n, 2)] = value.astype(jnp.bfloat16)
            self.store(n).start()
        loop(self.thirds, part)

    def copy(self, m):
        away, k = self.owner_of(m), self.spot.core ^ lax.rem(m, 2)
        return pltpu.make_async_remote_copy(
            src_ref=self.pg.at[m], dst_ref=self.gr.at[away, self.spot.core], send_sem=self.send.at[m],
            recv_sem=self.recv.at[away, self.spot.core], device_id=self.spot.at(self.spot.dp ^ away, k), device_id_type=MESH)

    def own(self):
        return pltpu.make_async_copy(self.pg.at[4], self.gr.at[0, self.spot.core], self.own_sem)

    def start(self, m):
        @pl.when(m < 2)
        def _():
            self.relay(jnp.minimum(m, 1)).start()

        @pl.when((m >= 2) & (m != 4))
        def _():
            self.copy(m).start()

        @pl.when(m == 4)
        def _():
            self.own().start()

    def turn(self, m, begin, late):
        early = self.jobs - 2
        pause = begin + early

        def job_at(m):
            return jnp.where(m < pause, m - begin, m - late + early)

        @pl.when((m == pause) | (m == late + 2))
        def _():
            for c in (1, 2):
                self.store(job_at(m - 1) * self.thirds + c).wait()

        @pl.when(((m >= begin) & (m < pause)) | (m == late) | (m == late + 1))
        def _():
            self.job(job_at(m))

        @pl.when(((m > begin) & (m <= pause)) | (m == late + 1) | (m == late + 2))
        def _():
            self.start(job_at(m - 1))

    def settle(self):
        for away in range(3):
            for k in (0, 1):
                @pl.when((away != 0) | (self.spot.core != k))
                def _():
                    wait_for(self.gr.at[away, k], self.recv.at[away, k], self.send.at[2])
        self.own().wait()
        for m in range(self.jobs):
            if m < 2:
                self.relay(m).wait_send()
            elif m != 4:
                self.copy(jnp.int32(m)).wait_send()


class Sums:
    window, lag = 5, 1

    def __init__(self, spot, parts, share, d_ref, dz_here, w_here, held, total, send, recv, out_sem, back_send, back_recv):
        self.spot, self.parts, self.share, self.d_ref, self.dz_here, self.w_here, self.held, self.total = spot, parts, share, d_ref, dz_here, w_here, held, total
        self.send, self.recv, self.out_sem, self.back_send, self.back_recv = send, recv, out_sem, back_send, back_recv
        self.size, self.depth = total.shape[1], total.shape[2]
        self.turns = spot.steps * parts
        self.skip = self.size - share[0][1]

    def rows(self, piece):
        return pl.ds(pl.multiple_of(lax.rem(piece + self.parts - 1, self.parts) * self.size, 16), self.size)

    def third(self, n):
        return pl.ds(pl.multiple_of(n * (self.depth // 3), 128), self.depth // 3)

    def sends(self, step, way):
        return (self.spot.passed(way) < self.spot.steps) & (self.spot.passed(way) <= step)

    def passing(self, m, way, turn):
        rows = self.rows(lax.rem(m, self.parts))
        return pltpu.make_async_remote_copy(
            src_ref=self.held.at[way, turn // self.parts, rows], dst_ref=self.held.at[way, m // self.parts, rows],
            send_sem=self.send.at[way, m], recv_sem=self.recv.at[way, m], device_id=self.spot.on_line(self.spot.onward(way, 1)),
            device_id_type=MESH)

    def landed(self, m, way):
        wait_for(self.held.at[way, m // self.parts, self.rows(lax.rem(m, self.parts))], self.recv.at[way, m], self.send.at[way, m])

    def product(self, goal, rows, col):
        return lax.dot_general(self.dz_here[rows], self.w_here[goal, self.third(col)], (((1,), (1,)), ((), ())),
                               preferred_element_type=jnp.float32)

    def store(self, piece):
        s = lax.rem(piece, 2)
        return pltpu.make_async_copy(self.total.at[s], self.d_ref.at[self.rows(piece)], self.out_sem.at[s])

    def hand(self, kind):
        to, taken = share_rows(self.share, kind)
        return pltpu.make_async_remote_copy(
            src_ref=self.total.at[0, pl.ds(self.skip + taken.start, taken.size)], dst_ref=self.d_ref.at[to], send_sem=self.back_send.at[kind],
            recv_sem=self.back_recv.at[kind], device_id=self.spot.at(self.spot.others[kind], self.spot.core), device_id_type=MESH)

    def send_sum(self, m, way):
        step, rows = m // self.parts, self.rows(lax.rem(m, self.parts))
        first = self.spot.passed(way) == 0
        held = self.held

        @pl.when(first & (m >= self.window))
        def _():
            self.passing(jnp.maximum(m - self.window, 0), way, 0).wait_send()

        @pl.when(jnp.logical_not(first))
        def _():
            self.landed(m - self.parts, way)

        def column(col):
            lanes = self.third(col)
            value = self.product(self.spot.onward(way, self.spot.steps - step), rows, col)

            @pl.when(first)
            def _():
                held[way, step, rows, lanes] = value.astype(jnp.bfloat16)

            @pl.when(jnp.logical_not(first))
            def _():
                held[way, step - 1, rows, lanes] = (value + held[way, step - 1, rows, lanes].astype(jnp.float32)).astype(jnp.bfloat16)
        loop(3, column)
        self.passing(m, way, jnp.where(first, m, m - self.parts)).start()

    def finish(self, piece):
        rows, s = self.rows(piece), lax.rem(piece, 2)
        held, total, last = self.held, self.total, self.spot.steps - 1

        @pl.when(piece >= 2)
        def _():
            self.store(piece - 2).wait()

        @pl.when(piece == 2)
        def _():
            for kind in range(3):
                self.hand(kind).wait_send()

        def each(way):
            @pl.when(self.spot.passed(way) > 0)
            def _():
                self.landed(self.turns - self.parts + piece, way)
        loop(2, each)

        def column(col):
            value = self.product(self.spot.chip, rows, col)
            lanes = self.third(col)

            @pl.when(self.spot.ends)
            def _():
                way = jnp.where(self.spot.chip == 0, 1, 0)
                total[s, :, lanes] = (value + held[way, last, rows, lanes].astype(jnp.float32)).astype(jnp.bfloat16)

            @pl.when(jnp.logical_not(self.spot.ends))
            def _():
                total[s, :, lanes] = (value + held[0, last, rows, lanes].astype(jnp.float32)
                                      + held[1, last, rows, lanes].astype(jnp.float32)).astype(jnp.bfloat16)
        loop(3, column)
        self.store(piece).start()

        @pl.when(piece == 0)
        def _():
            for kind in (2, 0, 1):
                self.hand(kind).start()

    def turn(self, m):
        def each(way):
            @pl.when((m < self.turns) & self.sends(m // self.parts, way))
            def _():
                self.send_sum(m, way)
        loop(2, each)

    def turn_end(self, m):
        first = self.turns - self.parts + self.lag

        @pl.when((m >= first) & (m < first + self.parts))
        def _():
            self.finish(m - first)

    def settle(self):
        def drain(m):
            def each(way):
                first = self.spot.passed(way) == 0

                @pl.when(self.sends(m // self.parts, way) & (jnp.logical_not(first) | (m >= self.turns - self.window)))
                def _():
                    self.passing(m, way, 0).wait_send()
            loop(2, each)
        loop(self.turns, drain)
        for piece in (self.parts - 2, self.parts - 1):
            self.store(piece).wait()
        for kind in range(3):
            self.hand(kind).wait_recv()


def share_rows(share, kind):
    skip = share[2][0] + share[2][1] - share[3][0] if kind == 2 else 0
    first, length = share[1 + kind]
    return pl.ds(first + skip, length - skip), pl.ds(skip, length - skip)


class Bases:
    def __init__(self, left, right, out, held, parts, load_sem, store_sem):
        self.sources, self.out, self.held, self.parts, self.load_sem, self.store_sem = (left, right), out, held, parts, load_sem, store_sem
        self.groups, self.pairs = left.shape[1], left.shape[2] // 2
        self.units = left.shape[0] * self.groups

    def at(self, u):
        return u // self.groups, lax.rem(u, self.groups), lax.rem(u, 2)

    def load(self, u, start):
        t, r, slot = self.at(u)
        for n, source in enumerate(self.sources):
            copy = pltpu.make_async_copy(source.at[t, r], self.held.at[slot, n], self.load_sem.at[slot, n])
            (copy.start if start else copy.wait)()

    def store(self, u, start):
        t, r, slot = self.at(u)
        for n in (0, 1):
            copy = pltpu.make_async_copy(self.parts.at[slot, n], self.out.at[n, t, r], self.store_sem.at[slot, n])
            (copy.start if start else copy.wait)()

    def unit(self, u):
        @pl.when(u + 1 < self.units)
        def _():
            self.load(u + 1, True)
        self.load(u, False)

        @pl.when(u >= 2)
        def _():
            self.store(u - 2, False)
        slot = lax.rem(u, 2)
        for n in (0, 1):
            for q in range(self.pairs):
                both = jnp.concatenate([self.held[slot, n, 2 * q], self.held[slot, n, 2 * q + 1]], axis=1)
                high, low = split(both)
                rows = pl.ds(q * BLOCK, BLOCK)
                self.parts[slot, n, 0, rows] = high
                self.parts[slot, n, 1, rows] = low
        self.store(u, True)

    def some(self, first, count):
        def one(i):
            @pl.when(first + i < self.units)
            def _():
                self.unit(first + i)
        loop(count, one)

    def settle(self):
        for u in (self.units - 2, self.units - 1):
            self.store(jnp.int32(u), False)


class Stitched:
    def __init__(self, spot, share, y_ref, st_ref, y_send, y_recv, core_send, core_recv, give_send, give_recv, given_send, given_recv, own_sem):
        self.spot, self.share, self.y_ref, self.st_ref = spot, share, y_ref, st_ref
        self.y_send, self.y_recv, self.core_send, self.core_recv = y_send, y_recv, core_send, core_recv
        self.give_send, self.give_recv, self.given_send, self.given_recv, self.own_sem = give_send, give_recv, given_send, given_recv, own_sem
        self.towers, self.cols = y_ref.shape[0], y_ref.shape[2]
        self.bands = (share[0], (0, share[0][0]))
        self.events = 2 * self.towers * spot.steps

    def lanes(self, shard, k):
        return pl.ds(pl.multiple_of((2 * shard + k) * self.cols, 128), self.cols)

    def place(self, shard, k, t, b):
        return self.st_ref.at[t, pl.ds(*self.bands[b]), self.lanes(shard, k)]

    def source(self, t, b):
        return self.y_ref.at[t, pl.ds(*self.bands[b])]

    def leave(self, step, way, t, b, own=False):
        s = self.spot
        dst = self.place(s.onward(way, -step), s.core, t, b)
        return pltpu.make_async_remote_copy(
            src_ref=self.source(t, b) if own else dst, dst_ref=dst, send_sem=self.y_send.at[way, step, b, t],
            recv_sem=self.y_recv.at[way, step, b, t], device_id=s.on_line(s.onward(way, 1)), device_id_type=MESH)

    def to_core(self, shard, t, b, own=False):
        s = self.spot
        dst = self.place(shard, s.core, t, b)
        return pltpu.make_async_remote_copy(
            src_ref=self.source(t, b) if own else dst, dst_ref=dst, send_sem=self.core_send.at[shard, b, t],
            recv_sem=self.core_recv.at[shard, b, t], device_id=s.at(s.dp, 1 - s.core), device_id_type=MESH)

    def give(self, kind, shard, t, own=False):
        s = self.spot
        to, taken = share_rows(self.share, kind)
        src = pl.ds(self.share[0][0] + taken.start, taken.size)
        return pltpu.make_async_remote_copy(
            src_ref=self.y_ref.at[t, src] if own else self.st_ref.at[t, src, self.lanes(shard, s.core)],
            dst_ref=self.st_ref.at[t, to, self.lanes(shard, s.core)], send_sem=self.give_send.at[kind, shard, t],
            recv_sem=self.give_recv.at[kind, shard, t], device_id=s.at(s.others[kind], s.core), device_id_type=MESH)

    def given_place(self, kind, shard, t, k):
        return self.st_ref.at[t, share_rows(self.share, kind)[0], self.lanes(shard, k)]

    def given(self, kind, shard, t):
        s = self.spot
        ref = self.given_place(kind, shard, t, s.core)
        return pltpu.make_async_remote_copy(
            src_ref=ref, dst_ref=ref, send_sem=self.given_send.at[kind, shard, t], recv_sem=self.given_recv.at[kind, shard, t],
            device_id=s.at(s.dp, 1 - s.core), device_id_type=MESH)

    def own(self, t, b):
        return pltpu.make_async_copy(self.source(t, b), self.place(self.spot.chip, self.spot.core, t, b), self.own_sem.at[b, t])

    def start(self):
        for b in (0, 1):
            def tower(t):
                def each(way):
                    @pl.when(self.spot.leaves(0, way))
                    def _():
                        self.leave(0, way, t, b, True).start()
                loop(2, each)
                self.to_core(self.spot.chip, t, b, True).start()
                if b == 0:
                    for kind in (2, 0, 1):
                        self.give(kind, self.spot.chip, t, True).start()
                self.own(t, b).start()
            loop(self.towers, tower)

    def event(self, n):
        step, t = n // (2 * self.towers), lax.rem(n, self.towers)
        for b in (0, 1):
            def each(way):
                @pl.when(self.spot.comes(step, way))
                def _():
                    shard = self.spot.onward(way, -1 - step)
                    wait_for(self.place(shard, self.spot.core, t, b), self.y_recv.at[way, step, b, t], self.y_send.at[way, step, b, t])

                    @pl.when((step + 1 < self.spot.steps) & self.spot.leaves(step + 1, way))
                    def _():
                        self.leave(jnp.minimum(step + 1, self.spot.steps - 1), way, t, b).start()
                    self.to_core(shard, t, b).start()
                    if b == 0:
                        for kind in (2, 0, 1):
                            self.give(kind, shard, t).start()

            @pl.when(lax.rem(n, 2 * self.towers) // self.towers == b)
            def _():
                loop(2, each)

    def receive(self):
        def one(n):
            shard, t = n // self.towers, lax.rem(n, self.towers)
            for kind in range(3):
                wait_for(self.given_place(kind, shard, t, self.spot.core), self.give_recv.at[kind, shard, t], self.give_send.at[kind, shard, t])
                self.given(kind, shard, t).start()
        loop(self.spot.chips * self.towers, one)

    def settle(self):
        def one(n):
            shard, t = n // self.towers, lax.rem(n, self.towers)
            for b in (0, 1):
                wait_for(self.place(shard, 1 - self.spot.core, t, b), self.core_recv.at[shard, b, t], self.core_send.at[shard, b, t])
                self.to_core(shard, t, b).wait_send()

                @pl.when(shard < self.spot.steps)
                def _():
                    def each(way):
                        @pl.when(self.spot.leaves(shard, way))
                        def _():
                            self.leave(jnp.minimum(shard, self.spot.steps - 1), way, t, b).wait_send()
                    loop(2, each)
            for kind in range(3):
                self.give(kind, shard, t).wait_send()
                self.given(kind, shard, t).wait_send()
                wait_for(self.given_place(kind, shard, t, 1 - self.spot.core), self.given_recv.at[kind, shard, t], self.given_send.at[kind, shard, t])
        loop(self.spot.chips * self.towers, one)
        for t in range(self.towers):
            for b in (0, 1):
                self.own(t, b).wait()


def front_kernel(chips, parts, share, f_ref, w_ref, o_ref, n_ref, sp_ref, left_ref, right_ref,
                 fg_first, wg_first, dz_first, fg_ref, wg_ref, dz_ref, y_ref, sg_ref, tot_ref, bases_ref, d_ref, gr_ref, pg_ref, relay_ref,
                 offer_f, taken, offer_o, wide, low, base_in, base_out, tot,
                 og, f_tile, w_tile, acc, theirs, live, act, dz_here, y_here, sums_here,
                 held, w_here, dz_wide, total, f_part, g_part, r_part,
                 f_send, f_recv, w_send, w_recv, a_send, a_recv, z_send, z_recv, out_sem,
                 wide_sem, p_sem, x_send, x_recv, l_sem, base_load, base_store,
                 d_send, d_recv, o_sem, b_send, b_recv, g_load, g_send, g_recv, rs_send, rs_recv, own_sem):
    spot = Spot(chips)
    keep, rows = share[0][0], sum(share[0])
    size = rows // parts
    fixed = rows - size
    spare = keep - fixed
    cols = o_ref.shape[2]
    tot[0] = jnp.zeros_like(tot[0]) + jnp.sum(n_ref[...].astype(jnp.float32), axis=1, keepdims=True)
    spot.greet()

    def offer(kind, what):
        src = (f_ref.at[0], f_ref.at[1], o_ref, tot.at[0])[what]
        dst = (offer_f.at[0, 1 + kind], offer_f.at[1, 1 + kind], offer_o.at[1 + kind], tot.at[1 + kind])[what]
        if what < 3:
            src = src.at[pl.ds(*share[1 + kind])] if what < 2 else src.at[:, pl.ds(*share[1 + kind])]
        return pltpu.make_async_remote_copy(
            src_ref=src, dst_ref=dst, send_sem=x_send.at[what, kind], recv_sem=x_recv.at[what, kind],
            device_id=spot.at(spot.others[kind], spot.core), device_id_type=MESH)

    def choose(width, read, write):
        weigh = [jnp.broadcast_to(jnp.where(tot[kind, :1, :width] > keep, 1.0, 0.0), (16, width)) for kind in range(4)]

        def strip(i):
            at = pl.ds(pl.multiple_of(i * 16, 16), 16)
            value = read(0, at).astype(jnp.float32) * weigh[0]
            for kind in range(1, 4):
                value = value + read(kind, at).astype(jnp.float32) * weigh[kind]
            write(i * 16, value.astype(jnp.bfloat16))
        loop(share[0][1] // 16, strip)

    def take(t):
        def write(row, value):
            taken[t, pl.ds(pl.multiple_of(spare + row, 16), 16)] = value
        choose(offer_f.shape[3], lambda kind, at: offer_f[t, kind, at], write)

    towers = []
    for t, (fg, wg, dz) in enumerate(((fg_first, wg_first, dz_first), (fg_ref, wg_ref, dz_ref))):
        features = Features(spot, f_ref.at[t], taken.at[t], fg, size, f_send.at[t], f_recv.at[t])
        weights = Weights(spot, low.at[t], wg, p_sem.at[t, 4], w_send.at[t], w_recv.at[t])
        products = Products(spot, features, wg, f_tile, w_tile, acc, theirs.at[t], p_sem.at[t, pl.ds(0, 2)], p_sem.at[t, pl.ds(2, 2)],
                            a_send.at[t], a_recv.at[t])
        backward = Backward(spot, size, dz_here, dz, z_send.at[t], z_recv.at[t], out_sem.at[t])
        towers.append((features, weights, products, backward))
    features, weights, products, backward = towers[0]
    gradients = Sums(spot, parts, share, d_ref, dz_wide, w_here, held, total, d_send, d_recv, o_sem, b_send, b_recv)
    grads = Grads(spot, fg_first, dz_wide, gr_ref, pg_ref, relay_ref, f_part, g_part, r_part, g_load.at[0], g_load.at[1], g_load.at[2],
                  g_send, g_recv, rs_send, rs_recv, own_sem)
    bases = Bases(left_ref, right_ref, bases_ref, base_in, base_out, base_load, base_store)

    def copy(n, src, dst):
        made = pltpu.make_async_copy(src, dst, l_sem.at[n])
        made.start()
        return made

    for what in (3, 0):
        for kind in (2, 0, 1):
            offer(kind, what).start()
    loop(parts - 1, lambda q: features.launch(q, False))
    needed = [copy(0, f_ref.at[0, pl.ds(*share[0])], offer_f.at[0, 0])]
    later = [copy(1, f_ref.at[1, pl.ds(*share[0])], offer_f.at[1, 0])]
    if spare:
        needed.append(copy(2, f_ref.at[0, pl.ds(fixed, spare)], taken.at[0, pl.ds(0, spare)]))
        later.append(copy(3, f_ref.at[1, pl.ds(fixed, spare)], taken.at[1, pl.ds(0, spare)]))
    later += [copy(4, o_ref.at[:, pl.ds(*share[0])], offer_o.at[0]), copy(5, o_ref.at[:, pl.ds(0, keep)], og.at[:, pl.ds(0, keep)]),
              copy(6, f_ref.at[0, pl.ds(0, fixed)], fg_first.at[pl.ds(0, fixed), features.lanes(spot.chip)]),
              copy(7, f_ref.at[1, pl.ds(0, fixed)], fg_ref.at[pl.ds(0, fixed), features.lanes(spot.chip)])]
    weights.round(w_ref.at[0], wide, wide_sem)
    weights.start()
    for made in needed:
        made.wait()
    for what in (3, 0):
        for kind in range(3):
            offer(kind, what).wait_recv()
    take(0)
    features.launch(parts - 1, True)
    later += [copy(8, tot, tot_ref), copy(9, taken.at[0], fg_first.at[pl.ds(fixed, size), features.lanes(spot.chip)])]
    live_rows_of(tot, share, live)
    clear(acc)
    sums_here[...] = jnp.zeros_like(sums_here)
    towers[1][1].round(w_ref.at[1], wide, wide_sem)
    share_of = -(-bases.units // (2 * parts))

    def serve(step, q):
        features.serve(step, q)
        bases.some((step * parts + q) * share_of, share_of)
    bases.load(jnp.int32(0), True)
    loop(parts, lambda q: serve(0, q))
    weights.relay()
    for what in (2, 1):
        for kind in (2, 0, 1):
            offer(kind, what).start()
    loop(parts, lambda q: serve(1, q))
    weights.finish()
    towers[1][1].start()
    for made in later:
        made.wait()
    products.multiply()
    for kind in range(3):
        offer(kind, 2).wait_recv()
    for t in range(2):
        def write(row, value):
            og[t, pl.ds(pl.multiple_of(keep + row, 16), 16)] = value
        choose(cols, lambda kind, at: offer_o[kind, t, at], write)

    def strip(t, at):
        activated, slope = gelu_and_slope(acc[at, :cols] + theirs[t, at] + sp_ref[t : t + 1])
        mask = live[at]
        dy = [og[n, at].astype(jnp.float32) * mask for n in range(2)]
        dz = slope * (sp_ref[2 + t : 3 + t] * dy[0] + sp_ref[4 + t : 5 + t] * dy[1])
        if t == 0:
            act[at] = activated
        else:
            other = act[at]
            for n in range(2):
                y_here[n, at] = ((sp_ref[2 + 2 * n : 3 + 2 * n] * other + sp_ref[3 + 2 * n : 4 + 2 * n] * activated) * mask).astype(jnp.bfloat16)
        dz_here[at] = dz.astype(jnp.bfloat16)
        for n, term in enumerate((dz, activated * dy[0], activated * dy[1])):
            sums_here[2 * n + t] += fold(term)

    def stage(t, k):
        _, _, products, backward = towers[t]

        @pl.when(k < parts)
        def _():
            products.complete(k)

        @pl.when(k > 0)
        def _():
            products.swap(k - 1).wait_recv()
            loop(size // 16, lambda i: strip(t, pl.ds(pl.multiple_of((k - 1) * size + i * 16, 16), 16)))
            backward.start(k - 1)
    loop(parts + 1, lambda k: stage(0, k))

    def settle(t, q):
        towers[t][0].settle(q)
        towers[t][2].swap(q).wait_send()
        towers[t][3].settle(q)
    for kind in range(3):
        offer(kind, 1).wait_recv()
    take(1)
    loop(parts, lambda q: settle(0, q))
    loads = first_loads(chips, wg_first, dz_first, w_here, dz_wide, l_sem.at[pl.ds(11, chips + 1)])
    features, weights, products, backward = towers[1]
    loop(parts - 1, lambda q: features.launch(q, False))
    features.launch(parts - 1, True)
    last = copy(0, taken.at[1], fg_ref.at[pl.ds(fixed, size), features.lanes(spot.chip)])
    grads.load(jnp.int32(0)).start()
    clear(acc)
    for made in loads:
        made.wait()

    def turn(m):
        gradients.turn(m)
        grads.turn(m, 2, 10)

        @pl.when(m == 2)
        def _():
            weights.relay()

        @pl.when((m >= 2) & (m < 2 + parts))
        def _():
            features.serve(0, m - 2)

        @pl.when((m >= 4 + parts) & (m < 4 + 2 * parts))
        def _():
            features.serve(1, m - 4 - parts)

        @pl.when(m == 4 + 2 * parts)
        def _():
            weights.finish()
            last.wait()
            products.multiply()
        gradients.turn_end(m)
    loop(gradients.turns + gradients.lag, turn)
    loop(parts + 1, lambda k: stage(1, k))
    last = copy(0, y_here, y_ref)
    sg_ref[...] = jnp.zeros_like(sg_ref)
    for n in range(6):
        sg_ref[n : n + 1] = jnp.sum(sums_here[n], axis=0, keepdims=True)
    loop(parts, lambda q: settle(1, q))
    for t in range(2):
        towers[t][1].settle()
    gradients.settle()
    grads.settle()
    bases.settle()
    last.wait()
    for what in range(4):
        for kind in range(3):
            offer(kind, what).wait_send()


def first_loads(chips, wg, dz, w_here, dz_wide, sem):
    depth = w_here.shape[1]
    loads = [pltpu.make_async_copy(dz, dz_wide, sem.at[chips])]
    loads += [pltpu.make_async_copy(wg.at[pl.ds(n * depth, depth)], w_here.at[n], sem.at[n]) for n in range(chips)]
    for copy in loads:
        copy.start()
    return loads


def third_kernel(chips, parts, share, y_ref, fg_ref, wg_ref, dz_ref, ps_ref, st_ref, d_ref, gr_ref, sr_ref, pg_ref, relay_ref,
                 held, w_here, dz_wide, total, f_part, g_part, r_part, l_sem,
                 d_send, d_recv, o_sem, b_send, b_recv, g_load, g_send, g_recv, rs_send, rs_recv, own_sem, s_send, s_recv,
                 y_send, y_recv, core_send, core_recv, give_send, give_recv, given_send, given_recv, y_own):
    spot = Spot(chips)
    spot.greet()
    gradients = Sums(spot, parts, share, d_ref, dz_wide, w_here, held, total, d_send, d_recv, o_sem, b_send, b_recv)
    grads = Grads(spot, fg_ref, dz_wide, gr_ref, pg_ref, relay_ref, f_part, g_part, r_part, g_load.at[0], g_load.at[1], g_load.at[2],
                  g_send, g_recv, rs_send, rs_recv, own_sem)
    stitched = Stitched(spot, share, y_ref, st_ref, y_send, y_recv, core_send, core_recv, give_send, give_recv, given_send, given_recv, y_own)

    def small(kind):
        return pltpu.make_async_remote_copy(
            src_ref=ps_ref, dst_ref=sr_ref.at[spot.dp], send_sem=s_send.at[kind], recv_sem=s_recv.at[kind],
            device_id=spot.at(spot.others[kind], spot.core), device_id_type=MESH)

    loads = first_loads(chips, wg_ref, dz_ref, w_here, dz_wide, l_sem)
    grads.load(jnp.int32(0)).start()
    stitched.start()
    own = pltpu.make_async_copy(ps_ref, sr_ref.at[spot.dp], l_sem.at[chips + 1])
    own.start()
    for kind in range(3):
        small(kind).start()
    for copy in loads:
        copy.wait()

    def turn(m):
        gradients.turn(m)
        grads.turn(m, 0, 8)

        @pl.when((m >= 1) & (m <= stitched.events))
        def _():
            stitched.event(m - 1)
        gradients.turn_end(m)
    loop(gradients.turns + gradients.lag, turn)
    stitched.receive()
    gradients.settle()
    stitched.settle()
    grads.settle()
    for kind in range(3):
        small(kind).wait()
    own.wait()


def call(kernel, name, ident, out, scratch, operands, small_in=(), small_out=(), flops=0):
    anywhere, here = pl.BlockSpec(memory_space=pl.ANY), pl.BlockSpec(memory_space=pltpu.VMEM)
    return pl.pallas_call(
        kernel,
        out_shape=out,
        in_specs=[here if n in small_in else anywhere for n in range(len(operands))],
        out_specs=[here if n in small_out else anywhere for n in range(len(out))],
        scratch_shapes=scratch,
        compiler_params=pltpu.CompilerParams(collective_id=ident, has_side_effects=True, vmem_limit_bytes=62 * 2**20),
        cost_estimate=pl.CostEstimate(flops=flops, bytes_accessed=500 * 2**20, transcendentals=0),
        name=name,
    )(*operands)


def parts_of(share):
    rows = sum(share[0])
    return max(n for n in range(1, rows // 16) if rows % (16 * n) == 0 and rows // n >= share[0][1])


def shared_pass(features, weights, out_grad, counts, small_params, left, right, chips, share):
    parts = parts_of(share)
    towers, slots, depth = features.shape
    cols = weights.shape[2]
    keep, size = share[0]
    rows = keep + size
    steps = chips - 1
    piece = rows // parts
    dma, vmem = pltpu.SemaphoreType.DMA, pltpu.VMEM
    bf16, f32 = jnp.bfloat16, jnp.float32
    S = jax.ShapeDtypeStruct
    beside = (left.shape[2] // 2 * BLOCK, 2 * BLOCK)
    wide = [S((rows, chips * depth), bf16), S((chips * depth, 2 * cols), bf16), S((rows, 2 * cols), bf16)]
    _, _, _, *second, result, small, told, bases, d_first, gr_first, _, _ = call(
        functools.partial(front_kernel, chips, parts, share), "front", 3,
        wide + wide + [S((towers, rows, cols), bf16), S((8, cols), f32), S((4, 8, depth), f32), S((2,) + left.shape[:2] + (2,) + beside, bf16)]
        + sums_out(slots, depth, cols),
        [vmem((towers, 4, size, depth), bf16), vmem((towers, piece, depth), bf16), vmem((4, towers, size, cols), bf16),
         vmem((2, depth // 8, cols), f32), vmem((towers, 2, depth, cols), bf16), vmem((2, 2) + left.shape[2:], f32), vmem((2, 2, 2) + beside, bf16),
         vmem((4, 8, depth), f32), vmem((towers, rows, cols), bf16), vmem((2, rows, depth), bf16), vmem((2, depth, 2 * cols), bf16),
         vmem((rows, 2 * cols), f32), vmem((towers, rows, cols), f32), vmem((rows, cols), f32), vmem((rows, cols), f32), vmem((rows, cols), bf16),
         vmem((towers, rows, cols), bf16), vmem((6, 8, cols), f32)] + sums_scratch(chips, rows, parts, depth, cols)
        + [dma((towers, 2, steps, parts))] * 2 + [dma((towers, 4, 2))] * 2 + [dma((towers, parts))] * 5
        + [dma((2,)), dma((towers, 5)), dma((4, 3)), dma((4, 3)), dma((12 + chips,)), dma((2, 2)), dma((2, 2))] + sums_dma(steps, parts),
        (features, weights, out_grad, counts.reshape(1, -1), small_params, left, right), (3, 4), (7,), 5 * 2 * rows * 2 * cols * depth * chips)
    wide_f, wide_w, wide_dz = second
    return told, bases, (result, wide_f, wide_w, wide_dz, small), d_first, gr_first


def sums_out(slots, depth, cols):
    S, bf16 = jax.ShapeDtypeStruct, jnp.bfloat16
    return [S((slots, depth), bf16), S((3, 2, depth, cols), bf16), S((8, depth, cols), bf16), S((2, depth, cols), bf16)]


def sums_scratch(chips, rows, parts, depth, cols):
    vmem, bf16 = pltpu.VMEM, jnp.bfloat16
    return [vmem((2, chips - 1, rows, depth), bf16), vmem((chips, depth, 2 * cols), bf16), vmem((rows, 2 * cols), bf16),
            vmem((2, rows // parts, depth), bf16), vmem((2, rows, depth // 3), bf16)] + [vmem((2, depth // 3, cols), bf16)] * 2


def sums_dma(steps, parts):
    dma = pltpu.SemaphoreType.DMA
    return [dma((2, steps * parts))] * 2 + [dma((2,)), dma((3,)), dma((3,)), dma((3, 2)), dma((8,)), dma((3, 2)), dma((2,)), dma((2,)), dma(())]


def shared_sums(result, wide_f, wide_w, wide_dz, partial_s, slots, chips, share):
    parts = parts_of(share)
    towers, rows, cols = result.shape
    depth, steps = wide_w.shape[0] // chips, chips - 1
    dma = pltpu.SemaphoreType.DMA
    S = jax.ShapeDtypeStruct
    stitched, d_feat, grad_parts, smalls, _, _ = call(
        functools.partial(third_kernel, chips, parts, share), "third", 4,
        [S((towers, slots, 2 * chips * cols), jnp.bfloat16)] + sums_out(slots, depth, cols)[:2] + [S((4,) + partial_s.shape, jnp.float32)]
        + sums_out(slots, depth, cols)[2:],
        sums_scratch(chips, rows, parts, depth, cols) + [dma((chips + 2,))] + sums_dma(steps, parts) + [dma((3,))] * 2
        + [dma((2, steps, 2, towers))] * 2 + [dma((chips, 2, towers))] * 2 + [dma((3, chips, towers))] * 4 + [dma((2, towers))],
        (result, wide_f, wide_w, wide_dz, partial_s), flops=4 * rows * 2 * cols * depth * chips)
    return stitched, d_feat, grad_parts, smalls


def small_step(small_params, small_moment_one, small_moment_two, small_average, small_grad):
    first, second, direction = adam_part(small_moment_one, small_moment_two, small_grad)
    fresh = small_params - rate_small * direction
    return first, second, fresh, ema_decay * small_average + (1.0 - ema_decay) * fresh


def update(d_feat, stitched, full, parts, small_parts, states, small_states):
    small_grad = jnp.sum(small_parts, 0)[: small_states[0].shape[0]]
    *fresh, stitched, d_feat = soap(parts, full, stitched, d_feat, *states)
    return (stitched, d_feat) + tuple(fresh) + small_step(*small_states, small_grad)


def own_rows(features, out_grad, totals, passed, first, states, small_states):
    _, rows, _ = features.shape
    weights, small_params = states[0], small_states[0]
    cols = weights.shape[2]
    cores = lax.axis_size("mp")
    swap = [(i, i ^ 1) for i in range(cores)]
    ranges = ((0, rows // 2), (rows // 2, rows // 2))
    live_rows = (jnp.arange(rows, dtype=jnp.float32) < totals[0]).astype(jnp.float32)
    wide_f, wide_w = gather(features, weights.astype(jnp.bfloat16), cores // 2, ranges, 1)
    partial = jnp.einsum("tri,tio->tro", wide_f, wide_w, preferred_element_type=jnp.float32)
    product = partial[:, :, :cols] + lax.ppermute(partial[:, :, cols:], "mp", swap)
    result, back = jax.vjp(lambda a, b: stitch_local(a, b, live_rows), product, small_params)
    stitched = lax.all_gather(result.astype(jnp.bfloat16), "mp", axis=2, tiled=True)
    dz, small_part = back(out_grad.astype(jnp.float32))
    dz_low = dz.astype(jnp.bfloat16)
    wide_dz = jnp.concatenate([dz_low, lax.ppermute(dz_low, "mp", swap)], axis=2)
    partial_d = jnp.einsum("tro,tio->tri", wide_dz, wide_w, preferred_element_type=jnp.float32)
    partial_g = jnp.einsum("tri,tro->tio", wide_f, wide_dz, preferred_element_type=jnp.float32)
    small_part = jnp.pad(small_part, ((0, 2), (0, 0)))
    d_feat, parts, small_parts = reduce(
        partial_d.astype(jnp.bfloat16), partial_g.astype(jnp.bfloat16), small_part, cores // 2, ranges, 2
    )
    full = jnp.full((1,), rows, jnp.int32)
    return update((d_feat[0], d_feat[1]), stitched, full, (parts[:, :, 0], parts[:, :, 1]), small_parts, states, small_states)


def shares(rows):
    keep = rows * 15 // 32 // 16 * 16
    size = -(-(rows - keep) // 64) * 16
    return keep, ((keep, size), (keep + size, size), (keep + 2 * size, size), (rows - size, size))


def shared_rows(features, out_grad, totals, passed, first, states, small_states):
    rows = features.shape[1]
    keep, share = shares(rows)
    d_first, gr_first = first
    full = jnp.where(totals[:1] > keep, rows, keep)
    stitched, d_second, gr_second, small_parts = shared_sums(*passed, rows, lax.axis_size("mp") // 2, share)
    return update((d_first, d_second), stitched, full, (gr_first, gr_second), small_parts, states, small_states)


def line_body(
    features,
    counts,
    weights,
    small_params,
    out_grad,
    moment_one,
    moment_two,
    average,
    basis_left,
    basis_right,
    small_moment_one,
    small_moment_two,
    small_average,
):
    keep, share = shares(features.shape[1])
    told, bases, passed, *first = shared_pass(
        features, weights, out_grad, counts, small_params, basis_left, basis_right, lax.axis_size("mp") // 2, share
    )
    totals = told[:, 0, 0]
    return lax.cond(
        jnp.sum(totals > keep) == 1,
        shared_rows,
        own_rows,
        features,
        out_grad,
        totals,
        passed,
        first,
        (weights, moment_one, moment_two, average, bases),
        (small_params, small_moment_one, small_moment_two, small_average),
    )


def plain_body(
    features,
    counts,
    weights,
    small_params,
    out_grad,
    moment_one,
    moment_two,
    average,
    basis_left,
    basis_right,
    small_moment_one,
    small_moment_two,
    small_average,
):
    slot_count = features.shape[1]
    total = jnp.sum(counts)
    live_rows = (jnp.arange(slot_count, dtype=jnp.int32) < total).astype(jnp.float32)
    weights_low = lax.all_gather(weights.astype(jnp.bfloat16), "dp", axis=1, tiled=True)
    feats_full = lax.all_gather(features, "mp", axis=2, tiled=True)
    product = jnp.einsum(
        "tri,tio->tro", feats_full, weights_low, preferred_element_type=jnp.float32
    )
    result, back = jax.vjp(lambda a, b: stitch_local(a, b, live_rows), product, small_params)
    stitched = lax.all_gather(result.astype(jnp.bfloat16), "mp", axis=2, tiled=True)
    dz, small_part = back(out_grad.astype(jnp.float32))
    dz_low = dz.astype(jnp.bfloat16)
    grad_part = jnp.einsum("tri,tro->tio", feats_full, dz_low, preferred_element_type=jnp.float32)
    partial_sums = jnp.einsum(
        "tro,tio->tri", dz_low, weights_low, preferred_element_type=jnp.float32
    )
    d_feat = lax.psum_scatter(
        partial_sums.astype(jnp.float32), "mp", scatter_dimension=2, tiled=True
    )
    grad = lax.psum_scatter(grad_part, "dp", scatter_dimension=1, tiled=True)
    small_grad = lax.psum(small_part, "dp")
    towers, n_in, n_out = grad.shape
    blocks = grad.reshape(towers, n_in // BLOCK, BLOCK, n_out // BLOCK, BLOCK)
    rotated = jnp.einsum(
        "trcai,tracb,trcbj->tricj", basis_left, blocks, basis_right, precision=lax.Precision.HIGHEST
    ).reshape(towers, n_in, n_out)
    first, second, direction = adam_part(moment_one, moment_two, rotated)
    turned = direction.reshape(towers, n_in // BLOCK, BLOCK, n_out // BLOCK, BLOCK)
    step_back = jnp.einsum(
        "trcai,tricj,trcbj->tracb", basis_left, turned, basis_right, precision=lax.Precision.HIGHEST
    ).reshape(towers, n_in, n_out)
    new_weights = weights - rate_main * (step_back + decay_weight * weights)
    new_average = ema_decay * average + (1.0 - ema_decay) * new_weights
    return (
        stitched,
        d_feat.astype(jnp.bfloat16),
        first,
        second,
        new_weights,
        new_average,
        new_weights.astype(jnp.bfloat16),
    ) + small_step(small_params, small_moment_one, small_moment_two, small_average, small_grad)


def solution(mesh):
    def body(features, counts, weights, *rest):
        dp, mp = mesh.shape["dp"], mesh.shape["mp"]
        tiles = features.shape[2] % 128 == 0 and weights.shape[2] % 128 == 0
        suits = dp == 4 and mp == 2 * dp and tiles and features.shape[1] % 64 == 0
        return (line_body if suits else plain_body)(features, counts, weights, *rest)

    return jax.shard_map(
        body,
        mesh=mesh,
        in_specs=(
            P(None, "dp", "mp"),
            P("dp"),
            P(None, "dp", "mp"),
            P(None, "mp"),
            P(None, "dp", "mp"),
            P(None, "dp", "mp"),
            P(None, "dp", "mp"),
            P(None, "dp", "mp"),
            P(None, "dp", "mp", None, None),
            P(None, "dp", "mp", None, None),
            P(None, "mp"),
            P(None, "mp"),
            P(None, "mp"),
        ),
        out_specs=(
            P(None, "dp", None),
            P(None, "dp", "mp"),
            P(None, "dp", "mp"),
            P(None, "dp", "mp"),
            P(None, "dp", "mp"),
            P(None, "dp", "mp"),
            P(None, "dp", "mp"),
            P(None, "mp"),
            P(None, "mp"),
            P(None, "mp"),
            P(None, "mp"),
        ),
        check_vma=False,
    )
```

```python
import functools
import math

import jax
import jax.numpy as jnp
from jax import lax
from jax.experimental import pallas as pl
from jax.experimental.pallas import tpu as pltpu
from jax.sharding import PartitionSpec as P

BLOCK = 64
STEP = 5


beta_one = 0.5
beta_two = 0.5
ema_decay = 0.5
rate_main = 0.01
rate_small = 0.05
decay_weight = 0.01
eps = 1e-08


def stitch_local(product, small, live_rows):
    pre_act = product + small[0:2][:, None, :]
    activated = jax.nn.gelu(pre_act, approximate=True)
    first = small[2] * activated[0] + small[3] * activated[1]
    second = small[4] * activated[0] + small[5] * activated[1]
    return jnp.stack([first, second]) * live_rows[None, :, None]


def adam_part(moment_a, moment_b, grad):
    first = beta_one * moment_a + (1.0 - beta_one) * grad
    second = beta_two * moment_b + (1.0 - beta_two) * grad * grad
    direction = first / (1.0 - beta_one**STEP) / (jnp.sqrt(second / (1.0 - beta_two**STEP)) + eps)
    return (first, second, direction)

def split(v):
    high = v.astype(jnp.bfloat16)
    return high, (v - high.astype(jnp.float32)).astype(jnp.bfloat16)

def soap_blocks(grads, lefts, rights, moments):
    row = lax.broadcasted_iota(jnp.int32, (2 * BLOCK, 2 * BLOCK), 0) // BLOCK
    lane = lax.broadcasted_iota(jnp.int32, (2 * BLOCK, 2 * BLOCK), 1) // BLOCK
    own = row == lane

    def diagonal(v):
        return jnp.where(own, jnp.concatenate([v, v], axis=0), jnp.zeros((), v.dtype))

    def stationary(high, low, axis):
        return jnp.concatenate([high, high, low], axis=axis)

    def moving(v, axis):
        high, low = split(v)
        return jnp.concatenate([high, low, high], axis=axis)

    def dots(a, b, ca, cb):
        dims = (((ca,), (cb,)), ((), ()))
        return [lax.dot_general(x, y, dims, preferred_element_type=jnp.float32) for x, y in zip(a, b)]

    right = [(diagonal(high), diagonal(low)) for high, low in rights]
    values = dots([moving(v, 1) for v in grads], [stationary(*v, 0) for v in right], 1, 0)
    values = dots([stationary(*v, 0) for v in lefts], [moving(v, 0) for v in values], 0, 0)
    values = [jnp.where(lane[:BLOCK] == 0, v[:BLOCK], v[BLOCK:]) for v in values]
    states = [adam_part(a, b, v) for (a, b), v in zip(moments, values)]
    values = dots([moving(v[2], 1) for v in states], [stationary(*v, 1) for v in right], 1, 1)
    values = dots([stationary(*v, 1) for v in lefts], [moving(diagonal(v), 0) for v in values], 1, 0)
    return [(first, second, step) for (first, second, _), step in zip(states, values)]


def soap_body(together, strips, full, parts_a, parts_b, stitched, d_a, d_b, weights, moment_a, moment_b, average, left, right,
              first, second, new_weights, new_average, copy, stitched_out, d_feat_out):
    groups, pairs = left.shape[2], left.shape[4] // BLOCK
    length = stitched.shape[1]
    row = jnp.minimum(pl.program_id(1) * pl.num_programs(2) + pl.program_id(2), strips - 1) * length

    first_tower = pl.program_id(0) == 0

    def clear(i, _):
        rows = pl.ds(pl.multiple_of(i * 16, 16), 16)
        wanted = row + i * 16 < full[0]
        stitched_out[0, rows] = jnp.where(wanted, stitched[0, rows], 0)
        d_feat_out[0, rows] = jnp.where(wanted, jnp.where(first_tower, d_a[rows], d_b[rows]), 0)
        return 0

    lax.fori_loop(0, length // 16, clear, 0)

    def blocks(g, _):
        places = [(g * together + s, q) for s in range(together) for q in range(pairs)]
        ats = [(0, pl.ds(pl.multiple_of(r * BLOCK, BLOCK), BLOCK), pl.ds(2 * BLOCK * q, 2 * BLOCK)) for r, q in places]
        grads = []
        for at in ats:
            grads.append(sum(jnp.where(first_tower, parts_a[(k,) + at], parts_b[(k,) + at]).astype(jnp.float32)
                             for k in range(parts_a.shape[0])))
        def basis(ref, r, q):
            return tuple(ref[0, 0, r, k, BLOCK * q : BLOCK * (q + 1)] for k in (0, 1))

        done = soap_blocks(grads, [basis(left, *place) for place in places], [basis(right, *place) for place in places],
                           [(moment_a[at], moment_b[at]) for at in ats])
        olds = [(weights[at], average[at]) for at in ats]
        for at, (one, two, step), (held, mean) in zip(ats, done, olds):
            first[at] = one
            second[at] = two
            fresh = held - rate_main * (step + decay_weight * held)
            new_weights[at] = fresh
            new_average[at] = ema_decay * mean + (1.0 - ema_decay) * fresh
            copy[at] = fresh.astype(jnp.bfloat16)
        return 0

    lax.fori_loop(0, groups // together, blocks, 0)


def soap(parts, wanted, stitched, d_feat, weights, moment_a, moment_b, average, bases, group=6):
    towers, rows, cols = weights.shape
    half = parts[0].shape[2]
    steps = half // (BLOCK * group)
    flat = lambda t, p, g: (t, p * steps + g, 0)
    state = pl.BlockSpec((1, BLOCK * group, cols), flat)
    base = [pl.BlockSpec((1, 1, group) + bases.shape[3:], lambda t, p, g, n=n: (n, t, p * steps + g, 0, 0, 0)) for n in (0, 1)]
    full = jax.ShapeDtypeStruct(weights.shape, jnp.float32)
    strips = max(n for n in range(1, 2 * steps + 1) if stitched.shape[1] % (16 * n) == 0)

    def strip(p, g):
        return jnp.minimum(p * steps + g, strips - 1)

    def through(shape):
        return pl.BlockSpec((1, shape[1] // strips, shape[2]), lambda t, p, g: (t, strip(p, g), 0))

    def of_tower(n, shape, index, last):
        return pl.BlockSpec(shape, lambda t, p, g: tuple(jnp.where(t == n, a, b) for a, b in zip(index(p, g), last if n == 0 else index(0, 0))))

    pieces = [of_tower(n, (v.shape[0], 1, BLOCK * group, cols), lambda p, g: (0, p, g, 0), (0, 1, steps - 1, 0)) for n, v in enumerate(parts)]
    rows_of = [of_tower(n, (v.shape[0] // strips, v.shape[1]), lambda p, g: (strip(p, g), 0), (strips - 1, 0)) for n, v in enumerate(d_feat)]

    return pl.pallas_call(
        functools.partial(soap_body, group, strips),
        grid=(towers, 2, steps),
        in_specs=[pl.BlockSpec(memory_space=pltpu.SMEM),
                  *pieces, through(stitched.shape), *rows_of, state, state, state, state, *base],
        out_specs=[state] * 5 + [through(stitched.shape), through((towers,) + d_feat[0].shape)],
        out_shape=[full] * 4 + [jax.ShapeDtypeStruct(weights.shape, jnp.bfloat16)]
        + [jax.ShapeDtypeStruct(v, jnp.bfloat16) for v in (stitched.shape, (towers,) + d_feat[0].shape)],
        compiler_params=pltpu.CompilerParams(vmem_limit_bytes=60 * 2**20),
        cost_estimate=pl.CostEstimate(flops=8 * 2 * towers * rows * cols * 64, bytes_accessed=130 * 2**20, transcendentals=0),
        name="soap",
    )(wanted, *parts, stitched, *d_feat, weights, moment_a, moment_b, average, bases, bases)


MESH = pl.DeviceIdType.MESH


def place():
    mp = lax.axis_index("mp")
    return lax.axis_index("dp"), mp // 2, lax.rem(mp, 2)


def meet(devices):
    barrier = pltpu.get_barrier_semaphore()
    expected = 0
    for here, device in devices:
        @pl.when(here)
        def _():
            pl.semaphore_signal(barrier, inc=1, device_id=device, device_id_type=MESH)
        expected = expected + jnp.where(here, 1, 0)
    pl.semaphore_wait(barrier, expected)


def gather_kernel(chips, ranges, f_ref, w_ref, fg_ref, wg_ref, f_send, f_recv, w_send, w_recv, own_sem):
    dp, chip, core = place()
    towers, rows, depth = f_ref.shape
    cols = w_ref.shape[2]
    across, along = dp ^ 1, dp ^ 2
    at = lambda c, k: (c, 2 * chip + k)

    meet([(chip > 0, (dp, 2 * (chip - 1) + core)), (chip < chips - 1, (dp, 2 * (chip + 1) + core)),
          (chip >= 0, at(dp, 1 - core))] + [(chip >= 0, at(c, k)) for c in (across, along) for k in (0, 1)])

    def copies(step, way, t, k, shard, there):
        lanes = pl.ds(pl.multiple_of(shard * depth, 128), depth)
        rws = pl.ds(*ranges[k])
        src = fg_ref.at[t, rws, lanes]
        if step == 0:
            src = f_ref.at[t, rws]
        n = ((way * (chips - 1) + step) * towers + t) * len(ranges) + k
        return pltpu.make_async_remote_copy(
            src_ref=src, dst_ref=fg_ref.at[t, rws, lanes], send_sem=f_send.at[n], recv_sem=f_recv.at[n],
            device_id=(dp, 2 * there + core), device_id_type=MESH)

    def feature(step, way, t, k):
        return copies(step, way, t, k, chip - step if way == 0 else chip + step, chip + 1 if way == 0 else chip - 1)

    def incoming(step, way, t, k):
        return copies(step, way, t, k, chip - 1 - step if way == 0 else chip + 1 + step, chip)

    def sends(step, way):
        return (chip < chips - 1) & (chip >= step) if way == 0 else (chip > 0) & (chip + step < chips)

    def receives(step, way):
        return chip > step if way == 0 else chip + step < chips - 1

    def launch(t, k):
        for way in (0, 1):
            @pl.when(sends(0, way))
            def _():
                feature(0, way, t, k).start()

    def block(owner, slot, t):
        return wg_ref.at[t, pl.ds(pl.multiple_of(owner * depth, 128), depth), pl.ds(pl.multiple_of(slot * cols, 128), cols)]

    def weight(kind, k, t):
        to = at((across, along, dp)[kind], k)
        n = (kind * 2 + core) * 2 + t
        return pltpu.make_async_remote_copy(
            src_ref=w_ref.at[t, pl.ds(pl.multiple_of(k * depth, 128), depth)], dst_ref=block(dp, k ^ core, t),
            send_sem=w_send.at[(kind * 2 + k) * 2 + t], recv_sem=w_recv.at[n], device_id=to, device_id_type=MESH)

    def forward(kind, slot):
        owner, to, t = ((across, along, 0), (along, across, 1))[kind]
        n = 12 + kind * 2 + slot
        return pltpu.make_async_remote_copy(
            src_ref=block(owner, slot, t), dst_ref=block(owner, slot, t),
            send_sem=w_send.at[n], recv_sem=w_recv.at[n], device_id=at(to, core), device_id_type=MESH)

    def arrived(kind, slot, t):
        owner = (across, along, dp)[kind]
        n = (kind * 2 + (slot ^ core)) * 2 + t
        pltpu.make_async_remote_copy(
            src_ref=block(owner, slot, t), dst_ref=block(owner, slot, t), send_sem=w_send.at[n], recv_sem=w_recv.at[n],
            device_id=at(dp, core), device_id_type=MESH).wait_recv()

    mine = pl.ds(pl.multiple_of(chip * depth, 128), depth)
    own = [pltpu.make_async_copy(f_ref.at[t], fg_ref.at[t, :, mine], own_sem.at[t]) for t in range(towers)]
    own += [pltpu.make_async_copy(w_ref.at[t, pl.ds(pl.multiple_of(core * depth, 128), depth)], block(dp, 0, t), own_sem.at[2 + t])
            for t in range(towers)]

    pieces = [(t, k) for k in range(len(ranges)) for t in range(towers)]
    for t, k in pieces:
        launch(t, k)
    for copy in own:
        copy.start()
    for t in (0, 1):
        for k in (0, 1):
            weight(0, k, t).start()
            weight(1, k, 1 - t).start()
    for t in (0, 1):
        weight(2, 1 - core, t).start()

    for step in range(chips - 1):
        for t, k in pieces:
            for way in (0, 1):
                @pl.when(receives(step, way))
                def _():
                    incoming(step, way, t, k).wait_recv()
                if step + 1 < chips - 1:
                    @pl.when(sends(step + 1, way))
                    def _():
                        feature(step + 1, way, t, k).start()
            if step == 0 and (t, k) == pieces[-1]:
                for slot in (0, 1):
                    arrived(0, slot, 0)
                    forward(0, slot).start()
                    arrived(1, slot, 1)
                    forward(1, slot).start()

    for slot in (0, 1):
        arrived(0, slot, 1)
        arrived(1, slot, 0)
        forward(0, slot).wait_recv()
        forward(1, slot).wait_recv()
    for t in (0, 1):
        arrived(2, 1, t)
    for t in (0, 1):
        for k in (0, 1):
            weight(0, k, t).wait_send()
            weight(1, k, t).wait_send()
        weight(2, 1 - core, t).wait_send()
    for slot in (0, 1):
        forward(0, slot).wait_send()
        forward(1, slot).wait_send()
    for step in range(chips - 1):
        for t, k in pieces:
            for way in (0, 1):
                @pl.when(sends(step, way))
                def _():
                    feature(step, way, t, k).wait_send()
    for copy in own:
        copy.wait()


def gather(features, weights_low, chips, ranges, ident):
    towers, rows, depth = features.shape
    cols = weights_low.shape[2]
    count = 2 * (chips - 1) * towers * len(ranges)
    dma = pltpu.SemaphoreType.DMA
    anywhere = pl.BlockSpec(memory_space=pl.ANY)
    return pl.pallas_call(
        functools.partial(gather_kernel, chips, ranges),
        out_shape=[jax.ShapeDtypeStruct((towers, rows, chips * depth), jnp.bfloat16),
                   jax.ShapeDtypeStruct((towers, chips * depth, 2 * cols), jnp.bfloat16)],
        in_specs=[anywhere] * 2,
        out_specs=[anywhere] * 2,
        scratch_shapes=[dma((count,)), dma((count,)), dma((16,)), dma((16,)), dma((4,))],
        compiler_params=pltpu.CompilerParams(collective_id=ident, has_side_effects=True),
        cost_estimate=pl.CostEstimate(flops=0, bytes_accessed=800 * 2**20, transcendentals=0),
        name="gather",
    )(features, weights_low)


def reduce_kernel(chips, ranges, pd_ref, pg_ref, ps_ref, d_ref, gr_ref, sr_ref, held, term, total,
                  d_send, d_recv, t_sem, o_sem, g_send, g_recv, s_send, s_recv, own_sem):
    dp, chip, core = place()
    towers, rows, depth = d_ref.shape
    cols = pg_ref.shape[2] // 2
    across, along = dp ^ 1, dp ^ 2
    others = (across, along, dp ^ 3)
    at = lambda c, k: (c, 2 * chip + k)

    meet([(chip > 0, (dp, 2 * (chip - 1) + core)), (chip < chips - 1, (dp, 2 * (chip + 1) + core)),
          (chip >= 0, at(dp, 1 - core))] + [(chip >= 0, at(c, k)) for c in others for k in (0, 1)])

    def grad(kind, k, t):
        owner = (others + (dp,))[kind]
        return pltpu.make_async_remote_copy(
            src_ref=pg_ref.at[t, pl.ds(pl.multiple_of(owner * depth, 128), depth), pl.ds(pl.multiple_of((k ^ core) * cols, 128), cols)],
            dst_ref=gr_ref.at[dp, core, t], send_sem=g_send.at[(kind * 2 + k) * 2 + t],
            recv_sem=g_recv.at[(kind * 2 + core) * 2 + t], device_id=at(owner, k), device_id_type=MESH)

    def grad_arrived(kind, k, t):
        owner = (others + (dp,))[kind]
        pltpu.make_async_remote_copy(
            src_ref=gr_ref.at[owner, k, t], dst_ref=gr_ref.at[owner, k, t], send_sem=g_send.at[0],
            recv_sem=g_recv.at[(kind * 2 + k) * 2 + t], device_id=at(dp, core), device_id_type=MESH).wait_recv()

    def small(kind):
        return pltpu.make_async_remote_copy(
            src_ref=ps_ref, dst_ref=sr_ref.at[dp], send_sem=s_send.at[kind], recv_sem=s_recv.at[kind],
            device_id=at(others[kind], core), device_id_type=MESH)

    def target(step, way):
        return chip + chips - 1 - step if way == 0 else chip - (chips - 1 - step)

    def sends(step, way):
        return (chip < chips - 1) & (chip <= step) if way == 0 else (chip > 0) & (chips - 1 - chip <= step)

    def receives(step, way):
        return (chip > 0) & (chip <= step + 1) if way == 0 else (chip < chips - 1) & (chips - 1 - chip <= step + 1)

    def own_term(goal, t, k):
        return pd_ref.at[t, pl.ds(*ranges[k]), pl.ds(pl.multiple_of(goal * depth, 128), depth)]

    def partial(step, way, t, k, first):
        n = ((way * (chips - 1) + step) * towers + t) * len(ranges) + k
        src = own_term(target(step, way), t, k) if first else held.at[way, step - 1, t, pl.ds(*ranges[k])]
        there = chip + 1 if way == 0 else chip - 1
        return pltpu.make_async_remote_copy(
            src_ref=src, dst_ref=held.at[way, step, t, pl.ds(*ranges[k])], send_sem=d_send.at[n], recv_sem=d_recv.at[n],
            device_id=(dp, 2 * there + core), device_id_type=MESH)

    def landed(step, way, t, k):
        n = ((way * (chips - 1) + step) * towers + t) * len(ranges) + k
        ref = held.at[way, step, t, pl.ds(*ranges[k])]
        pltpu.make_async_remote_copy(src_ref=ref, dst_ref=ref, send_sem=d_send.at[n], recv_sem=d_recv.at[n],
                                     device_id=(dp, 2 * chip + core), device_id_type=MESH).wait_recv()

    pieces = [(t, k) for t in range(towers) for k in range(len(ranges))]
    ends = (chip == 0, chip == chips - 1)
    for t, k in pieces:
        for way in (0, 1):
            @pl.when(ends[way])
            def _():
                partial(0, way, t, k, True).start()
    own = [pltpu.make_async_copy(
        pg_ref.at[t, pl.ds(pl.multiple_of(dp * depth, 128), depth), pl.ds(0, cols)], gr_ref.at[dp, core, t], own_sem.at[t])
        for t in range(towers)]
    own.append(pltpu.make_async_copy(ps_ref, sr_ref.at[dp], own_sem.at[towers]))
    for copy in own:
        copy.start()
    for kind in range(3):
        small(kind).start()
    for t in range(towers):
        for kind in (2, 0, 1):
            for k in (0, 1):
                grad(kind, k, t).start()
        grad(3, 1 - core, t).start()

    strip = 16

    for step in range(1, chips - 1):
        for t, k in pieces:
            for way in (0, 1):
                @pl.when(sends(step, way) & ends[way])
                def _():
                    partial(step, way, t, k, True).start()

                @pl.when(sends(step, way) & jnp.logical_not(ends[way]))
                def _():
                    start, size = ranges[k]
                    load = pltpu.make_async_copy(own_term(target(step, way), t, k), term.at[way, pl.ds(0, size)], t_sem.at[way])
                    load.start()
                    landed(step - 1, way, t, k)
                    load.wait()

                    def add(i, _):
                        rws = pl.ds(pl.multiple_of(i * strip, strip), strip)
                        all_rows = pl.ds(pl.multiple_of(start + i * strip, strip), strip)
                        held[way, step - 1, t, all_rows] = (
                            held[way, step - 1, t, all_rows].astype(jnp.float32) + term[way, rws].astype(jnp.float32)
                        ).astype(jnp.bfloat16)
                        return 0
                    lax.fori_loop(0, size // strip, add, 0)
                    partial(step, way, t, k, False).start()

    stores = []
    for n, (t, k) in enumerate(pieces):
        s = n % 2
        start, size = ranges[k]
        load = pltpu.make_async_copy(own_term(chip, t, k), term.at[s, pl.ds(0, size)], t_sem.at[s])
        load.start()
        for way in (0, 1):
            @pl.when(receives(chips - 2, way))
            def _():
                landed(chips - 2, way, t, k)
        load.wait()
        if n >= 2:
            stores[n - 2].wait()

        def finish(i, _):
            rws = pl.ds(pl.multiple_of(i * strip, strip), strip)
            all_rows = pl.ds(pl.multiple_of(start + i * strip, strip), strip)
            value = term[s, rws].astype(jnp.float32)
            for way in (0, 1):
                here = receives(chips - 2, way)
                value = value + jnp.where(here, held[way, chips - 2, t, all_rows].astype(jnp.float32), 0.0)
            total[s, rws] = value.astype(jnp.bfloat16)
            return 0
        lax.fori_loop(0, size // strip, finish, 0)
        stores.append(pltpu.make_async_copy(total.at[s, pl.ds(0, size)], d_ref.at[t, pl.ds(start, size)], o_sem.at[s]))
        stores[n].start()
    for store in stores[-2:]:
        store.wait()

    for t in range(towers):
        for kind in range(3):
            for k in (0, 1):
                grad_arrived(kind, k, t)
        grad_arrived(3, 1 - core, t)
    for kind in range(3):
        small(kind).wait()
    for t in range(towers):
        for kind in range(3):
            for k in (0, 1):
                grad(kind, k, t).wait_send()
        grad(3, 1 - core, t).wait_send()
    for step in range(chips - 1):
        for t, k in pieces:
            for way in (0, 1):
                @pl.when(sends(step, way))
                def _():
                    partial(step, way, t, k, True).wait_send()
    for copy in own:
        copy.wait()


def reduce(partial_d, partial_g, partial_s, chips, ranges, ident):
    towers, rows, wide = partial_d.shape
    depth, cols = wide // chips, partial_g.shape[2] // 2
    count = 2 * (chips - 1) * towers * len(ranges)
    part = max(size for _, size in ranges)
    dma = pltpu.SemaphoreType.DMA
    bf16 = jnp.bfloat16
    out_shape = [jax.ShapeDtypeStruct((towers, rows, depth), bf16),
                 jax.ShapeDtypeStruct((4, 2, towers, depth, cols), bf16),
                 jax.ShapeDtypeStruct((4,) + partial_s.shape, jnp.float32)]
    return pl.pallas_call(
        functools.partial(reduce_kernel, chips, ranges),
        out_shape=out_shape,
        in_specs=[pl.BlockSpec(memory_space=pl.ANY)] * 3,
        out_specs=[pl.BlockSpec(memory_space=pl.ANY)] * len(out_shape),
        scratch_shapes=[pltpu.VMEM((2, chips - 1, towers, rows, depth), bf16),
                        pltpu.VMEM((2, part, depth), bf16), pltpu.VMEM((2, part, depth), bf16),
                        dma((count,)), dma((count,)), dma((2,)), dma((2,)), dma((16,)), dma((16,)), dma((3,)), dma((3,)), dma((towers + 1,))],
        compiler_params=pltpu.CompilerParams(collective_id=ident, has_side_effects=True, vmem_limit_bytes=56 * 2**20),
        cost_estimate=pl.CostEstimate(flops=0, bytes_accessed=800 * 2**20, transcendentals=0),
        name="reduce",
    )(partial_d, partial_g, partial_s)


def loop(count, body):
    def step(i, _):
        body(i)
        return 0
    lax.fori_loop(0, count, step, 0)


def wait_for(ref, sem, other):
    pltpu.make_async_remote_copy(src_ref=ref, dst_ref=ref, send_sem=other, recv_sem=sem, device_id=dict(dp=0, mp=0),
                                 device_id_type=MESH).wait_recv()


class Spot:
    def __init__(self, chips):
        self.dp, self.chip, self.core = place()
        self.chips, self.steps = chips, chips - 1
        self.others = (self.dp ^ 1, self.dp ^ 2, self.dp ^ 3)
        self.ends = (self.chip == 0) | (self.chip == self.steps)

    def at(self, dp, core):
        return dp, 2 * self.chip + core

    def on_line(self, chip):
        return self.dp, 2 * chip + self.core

    def passed(self, way):
        return jnp.where(way == 0, self.chip, self.steps - self.chip)

    def onward(self, way, n):
        return jnp.where(way == 0, self.chip + n, self.chip - n)

    def leaves(self, step, way):
        return (self.passed(way) < self.steps) & (self.passed(way) >= step)

    def comes(self, step, way):
        return self.passed(way) > step

    def greet(self):
        meet([(self.chip > 0, self.on_line(self.chip - 1)), (self.chip < self.steps, self.on_line(self.chip + 1)),
              (self.chip >= 0, self.at(self.dp, 1 - self.core))]
             + [(self.chip >= 0, self.at(c, k)) for c in self.others for k in (0, 1)])


class Features:
    def __init__(self, spot, f_ref, taken, fg, size, send, recv):
        self.spot, self.f_ref, self.taken, self.fg, self.size, self.send, self.recv = spot, f_ref, taken, fg, size, send, recv
        self.depth = f_ref.shape[1]

    def rows(self, q):
        return pl.ds(pl.multiple_of(q * self.size, 16), self.size)

    def lanes(self, shard):
        return pl.ds(pl.multiple_of(shard * self.depth, 128), self.depth)

    def copy(self, step, way, q, src=None):
        ref = self.fg.at[self.rows(q), self.lanes(self.spot.onward(way, -step))]
        return pltpu.make_async_remote_copy(
            src_ref=ref if src is None else src, dst_ref=ref, send_sem=self.send.at[way, step, q], recv_sem=self.recv.at[way, step, q],
            device_id=self.spot.on_line(self.spot.onward(way, 1)), device_id_type=MESH)

    def launch(self, q, last):
        def each(way):
            @pl.when(self.spot.leaves(0, way))
            def _():
                self.copy(0, way, q, self.taken if last else self.f_ref.at[self.rows(q)]).start()
        loop(2, each)

    def arrive(self, step, q):
        def each(way):
            @pl.when(self.spot.comes(step, way))
            def _():
                ref = self.fg.at[self.rows(q), self.lanes(self.spot.onward(way, -1 - step))]
                wait_for(ref, self.recv.at[way, step, q], self.send.at[way, step, q])
        loop(2, each)

    def serve(self, step, q):
        self.arrive(step, q)

        def each(way):
            @pl.when(self.spot.leaves(step + 1, way))
            def _():
                self.copy(step + 1, way, q).start()
        loop(2, each)

    def settle(self, q):
        for step in range(self.spot.steps):
            def each(way):
                @pl.when(self.spot.leaves(step, way))
                def _():
                    self.copy(step, way, q).wait_send()
            loop(2, each)


class Weights:
    def __init__(self, spot, low, wg, own_sem, send, recv):
        self.spot, self.low, self.wg, self.own_sem, self.send, self.recv = spot, low, wg, own_sem, send, recv
        self.depth, self.cols = low.shape[1], low.shape[2]

    def block(self, owner, slot):
        return self.wg.at[pl.ds(pl.multiple_of(owner * self.depth, 128), self.depth), pl.ds(pl.multiple_of(slot * self.cols, 128), self.cols)]

    def round(self, w_ref, wide, sem):
        part = wide.shape[1]
        parts = self.depth // part

        def load(n):
            return pltpu.make_async_copy(w_ref.at[pl.ds(pl.multiple_of(n * part, 16), part)], wide.at[lax.rem(n, 2)], sem.at[lax.rem(n, 2)])

        def one(n):
            @pl.when(n + 1 < 2 * parts)
            def _():
                load(n + 1).start()
            load(n).wait()

            def strip(i):
                rows = pl.ds(pl.multiple_of(i * 16, 16), 16)
                to = pl.ds(pl.multiple_of(lax.rem(n, parts) * part + i * 16, 16), 16)
                self.low[n // parts, to] = wide[lax.rem(n, 2), rows].astype(jnp.bfloat16)
            loop(part // 16, strip)
        load(jnp.int32(0)).start()
        loop(2 * parts, one)

    def send_own(self, kind, slot):
        s = self.spot
        k = s.core ^ slot
        return pltpu.make_async_remote_copy(
            src_ref=self.low.at[k], dst_ref=self.block(s.dp, slot), send_sem=self.send.at[kind, slot], recv_sem=self.recv.at[kind, slot],
            device_id=s.at((s.others[0], s.others[1], s.dp)[kind], k), device_id_type=MESH)

    def send_on(self, kind):
        s = self.spot
        ref = self.block(s.others[kind], kind)
        return pltpu.make_async_remote_copy(
            src_ref=ref, dst_ref=ref, send_sem=self.send.at[3, kind], recv_sem=self.recv.at[3, kind],
            device_id=s.at(s.others[1 - kind], s.core), device_id_type=MESH)

    def arrive(self, kind, slot):
        owner = (self.spot.others[0], self.spot.others[1], self.spot.dp)[kind]
        wait_for(self.block(owner, slot), self.recv.at[kind, slot], self.send.at[kind, slot])

    def own(self):
        return pltpu.make_async_copy(self.low.at[self.spot.core], self.block(self.spot.dp, 0), self.own_sem)

    def start(self):
        self.own().start()
        for slot in (0, 1):
            self.send_own(0, slot).start()
            self.send_own(1, 1 - slot).start()
        self.send_own(2, 1).start()

    def relay(self):
        for kind in (0, 1):
            self.arrive(kind, kind)
            self.send_on(kind).start()

    def finish(self):
        for kind in (0, 1):
            self.arrive(kind, 1 - kind)
            wait_for(self.block(self.spot.others[2], kind), self.recv.at[3, kind], self.send.at[3, kind])
        self.arrive(2, 1)
        self.own().wait()

    def settle(self):
        for kind in (0, 1):
            for slot in (0, 1):
                self.send_own(kind, slot).wait_send()
            self.send_on(kind).wait_send()
        self.send_own(2, 1).wait_send()


class Products:
    def __init__(self, spot, features, wg, f_tile, w_tile, acc, theirs, f_sem, w_sem, send, recv):
        self.spot, self.features, self.wg, self.f_tile, self.w_tile, self.acc, self.theirs = spot, features, wg, f_tile, w_tile, acc, theirs
        self.f_sem, self.w_sem, self.send, self.recv = f_sem, w_sem, send, recv
        self.cols = theirs.shape[1]

    def shard(self, j):
        return jnp.where(self.spot.chip == self.spot.steps, self.spot.steps - j, j)

    def load_w(self, j):
        depth = self.features.depth
        rows = pl.ds(pl.multiple_of(self.shard(j) * depth, 128), depth)
        return pltpu.make_async_copy(self.wg.at[rows], self.w_tile.at[lax.rem(j, 2)], self.w_sem.at[lax.rem(j, 2)])

    def load_f(self, j):
        lanes = self.features.lanes(self.shard(j))
        return pltpu.make_async_copy(self.features.fg.at[:, lanes], self.f_tile.at[lax.rem(j, 2)], self.f_sem.at[lax.rem(j, 2)])

    def here(self, j):
        return (j < self.spot.steps) | jnp.logical_not(self.spot.ends)

    def add(self, slot, rows):
        for col in range(0, 2 * self.cols, self.cols):
            lanes = pl.ds(col, self.cols)
            self.acc[rows, lanes] += jnp.dot(self.f_tile[slot, rows], self.w_tile[slot, :, lanes], preferred_element_type=jnp.float32)

    def multiply(self):
        def unit(j):
            @pl.when(j < self.spot.steps)
            def _():
                self.load_w(j + 1).start()

            @pl.when((j < self.spot.steps) & self.here(j + 1))
            def _():
                self.load_f(j + 1).start()
            self.load_w(j).wait()

            @pl.when(self.here(j))
            def _():
                self.load_f(j).wait()
                loop(self.acc.shape[0] // self.features.size, lambda q: self.add(lax.rem(j, 2), self.features.rows(q)))
        self.load_w(jnp.int32(0)).start()
        self.load_f(jnp.int32(0)).start()
        loop(self.spot.chips, unit)

    def swap(self, q):
        rows = self.features.rows(q)
        return pltpu.make_async_remote_copy(
            src_ref=self.acc.at[rows, pl.ds(self.cols, self.cols)], dst_ref=self.theirs.at[rows], send_sem=self.send.at[q],
            recv_sem=self.recv.at[q], device_id=self.spot.at(self.spot.dp, 1 - self.spot.core), device_id_type=MESH)

    def complete(self, q):
        slot = self.spot.steps % 2
        self.features.arrive(self.spot.steps - 1, q)

        @pl.when(self.spot.ends)
        def _():
            rows = self.features.rows(q)
            copy = pltpu.make_async_copy(self.features.fg.at[rows, self.features.lanes(self.shard(self.spot.steps))],
                                         self.f_tile.at[slot, rows], self.f_sem.at[slot])
            copy.start()
            copy.wait()
            self.add(slot, rows)
        self.swap(q).start()


class Backward:
    def __init__(self, spot, size, dz_here, dz_ref, send, recv, out_sem):
        self.spot, self.size, self.dz_here, self.dz_ref, self.send, self.recv, self.out_sem = spot, size, dz_here, dz_ref, send, recv, out_sem
        self.cols = dz_here.shape[1]

    def rows(self, q):
        return pl.ds(pl.multiple_of(q * self.size, 16), self.size)

    def swap(self, q):
        return pltpu.make_async_remote_copy(
            src_ref=self.dz_here.at[self.rows(q)], dst_ref=self.dz_ref.at[self.rows(q), pl.ds(self.cols, self.cols)],
            send_sem=self.send.at[q], recv_sem=self.recv.at[q], device_id=self.spot.at(self.spot.dp, 1 - self.spot.core), device_id_type=MESH)

    def keep(self, q):
        return pltpu.make_async_copy(self.dz_here.at[self.rows(q)], self.dz_ref.at[self.rows(q), pl.ds(0, self.cols)], self.out_sem.at[q])

    def start(self, q):
        self.swap(q).start()
        self.keep(q).start()

    def settle(self, q):
        self.swap(q).wait_recv()
        self.swap(q).wait_send()
        self.keep(q).wait()


def gelu_and_slope(v):
    factor, cubic = math.sqrt(2.0 / math.pi), 0.044715
    square = v * v
    th = jnp.tanh(factor * (v + cubic * (square * v)))
    slope = 0.5 * (1.0 + th) + 0.5 * v * (1.0 - th * th) * (factor * (1.0 + 3.0 * cubic * square))
    return 0.5 * v * (1.0 + th), slope


def live_rows_of(tot, share, live):
    keep = share[0][0]
    cols = live.shape[1]

    def strip(i):
        row = lax.broadcasted_iota(jnp.int32, (16, cols), 0).astype(jnp.float32) + (i * 16).astype(jnp.float32)
        here = jnp.where(row < tot[0, :1, :cols], 1.0, 0.0)
        there = jnp.zeros_like(here)
        for kind in range(4):
            count = tot[kind, :1, :cols]
            slot = row + float(share[kind][0] - keep)
            valid = (slot < count) & (count > keep)
            if kind == 3:
                valid = valid & (slot >= share[2][0] + share[2][1])
            there = there + jnp.where(valid, 1.0, 0.0)
        live[pl.ds(pl.multiple_of(i * 16, 16), 16)] = jnp.where(row < keep, here, there)
    loop(live.shape[0] // 16, strip)


def clear(ref):
    def strip(i):
        ref[pl.ds(pl.multiple_of(i * 16, 16), 16)] = jnp.zeros((16, ref.shape[1]), ref.dtype)
    loop(ref.shape[0] // 16, strip)


def fold(term):
    return term[:8] + term[8:]


class Grads:
    jobs, thirds = 8, 3

    def __init__(self, spot, fg, dz_here, gr, pg, relay, f_part, g_part, r_part, f_sem, g_sem, r_sem, send, recv, relay_send, relay_recv, own_sem):
        self.spot, self.fg, self.dz_here, self.gr, self.pg, self.relay_ref = spot, fg, dz_here, gr, pg, relay
        self.f_part, self.g_part, self.r_part, self.f_sem, self.g_sem, self.r_sem = f_part, g_part, r_part, f_sem, g_sem, r_sem
        self.send, self.recv, self.relay_send, self.relay_recv, self.own_sem = send, recv, relay_send, relay_recv, own_sem
        self.depth, self.cols = pg.shape[1], pg.shape[2]
        self.part = self.depth // self.thirds

    def owner_of(self, m):
        return jnp.where(m < 2, 3, jnp.where((m == 4) | (m == 5), 0, jnp.where((m == 2) | (m == 7), 1, 2)))

    def third(self, n):
        return pl.ds(pl.multiple_of(lax.rem(n, self.thirds) * self.part, 128), self.part)

    def load(self, n):
        first = (self.spot.dp ^ self.owner_of(n // self.thirds)) * self.depth + lax.rem(n, self.thirds) * self.part
        return pltpu.make_async_copy(self.fg.at[:, pl.ds(pl.multiple_of(first, 128), self.part)], self.f_part.at[lax.rem(n, 2)],
                                     self.f_sem.at[lax.rem(n, 2)])

    def store(self, n):
        return pltpu.make_async_copy(self.g_part.at[lax.rem(n, 2)], self.pg.at[n // self.thirds, self.third(n)], self.g_sem.at[lax.rem(n, 2)])

    def relay(self, m):
        return pltpu.make_async_remote_copy(
            src_ref=self.pg.at[m], dst_ref=self.relay_ref.at[m], send_sem=self.relay_send.at[m], recv_sem=self.relay_recv.at[m],
            device_id=self.spot.at(self.spot.dp ^ (m + 1), self.spot.core), device_id_type=MESH)

    def relayed(self, n):
        return pltpu.make_async_copy(self.relay_ref.at[jnp.maximum(n // self.thirds - (self.jobs - 2), 0), self.third(n)],
                                     self.r_part.at[lax.rem(n, 2)], self.r_sem.at[lax.rem(n, 2)])

    def job(self, m):
        joins = m >= self.jobs - 2
        lanes = pl.ds(pl.multiple_of(lax.rem(m, 2) * self.cols, 128), self.cols)

        @pl.when(joins)
        def _():
            k = jnp.maximum(m - (self.jobs - 2), 0)
            wait_for(self.relay_ref.at[k], self.relay_recv.at[k], self.relay_send.at[k])
            self.relayed(m * self.thirds).start()

        def part(c):
            n = m * self.thirds + c

            @pl.when(joins & (c + 1 < self.thirds))
            def _():
                self.relayed(n + 1).start()

            @pl.when(n + 1 < self.jobs * self.thirds)
            def _():
                self.load(n + 1).start()
            self.load(n).wait()

            @pl.when((n >= 2) & (n != (self.jobs - 2) * self.thirds) & (n != (self.jobs - 2) * self.thirds + 1))
            def _():
                self.store(n - 2).wait()

            @pl.when(joins)
            def _():
                self.relayed(n).wait()
            value = lax.dot_general(self.f_part[lax.rem(n, 2)], self.dz_here[:, lanes], (((0,), (0,)), ((), ())),
                                    preferred_element_type=jnp.float32)

            @pl.when(joins)
            def _():
                self.g_part[lax.rem(n, 2)] = (value + self.r_part[lax.rem(n, 2)].astype(jnp.float32)).astype(jnp.bfloat16)

            @pl.when(jnp.logical_not(joins))
            def _():
                self.g_part[lax.rem(n, 2)] = value.astype(jnp.bfloat16)
            self.store(n).start()
        loop(self.thirds, part)

    def copy(self, m):
        away, k = self.owner_of(m), self.spot.core ^ lax.rem(m, 2)
        return pltpu.make_async_remote_copy(
            src_ref=self.pg.at[m], dst_ref=self.gr.at[away, self.spot.core], send_sem=self.send.at[m],
            recv_sem=self.recv.at[away, self.spot.core], device_id=self.spot.at(self.spot.dp ^ away, k), device_id_type=MESH)

    def own(self):
        return pltpu.make_async_copy(self.pg.at[4], self.gr.at[0, self.spot.core], self.own_sem)

    def start(self, m):
        @pl.when(m < 2)
        def _():
            self.relay(jnp.minimum(m, 1)).start()

        @pl.when((m >= 2) & (m != 4))
        def _():
            self.copy(m).start()

        @pl.when(m == 4)
        def _():
            self.own().start()

    def turn(self, m, begin, late):
        early = self.jobs - 2
        pause = begin + early

        def job_at(m):
            return jnp.where(m < pause, m - begin, m - late + early)

        @pl.when((m == pause) | (m == late + 2))
        def _():
            for c in (1, 2):
                self.store(job_at(m - 1) * self.thirds + c).wait()

        @pl.when(((m >= begin) & (m < pause)) | (m == late) | (m == late + 1))
        def _():
            self.job(job_at(m))

        @pl.when(((m > begin) & (m <= pause)) | (m == late + 1) | (m == late + 2))
        def _():
            self.start(job_at(m - 1))

    def settle(self):
        for away in range(3):
            for k in (0, 1):
                @pl.when((away != 0) | (self.spot.core != k))
                def _():
                    wait_for(self.gr.at[away, k], self.recv.at[away, k], self.send.at[2])
        self.own().wait()
        for m in range(self.jobs):
            if m < 2:
                self.relay(m).wait_send()
            elif m != 4:
                self.copy(jnp.int32(m)).wait_send()


class Sums:
    window, lag = 5, 1

    def __init__(self, spot, parts, share, d_ref, dz_here, w_here, held, total, send, recv, out_sem, back_send, back_recv):
        self.spot, self.parts, self.share, self.d_ref, self.dz_here, self.w_here, self.held, self.total = spot, parts, share, d_ref, dz_here, w_here, held, total
        self.send, self.recv, self.out_sem, self.back_send, self.back_recv = send, recv, out_sem, back_send, back_recv
        self.size, self.depth = total.shape[1], total.shape[2]
        self.turns = spot.steps * parts
        self.skip = self.size - share[0][1]

    def rows(self, piece):
        return pl.ds(pl.multiple_of(lax.rem(piece + self.parts - 1, self.parts) * self.size, 16), self.size)

    def third(self, n):
        return pl.ds(pl.multiple_of(n * (self.depth // 3), 128), self.depth // 3)

    def sends(self, step, way):
        return (self.spot.passed(way) < self.spot.steps) & (self.spot.passed(way) <= step)

    def passing(self, m, way, turn):
        rows = self.rows(lax.rem(m, self.parts))
        return pltpu.make_async_remote_copy(
            src_ref=self.held.at[way, turn // self.parts, rows], dst_ref=self.held.at[way, m // self.parts, rows],
            send_sem=self.send.at[way, m], recv_sem=self.recv.at[way, m], device_id=self.spot.on_line(self.spot.onward(way, 1)),
            device_id_type=MESH)

    def landed(self, m, way):
        wait_for(self.held.at[way, m // self.parts, self.rows(lax.rem(m, self.parts))], self.recv.at[way, m], self.send.at[way, m])

    def product(self, goal, rows, col):
        return lax.dot_general(self.dz_here[rows], self.w_here[goal, self.third(col)], (((1,), (1,)), ((), ())),
                               preferred_element_type=jnp.float32)

    def store(self, piece):
        s = lax.rem(piece, 2)
        return pltpu.make_async_copy(self.total.at[s], self.d_ref.at[self.rows(piece)], self.out_sem.at[s])

    def hand(self, kind):
        to, taken = share_rows(self.share, kind)
        return pltpu.make_async_remote_copy(
            src_ref=self.total.at[0, pl.ds(self.skip + taken.start, taken.size)], dst_ref=self.d_ref.at[to], send_sem=self.back_send.at[kind],
            recv_sem=self.back_recv.at[kind], device_id=self.spot.at(self.spot.others[kind], self.spot.core), device_id_type=MESH)

    def send_sum(self, m, way):
        step, rows = m // self.parts, self.rows(lax.rem(m, self.parts))
        first = self.spot.passed(way) == 0
        held = self.held

        @pl.when(first & (m >= self.window))
        def _():
            self.passing(jnp.maximum(m - self.window, 0), way, 0).wait_send()

        @pl.when(jnp.logical_not(first))
        def _():
            self.landed(m - self.parts, way)

        def column(col):
            lanes = self.third(col)
            value = self.product(self.spot.onward(way, self.spot.steps - step), rows, col)

            @pl.when(first)
            def _():
                held[way, step, rows, lanes] = value.astype(jnp.bfloat16)

            @pl.when(jnp.logical_not(first))
            def _():
                held[way, step - 1, rows, lanes] = (value + held[way, step - 1, rows, lanes].astype(jnp.float32)).astype(jnp.bfloat16)
        loop(3, column)
        self.passing(m, way, jnp.where(first, m, m - self.parts)).start()

    def finish(self, piece):
        rows, s = self.rows(piece), lax.rem(piece, 2)
        held, total, last = self.held, self.total, self.spot.steps - 1

        @pl.when(piece >= 2)
        def _():
            self.store(piece - 2).wait()

        @pl.when(piece == 2)
        def _():
            for kind in range(3):
                self.hand(kind).wait_send()

        def each(way):
            @pl.when(self.spot.passed(way) > 0)
            def _():
                self.landed(self.turns - self.parts + piece, way)
        loop(2, each)

        def column(col):
            value = self.product(self.spot.chip, rows, col)
            lanes = self.third(col)

            @pl.when(self.spot.ends)
            def _():
                way = jnp.where(self.spot.chip == 0, 1, 0)
                total[s, :, lanes] = (value + held[way, last, rows, lanes].astype(jnp.float32)).astype(jnp.bfloat16)

            @pl.when(jnp.logical_not(self.spot.ends))
            def _():
                total[s, :, lanes] = (value + held[0, last, rows, lanes].astype(jnp.float32)
                                      + held[1, last, rows, lanes].astype(jnp.float32)).astype(jnp.bfloat16)
        loop(3, column)
        self.store(piece).start()

        @pl.when(piece == 0)
        def _():
            for kind in (2, 0, 1):
                self.hand(kind).start()

    def turn(self, m):
        def each(way):
            @pl.when((m < self.turns) & self.sends(m // self.parts, way))
            def _():
                self.send_sum(m, way)
        loop(2, each)

    def turn_end(self, m):
        first = self.turns - self.parts + self.lag

        @pl.when((m >= first) & (m < first + self.parts))
        def _():
            self.finish(m - first)

    def settle(self):
        def drain(m):
            def each(way):
                first = self.spot.passed(way) == 0

                @pl.when(self.sends(m // self.parts, way) & (jnp.logical_not(first) | (m >= self.turns - self.window)))
                def _():
                    self.passing(m, way, 0).wait_send()
            loop(2, each)
        loop(self.turns, drain)
        for piece in (self.parts - 2, self.parts - 1):
            self.store(piece).wait()

    def returned(self):
        for kind in range(3):
            self.hand(kind).wait_recv()


def share_rows(share, kind):
    skip = share[2][0] + share[2][1] - share[3][0] if kind == 2 else 0
    first, length = share[1 + kind]
    return pl.ds(first + skip, length - skip), pl.ds(skip, length - skip)


class Bases:
    def __init__(self, left, right, out, held, parts, load_sem, store_sem):
        self.sources, self.out, self.held, self.parts, self.load_sem, self.store_sem = (left, right), out, held, parts, load_sem, store_sem
        self.groups, self.pairs = left.shape[1], left.shape[2] // 2
        self.units = left.shape[0] * self.groups

    def at(self, u):
        return u // self.groups, lax.rem(u, self.groups), lax.rem(u, 2)

    def load(self, u, start):
        t, r, slot = self.at(u)
        for n, source in enumerate(self.sources):
            copy = pltpu.make_async_copy(source.at[t, r], self.held.at[slot, n], self.load_sem.at[slot, n])
            (copy.start if start else copy.wait)()

    def store(self, u, start):
        t, r, slot = self.at(u)
        for n in (0, 1):
            copy = pltpu.make_async_copy(self.parts.at[slot, n], self.out.at[n, t, r], self.store_sem.at[slot, n])
            (copy.start if start else copy.wait)()

    def unit(self, u):
        @pl.when(u + 1 < self.units)
        def _():
            self.load(u + 1, True)
        self.load(u, False)

        @pl.when(u >= 2)
        def _():
            self.store(u - 2, False)
        slot = lax.rem(u, 2)
        for n in (0, 1):
            for q in range(self.pairs):
                both = jnp.concatenate([self.held[slot, n, 2 * q], self.held[slot, n, 2 * q + 1]], axis=1)
                high, low = split(both)
                rows = pl.ds(q * BLOCK, BLOCK)
                self.parts[slot, n, 0, rows] = high
                self.parts[slot, n, 1, rows] = low
        self.store(u, True)

    def some(self, first, count):
        def one(i):
            @pl.when(first + i < self.units)
            def _():
                self.unit(first + i)
        loop(count, one)

    def settle(self):
        for u in (self.units - 2, self.units - 1):
            self.store(jnp.int32(u), False)


class Stitched:
    def __init__(self, spot, share, y_ref, st_ref, y_send, y_recv, core_send, core_recv, give_send, give_recv, given_send, given_recv, own_sem):
        self.spot, self.share, self.y_ref, self.st_ref = spot, share, y_ref, st_ref
        self.y_send, self.y_recv, self.core_send, self.core_recv = y_send, y_recv, core_send, core_recv
        self.give_send, self.give_recv, self.given_send, self.given_recv, self.own_sem = give_send, give_recv, given_send, given_recv, own_sem
        self.towers, self.cols = y_ref.shape[0], y_ref.shape[2]
        self.bands = (share[0], (0, share[0][0]))
        self.events = 2 * self.towers * spot.steps

    def lanes(self, shard, k):
        return pl.ds(pl.multiple_of((2 * shard + k) * self.cols, 128), self.cols)

    def place(self, shard, k, t, b):
        return self.st_ref.at[t, pl.ds(*self.bands[b]), self.lanes(shard, k)]

    def source(self, t, b):
        return self.y_ref.at[t, pl.ds(*self.bands[b])]

    def leave(self, step, way, t, b, own=False):
        s = self.spot
        dst = self.place(s.onward(way, -step), s.core, t, b)
        return pltpu.make_async_remote_copy(
            src_ref=self.source(t, b) if own else dst, dst_ref=dst, send_sem=self.y_send.at[way, step, b, t],
            recv_sem=self.y_recv.at[way, step, b, t], device_id=s.on_line(s.onward(way, 1)), device_id_type=MESH)

    def to_core(self, shard, t, b, own=False):
        s = self.spot
        dst = self.place(shard, s.core, t, b)
        return pltpu.make_async_remote_copy(
            src_ref=self.source(t, b) if own else dst, dst_ref=dst, send_sem=self.core_send.at[shard, b, t],
            recv_sem=self.core_recv.at[shard, b, t], device_id=s.at(s.dp, 1 - s.core), device_id_type=MESH)

    def give(self, kind, shard, t, own=False):
        s = self.spot
        to, taken = share_rows(self.share, kind)
        src = pl.ds(self.share[0][0] + taken.start, taken.size)
        return pltpu.make_async_remote_copy(
            src_ref=self.y_ref.at[t, src] if own else self.st_ref.at[t, src, self.lanes(shard, s.core)],
            dst_ref=self.st_ref.at[t, to, self.lanes(shard, s.core)], send_sem=self.give_send.at[kind, shard, t],
            recv_sem=self.give_recv.at[kind, shard, t], device_id=s.at(s.others[kind], s.core), device_id_type=MESH)

    def given_place(self, kind, shard, t, k):
        return self.st_ref.at[t, share_rows(self.share, kind)[0], self.lanes(shard, k)]

    def given(self, kind, shard, t):
        s = self.spot
        ref = self.given_place(kind, shard, t, s.core)
        return pltpu.make_async_remote_copy(
            src_ref=ref, dst_ref=ref, send_sem=self.given_send.at[kind, shard, t], recv_sem=self.given_recv.at[kind, shard, t],
            device_id=s.at(s.dp, 1 - s.core), device_id_type=MESH)

    def own(self, t, b):
        return pltpu.make_async_copy(self.source(t, b), self.place(self.spot.chip, self.spot.core, t, b), self.own_sem.at[b, t])

    def start(self):
        for b in (0, 1):
            def tower(t):
                def each(way):
                    @pl.when(self.spot.leaves(0, way))
                    def _():
                        self.leave(0, way, t, b, True).start()
                loop(2, each)
                self.to_core(self.spot.chip, t, b, True).start()
                if b == 0:
                    for kind in (2, 0, 1):
                        self.give(kind, self.spot.chip, t, True).start()
                self.own(t, b).start()
            loop(self.towers, tower)

    def event(self, n):
        step, t = n // (2 * self.towers), lax.rem(n, self.towers)
        for b in (0, 1):
            def each(way):
                @pl.when(self.spot.comes(step, way))
                def _():
                    shard = self.spot.onward(way, -1 - step)
                    wait_for(self.place(shard, self.spot.core, t, b), self.y_recv.at[way, step, b, t], self.y_send.at[way, step, b, t])

                    @pl.when((step + 1 < self.spot.steps) & self.spot.leaves(step + 1, way))
                    def _():
                        self.leave(jnp.minimum(step + 1, self.spot.steps - 1), way, t, b).start()
                    self.to_core(shard, t, b).start()
                    if b == 0:
                        for kind in (2, 0, 1):
                            self.give(kind, shard, t).start()

            @pl.when(lax.rem(n, 2 * self.towers) // self.towers == b)
            def _():
                loop(2, each)

    def receive(self):
        def one(n):
            shard, t = n // self.towers, lax.rem(n, self.towers)
            for kind in range(3):
                wait_for(self.given_place(kind, shard, t, self.spot.core), self.give_recv.at[kind, shard, t], self.give_send.at[kind, shard, t])
                self.given(kind, shard, t).start()
        loop(self.spot.chips * self.towers, one)

    def settle(self):
        def one(n):
            shard, t = n // self.towers, lax.rem(n, self.towers)
            for b in (0, 1):
                wait_for(self.place(shard, 1 - self.spot.core, t, b), self.core_recv.at[shard, b, t], self.core_send.at[shard, b, t])
                self.to_core(shard, t, b).wait_send()

                @pl.when(shard < self.spot.steps)
                def _():
                    def each(way):
                        @pl.when(self.spot.leaves(shard, way))
                        def _():
                            self.leave(jnp.minimum(shard, self.spot.steps - 1), way, t, b).wait_send()
                    loop(2, each)
            for kind in range(3):
                self.give(kind, shard, t).wait_send()
                self.given(kind, shard, t).wait_send()
                wait_for(self.given_place(kind, shard, t, 1 - self.spot.core), self.given_recv.at[kind, shard, t], self.given_send.at[kind, shard, t])
        loop(self.spot.chips * self.towers, one)
        for t in range(self.towers):
            for b in (0, 1):
                self.own(t, b).wait()


def front_kernel(chips, parts, share, f_ref, w_ref, o_ref, n_ref, sp_ref, left_ref, right_ref,
                 fg_first, wg_first, dz_first, fg_ref, wg_ref, dz_ref, tot_ref, bases_ref, st_ref, sr_ref,
                 d_first, gr_first, pg_first, relay_first, d_ref, gr_ref, pg_ref, relay_ref,
                 offer_f, taken, offer_o, wide, low, base_in, base_out, tot,
                 og, f_tile, w_tile, acc, theirs, live, act, dz_here, y_here, sums_here, sg,
                 held, w_here, dz_wide, total, f_part, g_part, r_part,
                 f_send, f_recv, w_send, w_recv, a_send, a_recv, z_send, z_recv, out_sem,
                 wide_sem, p_sem, x_send, x_recv, l_sem, base_load, base_store,
                 d_send, d_recv, o_sem, b_send, b_recv, g_load, g_send, g_recv, rs_send, rs_recv, own_sem, s_send, s_recv, ready,
                 y_send, y_recv, core_send, core_recv, give_send, give_recv, given_send, given_recv, y_own):
    spot = Spot(chips)
    keep, rows = share[0][0], sum(share[0])
    size = rows // parts
    fixed = rows - size
    spare = keep - fixed
    cols = o_ref.shape[2]
    tot[0] = jnp.zeros_like(tot[0]) + jnp.sum(n_ref[...].astype(jnp.float32), axis=1, keepdims=True)
    spot.greet()

    def offer(kind, what):
        src = (f_ref.at[0], f_ref.at[1], o_ref, tot.at[0])[what]
        dst = (offer_f.at[0, 1 + kind], offer_f.at[1, 1 + kind], offer_o.at[1 + kind], tot.at[1 + kind])[what]
        if what < 3:
            src = src.at[pl.ds(*share[1 + kind])] if what < 2 else src.at[:, pl.ds(*share[1 + kind])]
        return pltpu.make_async_remote_copy(
            src_ref=src, dst_ref=dst, send_sem=x_send.at[what, kind], recv_sem=x_recv.at[what, kind],
            device_id=spot.at(spot.others[kind], spot.core), device_id_type=MESH)

    def choose(width, read, write):
        weigh = [jnp.broadcast_to(jnp.where(tot[kind, :1, :width] > keep, 1.0, 0.0), (16, width)) for kind in range(4)]

        def strip(i):
            at = pl.ds(pl.multiple_of(i * 16, 16), 16)
            value = read(0, at).astype(jnp.float32) * weigh[0]
            for kind in range(1, 4):
                value = value + read(kind, at).astype(jnp.float32) * weigh[kind]
            write(i * 16, value.astype(jnp.bfloat16))
        loop(share[0][1] // 16, strip)

    def take(t):
        def write(row, value):
            taken[t, pl.ds(pl.multiple_of(spare + row, 16), 16)] = value
        choose(offer_f.shape[3], lambda kind, at: offer_f[t, kind, at], write)

    towers = []
    for t, (fg, wg, dz) in enumerate(((fg_first, wg_first, dz_first), (fg_ref, wg_ref, dz_ref))):
        features = Features(spot, f_ref.at[t], taken.at[t], fg, size, f_send.at[t], f_recv.at[t])
        weights = Weights(spot, low.at[t], wg, p_sem.at[t, 4], w_send.at[t], w_recv.at[t])
        products = Products(spot, features, wg, f_tile, w_tile, acc, theirs.at[t], p_sem.at[t, pl.ds(0, 2)], p_sem.at[t, pl.ds(2, 2)],
                            a_send.at[t], a_recv.at[t])
        backward = Backward(spot, size, dz_here, dz, z_send.at[t], z_recv.at[t], out_sem.at[t])
        towers.append((features, weights, products, backward))
    features, weights, products, backward = towers[0]
    sums = []
    for t, (fg, d, gr, pg, relay) in enumerate(((fg_first, d_first, gr_first, pg_first, relay_first), (fg_ref, d_ref, gr_ref, pg_ref, relay_ref))):
        sums.append((Sums(spot, parts, share, d, dz_wide, w_here, held, total, d_send.at[t], d_recv.at[t], o_sem, b_send.at[t], b_recv.at[t]),
                     Grads(spot, fg, dz_wide, gr, pg, relay, f_part, g_part, r_part, g_load.at[0], g_load.at[1], g_load.at[2],
                           g_send.at[t], g_recv.at[t], rs_send.at[t], rs_recv.at[t], own_sem.at[t])))
    gradients, grads = sums[0]
    stitched = Stitched(spot, share, y_here, st_ref, y_send, y_recv, core_send, core_recv, give_send, give_recv, given_send, given_recv, y_own)
    bases = Bases(left_ref, right_ref, bases_ref, base_in, base_out, base_load, base_store)

    def copy(n, src, dst):
        made = pltpu.make_async_copy(src, dst, l_sem.at[n])
        made.start()
        return made

    for what in (3, 0):
        for kind in (2, 0, 1):
            offer(kind, what).start()
    loop(parts - 1, lambda q: features.launch(q, False))
    needed = [copy(0, f_ref.at[0, pl.ds(*share[0])], offer_f.at[0, 0])]
    later = [copy(1, f_ref.at[1, pl.ds(*share[0])], offer_f.at[1, 0])]
    if spare:
        needed.append(copy(2, f_ref.at[0, pl.ds(fixed, spare)], taken.at[0, pl.ds(0, spare)]))
        later.append(copy(3, f_ref.at[1, pl.ds(fixed, spare)], taken.at[1, pl.ds(0, spare)]))
    later += [copy(4, o_ref.at[:, pl.ds(*share[0])], offer_o.at[0]), copy(5, o_ref.at[:, pl.ds(0, keep)], og.at[:, pl.ds(0, keep)]),
              copy(6, f_ref.at[0, pl.ds(0, fixed)], fg_first.at[pl.ds(0, fixed), features.lanes(spot.chip)]),
              copy(7, f_ref.at[1, pl.ds(0, fixed)], fg_ref.at[pl.ds(0, fixed), features.lanes(spot.chip)])]
    weights.round(w_ref.at[0], wide, wide_sem)
    weights.start()
    for made in needed:
        made.wait()
    for what in (3, 0):
        for kind in range(3):
            offer(kind, what).wait_recv()
    take(0)
    features.launch(parts - 1, True)
    later += [copy(8, tot, tot_ref), copy(9, taken.at[0], fg_first.at[pl.ds(fixed, size), features.lanes(spot.chip)])]
    live_rows_of(tot, share, live)
    clear(acc)
    sums_here[...] = jnp.zeros_like(sums_here)
    towers[1][1].round(w_ref.at[1], wide, wide_sem)
    share_of = -(-bases.units // (2 * parts))

    def serve(step, q):
        features.serve(step, q)
        bases.some((step * parts + q) * share_of, share_of)
    bases.load(jnp.int32(0), True)
    loop(parts, lambda q: serve(0, q))
    weights.relay()
    for what in (2, 1):
        for kind in (2, 0, 1):
            offer(kind, what).start()
    loop(parts, lambda q: serve(1, q))
    weights.finish()
    towers[1][1].start()
    for made in later:
        made.wait()
    products.multiply()
    for kind in range(3):
        offer(kind, 2).wait_recv()
    for t in range(2):
        def write(row, value):
            og[t, pl.ds(pl.multiple_of(keep + row, 16), 16)] = value
        choose(cols, lambda kind, at: offer_o[kind, t, at], write)

    def strip(t, at):
        activated, slope = gelu_and_slope(acc[at, :cols] + theirs[t, at] + sp_ref[t : t + 1])
        mask = live[at]
        dy = [og[n, at].astype(jnp.float32) * mask for n in range(2)]
        dz = slope * (sp_ref[2 + t : 3 + t] * dy[0] + sp_ref[4 + t : 5 + t] * dy[1])
        if t == 0:
            act[at] = activated
        else:
            other = act[at]
            for n in range(2):
                y_here[n, at] = ((sp_ref[2 + 2 * n : 3 + 2 * n] * other + sp_ref[3 + 2 * n : 4 + 2 * n] * activated) * mask).astype(jnp.bfloat16)
        dz_here[at] = dz.astype(jnp.bfloat16)
        for n, term in enumerate((dz, activated * dy[0], activated * dy[1])):
            sums_here[2 * n + t] += fold(term)

    def stage(t, k):
        _, _, products, backward = towers[t]

        @pl.when(k < parts)
        def _():
            products.complete(k)

        @pl.when(k > 0)
        def _():
            products.swap(k - 1).wait_recv()
            loop(size // 16, lambda i: strip(t, pl.ds(pl.multiple_of((k - 1) * size + i * 16, 16), 16)))
            backward.start(k - 1)
    loop(parts + 1, lambda k: stage(0, k))

    def settle(t, q):
        towers[t][0].settle(q)
        towers[t][2].swap(q).wait_send()
        towers[t][3].settle(q)
    for kind in range(3):
        offer(kind, 1).wait_recv()
    take(1)
    loop(parts, lambda q: settle(0, q))
    loads = weight_loads(chips, wg_first, w_here, l_sem.at[pl.ds(11, chips)])
    loads.append(copy(11 + chips, dz_first, dz_wide))
    features, weights, products, backward = towers[1]
    loop(parts - 1, lambda q: features.launch(q, False))
    features.launch(parts - 1, True)
    last = copy(0, taken.at[1], fg_ref.at[pl.ds(fixed, size), features.lanes(spot.chip)])
    grads.load(jnp.int32(0)).start()
    clear(acc)
    for made in loads:
        made.wait()

    def turn(m):
        gradients.turn(m)
        grads.turn(m, 2, 10)

        @pl.when(m == 2)
        def _():
            weights.relay()

        @pl.when((m >= 2) & (m < 2 + parts))
        def _():
            features.serve(0, m - 2)

        @pl.when((m >= 3 + parts) & (m < 3 + 2 * parts))
        def _():
            features.serve(1, m - 3 - parts)

        @pl.when(m == 3 + 2 * parts)
        def _():
            weights.finish()
            last.wait()
            products.multiply()
        gradients.turn_end(m)
    loop(gradients.turns + gradients.lag, turn)

    gradients.settle()

    def neighbours(method):
        for side, here, chip in ((0, spot.chip > 0, spot.chip - 1), (1, spot.chip < spot.steps, spot.chip + 1)):
            @pl.when(here)
            def _():
                method(side, chip)
    neighbours(lambda side, chip: pl.semaphore_signal(ready.at[1 - side], inc=1, device_id=spot.on_line(chip), device_id_type=MESH))
    loads = weight_loads(chips, wg_ref, w_here, l_sem.at[pl.ds(11, chips)])
    loop(parts + 1, lambda k: stage(1, k))
    stitched.start()
    sg[...] = jnp.zeros_like(sg)
    for n in range(6):
        sg[n : n + 1] = jnp.sum(sums_here[n], axis=0, keepdims=True)
    own = copy(1, sg, sr_ref.at[spot.dp])

    def small(kind):
        return pltpu.make_async_remote_copy(
            src_ref=sg, dst_ref=sr_ref.at[spot.dp], send_sem=s_send.at[kind], recv_sem=s_recv.at[kind],
            device_id=spot.at(spot.others[kind], spot.core), device_id_type=MESH)
    for kind in range(3):
        small(kind).start()
    loop(parts, lambda q: settle(1, q))
    wide_dz = copy(11 + chips, dz_ref, dz_wide)
    gradients, grads = sums[1]
    grads.load(jnp.int32(0)).start()
    for made in loads:
        made.wait()
    wide_dz.wait()
    neighbours(lambda side, chip: pl.semaphore_wait(ready.at[side], 1))

    def second_turn(m):
        gradients.turn(m)
        grads.turn(m, 0, 7)

        @pl.when((m >= 1) & (m <= stitched.events))
        def _():
            stitched.event(m - 1)
        gradients.turn_end(m)
    loop(gradients.turns + gradients.lag, second_turn)
    stitched.receive()
    gradients.settle()
    stitched.settle()
    for t in range(2):
        sums[t][0].returned()
        sums[t][1].settle()
        towers[t][1].settle()
    bases.settle()
    own.wait()
    for kind in range(3):
        small(kind).wait()
    for what in range(4):
        for kind in range(3):
            offer(kind, what).wait_send()


def weight_loads(chips, wg, w_here, sem):
    depth = w_here.shape[1]
    loads = [pltpu.make_async_copy(wg.at[pl.ds(n * depth, depth)], w_here.at[n], sem.at[n]) for n in range(chips)]
    for copy in loads:
        copy.start()
    return loads


def call(kernel, name, ident, out, scratch, operands, small_in=(), flops=0):
    anywhere, here = pl.BlockSpec(memory_space=pl.ANY), pl.BlockSpec(memory_space=pltpu.VMEM)
    return pl.pallas_call(
        kernel,
        out_shape=out,
        in_specs=[here if n in small_in else anywhere for n in range(len(operands))],
        out_specs=[anywhere] * len(out),
        scratch_shapes=scratch,
        compiler_params=pltpu.CompilerParams(collective_id=ident, has_side_effects=True, vmem_limit_bytes=62 * 2**20),
        cost_estimate=pl.CostEstimate(flops=flops, bytes_accessed=500 * 2**20, transcendentals=0),
        name=name,
    )(*operands)


def parts_of(share):
    rows = sum(share[0])
    return max(n for n in range(1, rows // 16) if rows % (16 * n) == 0 and rows // n >= share[0][1])


def shared_pass(features, weights, out_grad, counts, small_params, left, right, chips, share):
    parts = parts_of(share)
    towers, slots, depth = features.shape
    cols = weights.shape[2]
    keep, size = share[0]
    rows = keep + size
    steps = chips - 1
    piece = rows // parts
    dma, vmem = pltpu.SemaphoreType.DMA, pltpu.VMEM
    bf16, f32 = jnp.bfloat16, jnp.float32
    S = jax.ShapeDtypeStruct
    beside = (left.shape[2] // 2 * BLOCK, 2 * BLOCK)
    wide = [S((rows, chips * depth), bf16), S((chips * depth, 2 * cols), bf16), S((rows, 2 * cols), bf16)]
    sums = [S((slots, depth), bf16), S((3, 2, depth, cols), bf16), S((8, depth, cols), bf16), S((2, depth, cols), bf16)]
    out = call(
        functools.partial(front_kernel, chips, parts, share), "passes", 3,
        wide + wide + [S((4, 8, depth), f32), S((2,) + left.shape[:2] + (2,) + beside, bf16),
                       S((towers, slots, 2 * chips * cols), bf16), S((4, 8, cols), f32)] + sums + sums,
        [vmem((towers, 4, size, depth), bf16), vmem((towers, piece, depth), bf16), vmem((4, towers, size, cols), bf16),
         vmem((2, depth // 8, cols), f32), vmem((towers, 2, depth, cols), bf16), vmem((2, 2) + left.shape[2:], f32), vmem((2, 2, 2) + beside, bf16),
         vmem((4, 8, depth), f32), vmem((towers, rows, cols), bf16), vmem((2, rows, depth), bf16), vmem((2, depth, 2 * cols), bf16),
         vmem((rows, 2 * cols), f32), vmem((towers, rows, cols), f32), vmem((rows, cols), f32), vmem((rows, cols), f32), vmem((rows, cols), bf16),
         vmem((towers, rows, cols), bf16), vmem((6, 8, cols), f32), vmem((8, cols), f32),
         vmem((2, steps, rows, depth), bf16), vmem((chips, depth, 2 * cols), bf16), vmem((rows, 2 * cols), bf16),
         vmem((2, piece, depth), bf16), vmem((2, rows, depth // 3), bf16)] + [vmem((2, depth // 3, cols), bf16)] * 2
        + [dma((towers, 2, steps, parts))] * 2 + [dma((towers, 4, 2))] * 2 + [dma((towers, parts))] * 5
        + [dma((2,)), dma((towers, 5)), dma((4, 3)), dma((4, 3)), dma((12 + chips,)), dma((2, 2)), dma((2, 2))]
        + [dma((towers, 2, steps * parts))] * 2 + [dma((2,)), dma((towers, 3)), dma((towers, 3)), dma((3, 2)), dma((towers, 8)), dma((towers, 3, 2)),
                                                   dma((towers, 2)), dma((towers, 2)), dma((towers,)), dma((3,)), dma((3,)), pltpu.SemaphoreType.REGULAR((2,))]
        + [dma((2, steps, 2, towers))] * 2 + [dma((chips, 2, towers))] * 2 + [dma((3, chips, towers))] * 4 + [dma((2, towers))],
        (features, weights, out_grad, counts.reshape(1, -1), small_params, left, right), (3, 4), 6 * 2 * rows * 2 * cols * depth * chips)
    told, bases, stitched, smalls, d_first, gr_first, _, _, d_second, gr_second, _, _ = out[6:]
    return told, bases, ((d_first, d_second), stitched, (gr_first, gr_second), smalls)


def small_step(small_params, small_moment_one, small_moment_two, small_average, small_grad):
    first, second, direction = adam_part(small_moment_one, small_moment_two, small_grad)
    fresh = small_params - rate_small * direction
    return first, second, fresh, ema_decay * small_average + (1.0 - ema_decay) * fresh


def update(d_feat, stitched, full, parts, small_parts, states, small_states):
    small_grad = jnp.sum(small_parts, 0)[: small_states[0].shape[0]]
    *fresh, stitched, d_feat = soap(parts, full, stitched, d_feat, *states)
    return (stitched, d_feat) + tuple(fresh) + small_step(*small_states, small_grad)


def own_rows(features, out_grad, totals, passed, states, small_states):
    _, rows, _ = features.shape
    weights, small_params = states[0], small_states[0]
    cols = weights.shape[2]
    cores = lax.axis_size("mp")
    swap = [(i, i ^ 1) for i in range(cores)]
    ranges = ((0, rows // 2), (rows // 2, rows // 2))
    live_rows = (jnp.arange(rows, dtype=jnp.float32) < totals[0]).astype(jnp.float32)
    wide_f, wide_w = gather(features, weights.astype(jnp.bfloat16), cores // 2, ranges, 1)
    partial = jnp.einsum("tri,tio->tro", wide_f, wide_w, preferred_element_type=jnp.float32)
    product = partial[:, :, :cols] + lax.ppermute(partial[:, :, cols:], "mp", swap)
    result, back = jax.vjp(lambda a, b: stitch_local(a, b, live_rows), product, small_params)
    stitched = lax.all_gather(result.astype(jnp.bfloat16), "mp", axis=2, tiled=True)
    dz, small_part = back(out_grad.astype(jnp.float32))
    dz_low = dz.astype(jnp.bfloat16)
    wide_dz = jnp.concatenate([dz_low, lax.ppermute(dz_low, "mp", swap)], axis=2)
    partial_d = jnp.einsum("tro,tio->tri", wide_dz, wide_w, preferred_element_type=jnp.float32)
    partial_g = jnp.einsum("tri,tro->tio", wide_f, wide_dz, preferred_element_type=jnp.float32)
    small_part = jnp.pad(small_part, ((0, 2), (0, 0)))
    d_feat, parts, small_parts = reduce(
        partial_d.astype(jnp.bfloat16), partial_g.astype(jnp.bfloat16), small_part, cores // 2, ranges, 2
    )
    full = jnp.full((1,), rows, jnp.int32)
    return update((d_feat[0], d_feat[1]), stitched, full, (parts[:, :, 0], parts[:, :, 1]), small_parts, states, small_states)


def shares(rows):
    keep = rows * 15 // 32 // 16 * 16
    size = -(-(rows - keep) // 64) * 16
    return keep, ((keep, size), (keep + size, size), (keep + 2 * size, size), (rows - size, size))


def shared_rows(features, out_grad, totals, passed, states, small_states):
    rows = features.shape[1]
    keep, _ = shares(rows)
    d_feat, stitched, parts, small_parts = passed
    full = jnp.where(totals[:1] > keep, rows, keep)
    return update(d_feat, stitched, full, parts, small_parts, states, small_states)


def line_body(
    features,
    counts,
    weights,
    small_params,
    out_grad,
    moment_one,
    moment_two,
    average,
    basis_left,
    basis_right,
    small_moment_one,
    small_moment_two,
    small_average,
):
    keep, share = shares(features.shape[1])
    told, bases, passed = shared_pass(
        features, weights, out_grad, counts, small_params, basis_left, basis_right, lax.axis_size("mp") // 2, share
    )
    totals = told[:, 0, 0]
    return lax.cond(
        jnp.sum(totals > keep) == 1,
        shared_rows,
        own_rows,
        features,
        out_grad,
        totals,
        passed,
        (weights, moment_one, moment_two, average, bases),
        (small_params, small_moment_one, small_moment_two, small_average),
    )


def plain_body(
    features,
    counts,
    weights,
    small_params,
    out_grad,
    moment_one,
    moment_two,
    average,
    basis_left,
    basis_right,
    small_moment_one,
    small_moment_two,
    small_average,
):
    slot_count = features.shape[1]
    total = jnp.sum(counts)
    live_rows = (jnp.arange(slot_count, dtype=jnp.int32) < total).astype(jnp.float32)
    weights_low = lax.all_gather(weights.astype(jnp.bfloat16), "dp", axis=1, tiled=True)
    feats_full = lax.all_gather(features, "mp", axis=2, tiled=True)
    product = jnp.einsum(
        "tri,tio->tro", feats_full, weights_low, preferred_element_type=jnp.float32
    )
    result, back = jax.vjp(lambda a, b: stitch_local(a, b, live_rows), product, small_params)
    stitched = lax.all_gather(result.astype(jnp.bfloat16), "mp", axis=2, tiled=True)
    dz, small_part = back(out_grad.astype(jnp.float32))
    dz_low = dz.astype(jnp.bfloat16)
    grad_part = jnp.einsum("tri,tro->tio", feats_full, dz_low, preferred_element_type=jnp.float32)
    partial_sums = jnp.einsum(
        "tro,tio->tri", dz_low, weights_low, preferred_element_type=jnp.float32
    )
    d_feat = lax.psum_scatter(
        partial_sums.astype(jnp.float32), "mp", scatter_dimension=2, tiled=True
    )
    grad = lax.psum_scatter(grad_part, "dp", scatter_dimension=1, tiled=True)
    small_grad = lax.psum(small_part, "dp")
    towers, n_in, n_out = grad.shape
    blocks = grad.reshape(towers, n_in // BLOCK, BLOCK, n_out // BLOCK, BLOCK)
    rotated = jnp.einsum(
        "trcai,tracb,trcbj->tricj", basis_left, blocks, basis_right, precision=lax.Precision.HIGHEST
    ).reshape(towers, n_in, n_out)
    first, second, direction = adam_part(moment_one, moment_two, rotated)
    turned = direction.reshape(towers, n_in // BLOCK, BLOCK, n_out // BLOCK, BLOCK)
    step_back = jnp.einsum(
        "trcai,tricj,trcbj->tracb", basis_left, turned, basis_right, precision=lax.Precision.HIGHEST
    ).reshape(towers, n_in, n_out)
    new_weights = weights - rate_main * (step_back + decay_weight * weights)
    new_average = ema_decay * average + (1.0 - ema_decay) * new_weights
    return (
        stitched,
        d_feat.astype(jnp.bfloat16),
        first,
        second,
        new_weights,
        new_average,
        new_weights.astype(jnp.bfloat16),
    ) + small_step(small_params, small_moment_one, small_moment_two, small_average, small_grad)


def solution(mesh):
    def body(features, counts, weights, *rest):
        dp, mp = mesh.shape["dp"], mesh.shape["mp"]
        tiles = features.shape[2] % 128 == 0 and weights.shape[2] % 128 == 0
        suits = dp == 4 and mp == 2 * dp and tiles and features.shape[1] % 64 == 0
        return (line_body if suits else plain_body)(features, counts, weights, *rest)

    return jax.shard_map(
        body,
        mesh=mesh,
        in_specs=(
            P(None, "dp", "mp"),
            P("dp"),
            P(None, "dp", "mp"),
            P(None, "mp"),
            P(None, "dp", "mp"),
            P(None, "dp", "mp"),
            P(None, "dp", "mp"),
            P(None, "dp", "mp"),
            P(None, "dp", "mp", None, None),
            P(None, "dp", "mp", None, None),
            P(None, "mp"),
            P(None, "mp"),
            P(None, "mp"),
        ),
        out_specs=(
            P(None, "dp", None),
            P(None, "dp", "mp"),
            P(None, "dp", "mp"),
            P(None, "dp", "mp"),
            P(None, "dp", "mp"),
            P(None, "dp", "mp"),
            P(None, "dp", "mp"),
            P(None, "mp"),
            P(None, "mp"),
            P(None, "mp"),
            P(None, "mp"),
        ),
        check_vma=False,
    )
```

```python
import functools
import math

import jax
import jax.numpy as jnp
from jax import lax
from jax.experimental import pallas as pl
from jax.experimental.pallas import tpu as pltpu
from jax.sharding import PartitionSpec as P

BLOCK = 64
STEP = 5


beta_one = 0.5
beta_two = 0.5
ema_decay = 0.5
rate_main = 0.01
rate_small = 0.05
decay_weight = 0.01
eps = 1e-08


def stitch_local(product, small, live_rows):
    pre_act = product + small[0:2][:, None, :]
    activated = jax.nn.gelu(pre_act, approximate=True)
    first = small[2] * activated[0] + small[3] * activated[1]
    second = small[4] * activated[0] + small[5] * activated[1]
    return jnp.stack([first, second]) * live_rows[None, :, None]


def adam_part(moment_a, moment_b, grad):
    first = beta_one * moment_a + (1.0 - beta_one) * grad
    second = beta_two * moment_b + (1.0 - beta_two) * grad * grad
    direction = first / (1.0 - beta_one**STEP) / (jnp.sqrt(second / (1.0 - beta_two**STEP)) + eps)
    return (first, second, direction)

def split(v):
    high = v.astype(jnp.bfloat16)
    return high, (v - high.astype(jnp.float32)).astype(jnp.bfloat16)

def soap_blocks(grads, lefts, rights, moments):
    row = lax.broadcasted_iota(jnp.int32, (2 * BLOCK, 2 * BLOCK), 0) // BLOCK
    lane = lax.broadcasted_iota(jnp.int32, (2 * BLOCK, 2 * BLOCK), 1) // BLOCK
    own = row == lane

    def diagonal(v):
        return jnp.where(own, jnp.concatenate([v, v], axis=0), jnp.zeros((), v.dtype))

    def stationary(high, low, axis):
        return jnp.concatenate([high, high, low], axis=axis)

    def moving(v, axis):
        high, low = split(v)
        return jnp.concatenate([high, low, high], axis=axis)

    def dots(a, b, ca, cb):
        dims = (((ca,), (cb,)), ((), ()))
        return [lax.dot_general(x, y, dims, preferred_element_type=jnp.float32) for x, y in zip(a, b)]

    right = [(diagonal(high), diagonal(low)) for high, low in rights]
    values = dots([moving(v, 1) for v in grads], [stationary(*v, 0) for v in right], 1, 0)
    values = dots([stationary(*v, 0) for v in lefts], [moving(v, 0) for v in values], 0, 0)
    values = [jnp.where(lane[:BLOCK] == 0, v[:BLOCK], v[BLOCK:]) for v in values]
    states = [adam_part(a, b, v) for (a, b), v in zip(moments, values)]
    values = dots([moving(v[2], 1) for v in states], [stationary(*v, 1) for v in right], 1, 1)
    values = dots([stationary(*v, 1) for v in lefts], [moving(diagonal(v), 0) for v in values], 1, 0)
    return [(first, second, step) for (first, second, _), step in zip(states, values)]


def soap_body(together, strips, full, parts_a, parts_b, stitched, d_a, d_b, weights, moment_a, moment_b, average, left, right,
              first, second, new_weights, new_average, copy, stitched_out, d_feat_out):
    groups, pairs = left.shape[2], left.shape[4] // BLOCK
    length = stitched.shape[1]
    row = jnp.minimum(pl.program_id(1) * pl.num_programs(2) + pl.program_id(2), strips - 1) * length

    first_tower = pl.program_id(0) == 0

    def clear(i, _):
        rows = pl.ds(pl.multiple_of(i * 16, 16), 16)
        wanted = row + i * 16 < full[0]
        stitched_out[0, rows] = jnp.where(wanted, stitched[0, rows], 0)
        d_feat_out[0, rows] = jnp.where(wanted, jnp.where(first_tower, d_a[rows], d_b[rows]), 0)
        return 0

    lax.fori_loop(0, length // 16, clear, 0)

    def blocks(g, _):
        places = [(g * together + s, q) for s in range(together) for q in range(pairs)]
        ats = [(0, pl.ds(pl.multiple_of(r * BLOCK, BLOCK), BLOCK), pl.ds(2 * BLOCK * q, 2 * BLOCK)) for r, q in places]
        grads = []
        for at in ats:
            grads.append(sum(jnp.where(first_tower, parts_a[(k,) + at], parts_b[(k,) + at]).astype(jnp.float32)
                             for k in range(parts_a.shape[0])))
        def basis(ref, r, q):
            return tuple(ref[0, 0, r, k, BLOCK * q : BLOCK * (q + 1)] for k in (0, 1))

        done = soap_blocks(grads, [basis(left, *place) for place in places], [basis(right, *place) for place in places],
                           [(moment_a[at], moment_b[at]) for at in ats])
        olds = [(weights[at], average[at]) for at in ats]
        for at, (one, two, step), (held, mean) in zip(ats, done, olds):
            first[at] = one
            second[at] = two
            fresh = held - rate_main * (step + decay_weight * held)
            new_weights[at] = fresh
            new_average[at] = ema_decay * mean + (1.0 - ema_decay) * fresh
            copy[at] = fresh.astype(jnp.bfloat16)
        return 0

    lax.fori_loop(0, groups // together, blocks, 0)


def soap(parts, wanted, stitched, d_feat, weights, moment_a, moment_b, average, bases, group=6):
    towers, rows, cols = weights.shape
    half = parts[0].shape[2]
    steps = half // (BLOCK * group)
    flat = lambda t, p, g: (t, p * steps + g, 0)
    state = pl.BlockSpec((1, BLOCK * group, cols), flat)
    base = [pl.BlockSpec((1, 1, group) + bases.shape[3:], lambda t, p, g, n=n: (n, t, p * steps + g, 0, 0, 0)) for n in (0, 1)]
    full = jax.ShapeDtypeStruct(weights.shape, jnp.float32)
    strips = max(n for n in range(1, 2 * steps + 1) if stitched.shape[1] % (16 * n) == 0)

    def strip(p, g):
        return jnp.minimum(p * steps + g, strips - 1)

    def through(shape):
        return pl.BlockSpec((1, shape[1] // strips, shape[2]), lambda t, p, g: (t, strip(p, g), 0))

    def of_tower(n, shape, index, last):
        return pl.BlockSpec(shape, lambda t, p, g: tuple(jnp.where(t == n, a, b) for a, b in zip(index(p, g), last if n == 0 else index(0, 0))))

    pieces = [of_tower(n, (v.shape[0], 1, BLOCK * group, cols), lambda p, g: (0, p, g, 0), (0, 1, steps - 1, 0)) for n, v in enumerate(parts)]
    rows_of = [of_tower(n, (v.shape[0] // strips, v.shape[1]), lambda p, g: (strip(p, g), 0), (strips - 1, 0)) for n, v in enumerate(d_feat)]

    return pl.pallas_call(
        functools.partial(soap_body, group, strips),
        grid=(towers, 2, steps),
        in_specs=[pl.BlockSpec(memory_space=pltpu.SMEM),
                  *pieces, through(stitched.shape), *rows_of, state, state, state, state, *base],
        out_specs=[state] * 5 + [through(stitched.shape), through((towers,) + d_feat[0].shape)],
        out_shape=[full] * 4 + [jax.ShapeDtypeStruct(weights.shape, jnp.bfloat16)]
        + [jax.ShapeDtypeStruct(v, jnp.bfloat16) for v in (stitched.shape, (towers,) + d_feat[0].shape)],
        compiler_params=pltpu.CompilerParams(vmem_limit_bytes=60 * 2**20),
        cost_estimate=pl.CostEstimate(flops=8 * 2 * towers * rows * cols * 64, bytes_accessed=130 * 2**20, transcendentals=0),
        name="soap",
    )(wanted, *parts, stitched, *d_feat, weights, moment_a, moment_b, average, bases, bases)


MESH = pl.DeviceIdType.MESH


def place():
    mp = lax.axis_index("mp")
    return lax.axis_index("dp"), mp // 2, lax.rem(mp, 2)


def meet(devices):
    barrier = pltpu.get_barrier_semaphore()
    expected = 0
    for here, device in devices:
        @pl.when(here)
        def _():
            pl.semaphore_signal(barrier, inc=1, device_id=device, device_id_type=MESH)
        expected = expected + jnp.where(here, 1, 0)
    pl.semaphore_wait(barrier, expected)


def gather_kernel(chips, ranges, f_ref, w_ref, fg_ref, wg_ref, f_send, f_recv, w_send, w_recv, own_sem):
    dp, chip, core = place()
    towers, rows, depth = f_ref.shape
    cols = w_ref.shape[2]
    across, along = dp ^ 1, dp ^ 2
    at = lambda c, k: (c, 2 * chip + k)

    meet([(chip > 0, (dp, 2 * (chip - 1) + core)), (chip < chips - 1, (dp, 2 * (chip + 1) + core)),
          (chip >= 0, at(dp, 1 - core))] + [(chip >= 0, at(c, k)) for c in (across, along) for k in (0, 1)])

    def copies(step, way, t, k, shard, there):
        lanes = pl.ds(pl.multiple_of(shard * depth, 128), depth)
        rws = pl.ds(*ranges[k])
        src = fg_ref.at[t, rws, lanes]
        if step == 0:
            src = f_ref.at[t, rws]
        n = ((way * (chips - 1) + step) * towers + t) * len(ranges) + k
        return pltpu.make_async_remote_copy(
            src_ref=src, dst_ref=fg_ref.at[t, rws, lanes], send_sem=f_send.at[n], recv_sem=f_recv.at[n],
            device_id=(dp, 2 * there + core), device_id_type=MESH)

    def feature(step, way, t, k):
        return copies(step, way, t, k, chip - step if way == 0 else chip + step, chip + 1 if way == 0 else chip - 1)

    def incoming(step, way, t, k):
        return copies(step, way, t, k, chip - 1 - step if way == 0 else chip + 1 + step, chip)

    def sends(step, way):
        return (chip < chips - 1) & (chip >= step) if way == 0 else (chip > 0) & (chip + step < chips)

    def receives(step, way):
        return chip > step if way == 0 else chip + step < chips - 1

    def launch(t, k):
        for way in (0, 1):
            @pl.when(sends(0, way))
            def _():
                feature(0, way, t, k).start()

    def block(owner, slot, t):
        return wg_ref.at[t, pl.ds(pl.multiple_of(owner * depth, 128), depth), pl.ds(pl.multiple_of(slot * cols, 128), cols)]

    def weight(kind, k, t):
        to = at((across, along, dp)[kind], k)
        n = (kind * 2 + core) * 2 + t
        return pltpu.make_async_remote_copy(
            src_ref=w_ref.at[t, pl.ds(pl.multiple_of(k * depth, 128), depth)], dst_ref=block(dp, k ^ core, t),
            send_sem=w_send.at[(kind * 2 + k) * 2 + t], recv_sem=w_recv.at[n], device_id=to, device_id_type=MESH)

    def forward(kind, slot):
        owner, to, t = ((across, along, 0), (along, across, 1))[kind]
        n = 12 + kind * 2 + slot
        return pltpu.make_async_remote_copy(
            src_ref=block(owner, slot, t), dst_ref=block(owner, slot, t),
            send_sem=w_send.at[n], recv_sem=w_recv.at[n], device_id=at(to, core), device_id_type=MESH)

    def arrived(kind, slot, t):
        owner = (across, along, dp)[kind]
        n = (kind * 2 + (slot ^ core)) * 2 + t
        pltpu.make_async_remote_copy(
            src_ref=block(owner, slot, t), dst_ref=block(owner, slot, t), send_sem=w_send.at[n], recv_sem=w_recv.at[n],
            device_id=at(dp, core), device_id_type=MESH).wait_recv()

    mine = pl.ds(pl.multiple_of(chip * depth, 128), depth)
    own = [pltpu.make_async_copy(f_ref.at[t], fg_ref.at[t, :, mine], own_sem.at[t]) for t in range(towers)]
    own += [pltpu.make_async_copy(w_ref.at[t, pl.ds(pl.multiple_of(core * depth, 128), depth)], block(dp, 0, t), own_sem.at[2 + t])
            for t in range(towers)]

    pieces = [(t, k) for k in range(len(ranges)) for t in range(towers)]
    for t, k in pieces:
        launch(t, k)
    for copy in own:
        copy.start()
    for t in (0, 1):
        for k in (0, 1):
            weight(0, k, t).start()
            weight(1, k, 1 - t).start()
    for t in (0, 1):
        weight(2, 1 - core, t).start()

    for step in range(chips - 1):
        for t, k in pieces:
            for way in (0, 1):
                @pl.when(receives(step, way))
                def _():
                    incoming(step, way, t, k).wait_recv()
                if step + 1 < chips - 1:
                    @pl.when(sends(step + 1, way))
                    def _():
                        feature(step + 1, way, t, k).start()
            if step == 0 and (t, k) == pieces[-1]:
                for slot in (0, 1):
                    arrived(0, slot, 0)
                    forward(0, slot).start()
                    arrived(1, slot, 1)
                    forward(1, slot).start()

    for slot in (0, 1):
        arrived(0, slot, 1)
        arrived(1, slot, 0)
        forward(0, slot).wait_recv()
        forward(1, slot).wait_recv()
    for t in (0, 1):
        arrived(2, 1, t)
    for t in (0, 1):
        for k in (0, 1):
            weight(0, k, t).wait_send()
            weight(1, k, t).wait_send()
        weight(2, 1 - core, t).wait_send()
    for slot in (0, 1):
        forward(0, slot).wait_send()
        forward(1, slot).wait_send()
    for step in range(chips - 1):
        for t, k in pieces:
            for way in (0, 1):
                @pl.when(sends(step, way))
                def _():
                    feature(step, way, t, k).wait_send()
    for copy in own:
        copy.wait()


def gather(features, weights_low, chips, ranges, ident):
    towers, rows, depth = features.shape
    cols = weights_low.shape[2]
    count = 2 * (chips - 1) * towers * len(ranges)
    dma = pltpu.SemaphoreType.DMA
    anywhere = pl.BlockSpec(memory_space=pl.ANY)
    return pl.pallas_call(
        functools.partial(gather_kernel, chips, ranges),
        out_shape=[jax.ShapeDtypeStruct((towers, rows, chips * depth), jnp.bfloat16),
                   jax.ShapeDtypeStruct((towers, chips * depth, 2 * cols), jnp.bfloat16)],
        in_specs=[anywhere] * 2,
        out_specs=[anywhere] * 2,
        scratch_shapes=[dma((count,)), dma((count,)), dma((16,)), dma((16,)), dma((4,))],
        compiler_params=pltpu.CompilerParams(collective_id=ident, has_side_effects=True),
        cost_estimate=pl.CostEstimate(flops=0, bytes_accessed=800 * 2**20, transcendentals=0),
        name="gather",
    )(features, weights_low)


def reduce_kernel(chips, ranges, pd_ref, pg_ref, ps_ref, d_ref, gr_ref, sr_ref, held, term, total,
                  d_send, d_recv, t_sem, o_sem, g_send, g_recv, s_send, s_recv, own_sem):
    dp, chip, core = place()
    towers, rows, depth = d_ref.shape
    cols = pg_ref.shape[2] // 2
    across, along = dp ^ 1, dp ^ 2
    others = (across, along, dp ^ 3)
    at = lambda c, k: (c, 2 * chip + k)

    meet([(chip > 0, (dp, 2 * (chip - 1) + core)), (chip < chips - 1, (dp, 2 * (chip + 1) + core)),
          (chip >= 0, at(dp, 1 - core))] + [(chip >= 0, at(c, k)) for c in others for k in (0, 1)])

    def grad(kind, k, t):
        owner = (others + (dp,))[kind]
        return pltpu.make_async_remote_copy(
            src_ref=pg_ref.at[t, pl.ds(pl.multiple_of(owner * depth, 128), depth), pl.ds(pl.multiple_of((k ^ core) * cols, 128), cols)],
            dst_ref=gr_ref.at[dp, core, t], send_sem=g_send.at[(kind * 2 + k) * 2 + t],
            recv_sem=g_recv.at[(kind * 2 + core) * 2 + t], device_id=at(owner, k), device_id_type=MESH)

    def grad_arrived(kind, k, t):
        owner = (others + (dp,))[kind]
        pltpu.make_async_remote_copy(
            src_ref=gr_ref.at[owner, k, t], dst_ref=gr_ref.at[owner, k, t], send_sem=g_send.at[0],
            recv_sem=g_recv.at[(kind * 2 + k) * 2 + t], device_id=at(dp, core), device_id_type=MESH).wait_recv()

    def small(kind):
        return pltpu.make_async_remote_copy(
            src_ref=ps_ref, dst_ref=sr_ref.at[dp], send_sem=s_send.at[kind], recv_sem=s_recv.at[kind],
            device_id=at(others[kind], core), device_id_type=MESH)

    def target(step, way):
        return chip + chips - 1 - step if way == 0 else chip - (chips - 1 - step)

    def sends(step, way):
        return (chip < chips - 1) & (chip <= step) if way == 0 else (chip > 0) & (chips - 1 - chip <= step)

    def receives(step, way):
        return (chip > 0) & (chip <= step + 1) if way == 0 else (chip < chips - 1) & (chips - 1 - chip <= step + 1)

    def own_term(goal, t, k):
        return pd_ref.at[t, pl.ds(*ranges[k]), pl.ds(pl.multiple_of(goal * depth, 128), depth)]

    def partial(step, way, t, k, first):
        n = ((way * (chips - 1) + step) * towers + t) * len(ranges) + k
        src = own_term(target(step, way), t, k) if first else held.at[way, step - 1, t, pl.ds(*ranges[k])]
        there = chip + 1 if way == 0 else chip - 1
        return pltpu.make_async_remote_copy(
            src_ref=src, dst_ref=held.at[way, step, t, pl.ds(*ranges[k])], send_sem=d_send.at[n], recv_sem=d_recv.at[n],
            device_id=(dp, 2 * there + core), device_id_type=MESH)

    def landed(step, way, t, k):
        n = ((way * (chips - 1) + step) * towers + t) * len(ranges) + k
        ref = held.at[way, step, t, pl.ds(*ranges[k])]
        pltpu.make_async_remote_copy(src_ref=ref, dst_ref=ref, send_sem=d_send.at[n], recv_sem=d_recv.at[n],
                                     device_id=(dp, 2 * chip + core), device_id_type=MESH).wait_recv()

    pieces = [(t, k) for t in range(towers) for k in range(len(ranges))]
    ends = (chip == 0, chip == chips - 1)
    for t, k in pieces:
        for way in (0, 1):
            @pl.when(ends[way])
            def _():
                partial(0, way, t, k, True).start()
    own = [pltpu.make_async_copy(
        pg_ref.at[t, pl.ds(pl.multiple_of(dp * depth, 128), depth), pl.ds(0, cols)], gr_ref.at[dp, core, t], own_sem.at[t])
        for t in range(towers)]
    own.append(pltpu.make_async_copy(ps_ref, sr_ref.at[dp], own_sem.at[towers]))
    for copy in own:
        copy.start()
    for kind in range(3):
        small(kind).start()
    for t in range(towers):
        for kind in (2, 0, 1):
            for k in (0, 1):
                grad(kind, k, t).start()
        grad(3, 1 - core, t).start()

    strip = 16

    for step in range(1, chips - 1):
        for t, k in pieces:
            for way in (0, 1):
                @pl.when(sends(step, way) & ends[way])
                def _():
                    partial(step, way, t, k, True).start()

                @pl.when(sends(step, way) & jnp.logical_not(ends[way]))
                def _():
                    start, size = ranges[k]
                    load = pltpu.make_async_copy(own_term(target(step, way), t, k), term.at[way, pl.ds(0, size)], t_sem.at[way])
                    load.start()
                    landed(step - 1, way, t, k)
                    load.wait()

                    def add(i, _):
                        rws = pl.ds(pl.multiple_of(i * strip, strip), strip)
                        all_rows = pl.ds(pl.multiple_of(start + i * strip, strip), strip)
                        held[way, step - 1, t, all_rows] = (
                            held[way, step - 1, t, all_rows].astype(jnp.float32) + term[way, rws].astype(jnp.float32)
                        ).astype(jnp.bfloat16)
                        return 0
                    lax.fori_loop(0, size // strip, add, 0)
                    partial(step, way, t, k, False).start()

    stores = []
    for n, (t, k) in enumerate(pieces):
        s = n % 2
        start, size = ranges[k]
        load = pltpu.make_async_copy(own_term(chip, t, k), term.at[s, pl.ds(0, size)], t_sem.at[s])
        load.start()
        for way in (0, 1):
            @pl.when(receives(chips - 2, way))
            def _():
                landed(chips - 2, way, t, k)
        load.wait()
        if n >= 2:
            stores[n - 2].wait()

        def finish(i, _):
            rws = pl.ds(pl.multiple_of(i * strip, strip), strip)
            all_rows = pl.ds(pl.multiple_of(start + i * strip, strip), strip)
            value = term[s, rws].astype(jnp.float32)
            for way in (0, 1):
                here = receives(chips - 2, way)
                value = value + jnp.where(here, held[way, chips - 2, t, all_rows].astype(jnp.float32), 0.0)
            total[s, rws] = value.astype(jnp.bfloat16)
            return 0
        lax.fori_loop(0, size // strip, finish, 0)
        stores.append(pltpu.make_async_copy(total.at[s, pl.ds(0, size)], d_ref.at[t, pl.ds(start, size)], o_sem.at[s]))
        stores[n].start()
    for store in stores[-2:]:
        store.wait()

    for t in range(towers):
        for kind in range(3):
            for k in (0, 1):
                grad_arrived(kind, k, t)
        grad_arrived(3, 1 - core, t)
    for kind in range(3):
        small(kind).wait()
    for t in range(towers):
        for kind in range(3):
            for k in (0, 1):
                grad(kind, k, t).wait_send()
        grad(3, 1 - core, t).wait_send()
    for step in range(chips - 1):
        for t, k in pieces:
            for way in (0, 1):
                @pl.when(sends(step, way))
                def _():
                    partial(step, way, t, k, True).wait_send()
    for copy in own:
        copy.wait()


def reduce(partial_d, partial_g, partial_s, chips, ranges, ident):
    towers, rows, wide = partial_d.shape
    depth, cols = wide // chips, partial_g.shape[2] // 2
    count = 2 * (chips - 1) * towers * len(ranges)
    part = max(size for _, size in ranges)
    dma = pltpu.SemaphoreType.DMA
    bf16 = jnp.bfloat16
    out_shape = [jax.ShapeDtypeStruct((towers, rows, depth), bf16),
                 jax.ShapeDtypeStruct((4, 2, towers, depth, cols), bf16),
                 jax.ShapeDtypeStruct((4,) + partial_s.shape, jnp.float32)]
    return pl.pallas_call(
        functools.partial(reduce_kernel, chips, ranges),
        out_shape=out_shape,
        in_specs=[pl.BlockSpec(memory_space=pl.ANY)] * 3,
        out_specs=[pl.BlockSpec(memory_space=pl.ANY)] * len(out_shape),
        scratch_shapes=[pltpu.VMEM((2, chips - 1, towers, rows, depth), bf16),
                        pltpu.VMEM((2, part, depth), bf16), pltpu.VMEM((2, part, depth), bf16),
                        dma((count,)), dma((count,)), dma((2,)), dma((2,)), dma((16,)), dma((16,)), dma((3,)), dma((3,)), dma((towers + 1,))],
        compiler_params=pltpu.CompilerParams(collective_id=ident, has_side_effects=True, vmem_limit_bytes=56 * 2**20),
        cost_estimate=pl.CostEstimate(flops=0, bytes_accessed=800 * 2**20, transcendentals=0),
        name="reduce",
    )(partial_d, partial_g, partial_s)


def loop(count, body):
    def step(i, _):
        body(i)
        return 0
    lax.fori_loop(0, count, step, 0)


def wait_for(ref, sem, other):
    pltpu.make_async_remote_copy(src_ref=ref, dst_ref=ref, send_sem=other, recv_sem=sem, device_id=dict(dp=0, mp=0),
                                 device_id_type=MESH).wait_recv()


class Spot:
    def __init__(self, chips):
        self.dp, self.chip, self.core = place()
        self.chips, self.steps = chips, chips - 1
        self.others = (self.dp ^ 1, self.dp ^ 2, self.dp ^ 3)
        self.ends = (self.chip == 0) | (self.chip == self.steps)

    def at(self, dp, core):
        return dp, 2 * self.chip + core

    def on_line(self, chip):
        return self.dp, 2 * chip + self.core

    def passed(self, way):
        return jnp.where(way == 0, self.chip, self.steps - self.chip)

    def onward(self, way, n):
        return jnp.where(way == 0, self.chip + n, self.chip - n)

    def leaves(self, step, way):
        return (self.passed(way) < self.steps) & (self.passed(way) >= step)

    def comes(self, step, way):
        return self.passed(way) > step

    def greet(self):
        meet([(self.chip > 0, self.on_line(self.chip - 1)), (self.chip < self.steps, self.on_line(self.chip + 1)),
              (self.chip >= 0, self.at(self.dp, 1 - self.core))]
             + [(self.chip >= 0, self.at(c, k)) for c in self.others for k in (0, 1)])


class Features:
    def __init__(self, spot, f_ref, taken, fg, size, send, recv):
        self.spot, self.f_ref, self.taken, self.fg, self.size, self.send, self.recv = spot, f_ref, taken, fg, size, send, recv
        self.depth = f_ref.shape[1]

    def rows(self, q):
        return pl.ds(pl.multiple_of(q * self.size, 16), self.size)

    def lanes(self, shard):
        return pl.ds(pl.multiple_of(shard * self.depth, 128), self.depth)

    def copy(self, step, way, q, src=None):
        ref = self.fg.at[self.rows(q), self.lanes(self.spot.onward(way, -step))]
        return pltpu.make_async_remote_copy(
            src_ref=ref if src is None else src, dst_ref=ref, send_sem=self.send.at[way, step, q], recv_sem=self.recv.at[way, step, q],
            device_id=self.spot.on_line(self.spot.onward(way, 1)), device_id_type=MESH)

    def launch(self, q, last):
        def each(way):
            @pl.when(self.spot.leaves(0, way))
            def _():
                self.copy(0, way, q, self.taken if last else self.f_ref.at[self.rows(q)]).start()
        loop(2, each)

    def arrive(self, step, q):
        def each(way):
            @pl.when(self.spot.comes(step, way))
            def _():
                ref = self.fg.at[self.rows(q), self.lanes(self.spot.onward(way, -1 - step))]
                wait_for(ref, self.recv.at[way, step, q], self.send.at[way, step, q])
        loop(2, each)

    def serve(self, step, q):
        self.arrive(step, q)

        def each(way):
            @pl.when(self.spot.leaves(step + 1, way))
            def _():
                self.copy(step + 1, way, q).start()
        loop(2, each)

    def settle(self, q):
        for step in range(self.spot.steps):
            def each(way):
                @pl.when(self.spot.leaves(step, way))
                def _():
                    self.copy(step, way, q).wait_send()
            loop(2, each)


class Weights:
    def __init__(self, spot, low, wg, own_sem, send, recv):
        self.spot, self.low, self.wg, self.own_sem, self.send, self.recv = spot, low, wg, own_sem, send, recv
        self.depth, self.cols = low.shape[1], low.shape[2]

    def block(self, owner, slot):
        return self.wg.at[pl.ds(pl.multiple_of(owner * self.depth, 128), self.depth), pl.ds(pl.multiple_of(slot * self.cols, 128), self.cols)]

    def round(self, w_ref, wide, sem):
        part = wide.shape[1]
        parts = self.depth // part

        def load(n):
            return pltpu.make_async_copy(w_ref.at[pl.ds(pl.multiple_of(n * part, 16), part)], wide.at[lax.rem(n, 2)], sem.at[lax.rem(n, 2)])

        def one(n):
            @pl.when(n + 1 < 2 * parts)
            def _():
                load(n + 1).start()
            load(n).wait()

            def strip(i):
                rows = pl.ds(pl.multiple_of(i * 16, 16), 16)
                to = pl.ds(pl.multiple_of(lax.rem(n, parts) * part + i * 16, 16), 16)
                self.low[n // parts, to] = wide[lax.rem(n, 2), rows].astype(jnp.bfloat16)
            loop(part // 16, strip)
        load(jnp.int32(0)).start()
        loop(2 * parts, one)

    def send_own(self, kind, slot):
        s = self.spot
        k = s.core ^ slot
        return pltpu.make_async_remote_copy(
            src_ref=self.low.at[k], dst_ref=self.block(s.dp, slot), send_sem=self.send.at[kind, slot], recv_sem=self.recv.at[kind, slot],
            device_id=s.at((s.others[0], s.others[1], s.dp)[kind], k), device_id_type=MESH)

    def send_on(self, kind):
        s = self.spot
        ref = self.block(s.others[kind], kind)
        return pltpu.make_async_remote_copy(
            src_ref=ref, dst_ref=ref, send_sem=self.send.at[3, kind], recv_sem=self.recv.at[3, kind],
            device_id=s.at(s.others[1 - kind], s.core), device_id_type=MESH)

    def arrive(self, kind, slot):
        owner = (self.spot.others[0], self.spot.others[1], self.spot.dp)[kind]
        wait_for(self.block(owner, slot), self.recv.at[kind, slot], self.send.at[kind, slot])

    def own(self):
        return pltpu.make_async_copy(self.low.at[self.spot.core], self.block(self.spot.dp, 0), self.own_sem)

    def start(self):
        self.own().start()
        for slot in (0, 1):
            self.send_own(0, slot).start()
            self.send_own(1, 1 - slot).start()
        self.send_own(2, 1).start()

    def relay(self):
        for kind in (0, 1):
            self.arrive(kind, kind)
            self.send_on(kind).start()

    def finish(self):
        for kind in (0, 1):
            self.arrive(kind, 1 - kind)
            wait_for(self.block(self.spot.others[2], kind), self.recv.at[3, kind], self.send.at[3, kind])
        self.arrive(2, 1)
        self.own().wait()

    def settle(self):
        for kind in (0, 1):
            for slot in (0, 1):
                self.send_own(kind, slot).wait_send()
            self.send_on(kind).wait_send()
        self.send_own(2, 1).wait_send()


class Products:
    def __init__(self, spot, features, wg, f_tile, w_tile, acc, theirs, f_sem, w_sem, send, recv):
        self.spot, self.features, self.wg, self.f_tile, self.w_tile, self.acc, self.theirs = spot, features, wg, f_tile, w_tile, acc, theirs
        self.f_sem, self.w_sem, self.send, self.recv = f_sem, w_sem, send, recv
        self.cols = theirs.shape[1]

    def shard(self, j):
        return jnp.where(self.spot.chip == self.spot.steps, self.spot.steps - j, j)

    def load_w(self, j):
        depth = self.features.depth
        rows = pl.ds(pl.multiple_of(self.shard(j) * depth, 128), depth)
        return pltpu.make_async_copy(self.wg.at[rows], self.w_tile.at[lax.rem(j, 2)], self.w_sem.at[lax.rem(j, 2)])

    def load_f(self, j):
        lanes = self.features.lanes(self.shard(j))
        return pltpu.make_async_copy(self.features.fg.at[:, lanes], self.f_tile.at[lax.rem(j, 2)], self.f_sem.at[lax.rem(j, 2)])

    def here(self, j):
        return (j < self.spot.steps) | jnp.logical_not(self.spot.ends)

    def add(self, slot, rows):
        for col in range(0, 2 * self.cols, self.cols):
            lanes = pl.ds(col, self.cols)
            self.acc[rows, lanes] += jnp.dot(self.f_tile[slot, rows], self.w_tile[slot, :, lanes], preferred_element_type=jnp.float32)

    def multiply(self):
        def unit(j):
            @pl.when(j < self.spot.steps)
            def _():
                self.load_w(j + 1).start()

            @pl.when((j < self.spot.steps) & self.here(j + 1))
            def _():
                self.load_f(j + 1).start()
            self.load_w(j).wait()

            @pl.when(self.here(j))
            def _():
                self.load_f(j).wait()
                loop(self.acc.shape[0] // self.features.size, lambda q: self.add(lax.rem(j, 2), self.features.rows(q)))
        self.load_w(jnp.int32(0)).start()
        self.load_f(jnp.int32(0)).start()
        loop(self.spot.chips, unit)

    def swap(self, q):
        rows = self.features.rows(q)
        return pltpu.make_async_remote_copy(
            src_ref=self.acc.at[rows, pl.ds(self.cols, self.cols)], dst_ref=self.theirs.at[rows], send_sem=self.send.at[q],
            recv_sem=self.recv.at[q], device_id=self.spot.at(self.spot.dp, 1 - self.spot.core), device_id_type=MESH)

    def complete(self, q):
        slot = self.spot.steps % 2
        self.features.arrive(self.spot.steps - 1, q)

        @pl.when(self.spot.ends)
        def _():
            rows = self.features.rows(q)
            copy = pltpu.make_async_copy(self.features.fg.at[rows, self.features.lanes(self.shard(self.spot.steps))],
                                         self.f_tile.at[slot, rows], self.f_sem.at[slot])
            copy.start()
            copy.wait()
            self.add(slot, rows)
        self.swap(q).start()


class Backward:
    def __init__(self, spot, size, dz_here, dz_ref, send, recv, out_sem):
        self.spot, self.size, self.dz_here, self.dz_ref, self.send, self.recv, self.out_sem = spot, size, dz_here, dz_ref, send, recv, out_sem
        self.cols = dz_here.shape[1]

    def rows(self, q):
        return pl.ds(pl.multiple_of(q * self.size, 16), self.size)

    def swap(self, q):
        return pltpu.make_async_remote_copy(
            src_ref=self.dz_here.at[self.rows(q)], dst_ref=self.dz_ref.at[self.rows(q), pl.ds(self.cols, self.cols)],
            send_sem=self.send.at[q], recv_sem=self.recv.at[q], device_id=self.spot.at(self.spot.dp, 1 - self.spot.core), device_id_type=MESH)

    def keep(self, q):
        return pltpu.make_async_copy(self.dz_here.at[self.rows(q)], self.dz_ref.at[self.rows(q), pl.ds(0, self.cols)], self.out_sem.at[q])

    def start(self, q):
        self.swap(q).start()
        self.keep(q).start()

    def settle(self, q):
        self.swap(q).wait_recv()
        self.swap(q).wait_send()
        self.keep(q).wait()


def gelu_and_slope(v):
    factor, cubic = math.sqrt(2.0 / math.pi), 0.044715
    square = v * v
    th = jnp.tanh(factor * (v + cubic * (square * v)))
    slope = 0.5 * (1.0 + th) + 0.5 * v * (1.0 - th * th) * (factor * (1.0 + 3.0 * cubic * square))
    return 0.5 * v * (1.0 + th), slope


def live_rows_of(tot, share, live):
    keep = share[0][0]
    cols = live.shape[1]

    def strip(i):
        row = lax.broadcasted_iota(jnp.int32, (16, cols), 0).astype(jnp.float32) + (i * 16).astype(jnp.float32)
        here = jnp.where(row < tot[0, :1, :cols], 1.0, 0.0)
        there = jnp.zeros_like(here)
        for kind in range(4):
            count = tot[kind, :1, :cols]
            slot = row + float(share[kind][0] - keep)
            valid = (slot < count) & (count > keep)
            if kind == 3:
                valid = valid & (slot >= share[2][0] + share[2][1])
            there = there + jnp.where(valid, 1.0, 0.0)
        live[pl.ds(pl.multiple_of(i * 16, 16), 16)] = jnp.where(row < keep, here, there)
    loop(live.shape[0] // 16, strip)


def clear(ref):
    def strip(i):
        ref[pl.ds(pl.multiple_of(i * 16, 16), 16)] = jnp.zeros((16, ref.shape[1]), ref.dtype)
    loop(ref.shape[0] // 16, strip)


def fold(term):
    return term[:8] + term[8:]


class Grads:
    jobs, thirds = 8, 3

    def __init__(self, spot, fg, dz_here, gr, pg, relay, f_part, g_part, r_part, f_sem, g_sem, r_sem, send, recv, relay_send, relay_recv, own_sem):
        self.spot, self.fg, self.dz_here, self.gr, self.pg, self.relay_ref = spot, fg, dz_here, gr, pg, relay
        self.f_part, self.g_part, self.r_part, self.f_sem, self.g_sem, self.r_sem = f_part, g_part, r_part, f_sem, g_sem, r_sem
        self.send, self.recv, self.relay_send, self.relay_recv, self.own_sem = send, recv, relay_send, relay_recv, own_sem
        self.depth, self.cols = pg.shape[1], pg.shape[2]
        self.part = self.depth // self.thirds

    def owner_of(self, m):
        return jnp.where(m < 2, 3, jnp.where((m == 4) | (m == 5), 0, jnp.where((m == 2) | (m == 7), 1, 2)))

    def third(self, n):
        return pl.ds(pl.multiple_of(lax.rem(n, self.thirds) * self.part, 128), self.part)

    def load(self, n):
        first = (self.spot.dp ^ self.owner_of(n // self.thirds)) * self.depth + lax.rem(n, self.thirds) * self.part
        return pltpu.make_async_copy(self.fg.at[:, pl.ds(pl.multiple_of(first, 128), self.part)], self.f_part.at[lax.rem(n, 2)],
                                     self.f_sem.at[lax.rem(n, 2)])

    def store(self, n):
        return pltpu.make_async_copy(self.g_part.at[lax.rem(n, 2)], self.pg.at[n // self.thirds, self.third(n)], self.g_sem.at[lax.rem(n, 2)])

    def relay(self, m):
        return pltpu.make_async_remote_copy(
            src_ref=self.pg.at[m], dst_ref=self.relay_ref.at[m], send_sem=self.relay_send.at[m], recv_sem=self.relay_recv.at[m],
            device_id=self.spot.at(self.spot.dp ^ (m + 1), self.spot.core), device_id_type=MESH)

    def relayed(self, n):
        return pltpu.make_async_copy(self.relay_ref.at[jnp.maximum(n // self.thirds - (self.jobs - 2), 0), self.third(n)],
                                     self.r_part.at[lax.rem(n, 2)], self.r_sem.at[lax.rem(n, 2)])

    def job(self, m):
        joins = m >= self.jobs - 2
        lanes = pl.ds(pl.multiple_of(lax.rem(m, 2) * self.cols, 128), self.cols)

        @pl.when(joins)
        def _():
            k = jnp.maximum(m - (self.jobs - 2), 0)
            wait_for(self.relay_ref.at[k], self.relay_recv.at[k], self.relay_send.at[k])
            self.relayed(m * self.thirds).start()

        def part(c):
            n = m * self.thirds + c

            @pl.when(joins & (c + 1 < self.thirds))
            def _():
                self.relayed(n + 1).start()

            @pl.when(n + 1 < self.jobs * self.thirds)
            def _():
                self.load(n + 1).start()
            self.load(n).wait()

            @pl.when((n >= 2) & (n != (self.jobs - 2) * self.thirds) & (n != (self.jobs - 2) * self.thirds + 1))
            def _():
                self.store(n - 2).wait()

            @pl.when(joins)
            def _():
                self.relayed(n).wait()
            value = lax.dot_general(self.f_part[lax.rem(n, 2)], self.dz_here[:, lanes], (((0,), (0,)), ((), ())),
                                    preferred_element_type=jnp.float32)

            @pl.when(joins)
            def _():
                self.g_part[lax.rem(n, 2)] = (value + self.r_part[lax.rem(n, 2)].astype(jnp.float32)).astype(jnp.bfloat16)

            @pl.when(jnp.logical_not(joins))
            def _():
                self.g_part[lax.rem(n, 2)] = value.astype(jnp.bfloat16)
            self.store(n).start()
        loop(self.thirds, part)

    def copy(self, m):
        away, k = self.owner_of(m), self.spot.core ^ lax.rem(m, 2)
        return pltpu.make_async_remote_copy(
            src_ref=self.pg.at[m], dst_ref=self.gr.at[away, self.spot.core], send_sem=self.send.at[m],
            recv_sem=self.recv.at[away, self.spot.core], device_id=self.spot.at(self.spot.dp ^ away, k), device_id_type=MESH)

    def own(self):
        return pltpu.make_async_copy(self.pg.at[4], self.gr.at[0, self.spot.core], self.own_sem)

    def start(self, m):
        @pl.when(m < 2)
        def _():
            self.relay(jnp.minimum(m, 1)).start()

        @pl.when((m >= 2) & (m != 4))
        def _():
            self.copy(m).start()

        @pl.when(m == 4)
        def _():
            self.own().start()

    def turn(self, m, begin, late):
        early = self.jobs - 2
        pause = begin + early

        def job_at(m):
            return jnp.where(m < pause, m - begin, m - late + early)

        @pl.when((m == pause) | (m == late + 2))
        def _():
            for c in (1, 2):
                self.store(job_at(m - 1) * self.thirds + c).wait()

        @pl.when(((m >= begin) & (m < pause)) | (m == late) | (m == late + 1))
        def _():
            self.job(job_at(m))

        @pl.when(((m > begin) & (m <= pause)) | (m == late + 1) | (m == late + 2))
        def _():
            self.start(job_at(m - 1))

    def settle(self):
        for away in range(3):
            for k in (0, 1):
                @pl.when((away != 0) | (self.spot.core != k))
                def _():
                    wait_for(self.gr.at[away, k], self.recv.at[away, k], self.send.at[2])
        self.own().wait()
        for m in range(self.jobs):
            if m < 2:
                self.relay(m).wait_send()
            elif m != 4:
                self.copy(jnp.int32(m)).wait_send()


class Sums:
    window, lag = 5, 1

    def __init__(self, spot, parts, share, d_ref, dz_here, w_here, held, total, send, recv, out_sem, back_send, back_recv):
        self.spot, self.parts, self.share, self.d_ref, self.dz_here, self.w_here, self.held, self.total = spot, parts, share, d_ref, dz_here, w_here, held, total
        self.send, self.recv, self.out_sem, self.back_send, self.back_recv = send, recv, out_sem, back_send, back_recv
        self.size, self.depth = total.shape[1], total.shape[2]
        self.turns = spot.steps * parts
        self.skip = self.size - share[0][1]

    def rows(self, piece):
        return pl.ds(pl.multiple_of(lax.rem(piece + self.parts - 1, self.parts) * self.size, 16), self.size)

    def third(self, n):
        return pl.ds(pl.multiple_of(n * (self.depth // 3), 128), self.depth // 3)

    def sends(self, step, way):
        return (self.spot.passed(way) < self.spot.steps) & (self.spot.passed(way) <= step)

    def passing(self, m, way, turn):
        rows = self.rows(lax.rem(m, self.parts))
        return pltpu.make_async_remote_copy(
            src_ref=self.held.at[way, turn // self.parts, rows], dst_ref=self.held.at[way, m // self.parts, rows],
            send_sem=self.send.at[way, m], recv_sem=self.recv.at[way, m], device_id=self.spot.on_line(self.spot.onward(way, 1)),
            device_id_type=MESH)

    def landed(self, m, way):
        wait_for(self.held.at[way, m // self.parts, self.rows(lax.rem(m, self.parts))], self.recv.at[way, m], self.send.at[way, m])

    def product(self, goal, rows, col):
        return lax.dot_general(self.dz_here[rows], self.w_here[goal, self.third(col)], (((1,), (1,)), ((), ())),
                               preferred_element_type=jnp.float32)

    def store(self, piece):
        s = lax.rem(piece, 2)
        return pltpu.make_async_copy(self.total.at[s], self.d_ref.at[self.rows(piece)], self.out_sem.at[s])

    def hand(self, kind):
        to, taken = share_rows(self.share, kind)
        return pltpu.make_async_remote_copy(
            src_ref=self.total.at[0, pl.ds(self.skip + taken.start, taken.size)], dst_ref=self.d_ref.at[to], send_sem=self.back_send.at[kind],
            recv_sem=self.back_recv.at[kind], device_id=self.spot.at(self.spot.others[kind], self.spot.core), device_id_type=MESH)

    def send_sum(self, m, way):
        step, rows = m // self.parts, self.rows(lax.rem(m, self.parts))
        first = self.spot.passed(way) == 0
        held = self.held

        @pl.when(first & (m >= self.window))
        def _():
            self.passing(jnp.maximum(m - self.window, 0), way, 0).wait_send()

        @pl.when(jnp.logical_not(first))
        def _():
            self.landed(m - self.parts, way)

        def column(col):
            lanes = self.third(col)
            value = self.product(self.spot.onward(way, self.spot.steps - step), rows, col)

            @pl.when(first)
            def _():
                held[way, step, rows, lanes] = value.astype(jnp.bfloat16)

            @pl.when(jnp.logical_not(first))
            def _():
                held[way, step - 1, rows, lanes] = (value + held[way, step - 1, rows, lanes].astype(jnp.float32)).astype(jnp.bfloat16)
        loop(3, column)
        self.passing(m, way, jnp.where(first, m, m - self.parts)).start()

    def finish(self, piece):
        rows, s = self.rows(piece), lax.rem(piece, 2)
        held, total, last = self.held, self.total, self.spot.steps - 1

        @pl.when(piece >= 2)
        def _():
            self.store(piece - 2).wait()

        @pl.when(piece == 2)
        def _():
            for kind in range(3):
                self.hand(kind).wait_send()

        def each(way):
            @pl.when(self.spot.passed(way) > 0)
            def _():
                self.landed(self.turns - self.parts + piece, way)
        loop(2, each)

        def column(col):
            value = self.product(self.spot.chip, rows, col)
            lanes = self.third(col)

            @pl.when(self.spot.ends)
            def _():
                way = jnp.where(self.spot.chip == 0, 1, 0)
                total[s, :, lanes] = (value + held[way, last, rows, lanes].astype(jnp.float32)).astype(jnp.bfloat16)

            @pl.when(jnp.logical_not(self.spot.ends))
            def _():
                total[s, :, lanes] = (value + held[0, last, rows, lanes].astype(jnp.float32)
                                      + held[1, last, rows, lanes].astype(jnp.float32)).astype(jnp.bfloat16)
        loop(3, column)
        self.store(piece).start()

        @pl.when(piece == 0)
        def _():
            for kind in (2, 0, 1):
                self.hand(kind).start()

    def turn(self, m):
        def each(way):
            @pl.when((m < self.turns) & self.sends(m // self.parts, way))
            def _():
                self.send_sum(m, way)
        loop(2, each)

    def turn_end(self, m):
        first = self.turns - self.parts + self.lag

        @pl.when((m >= first) & (m < first + self.parts))
        def _():
            self.finish(m - first)

    def settle(self):
        def drain(m):
            def each(way):
                first = self.spot.passed(way) == 0

                @pl.when(self.sends(m // self.parts, way) & (jnp.logical_not(first) | (m >= self.turns - self.window)))
                def _():
                    self.passing(m, way, 0).wait_send()
            loop(2, each)
        loop(self.turns, drain)
        for piece in (self.parts - 2, self.parts - 1):
            self.store(piece).wait()

    def returned(self):
        for kind in range(3):
            self.hand(kind).wait_recv()


def share_rows(share, kind):
    skip = share[2][0] + share[2][1] - share[3][0] if kind == 2 else 0
    first, length = share[1 + kind]
    return pl.ds(first + skip, length - skip), pl.ds(skip, length - skip)


class Bases:
    def __init__(self, left, right, out, held, parts, load_sem, store_sem):
        self.sources, self.out, self.held, self.parts, self.load_sem, self.store_sem = (left, right), out, held, parts, load_sem, store_sem
        self.groups, self.pairs = left.shape[1], left.shape[2] // 2
        self.units = left.shape[0] * self.groups

    def at(self, u):
        return u // self.groups, lax.rem(u, self.groups), lax.rem(u, 2)

    def load(self, u, start):
        t, r, slot = self.at(u)
        for n, source in enumerate(self.sources):
            copy = pltpu.make_async_copy(source.at[t, r], self.held.at[slot, n], self.load_sem.at[slot, n])
            (copy.start if start else copy.wait)()

    def store(self, u, start):
        t, r, slot = self.at(u)
        for n in (0, 1):
            copy = pltpu.make_async_copy(self.parts.at[slot, n], self.out.at[n, t, r], self.store_sem.at[slot, n])
            (copy.start if start else copy.wait)()

    def unit(self, u):
        @pl.when(u + 1 < self.units)
        def _():
            self.load(u + 1, True)
        self.load(u, False)

        @pl.when(u >= 2)
        def _():
            self.store(u - 2, False)
        slot = lax.rem(u, 2)
        for n in (0, 1):
            for q in range(self.pairs):
                both = jnp.concatenate([self.held[slot, n, 2 * q], self.held[slot, n, 2 * q + 1]], axis=1)
                high, low = split(both)
                rows = pl.ds(q * BLOCK, BLOCK)
                self.parts[slot, n, 0, rows] = high
                self.parts[slot, n, 1, rows] = low
        self.store(u, True)

    def some(self, first, count):
        def one(i):
            @pl.when(first + i < self.units)
            def _():
                self.unit(first + i)
        loop(count, one)

    def settle(self):
        for u in (self.units - 2, self.units - 1):
            self.store(jnp.int32(u), False)


class Stitched:
    def __init__(self, spot, share, y_ref, st_ref, y_send, y_recv, core_send, core_recv, give_send, give_recv, given_send, given_recv, own_sem):
        self.spot, self.share, self.y_ref, self.st_ref = spot, share, y_ref, st_ref
        self.y_send, self.y_recv, self.core_send, self.core_recv = y_send, y_recv, core_send, core_recv
        self.give_send, self.give_recv, self.given_send, self.given_recv, self.own_sem = give_send, give_recv, given_send, given_recv, own_sem
        self.towers, self.cols = y_ref.shape[0], y_ref.shape[2]
        self.bands = (share[0], (0, share[0][0]))
        self.events = 2 * self.towers * spot.steps

    def lanes(self, shard, k):
        return pl.ds(pl.multiple_of((2 * shard + k) * self.cols, 128), self.cols)

    def place(self, shard, k, t, b):
        return self.st_ref.at[t, pl.ds(*self.bands[b]), self.lanes(shard, k)]

    def source(self, t, b):
        return self.y_ref.at[t, pl.ds(*self.bands[b])]

    def leave(self, step, way, t, b, own=False):
        s = self.spot
        dst = self.place(s.onward(way, -step), s.core, t, b)
        return pltpu.make_async_remote_copy(
            src_ref=self.source(t, b) if own else dst, dst_ref=dst, send_sem=self.y_send.at[way, step, b, t],
            recv_sem=self.y_recv.at[way, step, b, t], device_id=s.on_line(s.onward(way, 1)), device_id_type=MESH)

    def to_core(self, shard, t, b, own=False):
        s = self.spot
        dst = self.place(shard, s.core, t, b)
        return pltpu.make_async_remote_copy(
            src_ref=self.source(t, b) if own else dst, dst_ref=dst, send_sem=self.core_send.at[shard, b, t],
            recv_sem=self.core_recv.at[shard, b, t], device_id=s.at(s.dp, 1 - s.core), device_id_type=MESH)

    def give(self, kind, shard, t, own=False):
        s = self.spot
        to, taken = share_rows(self.share, kind)
        src = pl.ds(self.share[0][0] + taken.start, taken.size)
        return pltpu.make_async_remote_copy(
            src_ref=self.y_ref.at[t, src] if own else self.st_ref.at[t, src, self.lanes(shard, s.core)],
            dst_ref=self.st_ref.at[t, to, self.lanes(shard, s.core)], send_sem=self.give_send.at[kind, shard, t],
            recv_sem=self.give_recv.at[kind, shard, t], device_id=s.at(s.others[kind], s.core), device_id_type=MESH)

    def given_place(self, kind, shard, t, k):
        return self.st_ref.at[t, share_rows(self.share, kind)[0], self.lanes(shard, k)]

    def given(self, kind, shard, t):
        s = self.spot
        ref = self.given_place(kind, shard, t, s.core)
        return pltpu.make_async_remote_copy(
            src_ref=ref, dst_ref=ref, send_sem=self.given_send.at[kind, shard, t], recv_sem=self.given_recv.at[kind, shard, t],
            device_id=s.at(s.dp, 1 - s.core), device_id_type=MESH)

    def own(self, t, b):
        return pltpu.make_async_copy(self.source(t, b), self.place(self.spot.chip, self.spot.core, t, b), self.own_sem.at[b, t])

    def start(self):
        for b in (0, 1):
            def tower(t):
                def each(way):
                    @pl.when(self.spot.leaves(0, way))
                    def _():
                        self.leave(0, way, t, b, True).start()
                loop(2, each)
                self.to_core(self.spot.chip, t, b, True).start()
                if b == 0:
                    for kind in (2, 0, 1):
                        self.give(kind, self.spot.chip, t, True).start()
                self.own(t, b).start()
            loop(self.towers, tower)

    def event(self, n):
        step, t = n // (2 * self.towers), lax.rem(n, self.towers)
        for b in (0, 1):
            def each(way):
                @pl.when(self.spot.comes(step, way))
                def _():
                    shard = self.spot.onward(way, -1 - step)
                    wait_for(self.place(shard, self.spot.core, t, b), self.y_recv.at[way, step, b, t], self.y_send.at[way, step, b, t])

                    @pl.when((step + 1 < self.spot.steps) & self.spot.leaves(step + 1, way))
                    def _():
                        self.leave(jnp.minimum(step + 1, self.spot.steps - 1), way, t, b).start()
                    self.to_core(shard, t, b).start()
                    if b == 0:
                        for kind in (2, 0, 1):
                            self.give(kind, shard, t).start()

            @pl.when(lax.rem(n, 2 * self.towers) // self.towers == b)
            def _():
                loop(2, each)

    def receive(self):
        def one(n):
            shard, t = n // self.towers, lax.rem(n, self.towers)
            for kind in range(3):
                wait_for(self.given_place(kind, shard, t, self.spot.core), self.give_recv.at[kind, shard, t], self.give_send.at[kind, shard, t])
                self.given(kind, shard, t).start()
        loop(self.spot.chips * self.towers, one)

    def settle(self):
        def one(n):
            shard, t = n // self.towers, lax.rem(n, self.towers)
            for b in (0, 1):
                wait_for(self.place(shard, 1 - self.spot.core, t, b), self.core_recv.at[shard, b, t], self.core_send.at[shard, b, t])
                self.to_core(shard, t, b).wait_send()

                @pl.when(shard < self.spot.steps)
                def _():
                    def each(way):
                        @pl.when(self.spot.leaves(shard, way))
                        def _():
                            self.leave(jnp.minimum(shard, self.spot.steps - 1), way, t, b).wait_send()
                    loop(2, each)
            for kind in range(3):
                self.give(kind, shard, t).wait_send()
                self.given(kind, shard, t).wait_send()
                wait_for(self.given_place(kind, shard, t, 1 - self.spot.core), self.given_recv.at[kind, shard, t], self.given_send.at[kind, shard, t])
        loop(self.spot.chips * self.towers, one)
        for t in range(self.towers):
            for b in (0, 1):
                self.own(t, b).wait()


def front_kernel(chips, parts, share, f_ref, w_ref, o_ref, n_ref, sp_ref, left_ref, right_ref,
                 fg_first, wg_first, dz_first, fg_ref, wg_ref, dz_ref, tot_ref, bases_ref, st_ref, sr_ref,
                 d_first, gr_first, pg_first, relay_first, d_ref, gr_ref, pg_ref, relay_ref,
                 offer_f, taken, offer_o, wide, low, base_in, base_out, tot,
                 og, f_tile, w_tile, acc, theirs, live, act, dz_here, y_here, sums_here, sg,
                 held, w_here, dz_wide, total, f_part, g_part, r_part,
                 f_send, f_recv, w_send, w_recv, a_send, a_recv, z_send, z_recv, out_sem,
                 wide_sem, p_sem, x_send, x_recv, l_sem, base_load, base_store,
                 d_send, d_recv, o_sem, b_send, b_recv, g_load, g_send, g_recv, rs_send, rs_recv, own_sem, s_send, s_recv, ready,
                 y_send, y_recv, core_send, core_recv, give_send, give_recv, given_send, given_recv, y_own):
    spot = Spot(chips)
    keep, rows = share[0][0], sum(share[0])
    size = rows // parts
    fixed = rows - size
    spare = keep - fixed
    cols = o_ref.shape[2]
    tot[0] = jnp.zeros_like(tot[0]) + jnp.sum(n_ref[...].astype(jnp.float32), axis=1, keepdims=True)
    spot.greet()

    def offer(kind, what):
        src = (f_ref.at[0], f_ref.at[1], o_ref, tot.at[0])[what]
        dst = (offer_f.at[0, 1 + kind], offer_f.at[1, 1 + kind], offer_o.at[1 + kind], tot.at[1 + kind])[what]
        if what < 3:
            src = src.at[pl.ds(*share[1 + kind])] if what < 2 else src.at[:, pl.ds(*share[1 + kind])]
        return pltpu.make_async_remote_copy(
            src_ref=src, dst_ref=dst, send_sem=x_send.at[what, kind], recv_sem=x_recv.at[what, kind],
            device_id=spot.at(spot.others[kind], spot.core), device_id_type=MESH)

    def choose(width, read, write):
        weigh = [jnp.broadcast_to(jnp.where(tot[kind, :1, :width] > keep, 1.0, 0.0), (16, width)) for kind in range(4)]

        def strip(i):
            at = pl.ds(pl.multiple_of(i * 16, 16), 16)
            value = read(0, at).astype(jnp.float32) * weigh[0]
            for kind in range(1, 4):
                value = value + read(kind, at).astype(jnp.float32) * weigh[kind]
            write(i * 16, value.astype(jnp.bfloat16))
        loop(share[0][1] // 16, strip)

    def take(t):
        def write(row, value):
            taken[t, pl.ds(pl.multiple_of(spare + row, 16), 16)] = value
        choose(offer_f.shape[3], lambda kind, at: offer_f[t, kind, at], write)

    towers = []
    for t, (fg, wg, dz) in enumerate(((fg_first, wg_first, dz_first), (fg_ref, wg_ref, dz_ref))):
        features = Features(spot, f_ref.at[t], taken.at[t], fg, size, f_send.at[t], f_recv.at[t])
        weights = Weights(spot, low.at[t], wg, p_sem.at[t, 4], w_send.at[t], w_recv.at[t])
        products = Products(spot, features, wg, f_tile, w_tile, acc, theirs.at[t], p_sem.at[t, pl.ds(0, 2)], p_sem.at[t, pl.ds(2, 2)],
                            a_send.at[t], a_recv.at[t])
        backward = Backward(spot, size, dz_here, dz, z_send.at[t], z_recv.at[t], out_sem.at[t])
        towers.append((features, weights, products, backward))
    features, weights, products, backward = towers[0]
    sums = []
    for t, (fg, d, gr, pg, relay) in enumerate(((fg_first, d_first, gr_first, pg_first, relay_first), (fg_ref, d_ref, gr_ref, pg_ref, relay_ref))):
        sums.append((Sums(spot, parts, share, d, dz_wide, w_here, held, total, d_send.at[t], d_recv.at[t], o_sem, b_send.at[t], b_recv.at[t]),
                     Grads(spot, fg, dz_wide, gr, pg, relay, f_part, g_part, r_part, g_load.at[0], g_load.at[1], g_load.at[2],
                           g_send.at[t], g_recv.at[t], rs_send.at[t], rs_recv.at[t], own_sem.at[t])))
    gradients, grads = sums[0]
    stitched = Stitched(spot, share, y_here, st_ref, y_send, y_recv, core_send, core_recv, give_send, give_recv, given_send, given_recv, y_own)
    bases = Bases(left_ref, right_ref, bases_ref, base_in, base_out, base_load, base_store)

    def copy(n, src, dst):
        made = pltpu.make_async_copy(src, dst, l_sem.at[n])
        made.start()
        return made

    for what in (3, 0):
        for kind in (2, 0, 1):
            offer(kind, what).start()
    loop(parts - 1, lambda q: features.launch(q, False))
    needed = [copy(0, f_ref.at[0, pl.ds(*share[0])], offer_f.at[0, 0])]
    later = [copy(1, f_ref.at[1, pl.ds(*share[0])], offer_f.at[1, 0])]
    if spare:
        needed.append(copy(2, f_ref.at[0, pl.ds(fixed, spare)], taken.at[0, pl.ds(0, spare)]))
        later.append(copy(3, f_ref.at[1, pl.ds(fixed, spare)], taken.at[1, pl.ds(0, spare)]))
    later += [copy(4, o_ref.at[:, pl.ds(*share[0])], offer_o.at[0]), copy(5, o_ref.at[:, pl.ds(0, keep)], og.at[:, pl.ds(0, keep)]),
              copy(6, f_ref.at[0, pl.ds(0, fixed)], fg_first.at[pl.ds(0, fixed), features.lanes(spot.chip)]),
              copy(7, f_ref.at[1, pl.ds(0, fixed)], fg_ref.at[pl.ds(0, fixed), features.lanes(spot.chip)])]
    weights.round(w_ref.at[0], wide, wide_sem)
    weights.start()
    for made in needed:
        made.wait()
    for what in (3, 0):
        for kind in range(3):
            offer(kind, what).wait_recv()
    take(0)
    features.launch(parts - 1, True)
    later += [copy(8, tot, tot_ref), copy(9, taken.at[0], fg_first.at[pl.ds(fixed, size), features.lanes(spot.chip)])]
    live_rows_of(tot, share, live)
    clear(acc)
    sums_here[...] = jnp.zeros_like(sums_here)
    towers[1][1].round(w_ref.at[1], wide, wide_sem)
    share_of = -(-bases.units // (2 * parts))

    def serve(step, q):
        features.serve(step, q)
        bases.some((step * parts + q) * share_of, share_of)
    bases.load(jnp.int32(0), True)
    loop(parts, lambda q: serve(0, q))
    weights.relay()
    for what in (2, 1):
        for kind in (2, 0, 1):
            offer(kind, what).start()
    loop(parts, lambda q: serve(1, q))
    weights.finish()
    towers[1][1].start()
    for made in later:
        made.wait()
    products.multiply()
    for kind in range(3):
        offer(kind, 2).wait_recv()
    for t in range(2):
        def write(row, value):
            og[t, pl.ds(pl.multiple_of(keep + row, 16), 16)] = value
        choose(cols, lambda kind, at: offer_o[kind, t, at], write)

    def strip(t, at):
        activated, slope = gelu_and_slope(acc[at, :cols] + theirs[t, at] + sp_ref[t : t + 1])
        mask = live[at]
        dy = [og[n, at].astype(jnp.float32) * mask for n in range(2)]
        dz = slope * (sp_ref[2 + t : 3 + t] * dy[0] + sp_ref[4 + t : 5 + t] * dy[1])
        if t == 0:
            act[at] = activated
        else:
            other = act[at]
            for n in range(2):
                y_here[n, at] = ((sp_ref[2 + 2 * n : 3 + 2 * n] * other + sp_ref[3 + 2 * n : 4 + 2 * n] * activated) * mask).astype(jnp.bfloat16)
        dz_here[at] = dz.astype(jnp.bfloat16)
        for n, term in enumerate((dz, activated * dy[0], activated * dy[1])):
            sums_here[2 * n + t] += fold(term)

    def stage(t, k):
        _, _, products, backward = towers[t]

        @pl.when(k < parts)
        def _():
            products.complete(k)

        @pl.when(k > 0)
        def _():
            products.swap(k - 1).wait_recv()
            loop(size // 16, lambda i: strip(t, pl.ds(pl.multiple_of((k - 1) * size + i * 16, 16), 16)))
            backward.start(k - 1)
    loop(parts + 1, lambda k: stage(0, k))

    def settle(t, q):
        towers[t][0].settle(q)
        towers[t][2].swap(q).wait_send()
        towers[t][3].settle(q)
    for kind in range(3):
        offer(kind, 1).wait_recv()
    take(1)
    loop(parts, lambda q: settle(0, q))
    loads = weight_loads(chips, wg_first, w_here, l_sem.at[pl.ds(11, chips)])
    loads.append(copy(11 + chips, dz_first, dz_wide))
    features, weights, products, backward = towers[1]
    loop(parts - 1, lambda q: features.launch(q, False))
    features.launch(parts - 1, True)
    last = copy(0, taken.at[1], fg_ref.at[pl.ds(fixed, size), features.lanes(spot.chip)])
    grads.load(jnp.int32(0)).start()
    clear(acc)
    for made in loads:
        made.wait()

    def turn(m):
        gradients.turn(m)
        grads.turn(m, 2, 10)

        @pl.when(m == 2)
        def _():
            weights.relay()

        @pl.when((m >= 2) & (m < 2 + parts))
        def _():
            features.serve(0, m - 2)

        @pl.when((m >= 4 + parts) & (m < 4 + 2 * parts))
        def _():
            features.serve(1, m - 4 - parts)

        @pl.when(m == 4 + 2 * parts)
        def _():
            weights.finish()
            last.wait()
            products.multiply()
        gradients.turn_end(m)
    loop(gradients.turns + gradients.lag, turn)

    gradients.settle()

    def neighbours(method):
        for side, here, chip in ((0, spot.chip > 0, spot.chip - 1), (1, spot.chip < spot.steps, spot.chip + 1)):
            @pl.when(here)
            def _():
                method(side, chip)
    neighbours(lambda side, chip: pl.semaphore_signal(ready.at[1 - side], inc=1, device_id=spot.on_line(chip), device_id_type=MESH))
    loads = weight_loads(chips, wg_ref, w_here, l_sem.at[pl.ds(11, chips)])
    loop(parts + 1, lambda k: stage(1, k))
    stitched.start()
    sg[...] = jnp.zeros_like(sg)
    for n in range(6):
        sg[n : n + 1] = jnp.sum(sums_here[n], axis=0, keepdims=True)
    own = copy(1, sg, sr_ref.at[spot.dp])

    def small(kind):
        return pltpu.make_async_remote_copy(
            src_ref=sg, dst_ref=sr_ref.at[spot.dp], send_sem=s_send.at[kind], recv_sem=s_recv.at[kind],
            device_id=spot.at(spot.others[kind], spot.core), device_id_type=MESH)
    for kind in range(3):
        small(kind).start()
    loop(parts, lambda q: settle(1, q))
    wide_dz = copy(11 + chips, dz_ref, dz_wide)
    gradients, grads = sums[1]
    grads.load(jnp.int32(0)).start()
    for made in loads:
        made.wait()
    wide_dz.wait()
    neighbours(lambda side, chip: pl.semaphore_wait(ready.at[side], 1))

    def second_turn(m):
        gradients.turn(m)
        grads.turn(m, 0, 7)

        @pl.when((m >= 1) & (m <= stitched.events))
        def _():
            stitched.event(m - 1)
        gradients.turn_end(m)
    loop(gradients.turns + gradients.lag, second_turn)
    stitched.receive()
    gradients.settle()
    stitched.settle()
    for t in range(2):
        sums[t][0].returned()
        sums[t][1].settle()
        towers[t][1].settle()
    bases.settle()
    own.wait()
    for kind in range(3):
        small(kind).wait()
    for what in range(4):
        for kind in range(3):
            offer(kind, what).wait_send()


def weight_loads(chips, wg, w_here, sem):
    depth = w_here.shape[1]
    loads = [pltpu.make_async_copy(wg.at[pl.ds(n * depth, depth)], w_here.at[n], sem.at[n]) for n in range(chips)]
    for copy in loads:
        copy.start()
    return loads


def call(kernel, name, ident, out, scratch, operands, small_in=(), flops=0):
    anywhere, here = pl.BlockSpec(memory_space=pl.ANY), pl.BlockSpec(memory_space=pltpu.VMEM)
    return pl.pallas_call(
        kernel,
        out_shape=out,
        in_specs=[here if n in small_in else anywhere for n in range(len(operands))],
        out_specs=[anywhere] * len(out),
        scratch_shapes=scratch,
        compiler_params=pltpu.CompilerParams(collective_id=ident, has_side_effects=True, vmem_limit_bytes=62 * 2**20),
        cost_estimate=pl.CostEstimate(flops=flops, bytes_accessed=500 * 2**20, transcendentals=0),
        name=name,
    )(*operands)


def parts_of(share):
    rows = sum(share[0])
    return max(n for n in range(1, rows // 16) if rows % (16 * n) == 0 and rows // n >= share[0][1])


def shared_pass(features, weights, out_grad, counts, small_params, left, right, chips, share):
    parts = parts_of(share)
    towers, slots, depth = features.shape
    cols = weights.shape[2]
    keep, size = share[0]
    rows = keep + size
    steps = chips - 1
    piece = rows // parts
    dma, vmem = pltpu.SemaphoreType.DMA, pltpu.VMEM
    bf16, f32 = jnp.bfloat16, jnp.float32
    S = jax.ShapeDtypeStruct
    beside = (left.shape[2] // 2 * BLOCK, 2 * BLOCK)
    wide = [S((rows, chips * depth), bf16), S((chips * depth, 2 * cols), bf16), S((rows, 2 * cols), bf16)]
    sums = [S((slots, depth), bf16), S((3, 2, depth, cols), bf16), S((8, depth, cols), bf16), S((2, depth, cols), bf16)]
    out = call(
        functools.partial(front_kernel, chips, parts, share), "passes", 3,
        wide + wide + [S((4, 8, depth), f32), S((2,) + left.shape[:2] + (2,) + beside, bf16),
                       S((towers, slots, 2 * chips * cols), bf16), S((4, 8, cols), f32)] + sums + sums,
        [vmem((towers, 4, size, depth), bf16), vmem((towers, piece, depth), bf16), vmem((4, towers, size, cols), bf16),
         vmem((2, depth // 8, cols), f32), vmem((towers, 2, depth, cols), bf16), vmem((2, 2) + left.shape[2:], f32), vmem((2, 2, 2) + beside, bf16),
         vmem((4, 8, depth), f32), vmem((towers, rows, cols), bf16), vmem((2, rows, depth), bf16), vmem((2, depth, 2 * cols), bf16),
         vmem((rows, 2 * cols), f32), vmem((towers, rows, cols), f32), vmem((rows, cols), f32), vmem((rows, cols), f32), vmem((rows, cols), bf16),
         vmem((towers, rows, cols), bf16), vmem((6, 8, cols), f32), vmem((8, cols), f32),
         vmem((2, steps, rows, depth), bf16), vmem((chips, depth, 2 * cols), bf16), vmem((rows, 2 * cols), bf16),
         vmem((2, piece, depth), bf16), vmem((2, rows, depth // 3), bf16)] + [vmem((2, depth // 3, cols), bf16)] * 2
        + [dma((towers, 2, steps, parts))] * 2 + [dma((towers, 4, 2))] * 2 + [dma((towers, parts))] * 5
        + [dma((2,)), dma((towers, 5)), dma((4, 3)), dma((4, 3)), dma((12 + chips,)), dma((2, 2)), dma((2, 2))]
        + [dma((towers, 2, steps * parts))] * 2 + [dma((2,)), dma((towers, 3)), dma((towers, 3)), dma((3, 2)), dma((towers, 8)), dma((towers, 3, 2)),
                                                   dma((towers, 2)), dma((towers, 2)), dma((towers,)), dma((3,)), dma((3,)), pltpu.SemaphoreType.REGULAR((2,))]
        + [dma((2, steps, 2, towers))] * 2 + [dma((chips, 2, towers))] * 2 + [dma((3, chips, towers))] * 4 + [dma((2, towers))],
        (features, weights, out_grad, counts.reshape(1, -1), small_params, left, right), (3, 4), 6 * 2 * rows * 2 * cols * depth * chips)
    told, bases, stitched, smalls, d_first, gr_first, _, _, d_second, gr_second, _, _ = out[6:]
    return told, bases, ((d_first, d_second), stitched, (gr_first, gr_second), smalls)


def small_step(small_params, small_moment_one, small_moment_two, small_average, small_grad):
    first, second, direction = adam_part(small_moment_one, small_moment_two, small_grad)
    fresh = small_params - rate_small * direction
    return first, second, fresh, ema_decay * small_average + (1.0 - ema_decay) * fresh


def update(d_feat, stitched, full, parts, small_parts, states, small_states):
    small_grad = jnp.sum(small_parts, 0)[: small_states[0].shape[0]]
    *fresh, stitched, d_feat = soap(parts, full, stitched, d_feat, *states)
    return (stitched, d_feat) + tuple(fresh) + small_step(*small_states, small_grad)


def own_rows(features, out_grad, totals, passed, states, small_states):
    _, rows, _ = features.shape
    weights, small_params = states[0], small_states[0]
    cols = weights.shape[2]
    cores = lax.axis_size("mp")
    swap = [(i, i ^ 1) for i in range(cores)]
    ranges = ((0, rows // 2), (rows // 2, rows // 2))
    live_rows = (jnp.arange(rows, dtype=jnp.float32) < totals[0]).astype(jnp.float32)
    wide_f, wide_w = gather(features, weights.astype(jnp.bfloat16), cores // 2, ranges, 1)
    partial = jnp.einsum("tri,tio->tro", wide_f, wide_w, preferred_element_type=jnp.float32)
    product = partial[:, :, :cols] + lax.ppermute(partial[:, :, cols:], "mp", swap)
    result, back = jax.vjp(lambda a, b: stitch_local(a, b, live_rows), product, small_params)
    stitched = lax.all_gather(result.astype(jnp.bfloat16), "mp", axis=2, tiled=True)
    dz, small_part = back(out_grad.astype(jnp.float32))
    dz_low = dz.astype(jnp.bfloat16)
    wide_dz = jnp.concatenate([dz_low, lax.ppermute(dz_low, "mp", swap)], axis=2)
    partial_d = jnp.einsum("tro,tio->tri", wide_dz, wide_w, preferred_element_type=jnp.float32)
    partial_g = jnp.einsum("tri,tro->tio", wide_f, wide_dz, preferred_element_type=jnp.float32)
    small_part = jnp.pad(small_part, ((0, 2), (0, 0)))
    d_feat, parts, small_parts = reduce(
        partial_d.astype(jnp.bfloat16), partial_g.astype(jnp.bfloat16), small_part, cores // 2, ranges, 2
    )
    full = jnp.full((1,), rows, jnp.int32)
    return update((d_feat[0], d_feat[1]), stitched, full, (parts[:, :, 0], parts[:, :, 1]), small_parts, states, small_states)


def shares(rows):
    keep = rows * 15 // 32 // 16 * 16
    size = -(-(rows - keep) // 64) * 16
    return keep, ((keep, size), (keep + size, size), (keep + 2 * size, size), (rows - size, size))


def shared_rows(features, out_grad, totals, passed, states, small_states):
    rows = features.shape[1]
    keep, _ = shares(rows)
    d_feat, stitched, parts, small_parts = passed
    full = jnp.where(totals[:1] > keep, rows, keep)
    return update(d_feat, stitched, full, parts, small_parts, states, small_states)


def line_body(
    features,
    counts,
    weights,
    small_params,
    out_grad,
    moment_one,
    moment_two,
    average,
    basis_left,
    basis_right,
    small_moment_one,
    small_moment_two,
    small_average,
):
    keep, share = shares(features.shape[1])
    told, bases, passed = shared_pass(
        features, weights, out_grad, counts, small_params, basis_left, basis_right, lax.axis_size("mp") // 2, share
    )
    totals = told[:, 0, 0]
    return lax.cond(
        jnp.sum(totals > keep) == 1,
        shared_rows,
        own_rows,
        features,
        out_grad,
        totals,
        passed,
        (weights, moment_one, moment_two, average, bases),
        (small_params, small_moment_one, small_moment_two, small_average),
    )


def plain_body(
    features,
    counts,
    weights,
    small_params,
    out_grad,
    moment_one,
    moment_two,
    average,
    basis_left,
    basis_right,
    small_moment_one,
    small_moment_two,
    small_average,
):
    slot_count = features.shape[1]
    total = jnp.sum(counts)
    live_rows = (jnp.arange(slot_count, dtype=jnp.int32) < total).astype(jnp.float32)
    weights_low = lax.all_gather(weights.astype(jnp.bfloat16), "dp", axis=1, tiled=True)
    feats_full = lax.all_gather(features, "mp", axis=2, tiled=True)
    product = jnp.einsum(
        "tri,tio->tro", feats_full, weights_low, preferred_element_type=jnp.float32
    )
    result, back = jax.vjp(lambda a, b: stitch_local(a, b, live_rows), product, small_params)
    stitched = lax.all_gather(result.astype(jnp.bfloat16), "mp", axis=2, tiled=True)
    dz, small_part = back(out_grad.astype(jnp.float32))
    dz_low = dz.astype(jnp.bfloat16)
    grad_part = jnp.einsum("tri,tro->tio", feats_full, dz_low, preferred_element_type=jnp.float32)
    partial_sums = jnp.einsum(
        "tro,tio->tri", dz_low, weights_low, preferred_element_type=jnp.float32
    )
    d_feat = lax.psum_scatter(
        partial_sums.astype(jnp.float32), "mp", scatter_dimension=2, tiled=True
    )
    grad = lax.psum_scatter(grad_part, "dp", scatter_dimension=1, tiled=True)
    small_grad = lax.psum(small_part, "dp")
    towers, n_in, n_out = grad.shape
    blocks = grad.reshape(towers, n_in // BLOCK, BLOCK, n_out // BLOCK, BLOCK)
    rotated = jnp.einsum(
        "trcai,tracb,trcbj->tricj", basis_left, blocks, basis_right, precision=lax.Precision.HIGHEST
    ).reshape(towers, n_in, n_out)
    first, second, direction = adam_part(moment_one, moment_two, rotated)
    turned = direction.reshape(towers, n_in // BLOCK, BLOCK, n_out // BLOCK, BLOCK)
    step_back = jnp.einsum(
        "trcai,tricj,trcbj->tracb", basis_left, turned, basis_right, precision=lax.Precision.HIGHEST
    ).reshape(towers, n_in, n_out)
    new_weights = weights - rate_main * (step_back + decay_weight * weights)
    new_average = ema_decay * average + (1.0 - ema_decay) * new_weights
    return (
        stitched,
        d_feat.astype(jnp.bfloat16),
        first,
        second,
        new_weights,
        new_average,
        new_weights.astype(jnp.bfloat16),
    ) + small_step(small_params, small_moment_one, small_moment_two, small_average, small_grad)


def solution(mesh):
    def body(features, counts, weights, *rest):
        dp, mp = mesh.shape["dp"], mesh.shape["mp"]
        tiles = features.shape[2] % 128 == 0 and weights.shape[2] % 128 == 0
        suits = dp == 4 and mp == 2 * dp and tiles and features.shape[1] % 64 == 0
        return (line_body if suits else plain_body)(features, counts, weights, *rest)

    return jax.shard_map(
        body,
        mesh=mesh,
        in_specs=(
            P(None, "dp", "mp"),
            P("dp"),
            P(None, "dp", "mp"),
            P(None, "mp"),
            P(None, "dp", "mp"),
            P(None, "dp", "mp"),
            P(None, "dp", "mp"),
            P(None, "dp", "mp"),
            P(None, "dp", "mp", None, None),
            P(None, "dp", "mp", None, None),
            P(None, "mp"),
            P(None, "mp"),
            P(None, "mp"),
        ),
        out_specs=(
            P(None, "dp", None),
            P(None, "dp", "mp"),
            P(None, "dp", "mp"),
            P(None, "dp", "mp"),
            P(None, "dp", "mp"),
            P(None, "dp", "mp"),
            P(None, "dp", "mp"),
            P(None, "mp"),
            P(None, "mp"),
            P(None, "mp"),
            P(None, "mp"),
        ),
        check_vma=False,
    )
```

```python
import functools
import math

import jax
import jax.numpy as jnp
from jax import lax
from jax.experimental import pallas as pl
from jax.experimental.pallas import tpu as pltpu
from jax.sharding import PartitionSpec as P

BLOCK = 64
STEP = 5


beta_one = 0.5
beta_two = 0.5
ema_decay = 0.5
rate_main = 0.01
rate_small = 0.05
decay_weight = 0.01
eps = 1e-08


def stitch_local(product, small, live_rows):
    pre_act = product + small[0:2][:, None, :]
    activated = jax.nn.gelu(pre_act, approximate=True)
    first = small[2] * activated[0] + small[3] * activated[1]
    second = small[4] * activated[0] + small[5] * activated[1]
    return jnp.stack([first, second]) * live_rows[None, :, None]


def adam_part(moment_a, moment_b, grad):
    first = beta_one * moment_a + (1.0 - beta_one) * grad
    second = beta_two * moment_b + (1.0 - beta_two) * grad * grad
    direction = first / (1.0 - beta_one**STEP) / (jnp.sqrt(second / (1.0 - beta_two**STEP)) + eps)
    return (first, second, direction)

def split(v):
    high = v.astype(jnp.bfloat16)
    return high, (v - high.astype(jnp.float32)).astype(jnp.bfloat16)

def soap_blocks(grads, lefts, rights, moments):
    row = lax.broadcasted_iota(jnp.int32, (2 * BLOCK, 2 * BLOCK), 0) // BLOCK
    lane = lax.broadcasted_iota(jnp.int32, (2 * BLOCK, 2 * BLOCK), 1) // BLOCK
    own = row == lane

    def diagonal(v):
        return jnp.where(own, jnp.concatenate([v, v], axis=0), jnp.zeros((), v.dtype))

    def stationary(high, low, axis):
        return jnp.concatenate([high, high, low], axis=axis)

    def moving(v, axis):
        high, low = split(v)
        return jnp.concatenate([high, low, high], axis=axis)

    def dots(a, b, ca, cb):
        dims = (((ca,), (cb,)), ((), ()))
        return [lax.dot_general(x, y, dims, preferred_element_type=jnp.float32) for x, y in zip(a, b)]

    right = [(diagonal(high), diagonal(low)) for high, low in rights]
    values = dots([moving(v, 1) for v in grads], [stationary(*v, 0) for v in right], 1, 0)
    values = dots([stationary(*v, 0) for v in lefts], [moving(v, 0) for v in values], 0, 0)
    values = [jnp.where(lane[:BLOCK] == 0, v[:BLOCK], v[BLOCK:]) for v in values]
    states = [adam_part(a, b, v) for (a, b), v in zip(moments, values)]
    values = dots([moving(v[2], 1) for v in states], [stationary(*v, 1) for v in right], 1, 1)
    values = dots([stationary(*v, 1) for v in lefts], [moving(diagonal(v), 0) for v in values], 1, 0)
    return [(first, second, step) for (first, second, _), step in zip(states, values)]


def soap_body(together, strips, full, parts_a, parts_b, stitched, d_a, d_b, weights, moment_a, moment_b, average, left, right,
              first, second, new_weights, new_average, copy, stitched_out, d_feat_out):
    groups, pairs = left.shape[2], left.shape[4] // BLOCK
    length = stitched.shape[1]
    row = jnp.minimum(pl.program_id(1) * pl.num_programs(2) + pl.program_id(2), strips - 1) * length

    first_tower = pl.program_id(0) == 0

    def clear(i, _):
        rows = pl.ds(pl.multiple_of(i * 16, 16), 16)
        wanted = row + i * 16 < full[0]
        stitched_out[0, rows] = jnp.where(wanted, stitched[0, rows], 0)
        d_feat_out[0, rows] = jnp.where(wanted, jnp.where(first_tower, d_a[rows], d_b[rows]), 0)
        return 0

    lax.fori_loop(0, length // 16, clear, 0)

    def blocks(g, _):
        places = [(g * together + s, q) for s in range(together) for q in range(pairs)]
        ats = [(0, pl.ds(pl.multiple_of(r * BLOCK, BLOCK), BLOCK), pl.ds(2 * BLOCK * q, 2 * BLOCK)) for r, q in places]
        grads = []
        for at in ats:
            grads.append(sum(jnp.where(first_tower, parts_a[(k,) + at], parts_b[(k,) + at]).astype(jnp.float32)
                             for k in range(parts_a.shape[0])))
        def basis(ref, r, q):
            return tuple(ref[0, 0, r, k, BLOCK * q : BLOCK * (q + 1)] for k in (0, 1))

        done = soap_blocks(grads, [basis(left, *place) for place in places], [basis(right, *place) for place in places],
                           [(moment_a[at], moment_b[at]) for at in ats])
        olds = [(weights[at], average[at]) for at in ats]
        for at, (one, two, step), (held, mean) in zip(ats, done, olds):
            first[at] = one
            second[at] = two
            fresh = held - rate_main * (step + decay_weight * held)
            new_weights[at] = fresh
            new_average[at] = ema_decay * mean + (1.0 - ema_decay) * fresh
            copy[at] = fresh.astype(jnp.bfloat16)
        return 0

    lax.fori_loop(0, groups // together, blocks, 0)


def soap(parts, wanted, stitched, d_feat, weights, moment_a, moment_b, average, bases, group=6):
    towers, rows, cols = weights.shape
    half = parts[0].shape[2]
    steps = half // (BLOCK * group)
    flat = lambda t, p, g: (t, p * steps + g, 0)
    state = pl.BlockSpec((1, BLOCK * group, cols), flat)
    base = [pl.BlockSpec((1, 1, group) + bases.shape[3:], lambda t, p, g, n=n: (n, t, p * steps + g, 0, 0, 0)) for n in (0, 1)]
    full = jax.ShapeDtypeStruct(weights.shape, jnp.float32)
    strips = max(n for n in range(1, 2 * steps + 1) if stitched.shape[1] % (16 * n) == 0)

    def strip(p, g):
        return jnp.minimum(p * steps + g, strips - 1)

    def through(shape):
        return pl.BlockSpec((1, shape[1] // strips, shape[2]), lambda t, p, g: (t, strip(p, g), 0))

    def of_tower(n, shape, index, last):
        return pl.BlockSpec(shape, lambda t, p, g: tuple(jnp.where(t == n, a, b) for a, b in zip(index(p, g), last if n == 0 else index(0, 0))))

    pieces = [of_tower(n, (v.shape[0], 1, BLOCK * group, cols), lambda p, g: (0, p, g, 0), (0, 1, steps - 1, 0)) for n, v in enumerate(parts)]
    rows_of = [of_tower(n, (v.shape[0] // strips, v.shape[1]), lambda p, g: (strip(p, g), 0), (strips - 1, 0)) for n, v in enumerate(d_feat)]

    return pl.pallas_call(
        functools.partial(soap_body, group, strips),
        grid=(towers, 2, steps),
        in_specs=[pl.BlockSpec(memory_space=pltpu.SMEM),
                  *pieces, through(stitched.shape), *rows_of, state, state, state, state, *base],
        out_specs=[state] * 5 + [through(stitched.shape), through((towers,) + d_feat[0].shape)],
        out_shape=[full] * 4 + [jax.ShapeDtypeStruct(weights.shape, jnp.bfloat16)]
        + [jax.ShapeDtypeStruct(v, jnp.bfloat16) for v in (stitched.shape, (towers,) + d_feat[0].shape)],
        compiler_params=pltpu.CompilerParams(vmem_limit_bytes=60 * 2**20),
        cost_estimate=pl.CostEstimate(flops=8 * 2 * towers * rows * cols * 64, bytes_accessed=130 * 2**20, transcendentals=0),
        name="soap",
    )(wanted, *parts, stitched, *d_feat, weights, moment_a, moment_b, average, bases, bases)


MESH = pl.DeviceIdType.MESH


def place():
    mp = lax.axis_index("mp")
    return lax.axis_index("dp"), mp // 2, lax.rem(mp, 2)


def meet(devices):
    barrier = pltpu.get_barrier_semaphore()
    expected = 0
    for here, device in devices:
        @pl.when(here)
        def _():
            pl.semaphore_signal(barrier, inc=1, device_id=device, device_id_type=MESH)
        expected = expected + jnp.where(here, 1, 0)
    pl.semaphore_wait(barrier, expected)


def gather_kernel(chips, ranges, f_ref, w_ref, fg_ref, wg_ref, f_send, f_recv, w_send, w_recv, own_sem):
    dp, chip, core = place()
    towers, rows, depth = f_ref.shape
    cols = w_ref.shape[2]
    across, along = dp ^ 1, dp ^ 2
    at = lambda c, k: (c, 2 * chip + k)

    meet([(chip > 0, (dp, 2 * (chip - 1) + core)), (chip < chips - 1, (dp, 2 * (chip + 1) + core)),
          (chip >= 0, at(dp, 1 - core))] + [(chip >= 0, at(c, k)) for c in (across, along) for k in (0, 1)])

    def copies(step, way, t, k, shard, there):
        lanes = pl.ds(pl.multiple_of(shard * depth, 128), depth)
        rws = pl.ds(*ranges[k])
        src = fg_ref.at[t, rws, lanes]
        if step == 0:
            src = f_ref.at[t, rws]
        n = ((way * (chips - 1) + step) * towers + t) * len(ranges) + k
        return pltpu.make_async_remote_copy(
            src_ref=src, dst_ref=fg_ref.at[t, rws, lanes], send_sem=f_send.at[n], recv_sem=f_recv.at[n],
            device_id=(dp, 2 * there + core), device_id_type=MESH)

    def feature(step, way, t, k):
        return copies(step, way, t, k, chip - step if way == 0 else chip + step, chip + 1 if way == 0 else chip - 1)

    def incoming(step, way, t, k):
        return copies(step, way, t, k, chip - 1 - step if way == 0 else chip + 1 + step, chip)

    def sends(step, way):
        return (chip < chips - 1) & (chip >= step) if way == 0 else (chip > 0) & (chip + step < chips)

    def receives(step, way):
        return chip > step if way == 0 else chip + step < chips - 1

    def launch(t, k):
        for way in (0, 1):
            @pl.when(sends(0, way))
            def _():
                feature(0, way, t, k).start()

    def block(owner, slot, t):
        return wg_ref.at[t, pl.ds(pl.multiple_of(owner * depth, 128), depth), pl.ds(pl.multiple_of(slot * cols, 128), cols)]

    def weight(kind, k, t):
        to = at((across, along, dp)[kind], k)
        n = (kind * 2 + core) * 2 + t
        return pltpu.make_async_remote_copy(
            src_ref=w_ref.at[t, pl.ds(pl.multiple_of(k * depth, 128), depth)], dst_ref=block(dp, k ^ core, t),
            send_sem=w_send.at[(kind * 2 + k) * 2 + t], recv_sem=w_recv.at[n], device_id=to, device_id_type=MESH)

    def forward(kind, slot):
        owner, to, t = ((across, along, 0), (along, across, 1))[kind]
        n = 12 + kind * 2 + slot
        return pltpu.make_async_remote_copy(
            src_ref=block(owner, slot, t), dst_ref=block(owner, slot, t),
            send_sem=w_send.at[n], recv_sem=w_recv.at[n], device_id=at(to, core), device_id_type=MESH)

    def arrived(kind, slot, t):
        owner = (across, along, dp)[kind]
        n = (kind * 2 + (slot ^ core)) * 2 + t
        pltpu.make_async_remote_copy(
            src_ref=block(owner, slot, t), dst_ref=block(owner, slot, t), send_sem=w_send.at[n], recv_sem=w_recv.at[n],
            device_id=at(dp, core), device_id_type=MESH).wait_recv()

    mine = pl.ds(pl.multiple_of(chip * depth, 128), depth)
    own = [pltpu.make_async_copy(f_ref.at[t], fg_ref.at[t, :, mine], own_sem.at[t]) for t in range(towers)]
    own += [pltpu.make_async_copy(w_ref.at[t, pl.ds(pl.multiple_of(core * depth, 128), depth)], block(dp, 0, t), own_sem.at[2 + t])
            for t in range(towers)]

    pieces = [(t, k) for k in range(len(ranges)) for t in range(towers)]
    for t, k in pieces:
        launch(t, k)
    for copy in own:
        copy.start()
    for t in (0, 1):
        for k in (0, 1):
            weight(0, k, t).start()
            weight(1, k, 1 - t).start()
    for t in (0, 1):
        weight(2, 1 - core, t).start()

    for step in range(chips - 1):
        for t, k in pieces:
            for way in (0, 1):
                @pl.when(receives(step, way))
                def _():
                    incoming(step, way, t, k).wait_recv()
                if step + 1 < chips - 1:
                    @pl.when(sends(step + 1, way))
                    def _():
                        feature(step + 1, way, t, k).start()
            if step == 0 and (t, k) == pieces[-1]:
                for slot in (0, 1):
                    arrived(0, slot, 0)
                    forward(0, slot).start()
                    arrived(1, slot, 1)
                    forward(1, slot).start()

    for slot in (0, 1):
        arrived(0, slot, 1)
        arrived(1, slot, 0)
        forward(0, slot).wait_recv()
        forward(1, slot).wait_recv()
    for t in (0, 1):
        arrived(2, 1, t)
    for t in (0, 1):
        for k in (0, 1):
            weight(0, k, t).wait_send()
            weight(1, k, t).wait_send()
        weight(2, 1 - core, t).wait_send()
    for slot in (0, 1):
        forward(0, slot).wait_send()
        forward(1, slot).wait_send()
    for step in range(chips - 1):
        for t, k in pieces:
            for way in (0, 1):
                @pl.when(sends(step, way))
                def _():
                    feature(step, way, t, k).wait_send()
    for copy in own:
        copy.wait()


def gather(features, weights_low, chips, ranges, ident):
    towers, rows, depth = features.shape
    cols = weights_low.shape[2]
    count = 2 * (chips - 1) * towers * len(ranges)
    dma = pltpu.SemaphoreType.DMA
    anywhere = pl.BlockSpec(memory_space=pl.ANY)
    return pl.pallas_call(
        functools.partial(gather_kernel, chips, ranges),
        out_shape=[jax.ShapeDtypeStruct((towers, rows, chips * depth), jnp.bfloat16),
                   jax.ShapeDtypeStruct((towers, chips * depth, 2 * cols), jnp.bfloat16)],
        in_specs=[anywhere] * 2,
        out_specs=[anywhere] * 2,
        scratch_shapes=[dma((count,)), dma((count,)), dma((16,)), dma((16,)), dma((4,))],
        compiler_params=pltpu.CompilerParams(collective_id=ident, has_side_effects=True),
        cost_estimate=pl.CostEstimate(flops=0, bytes_accessed=800 * 2**20, transcendentals=0),
        name="gather",
    )(features, weights_low)


def reduce_kernel(chips, ranges, pd_ref, pg_ref, ps_ref, d_ref, gr_ref, sr_ref, held, term, total,
                  d_send, d_recv, t_sem, o_sem, g_send, g_recv, s_send, s_recv, own_sem):
    dp, chip, core = place()
    towers, rows, depth = d_ref.shape
    cols = pg_ref.shape[2] // 2
    across, along = dp ^ 1, dp ^ 2
    others = (across, along, dp ^ 3)
    at = lambda c, k: (c, 2 * chip + k)

    meet([(chip > 0, (dp, 2 * (chip - 1) + core)), (chip < chips - 1, (dp, 2 * (chip + 1) + core)),
          (chip >= 0, at(dp, 1 - core))] + [(chip >= 0, at(c, k)) for c in others for k in (0, 1)])

    def grad(kind, k, t):
        owner = (others + (dp,))[kind]
        return pltpu.make_async_remote_copy(
            src_ref=pg_ref.at[t, pl.ds(pl.multiple_of(owner * depth, 128), depth), pl.ds(pl.multiple_of((k ^ core) * cols, 128), cols)],
            dst_ref=gr_ref.at[dp, core, t], send_sem=g_send.at[(kind * 2 + k) * 2 + t],
            recv_sem=g_recv.at[(kind * 2 + core) * 2 + t], device_id=at(owner, k), device_id_type=MESH)

    def grad_arrived(kind, k, t):
        owner = (others + (dp,))[kind]
        pltpu.make_async_remote_copy(
            src_ref=gr_ref.at[owner, k, t], dst_ref=gr_ref.at[owner, k, t], send_sem=g_send.at[0],
            recv_sem=g_recv.at[(kind * 2 + k) * 2 + t], device_id=at(dp, core), device_id_type=MESH).wait_recv()

    def small(kind):
        return pltpu.make_async_remote_copy(
            src_ref=ps_ref, dst_ref=sr_ref.at[dp], send_sem=s_send.at[kind], recv_sem=s_recv.at[kind],
            device_id=at(others[kind], core), device_id_type=MESH)

    def target(step, way):
        return chip + chips - 1 - step if way == 0 else chip - (chips - 1 - step)

    def sends(step, way):
        return (chip < chips - 1) & (chip <= step) if way == 0 else (chip > 0) & (chips - 1 - chip <= step)

    def receives(step, way):
        return (chip > 0) & (chip <= step + 1) if way == 0 else (chip < chips - 1) & (chips - 1 - chip <= step + 1)

    def own_term(goal, t, k):
        return pd_ref.at[t, pl.ds(*ranges[k]), pl.ds(pl.multiple_of(goal * depth, 128), depth)]

    def partial(step, way, t, k, first):
        n = ((way * (chips - 1) + step) * towers + t) * len(ranges) + k
        src = own_term(target(step, way), t, k) if first else held.at[way, step - 1, t, pl.ds(*ranges[k])]
        there = chip + 1 if way == 0 else chip - 1
        return pltpu.make_async_remote_copy(
            src_ref=src, dst_ref=held.at[way, step, t, pl.ds(*ranges[k])], send_sem=d_send.at[n], recv_sem=d_recv.at[n],
            device_id=(dp, 2 * there + core), device_id_type=MESH)

    def landed(step, way, t, k):
        n = ((way * (chips - 1) + step) * towers + t) * len(ranges) + k
        ref = held.at[way, step, t, pl.ds(*ranges[k])]
        pltpu.make_async_remote_copy(src_ref=ref, dst_ref=ref, send_sem=d_send.at[n], recv_sem=d_recv.at[n],
                                     device_id=(dp, 2 * chip + core), device_id_type=MESH).wait_recv()

    pieces = [(t, k) for t in range(towers) for k in range(len(ranges))]
    ends = (chip == 0, chip == chips - 1)
    for t, k in pieces:
        for way in (0, 1):
            @pl.when(ends[way])
            def _():
                partial(0, way, t, k, True).start()
    own = [pltpu.make_async_copy(
        pg_ref.at[t, pl.ds(pl.multiple_of(dp * depth, 128), depth), pl.ds(0, cols)], gr_ref.at[dp, core, t], own_sem.at[t])
        for t in range(towers)]
    own.append(pltpu.make_async_copy(ps_ref, sr_ref.at[dp], own_sem.at[towers]))
    for copy in own:
        copy.start()
    for kind in range(3):
        small(kind).start()
    for t in range(towers):
        for kind in (2, 0, 1):
            for k in (0, 1):
                grad(kind, k, t).start()
        grad(3, 1 - core, t).start()

    strip = 16

    for step in range(1, chips - 1):
        for t, k in pieces:
            for way in (0, 1):
                @pl.when(sends(step, way) & ends[way])
                def _():
                    partial(step, way, t, k, True).start()

                @pl.when(sends(step, way) & jnp.logical_not(ends[way]))
                def _():
                    start, size = ranges[k]
                    load = pltpu.make_async_copy(own_term(target(step, way), t, k), term.at[way, pl.ds(0, size)], t_sem.at[way])
                    load.start()
                    landed(step - 1, way, t, k)
                    load.wait()

                    def add(i, _):
                        rws = pl.ds(pl.multiple_of(i * strip, strip), strip)
                        all_rows = pl.ds(pl.multiple_of(start + i * strip, strip), strip)
                        held[way, step - 1, t, all_rows] = (
                            held[way, step - 1, t, all_rows].astype(jnp.float32) + term[way, rws].astype(jnp.float32)
                        ).astype(jnp.bfloat16)
                        return 0
                    lax.fori_loop(0, size // strip, add, 0)
                    partial(step, way, t, k, False).start()

    stores = []
    for n, (t, k) in enumerate(pieces):
        s = n % 2
        start, size = ranges[k]
        load = pltpu.make_async_copy(own_term(chip, t, k), term.at[s, pl.ds(0, size)], t_sem.at[s])
        load.start()
        for way in (0, 1):
            @pl.when(receives(chips - 2, way))
            def _():
                landed(chips - 2, way, t, k)
        load.wait()
        if n >= 2:
            stores[n - 2].wait()

        def finish(i, _):
            rws = pl.ds(pl.multiple_of(i * strip, strip), strip)
            all_rows = pl.ds(pl.multiple_of(start + i * strip, strip), strip)
            value = term[s, rws].astype(jnp.float32)
            for way in (0, 1):
                here = receives(chips - 2, way)
                value = value + jnp.where(here, held[way, chips - 2, t, all_rows].astype(jnp.float32), 0.0)
            total[s, rws] = value.astype(jnp.bfloat16)
            return 0
        lax.fori_loop(0, size // strip, finish, 0)
        stores.append(pltpu.make_async_copy(total.at[s, pl.ds(0, size)], d_ref.at[t, pl.ds(start, size)], o_sem.at[s]))
        stores[n].start()
    for store in stores[-2:]:
        store.wait()

    for t in range(towers):
        for kind in range(3):
            for k in (0, 1):
                grad_arrived(kind, k, t)
        grad_arrived(3, 1 - core, t)
    for kind in range(3):
        small(kind).wait()
    for t in range(towers):
        for kind in range(3):
            for k in (0, 1):
                grad(kind, k, t).wait_send()
        grad(3, 1 - core, t).wait_send()
    for step in range(chips - 1):
        for t, k in pieces:
            for way in (0, 1):
                @pl.when(sends(step, way))
                def _():
                    partial(step, way, t, k, True).wait_send()
    for copy in own:
        copy.wait()


def reduce(partial_d, partial_g, partial_s, chips, ranges, ident):
    towers, rows, wide = partial_d.shape
    depth, cols = wide // chips, partial_g.shape[2] // 2
    count = 2 * (chips - 1) * towers * len(ranges)
    part = max(size for _, size in ranges)
    dma = pltpu.SemaphoreType.DMA
    bf16 = jnp.bfloat16
    out_shape = [jax.ShapeDtypeStruct((towers, rows, depth), bf16),
                 jax.ShapeDtypeStruct((4, 2, towers, depth, cols), bf16),
                 jax.ShapeDtypeStruct((4,) + partial_s.shape, jnp.float32)]
    return pl.pallas_call(
        functools.partial(reduce_kernel, chips, ranges),
        out_shape=out_shape,
        in_specs=[pl.BlockSpec(memory_space=pl.ANY)] * 3,
        out_specs=[pl.BlockSpec(memory_space=pl.ANY)] * len(out_shape),
        scratch_shapes=[pltpu.VMEM((2, chips - 1, towers, rows, depth), bf16),
                        pltpu.VMEM((2, part, depth), bf16), pltpu.VMEM((2, part, depth), bf16),
                        dma((count,)), dma((count,)), dma((2,)), dma((2,)), dma((16,)), dma((16,)), dma((3,)), dma((3,)), dma((towers + 1,))],
        compiler_params=pltpu.CompilerParams(collective_id=ident, has_side_effects=True, vmem_limit_bytes=56 * 2**20),
        cost_estimate=pl.CostEstimate(flops=0, bytes_accessed=800 * 2**20, transcendentals=0),
        name="reduce",
    )(partial_d, partial_g, partial_s)


def loop(count, body):
    def step(i, _):
        body(i)
        return 0
    lax.fori_loop(0, count, step, 0)


def wait_for(ref, sem, other):
    pltpu.make_async_remote_copy(src_ref=ref, dst_ref=ref, send_sem=other, recv_sem=sem, device_id=dict(dp=0, mp=0),
                                 device_id_type=MESH).wait_recv()


class Spot:
    def __init__(self, chips):
        self.dp, self.chip, self.core = place()
        self.chips, self.steps = chips, chips - 1
        self.others = (self.dp ^ 1, self.dp ^ 2, self.dp ^ 3)
        self.ends = (self.chip == 0) | (self.chip == self.steps)

    def at(self, dp, core):
        return dp, 2 * self.chip + core

    def on_line(self, chip):
        return self.dp, 2 * chip + self.core

    def passed(self, way):
        return jnp.where(way == 0, self.chip, self.steps - self.chip)

    def onward(self, way, n):
        return jnp.where(way == 0, self.chip + n, self.chip - n)

    def leaves(self, step, way):
        return (self.passed(way) < self.steps) & (self.passed(way) >= step)

    def comes(self, step, way):
        return self.passed(way) > step

    def greet(self):
        meet([(self.chip > 0, self.on_line(self.chip - 1)), (self.chip < self.steps, self.on_line(self.chip + 1)),
              (self.chip >= 0, self.at(self.dp, 1 - self.core))]
             + [(self.chip >= 0, self.at(c, k)) for c in self.others for k in (0, 1)])


class Features:
    def __init__(self, spot, f_ref, taken, fg, size, send, recv):
        self.spot, self.f_ref, self.taken, self.fg, self.size, self.send, self.recv = spot, f_ref, taken, fg, size, send, recv
        self.depth = f_ref.shape[1]

    def rows(self, q):
        return pl.ds(pl.multiple_of(q * self.size, 16), self.size)

    def lanes(self, shard):
        return pl.ds(pl.multiple_of(shard * self.depth, 128), self.depth)

    def copy(self, step, way, q, src=None):
        ref = self.fg.at[self.rows(q), self.lanes(self.spot.onward(way, -step))]
        return pltpu.make_async_remote_copy(
            src_ref=ref if src is None else src, dst_ref=ref, send_sem=self.send.at[way, step, q], recv_sem=self.recv.at[way, step, q],
            device_id=self.spot.on_line(self.spot.onward(way, 1)), device_id_type=MESH)

    def launch(self, q, last):
        def each(way):
            @pl.when(self.spot.leaves(0, way))
            def _():
                self.copy(0, way, q, self.taken if last else self.f_ref.at[self.rows(q)]).start()
        loop(2, each)

    def arrive(self, step, q):
        def each(way):
            @pl.when(self.spot.comes(step, way))
            def _():
                ref = self.fg.at[self.rows(q), self.lanes(self.spot.onward(way, -1 - step))]
                wait_for(ref, self.recv.at[way, step, q], self.send.at[way, step, q])
        loop(2, each)

    def serve(self, step, q):
        self.arrive(step, q)

        def each(way):
            @pl.when(self.spot.leaves(step + 1, way))
            def _():
                self.copy(step + 1, way, q).start()
        loop(2, each)

    def settle(self, q):
        for step in range(self.spot.steps):
            def each(way):
                @pl.when(self.spot.leaves(step, way))
                def _():
                    self.copy(step, way, q).wait_send()
            loop(2, each)


class Weights:
    def __init__(self, spot, low, wg, own_sem, send, recv):
        self.spot, self.low, self.wg, self.own_sem, self.send, self.recv = spot, low, wg, own_sem, send, recv
        self.depth, self.cols = low.shape[1], low.shape[2]

    def block(self, owner, slot):
        return self.wg.at[pl.ds(pl.multiple_of(owner * self.depth, 128), self.depth), pl.ds(pl.multiple_of(slot * self.cols, 128), self.cols)]

    def round(self, w_ref, wide, sem):
        part = wide.shape[1]
        parts = self.depth // part

        def load(n):
            return pltpu.make_async_copy(w_ref.at[pl.ds(pl.multiple_of(n * part, 16), part)], wide.at[lax.rem(n, 2)], sem.at[lax.rem(n, 2)])

        def one(n):
            @pl.when(n + 1 < 2 * parts)
            def _():
                load(n + 1).start()
            load(n).wait()

            def strip(i):
                rows = pl.ds(pl.multiple_of(i * 16, 16), 16)
                to = pl.ds(pl.multiple_of(lax.rem(n, parts) * part + i * 16, 16), 16)
                self.low[n // parts, to] = wide[lax.rem(n, 2), rows].astype(jnp.bfloat16)
            loop(part // 16, strip)
        load(jnp.int32(0)).start()
        loop(2 * parts, one)

    def send_own(self, kind, slot):
        s = self.spot
        k = s.core ^ slot
        return pltpu.make_async_remote_copy(
            src_ref=self.low.at[k], dst_ref=self.block(s.dp, slot), send_sem=self.send.at[kind, slot], recv_sem=self.recv.at[kind, slot],
            device_id=s.at((s.others[0], s.others[1], s.dp)[kind], k), device_id_type=MESH)

    def send_on(self, kind):
        s = self.spot
        ref = self.block(s.others[kind], kind)
        return pltpu.make_async_remote_copy(
            src_ref=ref, dst_ref=ref, send_sem=self.send.at[3, kind], recv_sem=self.recv.at[3, kind],
            device_id=s.at(s.others[1 - kind], s.core), device_id_type=MESH)

    def arrive(self, kind, slot):
        owner = (self.spot.others[0], self.spot.others[1], self.spot.dp)[kind]
        wait_for(self.block(owner, slot), self.recv.at[kind, slot], self.send.at[kind, slot])

    def own(self):
        return pltpu.make_async_copy(self.low.at[self.spot.core], self.block(self.spot.dp, 0), self.own_sem)

    def start(self):
        self.own().start()
        for slot in (0, 1):
            self.send_own(0, slot).start()
            self.send_own(1, 1 - slot).start()
        self.send_own(2, 1).start()

    def relay(self):
        for kind in (0, 1):
            self.arrive(kind, kind)
            self.send_on(kind).start()

    def finish(self):
        for kind in (0, 1):
            self.arrive(kind, 1 - kind)
            wait_for(self.block(self.spot.others[2], kind), self.recv.at[3, kind], self.send.at[3, kind])
        self.arrive(2, 1)
        self.own().wait()

    def settle(self):
        for kind in (0, 1):
            for slot in (0, 1):
                self.send_own(kind, slot).wait_send()
            self.send_on(kind).wait_send()
        self.send_own(2, 1).wait_send()


class Products:
    def __init__(self, spot, features, wg, f_tile, w_tile, acc, theirs, f_sem, w_sem, send, recv):
        self.spot, self.features, self.wg, self.f_tile, self.w_tile, self.acc, self.theirs = spot, features, wg, f_tile, w_tile, acc, theirs
        self.f_sem, self.w_sem, self.send, self.recv = f_sem, w_sem, send, recv
        self.cols = theirs.shape[1]

    def shard(self, j):
        return jnp.where(self.spot.chip == self.spot.steps, self.spot.steps - j, j)

    def load_w(self, j):
        depth = self.features.depth
        rows = pl.ds(pl.multiple_of(self.shard(j) * depth, 128), depth)
        return pltpu.make_async_copy(self.wg.at[rows], self.w_tile.at[lax.rem(j, 2)], self.w_sem.at[lax.rem(j, 2)])

    def load_f(self, j):
        lanes = self.features.lanes(self.shard(j))
        return pltpu.make_async_copy(self.features.fg.at[:, lanes], self.f_tile.at[lax.rem(j, 2)], self.f_sem.at[lax.rem(j, 2)])

    def here(self, j):
        return (j < self.spot.steps) | jnp.logical_not(self.spot.ends)

    def add(self, slot, rows):
        for col in range(0, 2 * self.cols, self.cols):
            lanes = pl.ds(col, self.cols)
            self.acc[rows, lanes] += jnp.dot(self.f_tile[slot, rows], self.w_tile[slot, :, lanes], preferred_element_type=jnp.float32)

    def multiply(self):
        def unit(j):
            @pl.when(j < self.spot.steps)
            def _():
                self.load_w(j + 1).start()

            @pl.when((j < self.spot.steps) & self.here(j + 1))
            def _():
                self.load_f(j + 1).start()
            self.load_w(j).wait()

            @pl.when(self.here(j))
            def _():
                self.load_f(j).wait()
                loop(self.acc.shape[0] // self.features.size, lambda q: self.add(lax.rem(j, 2), self.features.rows(q)))
        self.load_w(jnp.int32(0)).start()
        self.load_f(jnp.int32(0)).start()
        loop(self.spot.chips, unit)

    def swap(self, q):
        rows = self.features.rows(q)
        return pltpu.make_async_remote_copy(
            src_ref=self.acc.at[rows, pl.ds(self.cols, self.cols)], dst_ref=self.theirs.at[rows], send_sem=self.send.at[q],
            recv_sem=self.recv.at[q], device_id=self.spot.at(self.spot.dp, 1 - self.spot.core), device_id_type=MESH)

    def complete(self, q):
        slot = self.spot.steps % 2
        self.features.arrive(self.spot.steps - 1, q)

        @pl.when(self.spot.ends)
        def _():
            rows = self.features.rows(q)
            copy = pltpu.make_async_copy(self.features.fg.at[rows, self.features.lanes(self.shard(self.spot.steps))],
                                         self.f_tile.at[slot, rows], self.f_sem.at[slot])
            copy.start()
            copy.wait()
            self.add(slot, rows)
        self.swap(q).start()


class Backward:
    def __init__(self, spot, size, dz_here, dz_ref, send, recv, out_sem):
        self.spot, self.size, self.dz_here, self.dz_ref, self.send, self.recv, self.out_sem = spot, size, dz_here, dz_ref, send, recv, out_sem
        self.cols = dz_here.shape[1]

    def rows(self, q):
        return pl.ds(pl.multiple_of(q * self.size, 16), self.size)

    def swap(self, q):
        return pltpu.make_async_remote_copy(
            src_ref=self.dz_here.at[self.rows(q)], dst_ref=self.dz_ref.at[self.rows(q), pl.ds(self.cols, self.cols)],
            send_sem=self.send.at[q], recv_sem=self.recv.at[q], device_id=self.spot.at(self.spot.dp, 1 - self.spot.core), device_id_type=MESH)

    def keep(self, q):
        return pltpu.make_async_copy(self.dz_here.at[self.rows(q)], self.dz_ref.at[self.rows(q), pl.ds(0, self.cols)], self.out_sem.at[q])

    def start(self, q):
        self.swap(q).start()
        self.keep(q).start()

    def settle(self, q):
        self.swap(q).wait_recv()
        self.swap(q).wait_send()
        self.keep(q).wait()


def gelu_and_slope(v):
    factor, cubic = math.sqrt(2.0 / math.pi), 0.044715
    square = v * v
    th = jnp.tanh(factor * (v + cubic * (square * v)))
    slope = 0.5 * (1.0 + th) + 0.5 * v * (1.0 - th * th) * (factor * (1.0 + 3.0 * cubic * square))
    return 0.5 * v * (1.0 + th), slope


def live_rows_of(tot, share, live):
    keep = share[0][0]
    cols = live.shape[1]

    def strip(i):
        row = lax.broadcasted_iota(jnp.int32, (16, cols), 0).astype(jnp.float32) + (i * 16).astype(jnp.float32)
        here = jnp.where(row < tot[0, :1, :cols], 1.0, 0.0)
        there = jnp.zeros_like(here)
        for kind in range(4):
            count = tot[kind, :1, :cols]
            slot = row + float(share[kind][0] - keep)
            valid = (slot < count) & (count > keep)
            if kind == 3:
                valid = valid & (slot >= share[2][0] + share[2][1])
            there = there + jnp.where(valid, 1.0, 0.0)
        live[pl.ds(pl.multiple_of(i * 16, 16), 16)] = jnp.where(row < keep, here, there)
    loop(live.shape[0] // 16, strip)


def clear(ref):
    def strip(i):
        ref[pl.ds(pl.multiple_of(i * 16, 16), 16)] = jnp.zeros((16, ref.shape[1]), ref.dtype)
    loop(ref.shape[0] // 16, strip)


def fold(term):
    return term[:8] + term[8:]


class Grads:
    jobs, thirds = 8, 3

    def __init__(self, spot, fg, dz_here, gr, pg, relay, f_part, g_part, r_part, f_sem, g_sem, r_sem, send, recv, relay_send, relay_recv, own_sem):
        self.spot, self.fg, self.dz_here, self.gr, self.pg, self.relay_ref = spot, fg, dz_here, gr, pg, relay
        self.f_part, self.g_part, self.r_part, self.f_sem, self.g_sem, self.r_sem = f_part, g_part, r_part, f_sem, g_sem, r_sem
        self.send, self.recv, self.relay_send, self.relay_recv, self.own_sem = send, recv, relay_send, relay_recv, own_sem
        self.depth, self.cols = pg.shape[1], pg.shape[2]
        self.part = self.depth // self.thirds

    def owner_of(self, m):
        return jnp.where(m < 2, 3, jnp.where((m == 4) | (m == 5), 0, jnp.where((m == 2) | (m == 7), 1, 2)))

    def third(self, n):
        return pl.ds(pl.multiple_of(lax.rem(n, self.thirds) * self.part, 128), self.part)

    def load(self, n):
        first = (self.spot.dp ^ self.owner_of(n // self.thirds)) * self.depth + lax.rem(n, self.thirds) * self.part
        return pltpu.make_async_copy(self.fg.at[:, pl.ds(pl.multiple_of(first, 128), self.part)], self.f_part.at[lax.rem(n, 2)],
                                     self.f_sem.at[lax.rem(n, 2)])

    def store(self, n):
        return pltpu.make_async_copy(self.g_part.at[lax.rem(n, 2)], self.pg.at[n // self.thirds, self.third(n)], self.g_sem.at[lax.rem(n, 2)])

    def relay(self, m):
        return pltpu.make_async_remote_copy(
            src_ref=self.pg.at[m], dst_ref=self.relay_ref.at[m], send_sem=self.relay_send.at[m], recv_sem=self.relay_recv.at[m],
            device_id=self.spot.at(self.spot.dp ^ (m + 1), self.spot.core), device_id_type=MESH)

    def relayed(self, n):
        return pltpu.make_async_copy(self.relay_ref.at[jnp.maximum(n // self.thirds - (self.jobs - 2), 0), self.third(n)],
                                     self.r_part.at[lax.rem(n, 2)], self.r_sem.at[lax.rem(n, 2)])

    def job(self, m):
        joins = m >= self.jobs - 2
        lanes = pl.ds(pl.multiple_of(lax.rem(m, 2) * self.cols, 128), self.cols)

        @pl.when(joins)
        def _():
            k = jnp.maximum(m - (self.jobs - 2), 0)
            wait_for(self.relay_ref.at[k], self.relay_recv.at[k], self.relay_send.at[k])
            self.relayed(m * self.thirds).start()

        def part(c):
            n = m * self.thirds + c

            @pl.when(joins & (c + 1 < self.thirds))
            def _():
                self.relayed(n + 1).start()

            @pl.when(n + 1 < self.jobs * self.thirds)
            def _():
                self.load(n + 1).start()
            self.load(n).wait()

            @pl.when((n >= 2) & (n != (self.jobs - 2) * self.thirds) & (n != (self.jobs - 2) * self.thirds + 1))
            def _():
                self.store(n - 2).wait()

            @pl.when(joins)
            def _():
                self.relayed(n).wait()
            value = lax.dot_general(self.f_part[lax.rem(n, 2)], self.dz_here[:, lanes], (((0,), (0,)), ((), ())),
                                    preferred_element_type=jnp.float32)

            @pl.when(joins)
            def _():
                self.g_part[lax.rem(n, 2)] = (value + self.r_part[lax.rem(n, 2)].astype(jnp.float32)).astype(jnp.bfloat16)

            @pl.when(jnp.logical_not(joins))
            def _():
                self.g_part[lax.rem(n, 2)] = value.astype(jnp.bfloat16)
            self.store(n).start()
        loop(self.thirds, part)

    def copy(self, m):
        away, k = self.owner_of(m), self.spot.core ^ lax.rem(m, 2)
        return pltpu.make_async_remote_copy(
            src_ref=self.pg.at[m], dst_ref=self.gr.at[away, self.spot.core], send_sem=self.send.at[m],
            recv_sem=self.recv.at[away, self.spot.core], device_id=self.spot.at(self.spot.dp ^ away, k), device_id_type=MESH)

    def own(self):
        return pltpu.make_async_copy(self.pg.at[4], self.gr.at[0, self.spot.core], self.own_sem)

    def start(self, m):
        @pl.when(m < 2)
        def _():
            self.relay(jnp.minimum(m, 1)).start()

        @pl.when((m >= 2) & (m != 4))
        def _():
            self.copy(m).start()

        @pl.when(m == 4)
        def _():
            self.own().start()

    def turn(self, m, begin, late):
        early = self.jobs - 2
        pause = begin + early

        def job_at(m):
            return jnp.where(m < pause, m - begin, m - late + early)

        @pl.when((m == pause) | (m == late + 2))
        def _():
            for c in (1, 2):
                self.store(job_at(m - 1) * self.thirds + c).wait()

        @pl.when(((m >= begin) & (m < pause)) | (m == late) | (m == late + 1))
        def _():
            self.job(job_at(m))

        @pl.when(((m > begin) & (m <= pause)) | (m == late + 1) | (m == late + 2))
        def _():
            self.start(job_at(m - 1))

    def settle(self):
        for away in range(3):
            for k in (0, 1):
                @pl.when((away != 0) | (self.spot.core != k))
                def _():
                    wait_for(self.gr.at[away, k], self.recv.at[away, k], self.send.at[2])
        self.own().wait()
        for m in range(self.jobs):
            if m < 2:
                self.relay(m).wait_send()
            elif m != 4:
                self.copy(jnp.int32(m)).wait_send()


class Sums:
    window, lag = 5, 1

    def __init__(self, spot, parts, share, d_ref, dz_here, w_here, held, total, send, recv, out_sem, back_send, back_recv):
        self.spot, self.parts, self.share, self.d_ref, self.dz_here, self.w_here, self.held, self.total = spot, parts, share, d_ref, dz_here, w_here, held, total
        self.send, self.recv, self.out_sem, self.back_send, self.back_recv = send, recv, out_sem, back_send, back_recv
        self.size, self.depth = total.shape[1], total.shape[2]
        self.turns = spot.steps * parts
        self.skip = self.size - share[0][1]

    def rows(self, piece):
        return pl.ds(pl.multiple_of(lax.rem(piece + self.parts - 1, self.parts) * self.size, 16), self.size)

    def third(self, n):
        return pl.ds(pl.multiple_of(n * (self.depth // 3), 128), self.depth // 3)

    def sends(self, step, way):
        return (self.spot.passed(way) < self.spot.steps) & (self.spot.passed(way) <= step)

    def passing(self, m, way, turn):
        rows = self.rows(lax.rem(m, self.parts))
        return pltpu.make_async_remote_copy(
            src_ref=self.held.at[way, turn // self.parts, rows], dst_ref=self.held.at[way, m // self.parts, rows],
            send_sem=self.send.at[way, m], recv_sem=self.recv.at[way, m], device_id=self.spot.on_line(self.spot.onward(way, 1)),
            device_id_type=MESH)

    def landed(self, m, way):
        wait_for(self.held.at[way, m // self.parts, self.rows(lax.rem(m, self.parts))], self.recv.at[way, m], self.send.at[way, m])

    def product(self, goal, rows, col):
        return lax.dot_general(self.dz_here[rows], self.w_here[goal, self.third(col)], (((1,), (1,)), ((), ())),
                               preferred_element_type=jnp.float32)

    def store(self, piece):
        s = lax.rem(piece, 2)
        return pltpu.make_async_copy(self.total.at[s], self.d_ref.at[self.rows(piece)], self.out_sem.at[s])

    def hand(self, kind):
        to, taken = share_rows(self.share, kind)
        return pltpu.make_async_remote_copy(
            src_ref=self.total.at[0, pl.ds(self.skip + taken.start, taken.size)], dst_ref=self.d_ref.at[to], send_sem=self.back_send.at[kind],
            recv_sem=self.back_recv.at[kind], device_id=self.spot.at(self.spot.others[kind], self.spot.core), device_id_type=MESH)

    def send_sum(self, m, way):
        step, rows = m // self.parts, self.rows(lax.rem(m, self.parts))
        first = self.spot.passed(way) == 0
        held = self.held

        @pl.when(first & (m >= self.window))
        def _():
            self.passing(jnp.maximum(m - self.window, 0), way, 0).wait_send()

        @pl.when(jnp.logical_not(first))
        def _():
            self.landed(m - self.parts, way)

        def column(col):
            lanes = self.third(col)
            value = self.product(self.spot.onward(way, self.spot.steps - step), rows, col)

            @pl.when(first)
            def _():
                held[way, step, rows, lanes] = value.astype(jnp.bfloat16)

            @pl.when(jnp.logical_not(first))
            def _():
                held[way, step - 1, rows, lanes] = (value + held[way, step - 1, rows, lanes].astype(jnp.float32)).astype(jnp.bfloat16)
        loop(3, column)
        self.passing(m, way, jnp.where(first, m, m - self.parts)).start()

    def finish(self, piece):
        rows, s = self.rows(piece), lax.rem(piece, 2)
        held, total, last = self.held, self.total, self.spot.steps - 1

        @pl.when(piece >= 2)
        def _():
            self.store(piece - 2).wait()

        @pl.when(piece == 2)
        def _():
            for kind in range(3):
                self.hand(kind).wait_send()

        def each(way):
            @pl.when(self.spot.passed(way) > 0)
            def _():
                self.landed(self.turns - self.parts + piece, way)
        loop(2, each)

        def column(col):
            value = self.product(self.spot.chip, rows, col)
            lanes = self.third(col)

            @pl.when(self.spot.ends)
            def _():
                way = jnp.where(self.spot.chip == 0, 1, 0)
                total[s, :, lanes] = (value + held[way, last, rows, lanes].astype(jnp.float32)).astype(jnp.bfloat16)

            @pl.when(jnp.logical_not(self.spot.ends))
            def _():
                total[s, :, lanes] = (value + held[0, last, rows, lanes].astype(jnp.float32)
                                      + held[1, last, rows, lanes].astype(jnp.float32)).astype(jnp.bfloat16)
        loop(3, column)
        self.store(piece).start()

        @pl.when(piece == 0)
        def _():
            for kind in (2, 0, 1):
                self.hand(kind).start()

    def turn(self, m):
        def each(way):
            @pl.when((m < self.turns) & self.sends(m // self.parts, way))
            def _():
                self.send_sum(m, way)
        loop(2, each)

    def turn_end(self, m):
        first = self.turns - self.parts + self.lag

        @pl.when((m >= first) & (m < first + self.parts))
        def _():
            self.finish(m - first)

    def settle(self):
        def drain(m):
            def each(way):
                first = self.spot.passed(way) == 0

                @pl.when(self.sends(m // self.parts, way) & (jnp.logical_not(first) | (m >= self.turns - self.window)))
                def _():
                    self.passing(m, way, 0).wait_send()
            loop(2, each)
        loop(self.turns, drain)
        for piece in (self.parts - 2, self.parts - 1):
            self.store(piece).wait()

    def returned(self):
        for kind in range(3):
            self.hand(kind).wait_recv()


def share_rows(share, kind):
    skip = share[2][0] + share[2][1] - share[3][0] if kind == 2 else 0
    first, length = share[1 + kind]
    return pl.ds(first + skip, length - skip), pl.ds(skip, length - skip)


class Bases:
    def __init__(self, left, right, out, held, parts, load_sem, store_sem):
        self.sources, self.out, self.held, self.parts, self.load_sem, self.store_sem = (left, right), out, held, parts, load_sem, store_sem
        self.groups, self.pairs = left.shape[1], left.shape[2] // 2
        self.units = left.shape[0] * self.groups

    def at(self, u):
        return u // self.groups, lax.rem(u, self.groups), lax.rem(u, 2)

    def load(self, u, start):
        t, r, slot = self.at(u)
        for n, source in enumerate(self.sources):
            copy = pltpu.make_async_copy(source.at[t, r], self.held.at[slot, n], self.load_sem.at[slot, n])
            (copy.start if start else copy.wait)()

    def store(self, u, start):
        t, r, slot = self.at(u)
        for n in (0, 1):
            copy = pltpu.make_async_copy(self.parts.at[slot, n], self.out.at[n, t, r], self.store_sem.at[slot, n])
            (copy.start if start else copy.wait)()

    def unit(self, u):
        @pl.when(u + 1 < self.units)
        def _():
            self.load(u + 1, True)
        self.load(u, False)

        @pl.when(u >= 2)
        def _():
            self.store(u - 2, False)
        slot = lax.rem(u, 2)
        for n in (0, 1):
            for q in range(self.pairs):
                both = jnp.concatenate([self.held[slot, n, 2 * q], self.held[slot, n, 2 * q + 1]], axis=1)
                high, low = split(both)
                rows = pl.ds(q * BLOCK, BLOCK)
                self.parts[slot, n, 0, rows] = high
                self.parts[slot, n, 1, rows] = low
        self.store(u, True)

    def some(self, first, count):
        def one(i):
            @pl.when(first + i < self.units)
            def _():
                self.unit(first + i)
        loop(count, one)

    def settle(self):
        for u in (self.units - 2, self.units - 1):
            self.store(jnp.int32(u), False)


class Stitched:
    def __init__(self, spot, share, y_ref, st_ref, y_send, y_recv, core_send, core_recv, give_send, give_recv, given_send, given_recv, own_sem):
        self.spot, self.share, self.y_ref, self.st_ref = spot, share, y_ref, st_ref
        self.y_send, self.y_recv, self.core_send, self.core_recv = y_send, y_recv, core_send, core_recv
        self.give_send, self.give_recv, self.given_send, self.given_recv, self.own_sem = give_send, give_recv, given_send, given_recv, own_sem
        self.towers, self.cols = y_ref.shape[0], y_ref.shape[2]
        self.bands = (share[0], (0, share[0][0]))
        self.events = 2 * self.towers * spot.steps

    def lanes(self, shard, k):
        return pl.ds(pl.multiple_of((2 * shard + k) * self.cols, 128), self.cols)

    def place(self, shard, k, t, b):
        return self.st_ref.at[t, pl.ds(*self.bands[b]), self.lanes(shard, k)]

    def source(self, t, b):
        return self.y_ref.at[t, pl.ds(*self.bands[b])]

    def leave(self, step, way, t, b, own=False):
        s = self.spot
        dst = self.place(s.onward(way, -step), s.core, t, b)
        return pltpu.make_async_remote_copy(
            src_ref=self.source(t, b) if own else dst, dst_ref=dst, send_sem=self.y_send.at[way, step, b, t],
            recv_sem=self.y_recv.at[way, step, b, t], device_id=s.on_line(s.onward(way, 1)), device_id_type=MESH)

    def to_core(self, shard, t, b, own=False):
        s = self.spot
        dst = self.place(shard, s.core, t, b)
        return pltpu.make_async_remote_copy(
            src_ref=self.source(t, b) if own else dst, dst_ref=dst, send_sem=self.core_send.at[shard, b, t],
            recv_sem=self.core_recv.at[shard, b, t], device_id=s.at(s.dp, 1 - s.core), device_id_type=MESH)

    def give(self, kind, shard, t, own=False):
        s = self.spot
        to, taken = share_rows(self.share, kind)
        src = pl.ds(self.share[0][0] + taken.start, taken.size)
        return pltpu.make_async_remote_copy(
            src_ref=self.y_ref.at[t, src] if own else self.st_ref.at[t, src, self.lanes(shard, s.core)],
            dst_ref=self.st_ref.at[t, to, self.lanes(shard, s.core)], send_sem=self.give_send.at[kind, shard, t],
            recv_sem=self.give_recv.at[kind, shard, t], device_id=s.at(s.others[kind], s.core), device_id_type=MESH)

    def given_place(self, kind, shard, t, k):
        return self.st_ref.at[t, share_rows(self.share, kind)[0], self.lanes(shard, k)]

    def given(self, kind, shard, t):
        s = self.spot
        ref = self.given_place(kind, shard, t, s.core)
        return pltpu.make_async_remote_copy(
            src_ref=ref, dst_ref=ref, send_sem=self.given_send.at[kind, shard, t], recv_sem=self.given_recv.at[kind, shard, t],
            device_id=s.at(s.dp, 1 - s.core), device_id_type=MESH)

    def own(self, t, b):
        return pltpu.make_async_copy(self.source(t, b), self.place(self.spot.chip, self.spot.core, t, b), self.own_sem.at[b, t])

    def start(self):
        for b in (0, 1):
            def tower(t):
                def each(way):
                    @pl.when(self.spot.leaves(0, way))
                    def _():
                        self.leave(0, way, t, b, True).start()
                loop(2, each)
                self.to_core(self.spot.chip, t, b, True).start()
                if b == 0:
                    for kind in (2, 0, 1):
                        self.give(kind, self.spot.chip, t, True).start()
                self.own(t, b).start()
            loop(self.towers, tower)

    def event(self, n):
        step, t = n // (2 * self.towers), lax.rem(n, self.towers)
        for b in (0, 1):
            def each(way):
                @pl.when(self.spot.comes(step, way))
                def _():
                    shard = self.spot.onward(way, -1 - step)
                    wait_for(self.place(shard, self.spot.core, t, b), self.y_recv.at[way, step, b, t], self.y_send.at[way, step, b, t])

                    @pl.when((step + 1 < self.spot.steps) & self.spot.leaves(step + 1, way))
                    def _():
                        self.leave(jnp.minimum(step + 1, self.spot.steps - 1), way, t, b).start()
                    self.to_core(shard, t, b).start()
                    if b == 0:
                        for kind in (2, 0, 1):
                            self.give(kind, shard, t).start()

            @pl.when(lax.rem(n, 2 * self.towers) // self.towers == b)
            def _():
                loop(2, each)

    def receive(self):
        def one(n):
            shard, t = n // self.towers, lax.rem(n, self.towers)
            for kind in range(3):
                wait_for(self.given_place(kind, shard, t, self.spot.core), self.give_recv.at[kind, shard, t], self.give_send.at[kind, shard, t])
                self.given(kind, shard, t).start()
        loop(self.spot.chips * self.towers, one)

    def settle(self):
        def one(n):
            shard, t = n // self.towers, lax.rem(n, self.towers)
            for b in (0, 1):
                wait_for(self.place(shard, 1 - self.spot.core, t, b), self.core_recv.at[shard, b, t], self.core_send.at[shard, b, t])
                self.to_core(shard, t, b).wait_send()

                @pl.when(shard < self.spot.steps)
                def _():
                    def each(way):
                        @pl.when(self.spot.leaves(shard, way))
                        def _():
                            self.leave(jnp.minimum(shard, self.spot.steps - 1), way, t, b).wait_send()
                    loop(2, each)
            for kind in range(3):
                self.give(kind, shard, t).wait_send()
                self.given(kind, shard, t).wait_send()
                wait_for(self.given_place(kind, shard, t, 1 - self.spot.core), self.given_recv.at[kind, shard, t], self.given_send.at[kind, shard, t])
        loop(self.spot.chips * self.towers, one)
        for t in range(self.towers):
            for b in (0, 1):
                self.own(t, b).wait()


def front_kernel(chips, parts, share, f_ref, w_ref, o_ref, n_ref, sp_ref, left_ref, right_ref,
                 fg_first, wg_first, dz_first, fg_ref, wg_ref, dz_ref, tot_ref, bases_ref, st_ref, sr_ref,
                 d_first, gr_first, pg_first, relay_first, d_ref, gr_ref, pg_ref, relay_ref,
                 offer_f, taken, offer_o, wide, low, base_in, base_out, tot,
                 og, f_tile, w_tile, acc, theirs, live, act, dz_here, y_here, sums_here, sg,
                 held, w_here, dz_wide, total, f_part, g_part, r_part,
                 f_send, f_recv, w_send, w_recv, a_send, a_recv, z_send, z_recv, out_sem,
                 wide_sem, p_sem, x_send, x_recv, l_sem, base_load, base_store,
                 d_send, d_recv, o_sem, b_send, b_recv, g_load, g_send, g_recv, rs_send, rs_recv, own_sem, s_send, s_recv, ready,
                 y_send, y_recv, core_send, core_recv, give_send, give_recv, given_send, given_recv, y_own):
    spot = Spot(chips)
    keep, rows = share[0][0], sum(share[0])
    size = rows // parts
    fixed = rows - size
    spare = keep - fixed
    cols = o_ref.shape[2]
    tot[0] = jnp.zeros_like(tot[0]) + jnp.sum(n_ref[...].astype(jnp.float32), axis=1, keepdims=True)
    spot.greet()

    def offer(kind, what):
        src = (f_ref.at[0], f_ref.at[1], o_ref, tot.at[0])[what]
        dst = (offer_f.at[0, 1 + kind], offer_f.at[1, 1 + kind], offer_o.at[1 + kind], tot.at[1 + kind])[what]
        if what < 3:
            src = src.at[pl.ds(*share[1 + kind])] if what < 2 else src.at[:, pl.ds(*share[1 + kind])]
        return pltpu.make_async_remote_copy(
            src_ref=src, dst_ref=dst, send_sem=x_send.at[what, kind], recv_sem=x_recv.at[what, kind],
            device_id=spot.at(spot.others[kind], spot.core), device_id_type=MESH)

    def choose(width, read, write):
        weigh = [jnp.broadcast_to(jnp.where(tot[kind, :1, :width] > keep, 1.0, 0.0), (16, width)) for kind in range(4)]

        def strip(i):
            at = pl.ds(pl.multiple_of(i * 16, 16), 16)
            value = read(0, at).astype(jnp.float32) * weigh[0]
            for kind in range(1, 4):
                value = value + read(kind, at).astype(jnp.float32) * weigh[kind]
            write(i * 16, value.astype(jnp.bfloat16))
        loop(share[0][1] // 16, strip)

    def take(t):
        def write(row, value):
            taken[t, pl.ds(pl.multiple_of(spare + row, 16), 16)] = value
        choose(offer_f.shape[3], lambda kind, at: offer_f[t, kind, at], write)

    towers = []
    for t, (fg, wg, dz) in enumerate(((fg_first, wg_first, dz_first), (fg_ref, wg_ref, dz_ref))):
        features = Features(spot, f_ref.at[t], taken.at[t], fg, size, f_send.at[t], f_recv.at[t])
        weights = Weights(spot, low.at[t], wg, p_sem.at[t, 4], w_send.at[t], w_recv.at[t])
        products = Products(spot, features, wg, f_tile, w_tile, acc, theirs.at[t], p_sem.at[t, pl.ds(0, 2)], p_sem.at[t, pl.ds(2, 2)],
                            a_send.at[t], a_recv.at[t])
        backward = Backward(spot, size, dz_here, dz, z_send.at[t], z_recv.at[t], out_sem.at[t])
        towers.append((features, weights, products, backward))
    features, weights, products, backward = towers[0]
    sums = []
    for t, (fg, d, gr, pg, relay) in enumerate(((fg_first, d_first, gr_first, pg_first, relay_first), (fg_ref, d_ref, gr_ref, pg_ref, relay_ref))):
        sums.append((Sums(spot, parts, share, d, dz_wide, w_here, held, total, d_send.at[t], d_recv.at[t], o_sem, b_send.at[t], b_recv.at[t]),
                     Grads(spot, fg, dz_wide, gr, pg, relay, f_part, g_part, r_part, g_load.at[0], g_load.at[1], g_load.at[2],
                           g_send.at[t], g_recv.at[t], rs_send.at[t], rs_recv.at[t], own_sem.at[t])))
    gradients, grads = sums[0]
    stitched = Stitched(spot, share, y_here, st_ref, y_send, y_recv, core_send, core_recv, give_send, give_recv, given_send, given_recv, y_own)
    bases = Bases(left_ref, right_ref, bases_ref, base_in, base_out, base_load, base_store)

    def copy(n, src, dst):
        made = pltpu.make_async_copy(src, dst, l_sem.at[n])
        made.start()
        return made

    for what in (3, 0):
        for kind in (2, 0, 1):
            offer(kind, what).start()
    loop(parts - 1, lambda q: features.launch(q, False))
    needed = [copy(0, f_ref.at[0, pl.ds(*share[0])], offer_f.at[0, 0])]
    later = [copy(1, f_ref.at[1, pl.ds(*share[0])], offer_f.at[1, 0])]
    if spare:
        needed.append(copy(2, f_ref.at[0, pl.ds(fixed, spare)], taken.at[0, pl.ds(0, spare)]))
        later.append(copy(3, f_ref.at[1, pl.ds(fixed, spare)], taken.at[1, pl.ds(0, spare)]))
    later += [copy(4, o_ref.at[:, pl.ds(*share[0])], offer_o.at[0]), copy(5, o_ref.at[:, pl.ds(0, keep)], og.at[:, pl.ds(0, keep)]),
              copy(6, f_ref.at[0, pl.ds(0, fixed)], fg_first.at[pl.ds(0, fixed), features.lanes(spot.chip)]),
              copy(7, f_ref.at[1, pl.ds(0, fixed)], fg_ref.at[pl.ds(0, fixed), features.lanes(spot.chip)])]
    weights.round(w_ref.at[0], wide, wide_sem)
    weights.start()
    for made in needed:
        made.wait()
    for what in (3, 0):
        for kind in range(3):
            offer(kind, what).wait_recv()
    take(0)
    features.launch(parts - 1, True)
    later += [copy(8, tot, tot_ref), copy(9, taken.at[0], fg_first.at[pl.ds(fixed, size), features.lanes(spot.chip)])]
    live_rows_of(tot, share, live)
    clear(acc)
    sums_here[...] = jnp.zeros_like(sums_here)
    towers[1][1].round(w_ref.at[1], wide, wide_sem)
    share_of = -(-bases.units // (2 * parts))

    def serve(step, q):
        features.serve(step, q)
        bases.some((step * parts + q) * share_of, share_of)
    bases.load(jnp.int32(0), True)
    loop(parts, lambda q: serve(0, q))
    weights.relay()
    for what in (2, 1):
        for kind in (2, 0, 1):
            offer(kind, what).start()
    loop(parts, lambda q: serve(1, q))
    weights.finish()
    towers[1][1].start()
    for made in later:
        made.wait()
    products.multiply()
    for kind in range(3):
        offer(kind, 2).wait_recv()
    for t in range(2):
        def write(row, value):
            og[t, pl.ds(pl.multiple_of(keep + row, 16), 16)] = value
        choose(cols, lambda kind, at: offer_o[kind, t, at], write)

    def strip(t, at):
        activated, slope = gelu_and_slope(acc[at, :cols] + theirs[t, at] + sp_ref[t : t + 1])
        mask = live[at]
        dy = [og[n, at].astype(jnp.float32) * mask for n in range(2)]
        dz = slope * (sp_ref[2 + t : 3 + t] * dy[0] + sp_ref[4 + t : 5 + t] * dy[1])
        if t == 0:
            act[at] = activated
        else:
            other = act[at]
            for n in range(2):
                y_here[n, at] = ((sp_ref[2 + 2 * n : 3 + 2 * n] * other + sp_ref[3 + 2 * n : 4 + 2 * n] * activated) * mask).astype(jnp.bfloat16)
        dz_here[at] = dz.astype(jnp.bfloat16)
        for n, term in enumerate((dz, activated * dy[0], activated * dy[1])):
            sums_here[2 * n + t] += fold(term)

    def stage(t, k):
        _, _, products, backward = towers[t]

        @pl.when(k < parts)
        def _():
            products.complete(k)

        @pl.when(k > 0)
        def _():
            products.swap(k - 1).wait_recv()
            loop(size // 16, lambda i: strip(t, pl.ds(pl.multiple_of((k - 1) * size + i * 16, 16), 16)))
            backward.start(k - 1)
    loop(parts + 1, lambda k: stage(0, k))

    def settle(t, q):
        towers[t][0].settle(q)
        towers[t][2].swap(q).wait_send()
        towers[t][3].settle(q)
    for kind in range(3):
        offer(kind, 1).wait_recv()
    take(1)
    loop(parts, lambda q: settle(0, q))
    loads = weight_loads(chips, wg_first, w_here, l_sem.at[pl.ds(11, chips)])
    loads.append(copy(11 + chips, dz_first, dz_wide))
    features, weights, products, backward = towers[1]
    loop(parts - 1, lambda q: features.launch(q, False))
    features.launch(parts - 1, True)
    last = copy(0, taken.at[1], fg_ref.at[pl.ds(fixed, size), features.lanes(spot.chip)])
    grads.load(jnp.int32(0)).start()
    clear(acc)
    for made in loads:
        made.wait()

    def turn(m):
        gradients.turn(m)
        grads.turn(m, 2, 10)

        @pl.when(m == 2)
        def _():
            weights.relay()

        @pl.when((m >= 2) & (m < 2 + parts))
        def _():
            features.serve(0, m - 2)

        @pl.when((m >= 3 + parts) & (m < 3 + 2 * parts))
        def _():
            features.serve(1, m - 3 - parts)

        @pl.when(m == 4 + 2 * parts)
        def _():
            weights.finish()
            last.wait()
            products.multiply()
        gradients.turn_end(m)
    loop(gradients.turns + gradients.lag, turn)

    gradients.settle()

    def neighbours(method):
        for side, here, chip in ((0, spot.chip > 0, spot.chip - 1), (1, spot.chip < spot.steps, spot.chip + 1)):
            @pl.when(here)
            def _():
                method(side, chip)
    neighbours(lambda side, chip: pl.semaphore_signal(ready.at[1 - side], inc=1, device_id=spot.on_line(chip), device_id_type=MESH))
    loads = weight_loads(chips, wg_ref, w_here, l_sem.at[pl.ds(11, chips)])
    loop(parts + 1, lambda k: stage(1, k))
    stitched.start()
    sg[...] = jnp.zeros_like(sg)
    for n in range(6):
        sg[n : n + 1] = jnp.sum(sums_here[n], axis=0, keepdims=True)
    own = copy(1, sg, sr_ref.at[spot.dp])

    def small(kind):
        return pltpu.make_async_remote_copy(
            src_ref=sg, dst_ref=sr_ref.at[spot.dp], send_sem=s_send.at[kind], recv_sem=s_recv.at[kind],
            device_id=spot.at(spot.others[kind], spot.core), device_id_type=MESH)
    for kind in range(3):
        small(kind).start()
    loop(parts, lambda q: settle(1, q))
    wide_dz = copy(11 + chips, dz_ref, dz_wide)
    gradients, grads = sums[1]
    grads.load(jnp.int32(0)).start()
    for made in loads:
        made.wait()
    wide_dz.wait()
    neighbours(lambda side, chip: pl.semaphore_wait(ready.at[side], 1))

    def second_turn(m):
        gradients.turn(m)
        grads.turn(m, 0, 7)

        @pl.when((m >= 1) & (m <= stitched.events))
        def _():
            stitched.event(m - 1)
        gradients.turn_end(m)
    loop(gradients.turns + gradients.lag, second_turn)
    stitched.receive()
    gradients.settle()
    stitched.settle()
    for t in range(2):
        sums[t][0].returned()
        sums[t][1].settle()
        towers[t][1].settle()
    bases.settle()
    own.wait()
    for kind in range(3):
        small(kind).wait()
    for what in range(4):
        for kind in range(3):
            offer(kind, what).wait_send()


def weight_loads(chips, wg, w_here, sem):
    depth = w_here.shape[1]
    loads = [pltpu.make_async_copy(wg.at[pl.ds(n * depth, depth)], w_here.at[n], sem.at[n]) for n in range(chips)]
    for copy in loads:
        copy.start()
    return loads


def call(kernel, name, ident, out, scratch, operands, small_in=(), flops=0):
    anywhere, here = pl.BlockSpec(memory_space=pl.ANY), pl.BlockSpec(memory_space=pltpu.VMEM)
    return pl.pallas_call(
        kernel,
        out_shape=out,
        in_specs=[here if n in small_in else anywhere for n in range(len(operands))],
        out_specs=[anywhere] * len(out),
        scratch_shapes=scratch,
        compiler_params=pltpu.CompilerParams(collective_id=ident, has_side_effects=True, vmem_limit_bytes=62 * 2**20),
        cost_estimate=pl.CostEstimate(flops=flops, bytes_accessed=500 * 2**20, transcendentals=0),
        name=name,
    )(*operands)


def parts_of(share):
    rows = sum(share[0])
    return max(n for n in range(1, rows // 16) if rows % (16 * n) == 0 and rows // n >= share[0][1])


def shared_pass(features, weights, out_grad, counts, small_params, left, right, chips, share):
    parts = parts_of(share)
    towers, slots, depth = features.shape
    cols = weights.shape[2]
    keep, size = share[0]
    rows = keep + size
    steps = chips - 1
    piece = rows // parts
    dma, vmem = pltpu.SemaphoreType.DMA, pltpu.VMEM
    bf16, f32 = jnp.bfloat16, jnp.float32
    S = jax.ShapeDtypeStruct
    beside = (left.shape[2] // 2 * BLOCK, 2 * BLOCK)
    wide = [S((rows, chips * depth), bf16), S((chips * depth, 2 * cols), bf16), S((rows, 2 * cols), bf16)]
    sums = [S((slots, depth), bf16), S((3, 2, depth, cols), bf16), S((8, depth, cols), bf16), S((2, depth, cols), bf16)]
    out = call(
        functools.partial(front_kernel, chips, parts, share), "passes", 3,
        wide + wide + [S((4, 8, depth), f32), S((2,) + left.shape[:2] + (2,) + beside, bf16),
                       S((towers, slots, 2 * chips * cols), bf16), S((4, 8, cols), f32)] + sums + sums,
        [vmem((towers, 4, size, depth), bf16), vmem((towers, piece, depth), bf16), vmem((4, towers, size, cols), bf16),
         vmem((2, depth // 8, cols), f32), vmem((towers, 2, depth, cols), bf16), vmem((2, 2) + left.shape[2:], f32), vmem((2, 2, 2) + beside, bf16),
         vmem((4, 8, depth), f32), vmem((towers, rows, cols), bf16), vmem((2, rows, depth), bf16), vmem((2, depth, 2 * cols), bf16),
         vmem((rows, 2 * cols), f32), vmem((towers, rows, cols), f32), vmem((rows, cols), f32), vmem((rows, cols), f32), vmem((rows, cols), bf16),
         vmem((towers, rows, cols), bf16), vmem((6, 8, cols), f32), vmem((8, cols), f32),
         vmem((2, steps, rows, depth), bf16), vmem((chips, depth, 2 * cols), bf16), vmem((rows, 2 * cols), bf16),
         vmem((2, piece, depth), bf16), vmem((2, rows, depth // 3), bf16)] + [vmem((2, depth // 3, cols), bf16)] * 2
        + [dma((towers, 2, steps, parts))] * 2 + [dma((towers, 4, 2))] * 2 + [dma((towers, parts))] * 5
        + [dma((2,)), dma((towers, 5)), dma((4, 3)), dma((4, 3)), dma((12 + chips,)), dma((2, 2)), dma((2, 2))]
        + [dma((towers, 2, steps * parts))] * 2 + [dma((2,)), dma((towers, 3)), dma((towers, 3)), dma((3, 2)), dma((towers, 8)), dma((towers, 3, 2)),
                                                   dma((towers, 2)), dma((towers, 2)), dma((towers,)), dma((3,)), dma((3,)), pltpu.SemaphoreType.REGULAR((2,))]
        + [dma((2, steps, 2, towers))] * 2 + [dma((chips, 2, towers))] * 2 + [dma((3, chips, towers))] * 4 + [dma((2, towers))],
        (features, weights, out_grad, counts.reshape(1, -1), small_params, left, right), (3, 4), 6 * 2 * rows * 2 * cols * depth * chips)
    told, bases, stitched, smalls, d_first, gr_first, _, _, d_second, gr_second, _, _ = out[6:]
    return told, bases, ((d_first, d_second), stitched, (gr_first, gr_second), smalls)


def small_step(small_params, small_moment_one, small_moment_two, small_average, small_grad):
    first, second, direction = adam_part(small_moment_one, small_moment_two, small_grad)
    fresh = small_params - rate_small * direction
    return first, second, fresh, ema_decay * small_average + (1.0 - ema_decay) * fresh


def update(d_feat, stitched, full, parts, small_parts, states, small_states):
    small_grad = jnp.sum(small_parts, 0)[: small_states[0].shape[0]]
    *fresh, stitched, d_feat = soap(parts, full, stitched, d_feat, *states)
    return (stitched, d_feat) + tuple(fresh) + small_step(*small_states, small_grad)


def own_rows(features, out_grad, totals, passed, states, small_states):
    _, rows, _ = features.shape
    weights, small_params = states[0], small_states[0]
    cols = weights.shape[2]
    cores = lax.axis_size("mp")
    swap = [(i, i ^ 1) for i in range(cores)]
    ranges = ((0, rows // 2), (rows // 2, rows // 2))
    live_rows = (jnp.arange(rows, dtype=jnp.float32) < totals[0]).astype(jnp.float32)
    wide_f, wide_w = gather(features, weights.astype(jnp.bfloat16), cores // 2, ranges, 1)
    partial = jnp.einsum("tri,tio->tro", wide_f, wide_w, preferred_element_type=jnp.float32)
    product = partial[:, :, :cols] + lax.ppermute(partial[:, :, cols:], "mp", swap)
    result, back = jax.vjp(lambda a, b: stitch_local(a, b, live_rows), product, small_params)
    stitched = lax.all_gather(result.astype(jnp.bfloat16), "mp", axis=2, tiled=True)
    dz, small_part = back(out_grad.astype(jnp.float32))
    dz_low = dz.astype(jnp.bfloat16)
    wide_dz = jnp.concatenate([dz_low, lax.ppermute(dz_low, "mp", swap)], axis=2)
    partial_d = jnp.einsum("tro,tio->tri", wide_dz, wide_w, preferred_element_type=jnp.float32)
    partial_g = jnp.einsum("tri,tro->tio", wide_f, wide_dz, preferred_element_type=jnp.float32)
    small_part = jnp.pad(small_part, ((0, 2), (0, 0)))
    d_feat, parts, small_parts = reduce(
        partial_d.astype(jnp.bfloat16), partial_g.astype(jnp.bfloat16), small_part, cores // 2, ranges, 2
    )
    full = jnp.full((1,), rows, jnp.int32)
    return update((d_feat[0], d_feat[1]), stitched, full, (parts[:, :, 0], parts[:, :, 1]), small_parts, states, small_states)


def shares(rows):
    keep = rows * 15 // 32 // 16 * 16
    size = -(-(rows - keep) // 64) * 16
    return keep, ((keep, size), (keep + size, size), (keep + 2 * size, size), (rows - size, size))


def shared_rows(features, out_grad, totals, passed, states, small_states):
    rows = features.shape[1]
    keep, _ = shares(rows)
    d_feat, stitched, parts, small_parts = passed
    full = jnp.where(totals[:1] > keep, rows, keep)
    return update(d_feat, stitched, full, parts, small_parts, states, small_states)


def line_body(
    features,
    counts,
    weights,
    small_params,
    out_grad,
    moment_one,
    moment_two,
    average,
    basis_left,
    basis_right,
    small_moment_one,
    small_moment_two,
    small_average,
):
    keep, share = shares(features.shape[1])
    told, bases, passed = shared_pass(
        features, weights, out_grad, counts, small_params, basis_left, basis_right, lax.axis_size("mp") // 2, share
    )
    totals = told[:, 0, 0]
    return lax.cond(
        jnp.sum(totals > keep) == 1,
        shared_rows,
        own_rows,
        features,
        out_grad,
        totals,
        passed,
        (weights, moment_one, moment_two, average, bases),
        (small_params, small_moment_one, small_moment_two, small_average),
    )


def plain_body(
    features,
    counts,
    weights,
    small_params,
    out_grad,
    moment_one,
    moment_two,
    average,
    basis_left,
    basis_right,
    small_moment_one,
    small_moment_two,
    small_average,
):
    slot_count = features.shape[1]
    total = jnp.sum(counts)
    live_rows = (jnp.arange(slot_count, dtype=jnp.int32) < total).astype(jnp.float32)
    weights_low = lax.all_gather(weights.astype(jnp.bfloat16), "dp", axis=1, tiled=True)
    feats_full = lax.all_gather(features, "mp", axis=2, tiled=True)
    product = jnp.einsum(
        "tri,tio->tro", feats_full, weights_low, preferred_element_type=jnp.float32
    )
    result, back = jax.vjp(lambda a, b: stitch_local(a, b, live_rows), product, small_params)
    stitched = lax.all_gather(result.astype(jnp.bfloat16), "mp", axis=2, tiled=True)
    dz, small_part = back(out_grad.astype(jnp.float32))
    dz_low = dz.astype(jnp.bfloat16)
    grad_part = jnp.einsum("tri,tro->tio", feats_full, dz_low, preferred_element_type=jnp.float32)
    partial_sums = jnp.einsum(
        "tro,tio->tri", dz_low, weights_low, preferred_element_type=jnp.float32
    )
    d_feat = lax.psum_scatter(
        partial_sums.astype(jnp.float32), "mp", scatter_dimension=2, tiled=True
    )
    grad = lax.psum_scatter(grad_part, "dp", scatter_dimension=1, tiled=True)
    small_grad = lax.psum(small_part, "dp")
    towers, n_in, n_out = grad.shape
    blocks = grad.reshape(towers, n_in // BLOCK, BLOCK, n_out // BLOCK, BLOCK)
    rotated = jnp.einsum(
        "trcai,tracb,trcbj->tricj", basis_left, blocks, basis_right, precision=lax.Precision.HIGHEST
    ).reshape(towers, n_in, n_out)
    first, second, direction = adam_part(moment_one, moment_two, rotated)
    turned = direction.reshape(towers, n_in // BLOCK, BLOCK, n_out // BLOCK, BLOCK)
    step_back = jnp.einsum(
        "trcai,tricj,trcbj->tracb", basis_left, turned, basis_right, precision=lax.Precision.HIGHEST
    ).reshape(towers, n_in, n_out)
    new_weights = weights - rate_main * (step_back + decay_weight * weights)
    new_average = ema_decay * average + (1.0 - ema_decay) * new_weights
    return (
        stitched,
        d_feat.astype(jnp.bfloat16),
        first,
        second,
        new_weights,
        new_average,
        new_weights.astype(jnp.bfloat16),
    ) + small_step(small_params, small_moment_one, small_moment_two, small_average, small_grad)


def solution(mesh):
    def body(features, counts, weights, *rest):
        dp, mp = mesh.shape["dp"], mesh.shape["mp"]
        tiles = features.shape[2] % 128 == 0 and weights.shape[2] % 128 == 0
        suits = dp == 4 and mp == 2 * dp and tiles and features.shape[1] % 64 == 0
        return (line_body if suits else plain_body)(features, counts, weights, *rest)

    return jax.shard_map(
        body,
        mesh=mesh,
        in_specs=(
            P(None, "dp", "mp"),
            P("dp"),
            P(None, "dp", "mp"),
            P(None, "mp"),
            P(None, "dp", "mp"),
            P(None, "dp", "mp"),
            P(None, "dp", "mp"),
            P(None, "dp", "mp"),
            P(None, "dp", "mp", None, None),
            P(None, "dp", "mp", None, None),
            P(None, "mp"),
            P(None, "mp"),
            P(None, "mp"),
        ),
        out_specs=(
            P(None, "dp", None),
            P(None, "dp", "mp"),
            P(None, "dp", "mp"),
            P(None, "dp", "mp"),
            P(None, "dp", "mp"),
            P(None, "dp", "mp"),
            P(None, "dp", "mp"),
            P(None, "mp"),
            P(None, "mp"),
            P(None, "mp"),
            P(None, "mp"),
        ),
        check_vma=False,
    )
```
